32 devices in a mesh: gx: 8 (over z, x), gy: 4 (over y, core).
Axes of the slice: x: 2, y: 2, z: 4, core: 2. Of those that a mesh axis runs over, the one named last changes fastest.
Arguments:
- transcript_profiles: bfloat16 [24576, 7000], P(('gx', 'gy')), may hold values from -6 to 6
- experiment_labels: int32 [24576], P(('gx', 'gy')), may hold values from 0 to 7
- measured_flags: int32 [8, 7000], replicated, may hold values 0 or 1
- retained_unit_flags: int32 [4, 24576, 800], P(None, ('gx', 'gy')), may hold values 0 or 1
- standard_normal_draws: float32 [24576, 100], P(('gx', 'gy')), may hold values from -5 to 5
- compressor_first_matrix: bfloat16 [7000, 800], P('gy', 'gx'), may hold values from -0.0625 to 0.0625
- compressor_second_matrix: bfloat16 [800, 800], P('gy', 'gx'), may hold values from -0.21875 to 0.21875
- posterior_matrix: bfloat16 [800, 200], P('gx', 'gy'), may hold values from -0.21875 to 0.21875
- posterior_intercepts: bfloat16 [200], P('gy'), may hold values from -1.5 to 1.5
- expander_first_matrix: bfloat16 [100, 800], P(None, 'gx'), may hold values from -0.625 to 0.625
- expander_second_matrix: bfloat16 [800, 800], P('gy', 'gx'), may hold values from -0.21875 to 0.21875
- output_matrix: bfloat16 [800, 7000], P('gx', 'gy'), may hold values from -0.21875 to 0.21875
- output_intercept: bfloat16 [7000], P('gy'), may hold values from -1.5 to 1.5
- normalizer_factors: bfloat16 [4, 800], P(None, 'gx'), may hold values from 0.5 to 1.5
- normalizer_translations: bfloat16 [4, 800], P(None, 'gx'), may hold values from -1.5 to 1.5
Outputs:
- reconstruction: bfloat16 [24576, 7000], P(('gx', 'gy'))
- latent_mean: float32 [24576, 100], P(('gx', 'gy'))
- mean_loss: float32 [], replicated
- input_grad: bfloat16 [24576, 7000], P(('gx', 'gy'))
- embedding_grad: float32 [7000, 800], P('gy', 'gx')
- encoder_grad: float32 [800, 800], P('gy', 'gx')
- projector_grad: float32 [800, 200], P('gx', 'gy')
- offsets_grad: float32 [200], P('gy')
- lifting_grad: float32 [100, 800], P(None, 'gx')
- decoder_grad: float32 [800, 800], P('gy', 'gx')
- readout_grad: float32 [800, 7000], P('gx', 'gy')
- baseline_grad: float32 [7000], P('gy')
- scales_grad: float32 [4, 800], P(None, 'gx')
- shifts_grad: float32 [4, 800], P(None, 'gx')
The draws below stay inside these ranges and needn't reach their ends.
All inputs are finite; a program needn't handle non-finite values. No bound on the sum of `retained_unit_flags` on one device may be relied on, other than what follows from the above.
Results may differ from the reference program's by a relative error of at most 0.023.
Values may be sent and summed in bfloat16 or wider, within the bound.
A program may use at most 256 MiB of HBM per device.

```python
import jax
import jax.numpy as jnp
from jax import lax

GENE_COUNT = 7000
HIDDEN_SIZE = 800
LATENT = 100
EXPERIMENT_TOTAL = 8
BATCH_PROFILES = 24576


def place_ends(drawn, stream_key, least, high):
    dims = drawn.shape
    spot = [jax.random.randint(jax.random.fold_in(stream_key, axis), (), 0, dims[axis]) for axis in range(len(dims))]
    drawn = drawn.at[tuple(spot)].set(least)
    longest = dims.index(max(dims))
    spot[longest] = (spot[longest] + 1) % dims[longest]
    return drawn.at[tuple(spot)].set(high)


def block_scale(stream_key, shape, pieces, least, largest):
    factor_of, own = 1.0, jax.random.fold_in(stream_key, 6)
    for axis_at, shards_of in pieces:
        heights = jnp.exp(jax.random.uniform(jax.random.fold_in(own, axis_at), (shards_of,), jnp.float32, least / len(pieces), largest / len(pieces)))
        factor_of = factor_of * jnp.repeat(heights, shape[axis_at] // shards_of).reshape([-1 if axis == axis_at else 1 for axis in range(len(shape))])
    return factor_of


def normal_values(stream_key, extent, scale, bound, split=(), kind=jnp.bfloat16):
    entries = scale * jax.random.normal(stream_key, extent, jnp.float32)
    if split:
        entries = entries * block_scale(stream_key, extent, split, -0.22, 0.18)
    return jnp.clip(entries, -bound, bound).astype(kind)


def setup_inputs(seed: int = 0) -> dict:
    streams_of = jax.random.split(jax.random.key(seed), 16)
    return {
        "transcript_profiles": normal_values(streams_of[0], (BATCH_PROFILES, GENE_COUNT), 1.0, 6.0, ((0, 32),)),
        "experiment_labels": place_ends(jax.random.randint(streams_of[1], (BATCH_PROFILES,), 0, EXPERIMENT_TOTAL), jax.random.fold_in(streams_of[1], 1), 0, EXPERIMENT_TOTAL - 1).astype(jnp.int32),
        "measured_flags": place_ends((jax.random.randint(streams_of[2], (EXPERIMENT_TOTAL, GENE_COUNT), 0, 4) < 3).astype(jnp.int32), jax.random.fold_in(streams_of[2], 1), 0, 1),
        "retained_unit_flags": place_ends((jax.random.randint(streams_of[3], (4, BATCH_PROFILES, HIDDEN_SIZE), 0, 5) < 4).astype(jnp.int32), jax.random.fold_in(streams_of[3], 1), 0, 1),
        "standard_normal_draws": normal_values(streams_of[4], (BATCH_PROFILES, LATENT), 1.0, 5.0, ((0, 32),), jnp.float32),
        "compressor_first_matrix": normal_values(streams_of[5], (GENE_COUNT, HIDDEN_SIZE), GENE_COUNT ** -0.5, 0.0625, ((0, 4), (1, 8))),
        "compressor_second_matrix": normal_values(streams_of[6], (HIDDEN_SIZE, HIDDEN_SIZE), HIDDEN_SIZE ** -0.5, 0.21875, ((0, 4), (1, 8))),
        "posterior_matrix": normal_values(streams_of[7], (HIDDEN_SIZE, 2 * LATENT), HIDDEN_SIZE ** -0.5, 0.21875, ((0, 8), (1, 4))),
        "posterior_intercepts": normal_values(streams_of[8], (2 * LATENT,), 0.3, 1.5, ((0, 4),)),
        "expander_first_matrix": normal_values(streams_of[9], (LATENT, HIDDEN_SIZE), LATENT ** -0.5, 0.625, ((1, 8),)),
        "expander_second_matrix": normal_values(streams_of[10], (HIDDEN_SIZE, HIDDEN_SIZE), HIDDEN_SIZE ** -0.5, 0.21875, ((0, 4), (1, 8))),
        "output_matrix": normal_values(streams_of[11], (HIDDEN_SIZE, GENE_COUNT), HIDDEN_SIZE ** -0.5, 0.21875, ((0, 8), (1, 4))),
        "output_intercept": normal_values(streams_of[12], (GENE_COUNT,), 0.3, 1.5, ((0, 4),)),
        "normalizer_factors": jnp.clip(1.0 + 0.1 * jax.random.normal(streams_of[13], (4, HIDDEN_SIZE), jnp.float32), 0.5, 1.5).astype(jnp.bfloat16),
        "normalizer_translations": normal_values(streams_of[14], (4, HIDDEN_SIZE), 0.3, 1.5, ((1, 8),)),
    }


norm_eps = 1e-05
keep_scale = 1.25
kl_weight = 5e-05

@jax.custom_vjp
def low(v):
    return lax.optimization_barrier(v.astype(jnp.bfloat16)).astype(jnp.float32)

@jax.custom_vjp
def low_back(v):
    return v

def low_keep(v):
    return (low(v), None)

def low_pass(kept, grad):
    return (grad,)

def back_keep(v):
    return (v, None)

def back_low(kept, grad):
    return (low(grad),)
low.defvjp(low_keep, low_pass)
low_back.defvjp(back_keep, back_low)

def dense(left_side, right_side):
    return jnp.dot(left_side, right_side, precision=lax.Precision.HIGHEST)

def normalize(hidden, gain_row, shift_row):
    center = lax.optimization_barrier(jnp.mean(hidden, axis=0))
    offset = hidden - center
    spread = lax.optimization_barrier(jnp.mean(offset * offset, axis=0))
    return gain_row * offset * lax.rsqrt(spread + norm_eps) + shift_row

def activate(normed, keeper):
    return normed * jax.nn.sigmoid(normed) * keeper

def reference(transcript_profiles, experiment_labels, measured_flags, retained_unit_flags, standard_normal_draws, compressor_first_matrix, compressor_second_matrix, posterior_matrix, posterior_intercepts, expander_first_matrix, expander_second_matrix, output_matrix, output_intercept, normalizer_factors, normalizer_translations):
    floats = tuple((argument.astype(jnp.float32) for argument in (transcript_profiles, compressor_first_matrix, compressor_second_matrix, posterior_matrix, posterior_intercepts, expander_first_matrix, expander_second_matrix, output_matrix, output_intercept, normalizer_factors, normalizer_translations)))
    study_ids = jnp.arange(EXPERIMENT_TOTAL, dtype=jnp.int32)
    study_picker = (experiment_labels.astype(jnp.int32)[:, None] == study_ids[None, :]).astype(jnp.float32)
    transcript_slab = dense(study_picker, measured_flags.astype(jnp.float32))
    keepers = jnp.where(retained_unit_flags > 0, jnp.float32(keep_scale), jnp.float32(0.0))
    noise = standard_normal_draws.astype(jnp.float32)

    def forward(inputs, embed_w, encoder_w, projector_w, offsets_w, lifting_w, decoder_w, readout_w, baseline_w, scales_w, shifts_w):
        layer_one = low(activate(normalize(low_back(dense(inputs, embed_w)), scales_w[0], shifts_w[0]), keepers[0]))
        layer_two = low(activate(normalize(low_back(dense(layer_one, encoder_w)), scales_w[1], shifts_w[1]), keepers[1]))
        moments = low_back(dense(layer_two, projector_w) + offsets_w)
        center = moments[:, :LATENT]
        log_var = moments[:, LATENT:]
        latent_sample = low(center + jnp.exp(0.5 * log_var) * noise)
        layer_three = low(activate(normalize(low_back(dense(latent_sample, lifting_w)), scales_w[2], shifts_w[2]), keepers[2]))
        layer_four = low(activate(normalize(low_back(dense(layer_three, decoder_w)), scales_w[3], shifts_w[3]), keepers[3]))
        output = low_back(dense(layer_four, readout_w) + baseline_w)
        residual = output - inputs
        rebuild = 0.5 * jnp.sum(transcript_slab * residual * residual)
        diverge = 0.5 * jnp.sum(jnp.exp(log_var) + center * center - 1.0 - log_var)
        return (rebuild + kl_weight * diverge, (output, center))
    objective, pullback, extras = jax.vjp(forward, *floats, has_aux=True)
    gradients = pullback(jnp.ones((), dtype=jnp.float32))
    output, center = extras
    return (output.astype(jnp.bfloat16), center, objective / BATCH_PROFILES, gradients[0].astype(jnp.bfloat16), gradients[1] / BATCH_PROFILES, gradients[2] / BATCH_PROFILES, gradients[3] / BATCH_PROFILES, gradients[4] / BATCH_PROFILES, gradients[5] / BATCH_PROFILES, gradients[6] / BATCH_PROFILES, gradients[7] / BATCH_PROFILES, gradients[8] / BATCH_PROFILES, gradients[9] / BATCH_PROFILES, gradients[10] / BATCH_PROFILES)
```

```python
import functools

import jax
import jax.numpy as jnp
from jax import lax
from jax.experimental import pallas as pl
from jax.experimental.pallas import tpu as pltpu
from jax.sharding import PartitionSpec as P

norm_eps = 1e-05
keep_scale = 1.25
kl_weight = 5e-05
MESH = pl.DeviceIdType.MESH
LANES = 128


def round_up(value, multiple):
    return -(-value // multiple) * multiple


class Plan:
    def __init__(self, nx, ny, cells, genes_piece, hidden_piece, latent):
        self.nx, self.ny, self.cells = nx, ny, cells
        self.g, self.h, self.latent = genes_piece, hidden_piece, latent
        self.genes, self.hidden = genes_piece * ny, hidden_piece * nx
        self.hp = round_up(hidden_piece + 1, 16)
        self.hh = self.hp * nx
        tiles = round_up(self.genes, LANES) // LANES
        self.gp = round_up(tiles, ny) // ny * LANES
        self.gg = self.gp * ny
        self.shift = self.gp - self.g
        self.strip = round_up(self.shift * ny, LANES)
        starts = [self.g * j // LANES for j in range(ny)]
        ends = [round_up(self.g * (j + 1), LANES) // LANES for j in range(ny)]
        self.frame_start = [s * LANES for s in starts]
        self.frame = max(e - s for s, e in zip(starts, ends)) * LANES
        self.groups = nx // ny
        self.mid = self.hidden // ny
        self.midp = self.hp * self.groups
        self.midl = round_up(self.midp, LANES)
        self.moments = 2 * latent // ny
        self.ml = round_up(self.moments, LANES)
        self.ll = round_up(latent + 8, LANES)
        self.small = 2 * self.midl + self.ml + self.ll
        self.o2, self.o4 = 0, self.midl
        self.op, self.ol = 2 * self.midl, 2 * self.midl + self.ml
        self.blocks = nx * ny
        rows = round_up(self.hp * 2 // 3, 16)
        self.cuts = ((0, rows), (rows, self.hp - rows)) if rows < self.hp else ((0, rows),)


class Flow:
    def __init__(self, plan, kind):
        gx, gy = lax.axis_index("gx"), lax.axis_index("gy")
        self.plan, self.gx, self.gy = plan, gx, gy
        self.sizes = (plan.ny // 2, plan.nx // 2, 2)
        self.core = lax.rem(gy, 2)
        self.at = (gy // 2, gx // 2, lax.rem(gx, 2))
        self.orders = (((0, 1, 2), (2, 1, 0)), ((1, 2, 0), (1, 0, 2)))[kind]
        first, second = self.orders
        self.most = tuple(max(self.sizes[i], self.sizes[j]) for i, j in zip(first, second))
        self.least = tuple(min(self.sizes[i], self.sizes[j]) for i, j in zip(first, second))
        self.limit = tuple(self.pick(self.sizes[i], self.sizes[j]) for i, j in zip(first, second))
        self.here = tuple(self.pick(self.at[i], self.at[j]) for i, j in zip(first, second))

    def pick(self, zero, one):
        if isinstance(zero, int) and isinstance(one, int) and zero == one:
            return zero
        return jnp.where(self.core == 0, zero, one)

    def device(self, spot):
        place = [None] * 3
        for axis in range(3):
            place[axis] = self.pick(
                spot[self.orders[0].index(axis)], spot[self.orders[1].index(axis)]
            )
        return (place[1] * 2 + place[2], place[0] * 2 + self.core)

    def twin(self):
        return (self.gx, self.gy + 1 - 2 * self.core)

    def step(self, axis, sign):
        to = self.here[axis] + sign
        spot = tuple(to if i == axis else self.here[i] for i in range(3))
        return jnp.logical_and(to >= 0, to < self.limit[axis]), self.device(spot)


def neighbours(plan):
    flow = Flow(plan, 0)
    out = [(None, flow.twin())]
    for axis in range(3):
        for sign in (-1, 1):
            out.append(flow.step(axis, sign))
    return out


def when(condition):
    return (lambda f: f()) if condition is None else pl.when(condition)


def greet(plan, extra=()):
    barrier = pltpu.get_barrier_semaphore()
    count = jnp.int32(len(extra))
    for there, device in neighbours(plan):
        @when(there)
        def _(device=device):
            pl.semaphore_signal(barrier, inc=1, device_id=device, device_id_type=MESH)
        count = count + (1 if there is None else there.astype(jnp.int32))
    for device in extra:
        pl.semaphore_signal(barrier, inc=1, device_id=device, device_id_type=MESH)
    pl.semaphore_wait(barrier, count)


class Gather:
    def __init__(self, plan, source, target, rows, width, send_sem, recv_sem):
        self.plan, self.source, self.target, self.width = plan, source, target, width
        self.send_sem, self.recv_sem = send_sem, recv_sem
        self.cuts = [(Flow(plan, kind), *cut) for kind, cut in enumerate(rows)]

    def slot(self, cut, gx, gy):
        _, start, rows = cut
        return self.target.at[
            pl.ds(pl.multiple_of(gx * self.plan.hp + start, 16), rows),
            pl.ds(pl.multiple_of(gy * self.width, LANES), self.width),
        ]

    def copies(self, kind, cut, spot, stage, sign, own):
        flow = cut[0]
        gx, gy = flow.device(spot)
        dst = self.slot(cut, gx, gy)
        src = self.source.at[pl.ds(cut[1], cut[2]), :] if own else dst
        index = gx * (self.plan.ny // 2) + gy // 2
        goals = [(None, flow.twin(), 6)]
        for axis in range(3):
            if axis < stage:
                continue
            for direction in (-1, 1):
                there, device = flow.step(axis, direction)
                if axis == stage and not own:
                    there = jnp.logical_and(there, sign == direction)
                goals.append((there, device, 2 * axis + (direction + 1) // 2))
        out = []
        for there, device, k in goals:
            out.append((there, pltpu.make_async_remote_copy(
                src_ref=src, dst_ref=dst,
                send_sem=self.send_sem.at[kind, index, k],
                recv_sem=self.recv_sem.at[kind, gx * self.plan.ny + gy],
                device_id=device, device_id_type=MESH,
            )))
        return out

    def arrived(self, kind, cut, gx, gy):
        ref = self.slot(cut, gx, gy)
        pltpu.make_async_copy(ref, ref, self.recv_sem.at[kind, gx * self.plan.ny + gy]).wait()

    def start_own(self):
        for kind, cut in enumerate(self.cuts):
            for there, copy in self.copies(kind, cut, cut[0].here, 0, None, True):
                when(there)(copy.start)

    def walk(self, visit, phase):
        for kind, cut in enumerate(self.cuts):
            flow = cut[0]
            p, q, r = flow.here
            np_, nq, nr = flow.limit
            mp, mq, mr = flow.most

            def along_r(kk, kind=kind, cut=cut, flow=flow):
                def one(n, _):
                    k = n // mp + 1
                    op = lax.rem(n, mp)
                    for sign in (-1, 1):
                        for side in ((-1, 1) if kk else (1,)):
                            orr, oq = r - sign * k, q - side * kk
                            good = (orr >= 0) & (orr < nr) & (oq >= 0) & (oq < nq) & (op < np_)
                            pl.when(good)(functools.partial(
                                visit, kind, cut, (op, oq, orr), 2, sign))
                    return 0
                lax.fori_loop(0, (mr - 1) * mp, one, 0)

            def along_q(kk, kind=kind, cut=cut, flow=flow):
                def one(op, _):
                    for sign in (-1, 1):
                        oq = q - sign * kk
                        good = (oq >= 0) & (oq < nq) & (op < np_)
                        pl.when(good)(functools.partial(visit, kind, cut, (op, oq, r), 1, sign))
                    return 0
                lax.fori_loop(0, mp, one, 0)

            if phase == 0:
                def line(n, _, kind=kind, cut=cut):
                    k = n + 1
                    for sign in (-1, 1):
                        op = p - sign * k
                        good = (op >= 0) & (op < np_)
                        pl.when(good)(functools.partial(visit, kind, cut, (op, q, r), 0, sign))
                    return 0
                lax.fori_loop(0, mp - 1, line, 0)
            if 1 <= phase < mq:
                along_q(phase)
            if 1 <= phase <= mq:
                along_r(phase - 1)

    def phases(self):
        return max(cut[0].most[1] for cut in self.cuts) + 1

    def forward(self, phase):
        def visit(kind, cut, spot, stage, sign):
            self.arrived(kind, cut, *cut[0].device(spot))
            for there, copy in self.copies(kind, cut, spot, stage, sign, False):
                when(there)(copy.start)
        self.walk(visit, phase)

    def finish_twin(self):
        plan = self.plan
        for kind, cut in enumerate(self.cuts):
            flow = cut[0]
            def one(n, _, kind=kind, cut=cut, flow=flow):
                gx, y = n // (plan.ny // 2), lax.rem(n, plan.ny // 2)
                self.arrived(kind, cut, gx, 2 * y + 1 - flow.core)
                return 0
            lax.fori_loop(0, plan.blocks // 2, one, 0)

    def finish_sends(self):
        for kind, cut in enumerate(self.cuts):
            for there, copy in self.copies(kind, cut, cut[0].here, 0, None, True):
                when(there)(copy.wait_send)
        def visit(kind, cut, spot, stage, sign):
            for there, copy in self.copies(kind, cut, spot, stage, sign, False):
                when(there)(copy.wait_send)
        for phase in range(self.phases()):
            self.walk(visit, phase)


def gather_kernel(plan, widths, *refs):
    n = len(widths)
    sources, targets = refs[:n], refs[n:2 * n]
    send_sem, recv_sem, own_sem = refs[2 * n:]
    gx, gy = lax.axis_index("gx"), lax.axis_index("gy")
    greet(plan)
    sets = send_sem.shape[0]
    gathers = []
    for u, width in enumerate(widths):
        place = targets[u].at[
            pl.ds(pl.multiple_of(gx * plan.hp, 16), plan.hp),
            pl.ds(pl.multiple_of(gy * width, LANES), width),
        ]
        pltpu.make_async_copy(sources[u], place, own_sem.at[u]).start()
        gathers.append(Gather(plan, sources[u], targets[u], plan.cuts, width,
                              send_sem.at[u % sets], recv_sem.at[u]))
    for u, gather in enumerate(gathers):
        if u >= sets:
            gathers[u - sets].finish_sends()
        gather.start_own()
        for phase in range(gather.phases()):
            gather.forward(phase)
    for u, width in enumerate(widths):
        gathers[u].finish_twin()
        if u >= n - sets:
            gathers[u].finish_sends()
        place = targets[u].at[
            pl.ds(pl.multiple_of(gx * plan.hp, 16), plan.hp),
            pl.ds(pl.multiple_of(gy * width, LANES), width),
        ]
        pltpu.make_async_copy(sources[u], place, own_sem.at[u]).wait()


def gather_all(plan, blocks):
    widths = tuple(block.shape[1] for block in blocks)
    n = len(blocks)
    sets = n if plan.blocks <= 32 else 1
    return pl.pallas_call(
        functools.partial(gather_kernel, plan, widths),
        out_shape=[jax.ShapeDtypeStruct((plan.hh, plan.ny * w), jnp.bfloat16) for w in widths],
        in_specs=[pl.BlockSpec(memory_space=pl.ANY)] * n,
        out_specs=[pl.BlockSpec(memory_space=pl.ANY)] * n,
        scratch_shapes=[
            pltpu.SemaphoreType.DMA((sets, len(plan.cuts), plan.blocks // 2, 7)),
            pltpu.SemaphoreType.DMA((n, len(plan.cuts), plan.blocks)),
            pltpu.SemaphoreType.DMA((n,)),
        ],
        compiler_params=pltpu.CompilerParams(collective_id=0, has_side_effects=True),
    )(*blocks)


class Meet:
    def __init__(self, plan, wide, tall, send_sem, recv_sem):
        self.plan, self.wide, self.tall = plan, wide, tall
        self.send_sem, self.recv_sem = send_sem, recv_sem
        self.gx, self.gy = lax.axis_index("gx"), lax.axis_index("gy")

    @staticmethod
    def peers(plan):
        gx, gy = lax.axis_index("gx"), lax.axis_index("gy")
        return ([(lax.rem(gx + k, plan.nx), gy) for k in range(1, plan.nx)]
                + [(gx, lax.rem(gy + k, plan.ny)) for k in range(1, plan.ny)])

    def copies(self, second):
        plan = self.plan
        n = plan.ny if second else plan.nx
        ref = self.tall if second else self.wide
        own = self.gy if second else self.gx
        out = []
        for k in range(1, n):
            to = lax.rem(own + k, n)
            at = (plan.nx - 1 if second else 0) + k - 1
            out.append(pltpu.make_async_remote_copy(
                src_ref=ref.at[own], dst_ref=ref.at[own],
                send_sem=self.send_sem.at[at], recv_sem=self.recv_sem.at[at],
                device_id=(self.gx, to) if second else (to, self.gy), device_id_type=MESH,
            ))
        return out

    def run(self, value, merge, members):
        plan = self.plan
        for second in (False, True):
            ref = self.tall if second else self.wide
            ref[self.gy if second else self.gx] = value
            copies = self.copies(second)
            for copy in copies:
                copy.start()
            for copy in copies:
                copy.wait_recv()
            value = merge([ref[i] for i in range(ref.shape[0])], members)
            members = members * plan.nx
            for copy in copies:
                copy.wait_send()
        return value


def merge_sums(parts, members):
    total = parts[0]
    for part in parts[1:]:
        total = total + part
    return total


def merge_moments(parts, members):
    n = len(parts)
    mean = merge_sums([part[0:1] for part in parts], 0) / n
    squares = merge_sums([part[1:2] for part in parts], 0)
    between = merge_sums([(part[0:1] - mean) * (part[0:1] - mean) for part in parts], 0)
    return jnp.concatenate([mean, squares + members * between], axis=0)


def meet_kernel(plan, merge, x_ref, o_ref, wide, tall, send_sem, recv_sem):
    peers = Meet.peers(plan)
    barrier = pltpu.get_barrier_semaphore()
    for device in peers:
        pl.semaphore_signal(barrier, inc=1, device_id=device, device_id_type=MESH)
    pl.semaphore_wait(barrier, len(peers))
    meet = Meet(plan, wide, tall, send_sem, recv_sem)
    o_ref[...] = meet.run(x_ref[...], merge, float(plan.cells))


def meet_all(plan, value, merge, collective_id):
    rows, width = value.shape
    n = plan.nx + plan.ny - 2
    return pl.pallas_call(
        functools.partial(meet_kernel, plan, merge),
        out_shape=jax.ShapeDtypeStruct(value.shape, jnp.float32),
        in_specs=[pl.BlockSpec(memory_space=pltpu.VMEM)],
        out_specs=pl.BlockSpec(memory_space=pltpu.VMEM),
        scratch_shapes=[
            pltpu.VMEM((plan.nx, rows, width), jnp.float32),
            pltpu.VMEM((plan.ny, rows, width), jnp.float32),
            pltpu.SemaphoreType.DMA((n,)),
            pltpu.SemaphoreType.DMA((n,)),
        ],
        compiler_params=pltpu.CompilerParams(collective_id=collective_id, has_side_effects=True),
    )(value)


def share_kernel(plan, row_ref, block_ref, row_out, block_out, wide, tall, send_sem, recv_sem):
    peers = Meet.peers(plan)
    barrier = pltpu.get_barrier_semaphore()
    for device in peers:
        pl.semaphore_signal(barrier, inc=1, device_id=device, device_id_type=MESH)
    pl.semaphore_wait(barrier, len(peers))
    meet = Meet(plan, wide, tall, send_sem, recv_sem)
    wide[meet.gx] = row_ref[...]
    tall[meet.gy] = block_ref[...]
    copies = meet.copies(False) + meet.copies(True)
    for copy in copies:
        copy.start()
    for copy in copies:
        copy.wait_recv()
    row_out[...] = wide[0]
    block_out[...] = tall[0]
    for copy in copies:
        copy.wait_send()


def share_all(plan, row, block, collective_id):
    n = plan.nx + plan.ny - 2
    return pl.pallas_call(
        functools.partial(share_kernel, plan),
        out_shape=[jax.ShapeDtypeStruct(row.shape, jnp.float32),
                   jax.ShapeDtypeStruct(block.shape, jnp.float32)],
        in_specs=[pl.BlockSpec(memory_space=pltpu.VMEM)] * 2,
        out_specs=[pl.BlockSpec(memory_space=pltpu.VMEM)] * 2,
        scratch_shapes=[
            pltpu.VMEM((plan.nx, *row.shape), jnp.float32),
            pltpu.VMEM((plan.ny, *block.shape), jnp.float32),
            pltpu.SemaphoreType.DMA((n,)),
            pltpu.SemaphoreType.DMA((n,)),
        ],
        compiler_params=pltpu.CompilerParams(collective_id=collective_id, has_side_effects=True),
    )(row, block)


class Reduce:
    def __init__(self, plan, width, part, twin, slots, send_sem, twin_sem, recv_sem):
        self.plan, self.width, self.part, self.twin, self.slots = plan, width, part, twin, slots
        self.send_sem, self.twin_sem, self.recv_sem = send_sem, twin_sem, recv_sem
        self.cuts = [(Flow(plan, kind), *cut) for kind, cut in enumerate(plan.cuts)]

    @staticmethod
    def slot_counts(plan):
        counts = []
        for kind in range(len(plan.cuts)):
            sizes = (plan.ny // 2, plan.nx // 2, 2)
            first, second = (((0, 1, 2), (2, 1, 0)), ((1, 2, 0), (1, 0, 2)))[kind]
            mp, mq, mr = (max(sizes[i], sizes[j]) for i, j in zip(first, second))
            a, b, c = (Reduce.sides(m) for m in (mp, mq, mr))
            far_r = (mr > 2) * (mr * mq * mp)
            counts.append((far_r, mq * mp * (c + (mq > 2)), mp * (c + b + (mp > 2)), c + b + a))
        return counts

    @staticmethod
    def sides(most):
        return 1 if most == 2 else (2 if most > 2 else 0)

    def block(self, ref, cut, gx, gy):
        return ref.at[
            pl.ds(pl.multiple_of(gx * self.plan.hp + cut[1], 16), cut[2]),
            pl.ds(pl.multiple_of(gy * self.width, LANES), self.width),
        ]

    def twin_block(self, cut, gx, y):
        return self.twin.at[
            pl.ds(pl.multiple_of(gx * self.plan.hp + cut[1], 16), cut[2]),
            pl.ds(pl.multiple_of(y * self.width, LANES), self.width),
        ]

    def twin_copy(self, kind, cut, gx, y):
        flow = cut[0]
        return pltpu.make_async_remote_copy(
            src_ref=self.block(self.part, cut, gx, 2 * y + 1 - flow.core),
            dst_ref=self.twin_block(cut, gx, y),
            send_sem=self.twin_sem.at[0, kind, gx * (self.plan.ny // 2) + y],
            recv_sem=self.twin_sem.at[1, kind, gx * (self.plan.ny // 2) + y],
            device_id=flow.twin(), device_id_type=MESH,
        )

    def each_twin(self, visit, ys=None):
        ny2 = self.plan.ny // 2
        for kind, cut in enumerate(self.cuts):
            def one(n, _, kind=kind, cut=cut):
                visit(self.twin_copy(kind, cut, n // ny2, lax.rem(n, ny2)))
                return 0
            lax.fori_loop(0, self.plan.blocks // 2, one, 0)

    def start_twin(self):
        self.each_twin(lambda copy: copy.start())

    def entry(self, kind, stage, spot, axis, came_from):
        flow = self.cuts[kind][0]
        mp, mq, mr = flow.most
        far_r, far_q, far_p, _ = Reduce.slot_counts(self.plan)[kind]
        sides = [Reduce.sides(m) for m in flow.most]
        dp, dq, dr = spot
        if stage == 2:
            return (dr * mq + dq) * mp + dp
        if stage == 1:
            base, which = far_r, (dq * mp + dp) * (sides[2] + (mq > 2))
        elif stage == 0:
            base, which = far_r + far_q, dp * (sides[2] + sides[1] + (mp > 2))
        else:
            base, which = far_r + far_q + far_p, 0
        offset = 0
        for later in (2, 1, 0):
            if later == stage:
                return base + which + offset
            if later == axis:
                side = 0 if sides[axis] == 1 else (came_from + 1) // 2
                return base + which + offset + side
            offset += sides[later]

    def slot(self, kind, index):
        cut = self.cuts[kind]
        total = sum(Reduce.slot_counts(self.plan)[kind])
        return self.slots[kind].at[index], self.recv_sem[kind].at[index]

    def gather_terms(self, kind, cut, spot, stage, sign):
        flow = cut[0]
        ny2 = self.plan.ny // 2
        gx, gy = flow.device(spot)
        y = gy // 2
        copy = self.twin_copy(kind, cut, gx, y)
        copy.wait_recv()
        own = self.block(self.part, cut, gx, gy)
        twin = self.twin_block(cut, gx, y)
        arrivals = []
        for axis in (2, 1, 0):
            if axis > stage:
                for side in (-1, 1):
                    there, _ = flow.step(axis, side)
                    if flow.most[axis] < 2:
                        continue
                    arrivals.append((there, self.entry(kind, stage, spot, axis, side)))
            elif axis == stage and flow.most[axis] > 2:
                away = self.here_away(flow, axis, sign)
                arrivals.append((away, self.entry(kind, stage, spot, axis, None)))
        return own, twin, arrivals

    def here_away(self, flow, axis, sign):
        to = flow.here[axis] - sign
        return (to >= 0) & (to < flow.limit[axis])

    def add_in(self, kind, cut, spot, stage, sign):
        own, twin, arrivals = self.gather_terms(kind, cut, spot, stage, sign)
        own[...] = (own[...].astype(jnp.float32) + twin[...].astype(jnp.float32)).astype(jnp.bfloat16)
        for there, index in arrivals:
            slot, sem = self.slot(kind, index)
            @when(there)
            def _(slot=slot, sem=sem):
                pltpu.make_async_copy(slot, slot, sem).wait()
                own[...] = (own[...].astype(jnp.float32) + slot[...].astype(jnp.float32)).astype(
                    jnp.bfloat16)
        return own

    def onward(self, kind, cut, spot, stage, sign):
        flow = cut[0]
        _, device = self.toward(flow, stage, sign)
        gx, gy = flow.device(spot)
        to = flow.here[stage] + sign
        index_same = self.entry(kind, stage, spot, stage, None) if flow.most[stage] > 2 else None
        done = to == spot[stage]
        p_same = flow.here[0] == spot[0]
        q_same = flow.here[1] == spot[1]
        if stage == 2:
            deeper = jnp.where(q_same, jnp.where(p_same,
                               self.entry(kind, -1, spot, 2, -sign),
                               self.entry(kind, 0, spot, 2, -sign)),
                               self.entry(kind, 1, spot, 2, -sign))
        elif stage == 1:
            deeper = jnp.where(p_same, self.entry(kind, -1, spot, 1, -sign),
                               self.entry(kind, 0, spot, 1, -sign))
        else:
            deeper = self.entry(kind, -1, spot, 0, -sign)
        index = deeper if index_same is None else jnp.where(done, deeper, index_same)
        slot, sem = self.slot(kind, index)
        ny2 = self.plan.ny // 2
        return pltpu.make_async_remote_copy(
            src_ref=self.block(self.part, cut, gx, gy), dst_ref=slot,
            send_sem=self.send_sem.at[kind, gx * ny2 + gy // 2], recv_sem=sem,
            device_id=device, device_id_type=MESH,
        )

    def toward(self, flow, axis, sign):
        return flow.step(axis, sign)

    def walk(self, visit, stage):
        for kind, cut in enumerate(self.cuts):
            flow = cut[0]
            p, q, r = flow.here
            np_, nq, nr = flow.limit
            mp, mq, mr = flow.most

            def one(n, _, kind=kind, cut=cut):
                if stage == 2:
                    k, dq, dp = mr - 1 - n // (mq * mp), lax.rem(n // mp, mq), lax.rem(n, mp)
                elif stage == 1:
                    k, dp = mq - 1 - n // mp, lax.rem(n, mp)
                else:
                    k = mp - 1 - n
                for sign in (-1, 1):
                    if stage == 2:
                        d = r + sign * k
                        spot, good = (dp, dq, d), (d >= 0) & (d < nr) & (dq < nq) & (dp < np_)
                    elif stage == 1:
                        d = q + sign * k
                        spot, good = (dp, d, r), (d >= 0) & (d < nq) & (dp < np_)
                    else:
                        d = p + sign * k
                        spot, good = (d, q, r), (d >= 0) & (d < np_)
                    pl.when(good)(functools.partial(visit, kind, cut, spot, stage, sign))
                return 0
            count = {2: (mr - 1) * mq * mp, 1: (mq - 1) * mp, 0: mp - 1}[stage]
            lax.fori_loop(0, count, one, 0)

    def pass_on(self, stage):
        def visit(kind, cut, spot, stage, sign):
            self.add_in(kind, cut, spot, stage, sign)
            self.onward(kind, cut, spot, stage, sign).start()
        self.walk(visit, stage)

    def own_sum(self, out_ref, factor):
        for kind, cut in enumerate(self.cuts):
            flow = cut[0]
            own = self.add_in(kind, cut, flow.here, -1, None)
            out_ref[pl.ds(cut[1], cut[2]), :] = own[...].astype(jnp.float32) * factor

    def finish_sends(self):
        self.each_twin(lambda copy: copy.wait_send())
        def visit(kind, cut, spot, stage, sign):
            self.onward(kind, cut, spot, stage, sign).wait_send()
        for stage in (2, 1, 0):
            self.walk(visit, stage)


def reduce_kernel(plan, width, factor, x_ref, o_ref, part, twin, *rest):
    n = len(plan.cuts)
    slots, (send_sem, twin_sem), recv_sem, load_sem = rest[:n], rest[n:n + 2], rest[n + 2:2 * n + 2], rest[-1]
    load = pltpu.make_async_copy(x_ref, part, load_sem)
    load.start()
    greet(plan)
    load.wait()
    reduce = Reduce(plan, width, part, twin, slots, send_sem, twin_sem, recv_sem)
    reduce.start_twin()
    for stage in (2, 1, 0):
        reduce.pass_on(stage)
    reduce.own_sum(o_ref, factor)
    reduce.finish_sends()


def reduce_all(plan, value, factor, collective_id):
    width = value.shape[1] // plan.ny
    counts = [sum(c) for c in Reduce.slot_counts(plan)]
    return pl.pallas_call(
        functools.partial(reduce_kernel, plan, width, factor),
        out_shape=jax.ShapeDtypeStruct((plan.hp, width), jnp.float32),
        in_specs=[pl.BlockSpec(memory_space=pl.ANY)],
        out_specs=pl.BlockSpec(memory_space=pltpu.VMEM),
        scratch_shapes=[
            pltpu.VMEM((plan.hh, plan.ny * width), jnp.bfloat16),
            pltpu.VMEM((plan.hh, plan.ny // 2 * width), jnp.bfloat16),
            *[pltpu.VMEM((c, cut[1], width), jnp.bfloat16) for c, cut in zip(counts, plan.cuts)],
            pltpu.SemaphoreType.DMA((len(plan.cuts), plan.blocks // 2)),
            pltpu.SemaphoreType.DMA((2, len(plan.cuts), plan.blocks // 2)),
            *[pltpu.SemaphoreType.DMA((c,)) for c in counts],
            pltpu.SemaphoreType.DMA,
        ],
        compiler_params=pltpu.CompilerParams(
            collective_id=collective_id, has_side_effects=True, vmem_limit_bytes=60 * 1024 * 1024),
    )(value)


def rows_dot(left, right):
    return lax.dot_general(left, right, (((1,), (0,)), ((), ())), preferred_element_type=jnp.float32)


def over_cells(left, right):
    return lax.dot_general(left, right, (((1,), (1,)), ((), ())), preferred_element_type=jnp.float32)


def over_rows(left, right):
    return lax.dot_general(left, right, (((0,), (0,)), ((), ())), preferred_element_type=jnp.float32)


def pad_to(value, rows, lanes):
    return jnp.pad(value, ((0, rows - value.shape[0]), (0, lanes - value.shape[1])))


def spread_rows(plan, value):
    split = value.reshape(plan.nx, plan.h, *value.shape[1:])
    wide = jnp.pad(split, ((0, 0), (0, plan.hp - plan.h)) + ((0, 0),) * (value.ndim - 1))
    return wide.reshape(plan.hh, *value.shape[1:])


def middle_piece(plan, matrix):
    turned = matrix.T.reshape(plan.h, plan.groups, plan.h)
    wide = jnp.pad(turned, ((0, plan.hp - plan.h), (0, 0), (0, plan.hp - plan.h)))
    return pad_to(wide.reshape(plan.hp, plan.midp), plan.hp, plan.midl)


def middle_back(plan, piece):
    cut = piece[:plan.h, :plan.midp].reshape(plan.h, plan.groups, plan.hp)[:, :, :plan.h]
    return cut.reshape(plan.h, plan.mid).T


def with_row(plan, block, row, first):
    spare = jnp.where(first, row, jnp.zeros_like(row))[None]
    return pad_to(jnp.concatenate([block, spare], axis=0), plan.hp, block.shape[1])


def on_device(
    nx, ny,
    transcript_profiles,
    experiment_labels,
    measured_flags,
    retained_unit_flags,
    standard_normal_draws,
    compressor_first_matrix,
    compressor_second_matrix,
    posterior_matrix,
    posterior_intercepts,
    expander_first_matrix,
    expander_second_matrix,
    output_matrix,
    output_intercept,
    normalizer_factors,
    normalizer_translations,
):
    cells = transcript_profiles.shape[0]
    plan = Plan(nx, ny, cells, output_matrix.shape[1], output_matrix.shape[0], expander_first_matrix.shape[0])
    total_cells = float(cells * nx * ny)
    gx, gy = lax.axis_index("gx"), lax.axis_index("gy")
    first = gx == 0

    wide = jnp.concatenate([
        pad_to(compressor_first_matrix.T, plan.hp, plan.g),
        with_row(plan, output_matrix, output_intercept, first)], axis=0)
    strip = lax.ppermute(wide[:, :plan.strip], "gy", [(j + 1, j) for j in range(ny - 1)])
    wide = jnp.concatenate([wide, strip], axis=1)
    wide = pad_to(wide, 2 * plan.hp, plan.gp + plan.strip + plan.shift * ny)
    wide = lax.dynamic_slice_in_dim(wide, gy * plan.shift, plan.gp, 1)
    last = jnp.concatenate([
        expander_first_matrix.T, normalizer_factors.T, normalizer_translations.T], axis=1)
    small = jnp.concatenate([
        middle_piece(plan, compressor_second_matrix),
        middle_piece(plan, expander_second_matrix),
        pad_to(with_row(plan, posterior_matrix, posterior_intercepts, first), plan.hp, plan.ml),
        pad_to(last, plan.hp, plan.ll)], axis=1)
    embed_all, small_all, readout_all = gather_all(plan, [wide[:plan.hp], small, wide[plan.hp:]])

    parts = small_all.reshape(plan.hh, ny, plan.small)
    encoder_all = parts[:, :, plan.o2:plan.o2 + plan.midp].reshape(plan.hh, plan.hh)
    decoder_all = parts[:, :, plan.o4:plan.o4 + plan.midp].reshape(plan.hh, plan.hh)
    projector_all = parts[:, :, plan.op:plan.op + plan.moments].reshape(plan.hh, 2 * plan.latent)
    lifting_all = parts[:, 0, plan.ol:plan.ol + plan.latent]
    rows = parts[:, 0, plan.ol + plan.latent:plan.ol + plan.latent + 8].astype(jnp.float32)
    gains = [rows[:, k:k + 1] for k in range(4)]
    biases = [rows[:, 4 + k:5 + k] for k in range(4)]

    profiles = transcript_profiles.T
    draws = standard_normal_draws.T
    keepers = [
        spread_rows(plan, retained_unit_flags[k].T).astype(jnp.bfloat16) for k in range(4)]
    spare = (lax.rem(jnp.arange(plan.hh), plan.hp) == plan.h)[:, None]

    def forward_layer(hidden, k, ones, ident):
        mean = jnp.mean(hidden, axis=1)
        offset = hidden - mean[:, None]
        squares = jnp.sum(offset * offset, axis=1)
        merged = meet_all(plan, jnp.stack([mean, squares]), merge_moments, 1)
        inverse = lax.rsqrt(merged[1] / total_cells + norm_eps)[:, None]
        scaled = (hidden - merged[0][:, None]) * inverse
        normed = gains[k] * scaled + biases[k]
        keeper = keepers[k].astype(jnp.float32) * keep_scale
        active = normed * jax.nn.sigmoid(normed) * keeper
        if ones:
            active = jnp.where(spare, 1.0, active)
        return active.astype(jnp.bfloat16), normed, scaled, inverse

    def backward_layer(upstream, kept, k, loss, ident):
        _, normed, scaled, inverse = kept
        sigma = jax.nn.sigmoid(normed)
        slope = upstream * (keepers[k].astype(jnp.float32) * keep_scale) * sigma * (
            1.0 + normed * (1.0 - sigma))
        pair = jnp.stack([jnp.sum(slope, axis=1), jnp.sum(slope * scaled, axis=1),
                          jnp.full((plan.hh,), loss)])
        merged = meet_all(plan, pair, merge_sums, 2)
        shift, gain = merged[0], merged[1]
        grad = gains[k] * inverse * (
            slope - (shift[:, None] + scaled * gain[:, None]) / total_cells)
        return grad.astype(jnp.bfloat16), gain, shift, merged[2, 0]

    one = forward_layer(rows_dot(embed_all[:, :plan.genes], profiles), 0, False, 1)
    two = forward_layer(rows_dot(encoder_all, one[0]), 1, True, 2)
    moments = over_rows(projector_all, two[0])
    center, log_var = moments[:plan.latent], moments[plan.latent:]
    spread = jnp.exp(0.5 * log_var)
    sample = (center + spread * draws).astype(jnp.bfloat16)
    three = forward_layer(rows_dot(lifting_all, sample), 2, False, 3)
    four = forward_layer(rows_dot(decoder_all, three[0]), 3, True, 4)

    output = over_rows(readout_all[:, :plan.genes], four[0])
    residual = output - profiles.astype(jnp.float32)
    picker = (jnp.arange(measured_flags.shape[0], dtype=jnp.int32)[:, None]
              == experiment_labels[None, :]).astype(jnp.bfloat16)
    slab = over_rows(measured_flags.astype(jnp.bfloat16), picker)
    weighted = slab * residual
    rebuild = 0.5 * jnp.sum(weighted * residual)
    diverge = 0.5 * jnp.sum(jnp.exp(log_var) + center * center - 1.0 - log_var)
    own_loss = rebuild + kl_weight * diverge
    output_grad = weighted.astype(jnp.bfloat16)

    def frames(product):
        padded = pad_to(product, plan.hh, max(plan.frame_start) + plan.frame)
        return jnp.concatenate(
            [padded[:, s:s + plan.frame] for s in plan.frame_start], axis=1).astype(jnp.bfloat16)

    readout_part = frames(over_cells(four[0], output_grad))
    upstream = rows_dot(readout_all[:, :plan.genes], output_grad)
    grad_four, gain_four, shift_four, loss_sum = backward_layer(upstream, four, 3, own_loss, 5)
    upstream = over_rows(decoder_all, grad_four)
    grad_three, gain_three, shift_three, _ = backward_layer(upstream, three, 2, own_loss, 6)
    sample_grad = over_rows(lifting_all, grad_three)
    center_grad = sample_grad + kl_weight * center
    logvar_grad = sample_grad * 0.5 * spread * draws + kl_weight * 0.5 * (jnp.exp(log_var) - 1.0)
    moment_grad = jnp.concatenate([center_grad, logvar_grad], axis=0).astype(jnp.bfloat16)
    upstream = rows_dot(projector_all, moment_grad)
    grad_two, gain_two, shift_two, _ = backward_layer(upstream, two, 1, own_loss, 7)
    upstream = over_rows(encoder_all, grad_two)
    grad_one, gain_one, shift_one, _ = backward_layer(upstream, one, 0, own_loss, 8)
    input_grad = (over_rows(embed_all[:, :plan.genes], grad_one) - weighted).astype(jnp.bfloat16)

    encoder_part = over_cells(grad_two, one[0]).reshape(plan.hh, ny, plan.midp)
    decoder_part = over_cells(grad_four, three[0]).reshape(plan.hh, ny, plan.midp)
    projector_part = over_cells(two[0], moment_grad).reshape(plan.hh, ny, plan.moments)
    lifting_part = over_cells(grad_three, sample)

    def lanes(value, width):
        return jnp.pad(value, ((0, 0), (0, 0), (0, width - value.shape[2])))

    small_part = jnp.concatenate([
        lanes(encoder_part, plan.midl), lanes(decoder_part, plan.midl),
        lanes(projector_part, plan.ml),
        jnp.broadcast_to(pad_to(lifting_part, plan.hh, plan.ll)[:, None, :], (plan.hh, ny, plan.ll)),
    ], axis=2).reshape(plan.hh, ny * plan.small).astype(jnp.bfloat16)
    embed_part = frames(over_cells(grad_one, profiles))

    readout_sum = reduce_all(plan, readout_part, 1.0 / total_cells, 3)
    small_sum = reduce_all(plan, small_part, 1.0 / total_cells, 4)
    embed_sum = reduce_all(plan, embed_part, 1.0 / total_cells, 3)
    starts = jnp.array([plan.g * j - plan.frame_start[j] for j in range(ny)], jnp.int32)
    readout_own = lax.dynamic_slice_in_dim(readout_sum, starts[gy], plan.g, 1)
    embed_own = lax.dynamic_slice_in_dim(embed_sum, starts[gy], plan.g, 1)

    row, lifting_own = share_all(plan, jnp.concatenate([
        readout_sum[plan.h:plan.h + 1],
        small_sum[plan.h:plan.h + 1, plan.op:plan.op + plan.ml]], axis=1),
        small_sum[:, plan.ol:plan.ol + plan.ll], 5)
    baseline_own = lax.dynamic_slice_in_dim(row[0, :plan.frame], starts[gy], plan.g, 0)

    def own_units(values):
        stack = jnp.stack(values, axis=0) / total_cells
        return lax.dynamic_slice_in_dim(stack, gx * plan.hp, plan.h, 1)

    small_h = small_sum[:plan.h]
    return (
        output.astype(jnp.bfloat16).T,
        center.T,
        loss_sum / total_cells,
        input_grad.T,
        embed_own[:plan.h].T,
        middle_back(plan, small_sum[:, plan.o2:plan.o2 + plan.midl]),
        small_h[:, plan.op:plan.op + plan.moments],
        row[0, plan.frame:plan.frame + plan.moments],
        lifting_own[:plan.h, :plan.latent].T,
        middle_back(plan, small_sum[:, plan.o4:plan.o4 + plan.midl]),
        readout_own[:plan.h],
        baseline_own,
        own_units([gain_one, gain_two, gain_three, gain_four]),
        own_units([shift_one, shift_two, shift_three, shift_four]),
    )


def solution(mesh):
    return jax.shard_map(
        functools.partial(on_device, mesh.shape["gx"], mesh.shape["gy"]),
        mesh=mesh,
        in_specs=(
            P(("gx", "gy"), None),
            P(("gx", "gy")),
            P(),
            P(None, ("gx", "gy"), None),
            P(("gx", "gy"), None),
            P("gy", "gx"),
            P("gy", "gx"),
            P("gx", "gy"),
            P("gy"),
            P(None, "gx"),
            P("gy", "gx"),
            P("gx", "gy"),
            P("gy"),
            P(None, "gx"),
            P(None, "gx"),
        ),
        out_specs=(
            P(("gx", "gy"), None),
            P(("gx", "gy"), None),
            P(),
            P(("gx", "gy"), None),
            P("gy", "gx"),
            P("gy", "gx"),
            P("gx", "gy"),
            P("gy"),
            P(None, "gx"),
            P("gy", "gx"),
            P("gx", "gy"),
            P("gy"),
            P(None, "gx"),
            P(None, "gx"),
        ),
        check_vma=False,
    )
```

```python
import functools

import jax
import jax.numpy as jnp
from jax import lax
from jax.experimental import pallas as pl
from jax.experimental.pallas import tpu as pltpu
from jax.sharding import PartitionSpec as P

norm_eps = 1e-05
keep_scale = 1.25
kl_weight = 5e-05
MESH = pl.DeviceIdType.MESH
LANES = 128


def round_up(value, multiple):
    return -(-value // multiple) * multiple


class Plan:
    def __init__(self, nx, ny, cells, genes_piece, hidden_piece, latent):
        self.nx, self.ny, self.cells = nx, ny, cells
        self.g, self.h, self.latent = genes_piece, hidden_piece, latent
        self.genes, self.hidden = genes_piece * ny, hidden_piece * nx
        self.hp = round_up(hidden_piece + 1, 16)
        self.hh = self.hp * nx
        tiles = round_up(self.genes, LANES) // LANES
        self.gp = round_up(tiles, ny) // ny * LANES
        self.gg = self.gp * ny
        self.shift = self.gp - self.g
        self.strip = round_up(self.shift * ny, LANES)
        starts = [self.g * j // LANES for j in range(ny)]
        ends = [round_up(self.g * (j + 1), LANES) // LANES for j in range(ny)]
        self.frame_start = [s * LANES for s in starts]
        self.frame = max(e - s for s, e in zip(starts, ends)) * LANES
        self.groups = nx // ny
        self.mid = self.hidden // ny
        self.midp = self.hp * self.groups
        self.midl = round_up(self.midp, LANES)
        self.moments = 2 * latent // ny
        self.ml = round_up(self.moments, LANES)
        self.ll = round_up(latent + 8, LANES)
        self.small = 2 * self.midl + self.ml + self.ll
        self.o2, self.o4 = 0, self.midl
        self.op, self.ol = 2 * self.midl, 2 * self.midl + self.ml
        self.blocks = nx * ny
        rows = round_up(self.hp * 2 // 3, 16)
        self.cuts = ((0, rows), (rows, self.hp - rows)) if rows < self.hp else ((0, rows),)


class Flow:
    def __init__(self, plan, kind):
        gx, gy = lax.axis_index("gx"), lax.axis_index("gy")
        self.plan, self.gx, self.gy = plan, gx, gy
        self.sizes = (plan.ny // 2, plan.nx // 2, 2)
        self.core = lax.rem(gy, 2)
        self.at = (gy // 2, gx // 2, lax.rem(gx, 2))
        self.orders = (((0, 1, 2), (2, 1, 0)), ((1, 2, 0), (1, 0, 2)))[kind]
        first, second = self.orders
        self.most = tuple(max(self.sizes[i], self.sizes[j]) for i, j in zip(first, second))
        self.least = tuple(min(self.sizes[i], self.sizes[j]) for i, j in zip(first, second))
        self.limit = tuple(self.pick(self.sizes[i], self.sizes[j]) for i, j in zip(first, second))
        self.here = tuple(self.pick(self.at[i], self.at[j]) for i, j in zip(first, second))

    def pick(self, zero, one):
        if isinstance(zero, int) and isinstance(one, int) and zero == one:
            return zero
        return jnp.where(self.core == 0, zero, one)

    def device(self, spot):
        place = [None] * 3
        for axis in range(3):
            place[axis] = self.pick(
                spot[self.orders[0].index(axis)], spot[self.orders[1].index(axis)]
            )
        return (place[1] * 2 + place[2], place[0] * 2 + self.core)

    def twin(self):
        return (self.gx, self.gy + 1 - 2 * self.core)

    def step(self, axis, sign):
        to = self.here[axis] + sign
        spot = tuple(to if i == axis else self.here[i] for i in range(3))
        return jnp.logical_and(to >= 0, to < self.limit[axis]), self.device(spot)


def neighbours(plan):
    flow = Flow(plan, 0)
    out = [(None, flow.twin())]
    for axis in range(3):
        for sign in (-1, 1):
            out.append(flow.step(axis, sign))
    return out


def when(condition):
    return (lambda f: f()) if condition is None else pl.when(condition)


def greet(plan, extra=()):
    barrier = pltpu.get_barrier_semaphore()
    count = jnp.int32(len(extra))
    for there, device in neighbours(plan):
        @when(there)
        def _(device=device):
            pl.semaphore_signal(barrier, inc=1, device_id=device, device_id_type=MESH)
        count = count + (1 if there is None else there.astype(jnp.int32))
    for device in extra:
        pl.semaphore_signal(barrier, inc=1, device_id=device, device_id_type=MESH)
    pl.semaphore_wait(barrier, count)


class Gather:
    def __init__(self, plan, source, target, width, send_sem, recv_sem):
        self.plan, self.source, self.target, self.width = plan, source, target, width
        self.send_sem, self.recv_sem = send_sem, recv_sem
        self.cuts = [(Flow(plan, kind), *cut) for kind, cut in enumerate(plan.cuts)]
        self.phases = 1 + max(sum(m - 1 for m in cut[0].most) for cut in self.cuts)

    def slot(self, cut, gx, gy):
        _, start, rows = cut
        return self.target.at[
            pl.ds(pl.multiple_of(gx * self.plan.hp + start, 16), rows),
            pl.ds(pl.multiple_of(gy * self.width, LANES), self.width),
        ]

    def own_copy(self, sem):
        plan = self.plan
        gx, gy = lax.axis_index("gx"), lax.axis_index("gy")
        place = self.target.at[
            pl.ds(pl.multiple_of(gx * plan.hp, 16), plan.hp),
            pl.ds(pl.multiple_of(gy * self.width, LANES), self.width),
        ]
        return pltpu.make_async_copy(self.source, place, sem)

    def copies(self, kind, cut, spot, own):
        flow = cut[0]
        gx, gy = flow.device(spot)
        dst = self.slot(cut, gx, gy)
        src = self.source.at[pl.ds(cut[1], cut[2]), :] if own else dst
        index = gx * (self.plan.ny // 2) + gy // 2
        goals = [(None, flow.twin(), 6)]
        level = None
        for axis in (2, 1, 0):
            for sign in (-1, 1):
                if flow.most[axis] < 2:
                    continue
                there, device = flow.step(axis, sign)
                if not own:
                    there = there & ((flow.here[axis] - spot[axis]) * sign >= 0)
                    if level is not None:
                        there = there & level
                goals.append((there, device, 2 * axis + (sign + 1) // 2))
            same = spot[axis] == flow.here[axis]
            level = same if level is None else level & same
        out = []
        for there, device, k in goals:
            out.append((there, pltpu.make_async_remote_copy(
                src_ref=src, dst_ref=dst,
                send_sem=self.send_sem.at[kind, index, k],
                recv_sem=self.recv_sem.at[kind, gx * self.plan.ny + gy],
                device_id=device, device_id_type=MESH,
            )))
        return out

    def arrived(self, kind, cut, gx, gy):
        ref = self.slot(cut, gx, gy)
        pltpu.make_async_copy(ref, ref, self.recv_sem.at[kind, gx * self.plan.ny + gy]).wait()

    def start_own(self):
        for kind, cut in enumerate(self.cuts):
            for there, copy in self.copies(kind, cut, cut[0].here, True):
                when(there)(copy.start)

    def walk(self, visit, phase=None):
        for kind, cut in enumerate(self.cuts):
            flow = cut[0]
            mp, mq, mr = flow.most

            def one(n, _, kind=kind, cut=cut, flow=flow):
                spot = (lax.rem(n, mp), lax.rem(n // mp, mq), n // (mp * mq))
                hops, good = 0, None
                for here, limit, at in zip(flow.here, flow.limit, spot):
                    hops = hops + jnp.abs(at - here)
                    good = at < limit if good is None else good & (at < limit)
                good = good & ((hops > 0) if phase is None else (hops == phase))
                pl.when(good)(functools.partial(visit, kind, cut, spot))
                return 0
            lax.fori_loop(0, mp * mq * mr, one, 0)

    def forward(self, phase):
        def visit(kind, cut, spot):
            self.arrived(kind, cut, *cut[0].device(spot))
            for there, copy in self.copies(kind, cut, spot, False):
                when(there)(copy.start)
        if phase < self.phases:
            self.walk(visit, phase)

    def finish_twin(self):
        plan = self.plan
        for kind, cut in enumerate(self.cuts):
            flow = cut[0]
            def one(n, _, kind=kind, cut=cut, flow=flow):
                gx, y = n // (plan.ny // 2), lax.rem(n, plan.ny // 2)
                self.arrived(kind, cut, gx, 2 * y + 1 - flow.core)
                return 0
            lax.fori_loop(0, plan.blocks // 2, one, 0)

    def finish_sends(self):
        for kind, cut in enumerate(self.cuts):
            for there, copy in self.copies(kind, cut, cut[0].here, True):
                when(there)(copy.wait_send)
        def visit(kind, cut, spot):
            for there, copy in self.copies(kind, cut, spot, False):
                when(there)(copy.wait_send)
        self.walk(visit)


class Meet:
    def __init__(self, plan, wide, tall, send_sem, recv_sem):
        self.plan, self.wide, self.tall = plan, wide, tall
        self.send_sem, self.recv_sem = send_sem, recv_sem
        self.gx, self.gy = lax.axis_index("gx"), lax.axis_index("gy")

    @staticmethod
    def peers(plan):
        gx, gy = lax.axis_index("gx"), lax.axis_index("gy")
        return ([(lax.rem(gx + k, plan.nx), gy) for k in range(1, plan.nx)]
                + [(gx, lax.rem(gy + k, plan.ny)) for k in range(1, plan.ny)])

    def copies(self, second):
        plan = self.plan
        n = plan.ny if second else plan.nx
        ref = self.tall if second else self.wide
        own = self.gy if second else self.gx
        out = []
        for k in range(1, n):
            to = lax.rem(own + k, n)
            at = (plan.nx - 1 if second else 0) + k - 1
            out.append(pltpu.make_async_remote_copy(
                src_ref=ref.at[own], dst_ref=ref.at[own],
                send_sem=self.send_sem.at[at], recv_sem=self.recv_sem.at[at],
                device_id=(self.gx, to) if second else (to, self.gy), device_id_type=MESH,
            ))
        return out

    def run(self, value, merge, members, between=None):
        plan = self.plan
        for second in (False, True):
            ref = self.tall if second else self.wide
            ref[self.gy if second else self.gx] = value
            copies = self.copies(second)
            for copy in copies:
                copy.start()
            if between is not None:
                between(second)
            for copy in copies:
                copy.wait_recv()
            value = merge([ref[i] for i in range(ref.shape[0])], members)
            members = members * plan.nx
            for copy in copies:
                copy.wait_send()
        return value


def merge_sums(parts, members):
    total = parts[0]
    for part in parts[1:]:
        total = total + part
    return total


def merge_moments(parts, members):
    n = len(parts)
    mean = merge_sums([part[0:1] for part in parts], 0) / n
    squares = merge_sums([part[1:2] for part in parts], 0)
    between = merge_sums([(part[0:1] - mean) * (part[0:1] - mean) for part in parts], 0)
    return jnp.concatenate([mean, squares + members * between], axis=0)


def tiled(column, plan):
    return jnp.concatenate([column] * (plan.cells // LANES), axis=1)


def lane_sums(value):
    total = value[:, :LANES]
    for at in range(LANES, value.shape[1], LANES):
        total = total + value[:, at:at + LANES]
    return total


def as_row(value):
    return jnp.sum(value.T, axis=0, keepdims=True)


def as_column(row):
    return jnp.broadcast_to(row, (LANES, LANES)).T


def aligned(start, rows=LANES):
    return pl.ds(pl.multiple_of(start, rows), rows)


def moment_rows(plan, h_ref, row_ref):
    def block(i, _):
        value = h_ref[aligned(i * LANES), :]
        sums = lane_sums(value)
        mean = jnp.sum(sums, axis=1, keepdims=True) / plan.cells
        offset = value - mean
        row_ref[0:1, aligned(i * LANES)] = as_row(sums) / plan.cells
        row_ref[1:2, aligned(i * LANES)] = as_row(lane_sums(offset * offset))
        return 0
    lax.fori_loop(0, plan.hh // LANES, block, 0)


def unit_column(plan, small_ref, i, lane):
    slab = small_ref[aligned(i * LANES), plan.ol + plan.ll - LANES:plan.ol + plan.ll]
    at = lane - (plan.ll - LANES)
    return jnp.broadcast_to(slab.astype(jnp.float32)[:, at:at + 1], (LANES, LANES))


def activate(plan, k, h_ref, row_ref, small_ref, keep_ref, out_ref, column_ref, total_cells, spare):
    def block(i, _):
        column_ref[0] = as_column(row_ref[0:1, aligned(i * LANES)])
        column_ref[1] = as_column(lax.rsqrt(row_ref[1:2, aligned(i * LANES)] / total_cells + norm_eps))
        column_ref[2] = unit_column(plan, small_ref, i, plan.latent + k)
        column_ref[3] = unit_column(plan, small_ref, i, plan.latent + 4 + k)

        def chunk(j, _):
            rows = aligned(i * LANES + j * 16, 16)
            mean, inverse, gain, bias = (
                tiled(column_ref[n, aligned(j * 16, 16), :], plan) for n in range(4))
            scaled = (h_ref[rows, :] - mean) * inverse
            h_ref[rows, :] = scaled
            normed = gain * scaled + bias
            active = normed * jax.nn.sigmoid(normed) * keep_ref[k, rows, :].astype(jnp.float32)
            if spare:
                row = lax.broadcasted_iota(jnp.int32, active.shape, 0) + (i * LANES + j * 16)
                active = jnp.where(lax.rem(row, plan.hp) == plan.h, 1.0, active)
            out_ref[rows, :] = active.astype(jnp.bfloat16)
            return 0
        lax.fori_loop(0, LANES // 16, chunk, 0)
        return 0
    lax.fori_loop(0, plan.hh // LANES, block, 0)


def keep_rows(plan, flags_ref, keep_ref, k):
    def lane(t, _):
        lanes = aligned(t * LANES)
        for group in range(plan.nx):
            for start in range(0, plan.hp, 16):
                at = group * plan.h + start
                value = flags_ref[at:at + 16, lanes].astype(jnp.float32) * keep_scale
                if start + 16 > plan.h:
                    row = lax.broadcasted_iota(jnp.int32, value.shape, 0)
                    value = jnp.where(row < plan.h - start, value, 0.0)
                at = group * plan.hp + start
                keep_ref[k, at:at + 16, lanes] = value.astype(jnp.bfloat16)
        return 0
    lax.fori_loop(0, plan.cells // LANES, lane, 0)


def forward_kernel(plan, total_cells, *refs):
    (w1, wsmall, wout, x_hbm, flags_hbm, draws_ref,
     embed_all, small_out, readout_all, center_out, log_var_out, sample_out, layers_out, scaled_out,
     keep_out, rows_out,
     w1_ref, small_ref, x_ref, keep_ref, flags_ref, h_ref, layer_ref, column_ref, latent_ref,
     wide, tall, send_sem, recv_sem, meet_send, meet_recv, own_sem, load_sem, flag_sem, out_sem) = refs
    mid = plan.midp
    load = pltpu.make_async_copy(x_hbm, x_ref, load_sem)
    deep = flags_ref.shape[0]

    def flags(k):
        return pltpu.make_async_copy(
            flags_hbm.at[k], flags_ref.at[k % deep, pl.ds(0, plan.hidden), :], flag_sem.at[k % deep])

    for k in range(deep):
        flags(k).start()
    load.start()
    sets = send_sem.shape[0]
    embed, small, readout = (
        Gather(plan, source, target, width, send_sem.at[u % sets], recv_sem.at[u])
        for u, (source, target, width) in enumerate((
            (w1, w1_ref, plan.gp), (wsmall, small_ref, plan.small), (wout, readout_all, plan.gp))))
    own = [g.own_copy(own_sem.at[u]) for u, g in enumerate((embed, small, readout))]
    for copy in own:
        copy.start()
    peers = Meet.peers(plan)
    barrier = pltpu.get_barrier_semaphore()
    for device in peers:
        pl.semaphore_signal(barrier, inc=1, device_id=device, device_id_type=MESH)
    pl.semaphore_wait(barrier, len(peers))

    def keepers(k):
        flags(k).wait()
        keep_rows(plan, flags_ref.at[k % deep], keep_ref, k)
        if k + deep < 4:
            flags(k + deep).start()

    embed.start_own()
    late = embed.phases - 2
    for phase in range(1, embed.phases):
        if phase <= 4:
            keepers(phase - 1)
        if phase == late:
            if sets == 1:
                pass
            else:
                small.start_own()
        embed.forward(phase)
    for k in range(embed.phases - 1, 4):
        keepers(k)
    if sets == 1:
        embed.finish_sends()
        small.start_own()
    load.wait()
    tail = layer_ref.shape[1] - plan.hh
    for k in range(4):
        if tail:
            layer_ref[k, plan.hh:, :] = jnp.zeros((tail, plan.cells), jnp.bfloat16)
    latent_ref[...] = jnp.zeros_like(latent_ref)
    latent_ref[2, 0:plan.latent, :] = draws_ref[...]
    own[0].wait()
    embed.finish_twin()
    outs = [pltpu.make_async_copy(w1_ref, embed_all, out_sem.at[0])]
    outs[0].start()

    done = 1
    for j in range(plan.ny):
        start, stop = j * plan.gp, min((j + 1) * plan.gp, plan.genes)
        part = rows_dot(w1_ref[:, start:stop], x_ref[start:stop, :])
        h_ref[0] = part if j == 0 else h_ref[0] + part
        if done < small.phases:
            small.forward(done)
            done += 1
        if j == 1 and sets > 1:
            readout.start_own()
    while done < small.phases:
        small.forward(done)
        done += 1
    own[1].wait()
    small.finish_twin()
    if sets == 1:
        small.finish_sends()
        readout.start_own()
    outs.append(pltpu.make_async_copy(small_ref, small_out, out_sem.at[1]))
    outs[-1].start()
    own[2].wait()

    state = {"phase": 1}

    def between(second):
        if state["phase"] < readout.phases:
            readout.forward(state["phase"])
            state["phase"] += 1

    def norm(k, spare):
        h = h_ref.at[k % 2]
        moment_rows(plan, h, rows_out.at[k])
        meet = Meet(plan, wide.at[k], tall.at[k], meet_send.at[k], meet_recv.at[k])
        rows_out[k] = meet.run(rows_out[k], merge_moments, float(plan.cells), between)
        activate(plan, k, h, rows_out.at[k], small_ref, keep_ref, layer_ref.at[k], column_ref,
                 total_cells, spare)
        for n, (source, target) in enumerate((
                (h, scaled_out.at[k]),
                (layer_ref.at[k, pl.ds(0, plan.hh), :], layers_out.at[k]),
                (keep_ref.at[k], keep_out.at[k]))):
            outs.append(pltpu.make_async_copy(source, target, out_sem.at[3 + 3 * k + n]))
            outs[-1].start()
        return outs[-3]

    def hidden(source, lane, target):
        for j in range(plan.ny):
            at = j * plan.small + lane
            part = rows_dot(small_ref[:, at:at + plan.midl], source[mid * j:mid * j + plan.midl, :])
            target[...] = part if j == 0 else target[...] + part

    wrote_one = norm(0, False)
    hidden(layer_ref.at[0], plan.o2, h_ref.at[1])
    wrote_two = norm(1, True)
    half = plan.ny // 2
    for j in range(plan.ny):
        at = j * plan.small + plan.op
        part = over_rows(small_ref[:, at:at + plan.ml], layer_ref[1, 0:plan.hh, :])
        spot = (j % half) * plan.moments
        latent_ref[j // half, spot:spot + plan.moments, :] = part[:plan.moments]
    center, log_var = latent_ref[0], latent_ref[1]
    sample = center + jnp.exp(0.5 * log_var) * latent_ref[2]
    row = lax.broadcasted_iota(jnp.int32, sample.shape, 0)
    sample_out[...] = jnp.where(row < plan.latent, sample, 0.0).astype(jnp.bfloat16)
    center_out[...] = latent_ref[0, 0:plan.latent, :]
    log_var_out[...] = latent_ref[1, 0:plan.latent, :]
    wrote_one.wait()
    h_ref[0] = rows_dot(small_ref[:, plan.ol:plan.ol + plan.ll], sample_out[...])
    norm(2, False)
    wrote_two.wait()
    hidden(layer_ref.at[2], plan.o4, h_ref.at[1])
    norm(3, True)
    while state["phase"] < readout.phases:
        between(False)
    readout.finish_twin()
    if sets > 1:
        embed.finish_sends()
        small.finish_sends()
    readout.finish_sends()
    for copy in outs:
        if copy is not wrote_one and copy is not wrote_two:
            copy.wait()


def forward_all(plan, total_cells, w1, wsmall, wout, profiles, flags, draws):
    any_spec, vmem = pl.BlockSpec(memory_space=pl.ANY), pl.BlockSpec(memory_space=pltpu.VMEM)
    f32, bf16 = jnp.float32, jnp.bfloat16
    n = plan.nx + plan.ny - 2
    cuts = len(plan.cuts)
    sets = 3 if plan.blocks <= 32 else 1
    shape = jax.ShapeDtypeStruct
    return pl.pallas_call(
        functools.partial(forward_kernel, plan, total_cells),
        out_shape=[
            shape((plan.hh, plan.gg), bf16), shape((plan.hh, plan.ny * plan.small), bf16),
            shape((plan.hh, plan.gg), bf16), shape((plan.latent, plan.cells), f32),
            shape((plan.latent, plan.cells), f32), shape((plan.ll, plan.cells), bf16),
            shape((4, plan.hh, plan.cells), bf16), shape((4, plan.hh, plan.cells), f32),
            shape((4, plan.hh, plan.cells), bf16), shape((4, 2, plan.hh), f32)],
        in_specs=[any_spec] * 5 + [vmem],
        out_specs=[any_spec] * 3 + [vmem] * 3 + [any_spec] * 3 + [vmem],
        scratch_shapes=[
            pltpu.VMEM((plan.hh, plan.gg), bf16),
            pltpu.VMEM((plan.hh, plan.ny * plan.small), bf16),
            pltpu.VMEM((plan.genes, plan.cells), bf16),
            pltpu.VMEM((4, plan.hh, plan.cells), bf16),
            pltpu.VMEM((2 if sets > 1 else 1, plan.hidden + 16, plan.cells), jnp.int32),
            pltpu.VMEM((2, plan.hh, plan.cells), f32),
            pltpu.VMEM((4, plan.hh + plan.midl - plan.midp, plan.cells), bf16),
            pltpu.VMEM((4, LANES, LANES), f32),
            pltpu.VMEM((3, plan.ll, plan.cells), f32),
            pltpu.VMEM((4, plan.nx, 2, plan.hh), f32),
            pltpu.VMEM((4, plan.ny, 2, plan.hh), f32),
            pltpu.SemaphoreType.DMA((sets, cuts, plan.blocks // 2, 7)),
            pltpu.SemaphoreType.DMA((3, cuts, plan.blocks)),
            pltpu.SemaphoreType.DMA((4, n)),
            pltpu.SemaphoreType.DMA((4, n)),
            pltpu.SemaphoreType.DMA((3,)),
            pltpu.SemaphoreType.DMA,
            pltpu.SemaphoreType.DMA((2,)),
            pltpu.SemaphoreType.DMA((15,)),
        ],
        compiler_params=pltpu.CompilerParams(
            collective_id=0, has_side_effects=True, vmem_limit_bytes=60 * 1024 * 1024),
    )(w1, wsmall, wout, profiles, flags, draws)


def meet_kernel(plan, merge, x_ref, o_ref, wide, tall, send_sem, recv_sem):
    peers = Meet.peers(plan)
    barrier = pltpu.get_barrier_semaphore()
    for device in peers:
        pl.semaphore_signal(barrier, inc=1, device_id=device, device_id_type=MESH)
    pl.semaphore_wait(barrier, len(peers))
    meet = Meet(plan, wide, tall, send_sem, recv_sem)
    o_ref[...] = meet.run(x_ref[...], merge, float(plan.cells))


def meet_all(plan, value, merge, collective_id):
    rows, width = value.shape
    n = plan.nx + plan.ny - 2
    return pl.pallas_call(
        functools.partial(meet_kernel, plan, merge),
        out_shape=jax.ShapeDtypeStruct(value.shape, jnp.float32),
        in_specs=[pl.BlockSpec(memory_space=pltpu.VMEM)],
        out_specs=pl.BlockSpec(memory_space=pltpu.VMEM),
        scratch_shapes=[
            pltpu.VMEM((plan.nx, rows, width), jnp.float32),
            pltpu.VMEM((plan.ny, rows, width), jnp.float32),
            pltpu.SemaphoreType.DMA((n,)),
            pltpu.SemaphoreType.DMA((n,)),
        ],
        compiler_params=pltpu.CompilerParams(collective_id=collective_id, has_side_effects=True),
    )(value)


def share_kernel(plan, row_ref, block_ref, row_out, block_out, wide, tall, send_sem, recv_sem):
    peers = Meet.peers(plan)
    barrier = pltpu.get_barrier_semaphore()
    for device in peers:
        pl.semaphore_signal(barrier, inc=1, device_id=device, device_id_type=MESH)
    pl.semaphore_wait(barrier, len(peers))
    meet = Meet(plan, wide, tall, send_sem, recv_sem)
    wide[meet.gx] = row_ref[...]
    tall[meet.gy] = block_ref[...]
    copies = meet.copies(False) + meet.copies(True)
    for copy in copies:
        copy.start()
    for copy in copies:
        copy.wait_recv()
    row_out[...] = wide[0]
    block_out[...] = tall[0]
    for copy in copies:
        copy.wait_send()


def share_all(plan, row, block, collective_id):
    n = plan.nx + plan.ny - 2
    return pl.pallas_call(
        functools.partial(share_kernel, plan),
        out_shape=[jax.ShapeDtypeStruct(row.shape, jnp.float32),
                   jax.ShapeDtypeStruct(block.shape, jnp.float32)],
        in_specs=[pl.BlockSpec(memory_space=pltpu.VMEM)] * 2,
        out_specs=[pl.BlockSpec(memory_space=pltpu.VMEM)] * 2,
        scratch_shapes=[
            pltpu.VMEM((plan.nx, *row.shape), jnp.float32),
            pltpu.VMEM((plan.ny, *block.shape), jnp.float32),
            pltpu.SemaphoreType.DMA((n,)),
            pltpu.SemaphoreType.DMA((n,)),
        ],
        compiler_params=pltpu.CompilerParams(collective_id=collective_id, has_side_effects=True),
    )(row, block)


class Reduce:
    def __init__(self, plan, width, part, twin, slots, send_sem, twin_sem, recv_sem):
        self.plan, self.width, self.part, self.twin, self.slots = plan, width, part, twin, slots
        self.send_sem, self.twin_sem, self.recv_sem = send_sem, twin_sem, recv_sem
        self.cuts = [(Flow(plan, kind), *cut) for kind, cut in enumerate(plan.cuts)]

    @staticmethod
    def slot_counts(plan):
        counts = []
        for kind in range(len(plan.cuts)):
            sizes = (plan.ny // 2, plan.nx // 2, 2)
            first, second = (((0, 1, 2), (2, 1, 0)), ((1, 2, 0), (1, 0, 2)))[kind]
            mp, mq, mr = (max(sizes[i], sizes[j]) for i, j in zip(first, second))
            a, b, c = (Reduce.sides(m) for m in (mp, mq, mr))
            far_r = (mr > 2) * (mr * mq * mp)
            counts.append((far_r, mq * mp * (c + (mq > 2)), mp * (c + b + (mp > 2)), c + b + a))
        return counts

    @staticmethod
    def sides(most):
        return 1 if most == 2 else (2 if most > 2 else 0)

    def block(self, ref, cut, gx, gy):
        return ref.at[
            pl.ds(pl.multiple_of(gx * self.plan.hp + cut[1], 16), cut[2]),
            pl.ds(pl.multiple_of(gy * self.width, LANES), self.width),
        ]

    def twin_block(self, cut, gx, y):
        return self.twin.at[
            pl.ds(pl.multiple_of(gx * self.plan.hp + cut[1], 16), cut[2]),
            pl.ds(pl.multiple_of(y * self.width, LANES), self.width),
        ]

    def twin_copy(self, kind, cut, gx, y):
        flow = cut[0]
        return pltpu.make_async_remote_copy(
            src_ref=self.block(self.part, cut, gx, 2 * y + 1 - flow.core),
            dst_ref=self.twin_block(cut, gx, y),
            send_sem=self.twin_sem.at[0, kind, gx * (self.plan.ny // 2) + y],
            recv_sem=self.twin_sem.at[1, kind, gx * (self.plan.ny // 2) + y],
            device_id=flow.twin(), device_id_type=MESH,
        )

    def each_twin(self, visit, ys=None):
        ny2 = self.plan.ny // 2
        for kind, cut in enumerate(self.cuts):
            def one(n, _, kind=kind, cut=cut):
                visit(self.twin_copy(kind, cut, n // ny2, lax.rem(n, ny2)))
                return 0
            lax.fori_loop(0, self.plan.blocks // 2, one, 0)

    def start_twin(self):
        self.each_twin(lambda copy: copy.start())

    def entry(self, kind, stage, spot, axis, came_from):
        flow = self.cuts[kind][0]
        mp, mq, mr = flow.most
        far_r, far_q, far_p, _ = Reduce.slot_counts(self.plan)[kind]
        sides = [Reduce.sides(m) for m in flow.most]
        dp, dq, dr = spot
        if stage == 2:
            return (dr * mq + dq) * mp + dp
        if stage == 1:
            base, which = far_r, (dq * mp + dp) * (sides[2] + (mq > 2))
        elif stage == 0:
            base, which = far_r + far_q, dp * (sides[2] + sides[1] + (mp > 2))
        else:
            base, which = far_r + far_q + far_p, 0
        offset = 0
        for later in (2, 1, 0):
            if later == stage:
                return base + which + offset
            if later == axis:
                side = 0 if sides[axis] == 1 else (came_from + 1) // 2
                return base + which + offset + side
            offset += sides[later]

    def slot(self, kind, index):
        cut = self.cuts[kind]
        total = sum(Reduce.slot_counts(self.plan)[kind])
        return self.slots[kind].at[index], self.recv_sem[kind].at[index]

    def gather_terms(self, kind, cut, spot, stage, sign):
        flow = cut[0]
        ny2 = self.plan.ny // 2
        gx, gy = flow.device(spot)
        y = gy // 2
        copy = self.twin_copy(kind, cut, gx, y)
        copy.wait_recv()
        own = self.block(self.part, cut, gx, gy)
        twin = self.twin_block(cut, gx, y)
        arrivals = []
        for axis in (2, 1, 0):
            if axis > stage:
                for side in (-1, 1):
                    there, _ = flow.step(axis, side)
                    if flow.most[axis] < 2:
                        continue
                    arrivals.append((there, self.entry(kind, stage, spot, axis, side)))
            elif axis == stage and flow.most[axis] > 2:
                away = self.here_away(flow, axis, sign)
                arrivals.append((away, self.entry(kind, stage, spot, axis, None)))
        return own, twin, arrivals

    def here_away(self, flow, axis, sign):
        to = flow.here[axis] - sign
        return (to >= 0) & (to < flow.limit[axis])

    def add_in(self, kind, cut, spot, stage, sign):
        own, twin, arrivals = self.gather_terms(kind, cut, spot, stage, sign)
        own[...] = (own[...].astype(jnp.float32) + twin[...].astype(jnp.float32)).astype(jnp.bfloat16)
        for there, index in arrivals:
            slot, sem = self.slot(kind, index)
            @when(there)
            def _(slot=slot, sem=sem):
                pltpu.make_async_copy(slot, slot, sem).wait()
                own[...] = (own[...].astype(jnp.float32) + slot[...].astype(jnp.float32)).astype(
                    jnp.bfloat16)
        return own

    def onward(self, kind, cut, spot, stage, sign):
        flow = cut[0]
        _, device = self.toward(flow, stage, sign)
        gx, gy = flow.device(spot)
        to = flow.here[stage] + sign
        index_same = self.entry(kind, stage, spot, stage, None) if flow.most[stage] > 2 else None
        done = to == spot[stage]
        p_same = flow.here[0] == spot[0]
        q_same = flow.here[1] == spot[1]
        if stage == 2:
            deeper = jnp.where(q_same, jnp.where(p_same,
                               self.entry(kind, -1, spot, 2, -sign),
                               self.entry(kind, 0, spot, 2, -sign)),
                               self.entry(kind, 1, spot, 2, -sign))
        elif stage == 1:
            deeper = jnp.where(p_same, self.entry(kind, -1, spot, 1, -sign),
                               self.entry(kind, 0, spot, 1, -sign))
        else:
            deeper = self.entry(kind, -1, spot, 0, -sign)
        index = deeper if index_same is None else jnp.where(done, deeper, index_same)
        slot, sem = self.slot(kind, index)
        ny2 = self.plan.ny // 2
        return pltpu.make_async_remote_copy(
            src_ref=self.block(self.part, cut, gx, gy), dst_ref=slot,
            send_sem=self.send_sem.at[kind, gx * ny2 + gy // 2], recv_sem=sem,
            device_id=device, device_id_type=MESH,
        )

    def toward(self, flow, axis, sign):
        return flow.step(axis, sign)

    def walk(self, visit, stage):
        for kind, cut in enumerate(self.cuts):
            flow = cut[0]
            p, q, r = flow.here
            np_, nq, nr = flow.limit
            mp, mq, mr = flow.most

            def one(n, _, kind=kind, cut=cut):
                if stage == 2:
                    k, dq, dp = mr - 1 - n // (mq * mp), lax.rem(n // mp, mq), lax.rem(n, mp)
                elif stage == 1:
                    k, dp = mq - 1 - n // mp, lax.rem(n, mp)
                else:
                    k = mp - 1 - n
                for sign in (-1, 1):
                    if stage == 2:
                        d = r + sign * k
                        spot, good = (dp, dq, d), (d >= 0) & (d < nr) & (dq < nq) & (dp < np_)
                    elif stage == 1:
                        d = q + sign * k
                        spot, good = (dp, d, r), (d >= 0) & (d < nq) & (dp < np_)
                    else:
                        d = p + sign * k
                        spot, good = (d, q, r), (d >= 0) & (d < np_)
                    pl.when(good)(functools.partial(visit, kind, cut, spot, stage, sign))
                return 0
            count = {2: (mr - 1) * mq * mp, 1: (mq - 1) * mp, 0: mp - 1}[stage]
            lax.fori_loop(0, count, one, 0)

    def pass_on(self, stage):
        def visit(kind, cut, spot, stage, sign):
            self.add_in(kind, cut, spot, stage, sign)
            self.onward(kind, cut, spot, stage, sign).start()
        self.walk(visit, stage)

    def own_sum(self, out_ref, factor):
        for kind, cut in enumerate(self.cuts):
            flow = cut[0]
            own = self.add_in(kind, cut, flow.here, -1, None)
            out_ref[pl.ds(cut[1], cut[2]), :] = own[...].astype(jnp.float32) * factor

    def finish_sends(self):
        self.each_twin(lambda copy: copy.wait_send())
        def visit(kind, cut, spot, stage, sign):
            self.onward(kind, cut, spot, stage, sign).wait_send()
        for stage in (2, 1, 0):
            self.walk(visit, stage)


def reduce_kernel(plan, width, factor, x_ref, o_ref, part, twin, *rest):
    n = len(plan.cuts)
    slots, (send_sem, twin_sem), recv_sem, load_sem = rest[:n], rest[n:n + 2], rest[n + 2:2 * n + 2], rest[-1]
    load = pltpu.make_async_copy(x_ref, part, load_sem)
    load.start()
    greet(plan)
    load.wait()
    reduce = Reduce(plan, width, part, twin, slots, send_sem, twin_sem, recv_sem)
    reduce.start_twin()
    for stage in (2, 1, 0):
        reduce.pass_on(stage)
    reduce.own_sum(o_ref, factor)
    reduce.finish_sends()


def reduce_all(plan, value, factor, collective_id):
    width = value.shape[1] // plan.ny
    counts = [sum(c) for c in Reduce.slot_counts(plan)]
    return pl.pallas_call(
        functools.partial(reduce_kernel, plan, width, factor),
        out_shape=jax.ShapeDtypeStruct((plan.hp, width), jnp.float32),
        in_specs=[pl.BlockSpec(memory_space=pl.ANY)],
        out_specs=pl.BlockSpec(memory_space=pltpu.VMEM),
        scratch_shapes=[
            pltpu.VMEM((plan.hh, plan.ny * width), jnp.bfloat16),
            pltpu.VMEM((plan.hh, plan.ny // 2 * width), jnp.bfloat16),
            *[pltpu.VMEM((c, cut[1], width), jnp.bfloat16) for c, cut in zip(counts, plan.cuts)],
            pltpu.SemaphoreType.DMA((len(plan.cuts), plan.blocks // 2)),
            pltpu.SemaphoreType.DMA((2, len(plan.cuts), plan.blocks // 2)),
            *[pltpu.SemaphoreType.DMA((c,)) for c in counts],
            pltpu.SemaphoreType.DMA,
        ],
        compiler_params=pltpu.CompilerParams(
            collective_id=collective_id, has_side_effects=True, vmem_limit_bytes=60 * 1024 * 1024),
    )(value)


def rows_dot(left, right):
    return lax.dot_general(left, right, (((1,), (0,)), ((), ())), preferred_element_type=jnp.float32)


def over_cells(left, right):
    return lax.dot_general(left, right, (((1,), (1,)), ((), ())), preferred_element_type=jnp.float32)


def over_rows(left, right):
    return lax.dot_general(left, right, (((0,), (0,)), ((), ())), preferred_element_type=jnp.float32)


def pad_to(value, rows, lanes):
    return jnp.pad(value, ((0, rows - value.shape[0]), (0, lanes - value.shape[1])))


def middle_piece(plan, matrix):
    turned = matrix.T.reshape(plan.h, plan.groups, plan.h)
    wide = jnp.pad(turned, ((0, plan.hp - plan.h), (0, 0), (0, plan.hp - plan.h)))
    return pad_to(wide.reshape(plan.hp, plan.midp), plan.hp, plan.midl)


def middle_back(plan, piece):
    cut = piece[:plan.h, :plan.midp].reshape(plan.h, plan.groups, plan.hp)[:, :, :plan.h]
    return cut.reshape(plan.h, plan.mid).T


def with_row(plan, block, row, first):
    spare = jnp.where(first, row, jnp.zeros_like(row))[None]
    return pad_to(jnp.concatenate([block, spare], axis=0), plan.hp, block.shape[1])


def on_device(
    nx, ny,
    transcript_profiles,
    experiment_labels,
    measured_flags,
    retained_unit_flags,
    standard_normal_draws,
    compressor_first_matrix,
    compressor_second_matrix,
    posterior_matrix,
    posterior_intercepts,
    expander_first_matrix,
    expander_second_matrix,
    output_matrix,
    output_intercept,
    normalizer_factors,
    normalizer_translations,
):
    cells = transcript_profiles.shape[0]
    plan = Plan(nx, ny, cells, output_matrix.shape[1], output_matrix.shape[0], expander_first_matrix.shape[0])
    total_cells = float(cells * nx * ny)
    gx, gy = lax.axis_index("gx"), lax.axis_index("gy")
    first = gx == 0

    wide = jnp.concatenate([
        pad_to(compressor_first_matrix.T, plan.hp, plan.g),
        with_row(plan, output_matrix, output_intercept, first)], axis=0)
    strip = lax.ppermute(wide[:, :plan.strip], "gy", [(j + 1, j) for j in range(ny - 1)])
    wide = jnp.concatenate([wide, strip], axis=1)
    wide = pad_to(wide, 2 * plan.hp, plan.gp + plan.strip + plan.shift * ny)
    wide = lax.dynamic_slice_in_dim(wide, gy * plan.shift, plan.gp, 1)
    last = jnp.concatenate([
        expander_first_matrix.T, normalizer_factors.T, normalizer_translations.T], axis=1)
    small = jnp.concatenate([
        middle_piece(plan, compressor_second_matrix),
        middle_piece(plan, expander_second_matrix),
        pad_to(with_row(plan, posterior_matrix, posterior_intercepts, first), plan.hp, plan.ml),
        pad_to(last, plan.hp, plan.ll)], axis=1)
    profiles = transcript_profiles.T
    draws = standard_normal_draws.T
    (embed_all, small_all, readout_all, center, log_var, sample, layers, scaled_values, keep_values,
     norm_rows) = forward_all(
        plan, total_cells, wide[:plan.hp], small, wide[plan.hp:], profiles,
        jnp.swapaxes(retained_unit_flags, 1, 2), draws)
    parts = small_all.reshape(plan.hh, ny, plan.small)
    encoder_all = parts[:, :, plan.o2:plan.o2 + plan.midp].reshape(plan.hh, plan.hh)
    decoder_all = parts[:, :, plan.o4:plan.o4 + plan.midp].reshape(plan.hh, plan.hh)
    projector_all = parts[:, :, plan.op:plan.op + plan.moments].reshape(plan.hh, 2 * plan.latent)
    lifting_all = parts[:, 0, plan.ol:plan.ol + plan.latent]
    rows = parts[:, 0, plan.ol + plan.latent:plan.ol + plan.latent + 8].astype(jnp.float32)
    gains = [rows[:, k:k + 1] for k in range(4)]
    biases = [rows[:, 4 + k:5 + k] for k in range(4)]

    spread = jnp.exp(0.5 * log_var)

    def kept_layer(k):
        inverse = lax.rsqrt(norm_rows[k, 1] / total_cells + norm_eps)[:, None]
        return layers[k], gains[k] * scaled_values[k] + biases[k], scaled_values[k], inverse

    one, two, three, four = (kept_layer(k) for k in range(4))

    def backward_layer(upstream, kept, k, loss, ident):
        _, normed, scaled, inverse = kept
        sigma = jax.nn.sigmoid(normed)
        slope = upstream * keep_values[k].astype(jnp.float32) * sigma * (
            1.0 + normed * (1.0 - sigma))
        pair = jnp.stack([jnp.sum(slope, axis=1), jnp.sum(slope * scaled, axis=1),
                          jnp.full((plan.hh,), loss)])
        merged = meet_all(plan, pair, merge_sums, 2)
        shift, gain = merged[0], merged[1]
        grad = gains[k] * inverse * (
            slope - (shift[:, None] + scaled * gain[:, None]) / total_cells)
        return grad.astype(jnp.bfloat16), gain, shift, merged[2, 0]

    output = over_rows(readout_all[:, :plan.genes], four[0])
    residual = output - profiles.astype(jnp.float32)
    picker = (jnp.arange(measured_flags.shape[0], dtype=jnp.int32)[:, None]
              == experiment_labels[None, :]).astype(jnp.bfloat16)
    slab = over_rows(measured_flags.astype(jnp.bfloat16), picker)
    weighted = slab * residual
    rebuild = 0.5 * jnp.sum(weighted * residual)
    diverge = 0.5 * jnp.sum(jnp.exp(log_var) + center * center - 1.0 - log_var)
    own_loss = rebuild + kl_weight * diverge
    output_grad = weighted.astype(jnp.bfloat16)

    def frames(product):
        padded = pad_to(product, plan.hh, max(plan.frame_start) + plan.frame)
        return jnp.concatenate(
            [padded[:, s:s + plan.frame] for s in plan.frame_start], axis=1).astype(jnp.bfloat16)

    readout_part = frames(over_cells(four[0], output_grad))
    upstream = rows_dot(readout_all[:, :plan.genes], output_grad)
    grad_four, gain_four, shift_four, loss_sum = backward_layer(upstream, four, 3, own_loss, 5)
    upstream = over_rows(decoder_all, grad_four)
    grad_three, gain_three, shift_three, _ = backward_layer(upstream, three, 2, own_loss, 6)
    sample_grad = over_rows(lifting_all, grad_three)[:plan.latent]
    center_grad = sample_grad + kl_weight * center
    logvar_grad = sample_grad * 0.5 * spread * draws + kl_weight * 0.5 * (jnp.exp(log_var) - 1.0)
    moment_grad = jnp.concatenate([center_grad, logvar_grad], axis=0).astype(jnp.bfloat16)
    upstream = rows_dot(projector_all, moment_grad)
    grad_two, gain_two, shift_two, _ = backward_layer(upstream, two, 1, own_loss, 7)
    upstream = over_rows(encoder_all, grad_two)
    grad_one, gain_one, shift_one, _ = backward_layer(upstream, one, 0, own_loss, 8)
    input_grad = (over_rows(embed_all[:, :plan.genes], grad_one) - weighted).astype(jnp.bfloat16)

    encoder_part = over_cells(grad_two, one[0]).reshape(plan.hh, ny, plan.midp)
    decoder_part = over_cells(grad_four, three[0]).reshape(plan.hh, ny, plan.midp)
    projector_part = over_cells(two[0], moment_grad).reshape(plan.hh, ny, plan.moments)
    lifting_part = over_cells(grad_three, sample)[:, :plan.latent]

    def lanes(value, width):
        return jnp.pad(value, ((0, 0), (0, 0), (0, width - value.shape[2])))

    small_part = jnp.concatenate([
        lanes(encoder_part, plan.midl), lanes(decoder_part, plan.midl),
        lanes(projector_part, plan.ml),
        jnp.broadcast_to(pad_to(lifting_part, plan.hh, plan.ll)[:, None, :], (plan.hh, ny, plan.ll)),
    ], axis=2).reshape(plan.hh, ny * plan.small).astype(jnp.bfloat16)
    embed_part = frames(over_cells(grad_one, profiles))

    readout_sum = reduce_all(plan, readout_part, 1.0 / total_cells, 3)
    small_sum = reduce_all(plan, small_part, 1.0 / total_cells, 4)
    embed_sum = reduce_all(plan, embed_part, 1.0 / total_cells, 3)
    starts = jnp.array([plan.g * j - plan.frame_start[j] for j in range(ny)], jnp.int32)
    readout_own = lax.dynamic_slice_in_dim(readout_sum, starts[gy], plan.g, 1)
    embed_own = lax.dynamic_slice_in_dim(embed_sum, starts[gy], plan.g, 1)

    row, lifting_own = share_all(plan, jnp.concatenate([
        readout_sum[plan.h:plan.h + 1],
        small_sum[plan.h:plan.h + 1, plan.op:plan.op + plan.ml]], axis=1),
        small_sum[:, plan.ol:plan.ol + plan.ll], 5)
    baseline_own = lax.dynamic_slice_in_dim(row[0, :plan.frame], starts[gy], plan.g, 0)

    def own_units(values):
        stack = jnp.stack(values, axis=0) / total_cells
        return lax.dynamic_slice_in_dim(stack, gx * plan.hp, plan.h, 1)

    small_h = small_sum[:plan.h]
    return (
        output.astype(jnp.bfloat16).T,
        center.T,
        loss_sum / total_cells,
        input_grad.T,
        embed_own[:plan.h].T,
        middle_back(plan, small_sum[:, plan.o2:plan.o2 + plan.midl]),
        small_h[:, plan.op:plan.op + plan.moments],
        row[0, plan.frame:plan.frame + plan.moments],
        lifting_own[:plan.h, :plan.latent].T,
        middle_back(plan, small_sum[:, plan.o4:plan.o4 + plan.midl]),
        readout_own[:plan.h],
        baseline_own,
        own_units([gain_one, gain_two, gain_three, gain_four]),
        own_units([shift_one, shift_two, shift_three, shift_four]),
    )


def solution(mesh):
    return jax.shard_map(
        functools.partial(on_device, mesh.shape["gx"], mesh.shape["gy"]),
        mesh=mesh,
        in_specs=(
            P(("gx", "gy"), None),
            P(("gx", "gy")),
            P(),
            P(None, ("gx", "gy"), None),
            P(("gx", "gy"), None),
            P("gy", "gx"),
            P("gy", "gx"),
            P("gx", "gy"),
            P("gy"),
            P(None, "gx"),
            P("gy", "gx"),
            P("gx", "gy"),
            P("gy"),
            P(None, "gx"),
            P(None, "gx"),
        ),
        out_specs=(
            P(("gx", "gy"), None),
            P(("gx", "gy"), None),
            P(),
            P(("gx", "gy"), None),
            P("gy", "gx"),
            P("gy", "gx"),
            P("gx", "gy"),
            P("gy"),
            P(None, "gx"),
            P("gy", "gx"),
            P("gx", "gy"),
            P("gy"),
            P(None, "gx"),
            P(None, "gx"),
        ),
        check_vma=False,
    )
```

```python
import functools

import jax
import jax.numpy as jnp
from jax import lax
from jax.experimental import pallas as pl
from jax.experimental.pallas import tpu as pltpu
from jax.sharding import PartitionSpec as P

norm_eps = 1e-05
keep_scale = 1.25
kl_weight = 5e-05
MESH = pl.DeviceIdType.MESH
LANES = 128


def round_up(value, multiple):
    return -(-value // multiple) * multiple


class Plan:
    def __init__(self, nx, ny, cells, genes_piece, hidden_piece, latent):
        self.nx, self.ny, self.cells = nx, ny, cells
        self.g, self.h, self.latent = genes_piece, hidden_piece, latent
        self.genes, self.hidden = genes_piece * ny, hidden_piece * nx
        self.hp = round_up(hidden_piece + 1, 16)
        self.hh = self.hp * nx
        tiles = round_up(self.genes, LANES) // LANES
        self.gp = round_up(tiles, ny) // ny * LANES
        self.gg = self.gp * ny
        self.shift = self.gp - self.g
        self.strip = round_up(self.shift * ny, LANES)
        starts = [self.g * j // LANES for j in range(ny)]
        ends = [round_up(self.g * (j + 1), LANES) // LANES for j in range(ny)]
        self.frame_start = [s * LANES for s in starts]
        self.frame = max(e - s for s, e in zip(starts, ends)) * LANES
        self.groups = nx // ny
        self.mid = self.hidden // ny
        self.midp = self.hp * self.groups
        self.midl = round_up(self.midp, LANES)
        self.moments = 2 * latent // ny
        self.ml = round_up(self.moments, LANES)
        self.ll = round_up(latent + 8, LANES)
        self.small = 2 * self.midl + self.ml + self.ll
        self.o2, self.o4 = 0, self.midl
        self.op, self.ol = 2 * self.midl, 2 * self.midl + self.ml
        self.blocks = nx * ny
        rows = round_up(self.hp * 2 // 3, 16)
        self.cuts = ((0, rows), (rows, self.hp - rows)) if rows < self.hp else ((0, rows),)
        self.fits = self.blocks <= 32 and self.hh * ny * self.frame <= 7 * 1024 * 1024


class Flow:
    def __init__(self, plan, kind):
        gx, gy = lax.axis_index("gx"), lax.axis_index("gy")
        self.plan, self.gx, self.gy = plan, gx, gy
        self.sizes = (plan.ny // 2, plan.nx // 2, 2)
        self.core = lax.rem(gy, 2)
        self.at = (gy // 2, gx // 2, lax.rem(gx, 2))
        self.orders = (((0, 1, 2), (2, 1, 0)), ((1, 2, 0), (1, 0, 2)))[kind]
        first, second = self.orders
        self.most = tuple(max(self.sizes[i], self.sizes[j]) for i, j in zip(first, second))
        self.least = tuple(min(self.sizes[i], self.sizes[j]) for i, j in zip(first, second))
        self.limit = tuple(self.pick(self.sizes[i], self.sizes[j]) for i, j in zip(first, second))
        self.here = tuple(self.pick(self.at[i], self.at[j]) for i, j in zip(first, second))

    def pick(self, zero, one):
        if isinstance(zero, int) and isinstance(one, int) and zero == one:
            return zero
        return jnp.where(self.core == 0, zero, one)

    def device(self, spot):
        place = [None] * 3
        for axis in range(3):
            place[axis] = self.pick(
                spot[self.orders[0].index(axis)], spot[self.orders[1].index(axis)]
            )
        return (place[1] * 2 + place[2], place[0] * 2 + self.core)

    def twin(self):
        return (self.gx, self.gy + 1 - 2 * self.core)

    def step(self, axis, sign):
        to = self.here[axis] + sign
        spot = tuple(to if i == axis else self.here[i] for i in range(3))
        return jnp.logical_and(to >= 0, to < self.limit[axis]), self.device(spot)


def neighbours(plan):
    flow = Flow(plan, 0)
    out = [(None, flow.twin())]
    for axis in range(3):
        for sign in (-1, 1):
            out.append(flow.step(axis, sign))
    return out


def when(condition):
    return (lambda f: f()) if condition is None else pl.when(condition)


def greet(plan, extra=()):
    barrier = pltpu.get_barrier_semaphore()
    count = jnp.int32(len(extra))
    for there, device in neighbours(plan):
        @when(there)
        def _(device=device):
            pl.semaphore_signal(barrier, inc=1, device_id=device, device_id_type=MESH)
        count = count + (1 if there is None else there.astype(jnp.int32))
    for device in extra:
        pl.semaphore_signal(barrier, inc=1, device_id=device, device_id_type=MESH)
    pl.semaphore_wait(barrier, count)


class Gather:
    def __init__(self, plan, source, target, width, send_sem, recv_sem):
        self.plan, self.source, self.target, self.width = plan, source, target, width
        self.send_sem, self.recv_sem = send_sem, recv_sem
        self.cuts = [(Flow(plan, kind), *cut) for kind, cut in enumerate(plan.cuts)]
        self.phases = 1 + max(sum(m - 1 for m in cut[0].most) for cut in self.cuts)

    def slot(self, cut, gx, gy):
        _, start, rows = cut
        return self.target.at[
            pl.ds(pl.multiple_of(gx * self.plan.hp + start, 16), rows),
            pl.ds(pl.multiple_of(gy * self.width, LANES), self.width),
        ]

    def own_copy(self, sem):
        plan = self.plan
        gx, gy = lax.axis_index("gx"), lax.axis_index("gy")
        place = self.target.at[
            pl.ds(pl.multiple_of(gx * plan.hp, 16), plan.hp),
            pl.ds(pl.multiple_of(gy * self.width, LANES), self.width),
        ]
        return pltpu.make_async_copy(self.source, place, sem)

    def copies(self, kind, cut, spot, own):
        flow = cut[0]
        gx, gy = flow.device(spot)
        dst = self.slot(cut, gx, gy)
        src = self.source.at[pl.ds(cut[1], cut[2]), :] if own else dst
        index = gx * (self.plan.ny // 2) + gy // 2
        goals = [(None, flow.twin(), 6)]
        level = None
        for axis in (2, 1, 0):
            for sign in (-1, 1):
                if flow.most[axis] < 2:
                    continue
                there, device = flow.step(axis, sign)
                if not own:
                    there = there & ((flow.here[axis] - spot[axis]) * sign >= 0)
                    if level is not None:
                        there = there & level
                goals.append((there, device, 2 * axis + (sign + 1) // 2))
            same = spot[axis] == flow.here[axis]
            level = same if level is None else level & same
        out = []
        for there, device, k in goals:
            out.append((there, pltpu.make_async_remote_copy(
                src_ref=src, dst_ref=dst,
                send_sem=self.send_sem.at[kind, index, k],
                recv_sem=self.recv_sem.at[kind, gx * self.plan.ny + gy],
                device_id=device, device_id_type=MESH,
            )))
        return out

    def arrived(self, kind, cut, gx, gy):
        ref = self.slot(cut, gx, gy)
        pltpu.make_async_copy(ref, ref, self.recv_sem.at[kind, gx * self.plan.ny + gy]).wait()

    def start_own(self):
        for kind, cut in enumerate(self.cuts):
            for there, copy in self.copies(kind, cut, cut[0].here, True):
                when(there)(copy.start)

    def walk(self, visit, phase=None):
        for kind, cut in enumerate(self.cuts):
            flow = cut[0]
            mp, mq, mr = flow.most

            def one(n, _, kind=kind, cut=cut, flow=flow):
                spot = (lax.rem(n, mp), lax.rem(n // mp, mq), n // (mp * mq))
                hops, good = 0, None
                for here, limit, at in zip(flow.here, flow.limit, spot):
                    hops = hops + jnp.abs(at - here)
                    good = at < limit if good is None else good & (at < limit)
                good = good & ((hops > 0) if phase is None else (hops == phase))
                pl.when(good)(functools.partial(visit, kind, cut, spot))
                return 0
            lax.fori_loop(0, mp * mq * mr, one, 0)

    def forward(self, phase):
        def visit(kind, cut, spot):
            self.arrived(kind, cut, *cut[0].device(spot))
            for there, copy in self.copies(kind, cut, spot, False):
                when(there)(copy.start)
        if phase < self.phases:
            self.walk(visit, phase)

    def finish_twin(self):
        plan = self.plan
        for kind, cut in enumerate(self.cuts):
            flow = cut[0]
            def one(n, _, kind=kind, cut=cut, flow=flow):
                gx, y = n // (plan.ny // 2), lax.rem(n, plan.ny // 2)
                self.arrived(kind, cut, gx, 2 * y + 1 - flow.core)
                return 0
            lax.fori_loop(0, plan.blocks // 2, one, 0)

    def finish_sends(self):
        for kind, cut in enumerate(self.cuts):
            for there, copy in self.copies(kind, cut, cut[0].here, True):
                when(there)(copy.wait_send)
        def visit(kind, cut, spot):
            for there, copy in self.copies(kind, cut, spot, False):
                when(there)(copy.wait_send)
        self.walk(visit)


class Meet:
    def __init__(self, plan, wide, tall, send_sem, recv_sem):
        self.plan, self.wide, self.tall = plan, wide, tall
        self.send_sem, self.recv_sem = send_sem, recv_sem
        self.gx, self.gy = lax.axis_index("gx"), lax.axis_index("gy")

    @staticmethod
    def peers(plan):
        gx, gy = lax.axis_index("gx"), lax.axis_index("gy")
        return ([(lax.rem(gx + k, plan.nx), gy) for k in range(1, plan.nx)]
                + [(gx, lax.rem(gy + k, plan.ny)) for k in range(1, plan.ny)])

    def copies(self, second):
        plan = self.plan
        n = plan.ny if second else plan.nx
        ref = self.tall if second else self.wide
        own = self.gy if second else self.gx
        out = []
        for k in range(1, n):
            to = lax.rem(own + k, n)
            at = (plan.nx - 1 if second else 0) + k - 1
            out.append(pltpu.make_async_remote_copy(
                src_ref=ref.at[own], dst_ref=ref.at[own],
                send_sem=self.send_sem.at[at], recv_sem=self.recv_sem.at[at],
                device_id=(self.gx, to) if second else (to, self.gy), device_id_type=MESH,
            ))
        return out

    def run(self, value, merge, members, between=None):
        plan = self.plan
        for second in (False, True):
            ref = self.tall if second else self.wide
            ref[self.gy if second else self.gx] = value
            copies = self.copies(second)
            for copy in copies:
                copy.start()
            if between is not None:
                between(second)
            for copy in copies:
                copy.wait_recv()
            value = merge([ref[i] for i in range(ref.shape[0])], members)
            members = members * plan.nx
            for copy in copies:
                copy.wait_send()
        return value


def merge_sums(parts, members):
    total = parts[0]
    for part in parts[1:]:
        total = total + part
    return total


def merge_moments(parts, members):
    n = len(parts)
    mean = merge_sums([part[0:1] for part in parts], 0) / n
    squares = merge_sums([part[1:2] for part in parts], 0)
    between = merge_sums([(part[0:1] - mean) * (part[0:1] - mean) for part in parts], 0)
    return jnp.concatenate([mean, squares + members * between], axis=0)


def tiled(column, plan):
    return jnp.concatenate([column] * (plan.cells // LANES), axis=1)


def lane_sums(value):
    total = value[:, :LANES]
    for at in range(LANES, value.shape[1], LANES):
        total = total + value[:, at:at + LANES]
    return total


def as_row(value):
    return jnp.sum(value.T, axis=0, keepdims=True)


def as_column(row):
    return jnp.broadcast_to(row, (LANES, LANES)).T


def aligned(start, rows=LANES):
    return pl.ds(pl.multiple_of(start, rows), rows)


def moment_rows(plan, h_ref, row_ref):
    def block(i, _):
        value = h_ref[aligned(i * LANES), :]
        sums = lane_sums(value)
        mean = jnp.sum(sums, axis=1, keepdims=True) / plan.cells
        offset = value - mean
        row_ref[0:1, aligned(i * LANES)] = as_row(sums) / plan.cells
        row_ref[1:2, aligned(i * LANES)] = as_row(lane_sums(offset * offset))
        return 0
    lax.fori_loop(0, plan.hh // LANES, block, 0)


def unit_column(plan, small_ref, i, lane):
    slab = small_ref[aligned(i * LANES), plan.ol + plan.ll - LANES:plan.ol + plan.ll]
    at = lane - (plan.ll - LANES)
    return jnp.broadcast_to(slab.astype(jnp.float32)[:, at:at + 1], (LANES, LANES))


def activate(plan, k, h_ref, row_ref, small_ref, keep_ref, out_ref, column_ref, total_cells, spare):
    def block(i, _):
        column_ref[0] = as_column(row_ref[0:1, aligned(i * LANES)])
        column_ref[1] = as_column(lax.rsqrt(row_ref[1:2, aligned(i * LANES)] / total_cells + norm_eps))
        column_ref[2] = unit_column(plan, small_ref, i, plan.latent + k)
        column_ref[3] = unit_column(plan, small_ref, i, plan.latent + 4 + k)

        def chunk(j, _):
            rows = aligned(i * LANES + j * 16, 16)
            mean, inverse, gain, bias = (
                tiled(column_ref[n, aligned(j * 16, 16), :], plan) for n in range(4))
            scaled = (h_ref[rows, :] - mean) * inverse
            h_ref[rows, :] = scaled
            normed = gain * scaled + bias
            active = normed * jax.nn.sigmoid(normed) * keep_ref[k, rows, :].astype(jnp.float32)
            if spare:
                row = lax.broadcasted_iota(jnp.int32, active.shape, 0) + (i * LANES + j * 16)
                active = jnp.where(lax.rem(row, plan.hp) == plan.h, 1.0, active)
            out_ref[rows, :] = active.astype(jnp.bfloat16)
            return 0
        lax.fori_loop(0, LANES // 16, chunk, 0)
        return 0
    lax.fori_loop(0, plan.hh // LANES, block, 0)


def keep_rows(plan, flags_ref, keep_ref, k):
    def lane(t, _):
        lanes = aligned(t * LANES)
        for group in range(plan.nx):
            for start in range(0, plan.hp, 16):
                at = group * plan.h + start
                value = flags_ref[at:at + 16, lanes].astype(jnp.float32) * keep_scale
                if start + 16 > plan.h:
                    row = lax.broadcasted_iota(jnp.int32, value.shape, 0)
                    value = jnp.where(row < plan.h - start, value, 0.0)
                at = group * plan.hp + start
                keep_ref[k, at:at + 16, lanes] = value.astype(jnp.bfloat16)
        return 0
    lax.fori_loop(0, plan.cells // LANES, lane, 0)


def forward_kernel(plan, total_cells, *refs):
    (w1, wsmall, wout, x_hbm, flags_hbm, draws_ref,
     embed_all, small_out, readout_all, center_out, log_var_out, sample_out, layers_out, scaled_out,
     keep_out, rows_out,
     w1_ref, small_ref, x_ref, keep_ref, flags_ref, h_ref, layer_ref, column_ref, latent_ref,
     wide, tall, send_sem, recv_sem, meet_send, meet_recv, own_sem, load_sem, flag_sem, out_sem) = refs
    mid = plan.midp
    load = pltpu.make_async_copy(x_hbm, x_ref, load_sem)
    deep = flags_ref.shape[0]

    def flags(k):
        return pltpu.make_async_copy(
            flags_hbm.at[k], flags_ref.at[k % deep, pl.ds(0, plan.hidden), :], flag_sem.at[k % deep])

    for k in range(deep):
        flags(k).start()
    load.start()
    sets = send_sem.shape[0]
    embed, small, readout = (
        Gather(plan, source, target, width, send_sem.at[u % sets], recv_sem.at[u])
        for u, (source, target, width) in enumerate((
            (w1, w1_ref, plan.gp), (wsmall, small_ref, plan.small), (wout, readout_all, plan.gp))))
    own = [g.own_copy(own_sem.at[u]) for u, g in enumerate((embed, small, readout))]
    for copy in own:
        copy.start()
    peers = Meet.peers(plan)
    barrier = pltpu.get_barrier_semaphore()
    for device in peers:
        pl.semaphore_signal(barrier, inc=1, device_id=device, device_id_type=MESH)
    pl.semaphore_wait(barrier, len(peers))

    def keepers(k):
        flags(k).wait()
        keep_rows(plan, flags_ref.at[k % deep], keep_ref, k)
        if k + deep < 4:
            flags(k + deep).start()

    embed.start_own()
    late = embed.phases - 2
    for phase in range(1, embed.phases):
        if phase <= 4:
            keepers(phase - 1)
        if phase == late:
            if sets == 1:
                pass
            else:
                small.start_own()
        embed.forward(phase)
    for k in range(embed.phases - 1, 4):
        keepers(k)
    if sets == 1:
        embed.finish_sends()
        small.start_own()
    load.wait()
    tail = layer_ref.shape[1] - plan.hh
    for k in range(4):
        if tail:
            layer_ref[k, plan.hh:, :] = jnp.zeros((tail, plan.cells), jnp.bfloat16)
    latent_ref[...] = jnp.zeros_like(latent_ref)
    latent_ref[2, 0:plan.latent, :] = draws_ref[...]
    own[0].wait()
    embed.finish_twin()
    outs = [pltpu.make_async_copy(w1_ref, embed_all, out_sem.at[0])]
    outs[0].start()

    done = 1
    for j in range(plan.ny):
        start, stop = j * plan.gp, min((j + 1) * plan.gp, plan.genes)
        part = rows_dot(w1_ref[:, start:stop], x_ref[start:stop, :])
        h_ref[0] = part if j == 0 else h_ref[0] + part
        if done < small.phases:
            small.forward(done)
            done += 1
        if j == 1 and sets > 1:
            readout.start_own()
    while done < small.phases:
        small.forward(done)
        done += 1
    own[1].wait()
    small.finish_twin()
    if sets == 1:
        small.finish_sends()
        readout.start_own()
    outs.append(pltpu.make_async_copy(small_ref, small_out, out_sem.at[1]))
    outs[-1].start()
    own[2].wait()

    state = {"phase": 1}

    def between(second):
        if state["phase"] < readout.phases:
            readout.forward(state["phase"])
            state["phase"] += 1

    def norm(k, spare):
        h = h_ref.at[k % 2]
        moment_rows(plan, h, rows_out.at[k])
        meet = Meet(plan, wide.at[k], tall.at[k], meet_send.at[k], meet_recv.at[k])
        rows_out[k] = meet.run(rows_out[k], merge_moments, float(plan.cells), between)
        activate(plan, k, h, rows_out.at[k], small_ref, keep_ref, layer_ref.at[k], column_ref,
                 total_cells, spare)
        for n, (source, target) in enumerate((
                (h, scaled_out.at[k]),
                (layer_ref.at[k, pl.ds(0, plan.hh), :], layers_out.at[k]),
                (keep_ref.at[k], keep_out.at[k]))):
            outs.append(pltpu.make_async_copy(source, target, out_sem.at[3 + 3 * k + n]))
            outs[-1].start()
        return outs[-3]

    def hidden(source, lane, target):
        for j in range(plan.ny):
            at = j * plan.small + lane
            part = rows_dot(small_ref[:, at:at + plan.midl], source[mid * j:mid * j + plan.midl, :])
            target[...] = part if j == 0 else target[...] + part

    wrote_one = norm(0, False)
    hidden(layer_ref.at[0], plan.o2, h_ref.at[1])
    wrote_two = norm(1, True)
    half = plan.ny // 2
    for j in range(plan.ny):
        at = j * plan.small + plan.op
        part = over_rows(small_ref[:, at:at + plan.ml], layer_ref[1, 0:plan.hh, :])
        spot = (j % half) * plan.moments
        latent_ref[j // half, spot:spot + plan.moments, :] = part[:plan.moments]
    center, log_var = latent_ref[0], latent_ref[1]
    sample = center + jnp.exp(0.5 * log_var) * latent_ref[2]
    row = lax.broadcasted_iota(jnp.int32, sample.shape, 0)
    sample_out[...] = jnp.where(row < plan.latent, sample, 0.0).astype(jnp.bfloat16)
    center_out[...] = latent_ref[0, 0:plan.latent, :]
    log_var_out[...] = latent_ref[1, 0:plan.latent, :]
    wrote_one.wait()
    h_ref[0] = rows_dot(small_ref[:, plan.ol:plan.ol + plan.ll], sample_out[...])
    norm(2, False)
    wrote_two.wait()
    hidden(layer_ref.at[2], plan.o4, h_ref.at[1])
    norm(3, True)
    while state["phase"] < readout.phases:
        between(False)
    readout.finish_twin()
    if sets > 1:
        embed.finish_sends()
        small.finish_sends()
    readout.finish_sends()
    for copy in outs:
        if copy is not wrote_one and copy is not wrote_two:
            copy.wait()


def forward_all(plan, total_cells, w1, wsmall, wout, profiles, flags, draws):
    any_spec, vmem = pl.BlockSpec(memory_space=pl.ANY), pl.BlockSpec(memory_space=pltpu.VMEM)
    f32, bf16 = jnp.float32, jnp.bfloat16
    n = plan.nx + plan.ny - 2
    cuts = len(plan.cuts)
    sets = 3 if plan.blocks <= 32 else 1
    shape = jax.ShapeDtypeStruct
    return pl.pallas_call(
        functools.partial(forward_kernel, plan, total_cells),
        out_shape=[
            shape((plan.hh, plan.gg), bf16), shape((plan.hh, plan.ny * plan.small), bf16),
            shape((plan.hh, plan.gg), bf16), shape((plan.latent, plan.cells), f32),
            shape((plan.latent, plan.cells), f32), shape((plan.ll, plan.cells), bf16),
            shape((4, plan.hh, plan.cells), bf16), shape((4, plan.hh, plan.cells), f32),
            shape((4, plan.hh, plan.cells), bf16), shape((4, 2, plan.hh), f32)],
        in_specs=[any_spec] * 5 + [vmem],
        out_specs=[any_spec] * 3 + [vmem] * 3 + [any_spec] * 3 + [vmem],
        scratch_shapes=[
            pltpu.VMEM((plan.hh, plan.gg), bf16),
            pltpu.VMEM((plan.hh, plan.ny * plan.small), bf16),
            pltpu.VMEM((plan.genes, plan.cells), bf16),
            pltpu.VMEM((4, plan.hh, plan.cells), bf16),
            pltpu.VMEM((2 if sets > 1 else 1, plan.hidden + 16, plan.cells), jnp.int32),
            pltpu.VMEM((2, plan.hh, plan.cells), f32),
            pltpu.VMEM((4, plan.hh + plan.midl - plan.midp, plan.cells), bf16),
            pltpu.VMEM((4, LANES, LANES), f32),
            pltpu.VMEM((3, plan.ll, plan.cells), f32),
            pltpu.VMEM((4, plan.nx, 2, plan.hh), f32),
            pltpu.VMEM((4, plan.ny, 2, plan.hh), f32),
            pltpu.SemaphoreType.DMA((sets, cuts, plan.blocks // 2, 7)),
            pltpu.SemaphoreType.DMA((3, cuts, plan.blocks)),
            pltpu.SemaphoreType.DMA((4, n)),
            pltpu.SemaphoreType.DMA((4, n)),
            pltpu.SemaphoreType.DMA((3,)),
            pltpu.SemaphoreType.DMA,
            pltpu.SemaphoreType.DMA((2,)),
            pltpu.SemaphoreType.DMA((15,)),
        ],
        compiler_params=pltpu.CompilerParams(
            collective_id=0, has_side_effects=True, vmem_limit_bytes=60 * 1024 * 1024),
    )(w1, wsmall, wout, profiles, flags, draws)


def meet_kernel(plan, merge, x_ref, o_ref, wide, tall, send_sem, recv_sem):
    peers = Meet.peers(plan)
    barrier = pltpu.get_barrier_semaphore()
    for device in peers:
        pl.semaphore_signal(barrier, inc=1, device_id=device, device_id_type=MESH)
    pl.semaphore_wait(barrier, len(peers))
    meet = Meet(plan, wide, tall, send_sem, recv_sem)
    o_ref[...] = meet.run(x_ref[...], merge, float(plan.cells))


def meet_all(plan, value, merge, collective_id):
    rows, width = value.shape
    n = plan.nx + plan.ny - 2
    return pl.pallas_call(
        functools.partial(meet_kernel, plan, merge),
        out_shape=jax.ShapeDtypeStruct(value.shape, jnp.float32),
        in_specs=[pl.BlockSpec(memory_space=pltpu.VMEM)],
        out_specs=pl.BlockSpec(memory_space=pltpu.VMEM),
        scratch_shapes=[
            pltpu.VMEM((plan.nx, rows, width), jnp.float32),
            pltpu.VMEM((plan.ny, rows, width), jnp.float32),
            pltpu.SemaphoreType.DMA((n,)),
            pltpu.SemaphoreType.DMA((n,)),
        ],
        compiler_params=pltpu.CompilerParams(collective_id=collective_id, has_side_effects=True),
    )(value)


def share_kernel(plan, row_ref, block_ref, row_out, block_out, wide, tall, send_sem, recv_sem):
    peers = Meet.peers(plan)
    barrier = pltpu.get_barrier_semaphore()
    for device in peers:
        pl.semaphore_signal(barrier, inc=1, device_id=device, device_id_type=MESH)
    pl.semaphore_wait(barrier, len(peers))
    meet = Meet(plan, wide, tall, send_sem, recv_sem)
    wide[meet.gx] = row_ref[...]
    tall[meet.gy] = block_ref[...]
    copies = meet.copies(False) + meet.copies(True)
    for copy in copies:
        copy.start()
    for copy in copies:
        copy.wait_recv()
    row_out[...] = wide[0]
    block_out[...] = tall[0]
    for copy in copies:
        copy.wait_send()


def share_all(plan, row, block, collective_id):
    n = plan.nx + plan.ny - 2
    return pl.pallas_call(
        functools.partial(share_kernel, plan),
        out_shape=[jax.ShapeDtypeStruct(row.shape, jnp.float32),
                   jax.ShapeDtypeStruct(block.shape, jnp.float32)],
        in_specs=[pl.BlockSpec(memory_space=pltpu.VMEM)] * 2,
        out_specs=[pl.BlockSpec(memory_space=pltpu.VMEM)] * 2,
        scratch_shapes=[
            pltpu.VMEM((plan.nx, *row.shape), jnp.float32),
            pltpu.VMEM((plan.ny, *block.shape), jnp.float32),
            pltpu.SemaphoreType.DMA((n,)),
            pltpu.SemaphoreType.DMA((n,)),
        ],
        compiler_params=pltpu.CompilerParams(collective_id=collective_id, has_side_effects=True),
    )(row, block)


class Reduce:
    def __init__(self, plan, width, part, twin, slots, send_sem, twin_sem, recv_sem):
        self.plan, self.width, self.part, self.twin, self.slots = plan, width, part, twin, slots
        self.send_sem, self.twin_sem, self.recv_sem = send_sem, twin_sem, recv_sem
        self.cuts = [(Flow(plan, kind), *cut) for kind, cut in enumerate(plan.cuts)]

    @staticmethod
    def slot_counts(plan):
        counts = []
        for kind in range(len(plan.cuts)):
            sizes = (plan.ny // 2, plan.nx // 2, 2)
            first, second = (((0, 1, 2), (2, 1, 0)), ((1, 2, 0), (1, 0, 2)))[kind]
            mp, mq, mr = (max(sizes[i], sizes[j]) for i, j in zip(first, second))
            a, b, c = (Reduce.sides(m) for m in (mp, mq, mr))
            far_r = (mr > 2) * (mr * mq * mp)
            counts.append((far_r, mq * mp * (c + (mq > 2)), mp * (c + b + (mp > 2)), c + b + a))
        return counts

    @staticmethod
    def sides(most):
        return 1 if most == 2 else (2 if most > 2 else 0)

    def block(self, ref, cut, gx, gy):
        return ref.at[
            pl.ds(pl.multiple_of(gx * self.plan.hp + cut[1], 16), cut[2]),
            pl.ds(pl.multiple_of(gy * self.width, LANES), self.width),
        ]

    def twin_block(self, cut, gx, y):
        return self.twin.at[
            pl.ds(pl.multiple_of(gx * self.plan.hp + cut[1], 16), cut[2]),
            pl.ds(pl.multiple_of(y * self.width, LANES), self.width),
        ]

    def twin_copy(self, kind, cut, gx, y):
        flow = cut[0]
        return pltpu.make_async_remote_copy(
            src_ref=self.block(self.part, cut, gx, 2 * y + 1 - flow.core),
            dst_ref=self.twin_block(cut, gx, y),
            send_sem=self.twin_sem.at[0, kind, gx * (self.plan.ny // 2) + y],
            recv_sem=self.twin_sem.at[1, kind, gx * (self.plan.ny // 2) + y],
            device_id=flow.twin(), device_id_type=MESH,
        )

    def each_twin(self, visit, ys=None):
        ny2 = self.plan.ny // 2
        for kind, cut in enumerate(self.cuts):
            def one(n, _, kind=kind, cut=cut):
                visit(self.twin_copy(kind, cut, n // ny2, lax.rem(n, ny2)))
                return 0
            lax.fori_loop(0, self.plan.blocks // 2, one, 0)

    def start_twin(self):
        self.each_twin(lambda copy: copy.start())

    def entry(self, kind, stage, spot, axis, came_from):
        flow = self.cuts[kind][0]
        mp, mq, mr = flow.most
        far_r, far_q, far_p, _ = Reduce.slot_counts(self.plan)[kind]
        sides = [Reduce.sides(m) for m in flow.most]
        dp, dq, dr = spot
        if stage == 2:
            return (dr * mq + dq) * mp + dp
        if stage == 1:
            base, which = far_r, (dq * mp + dp) * (sides[2] + (mq > 2))
        elif stage == 0:
            base, which = far_r + far_q, dp * (sides[2] + sides[1] + (mp > 2))
        else:
            base, which = far_r + far_q + far_p, 0
        offset = 0
        for later in (2, 1, 0):
            if later == stage:
                return base + which + offset
            if later == axis:
                side = 0 if sides[axis] == 1 else (came_from + 1) // 2
                return base + which + offset + side
            offset += sides[later]

    def slot(self, kind, index):
        cut = self.cuts[kind]
        total = sum(Reduce.slot_counts(self.plan)[kind])
        return self.slots[kind].at[index], self.recv_sem[kind].at[index]

    def gather_terms(self, kind, cut, spot, stage, sign):
        flow = cut[0]
        ny2 = self.plan.ny // 2
        gx, gy = flow.device(spot)
        y = gy // 2
        copy = self.twin_copy(kind, cut, gx, y)
        copy.wait_recv()
        own = self.block(self.part, cut, gx, gy)
        twin = self.twin_block(cut, gx, y)
        arrivals = []
        for axis in (2, 1, 0):
            if axis > stage:
                for side in (-1, 1):
                    there, _ = flow.step(axis, side)
                    if flow.most[axis] < 2:
                        continue
                    arrivals.append((there, self.entry(kind, stage, spot, axis, side)))
            elif axis == stage and flow.most[axis] > 2:
                away = self.here_away(flow, axis, sign)
                arrivals.append((away, self.entry(kind, stage, spot, axis, None)))
        return own, twin, arrivals

    def here_away(self, flow, axis, sign):
        to = flow.here[axis] - sign
        return (to >= 0) & (to < flow.limit[axis])

    def add_in(self, kind, cut, spot, stage, sign):
        own, twin, arrivals = self.gather_terms(kind, cut, spot, stage, sign)

        def add(other):
            def chunk(i, _):
                rows = aligned(i * 16, 16)
                total = own[rows, :].astype(jnp.float32) + other[rows, :].astype(jnp.float32)
                own[rows, :] = total.astype(jnp.bfloat16)
                return 0
            lax.fori_loop(0, cut[2] // 16, chunk, 0)

        add(twin)
        for there, index in arrivals:
            slot, sem = self.slot(kind, index)
            @when(there)
            def _(slot=slot, sem=sem):
                pltpu.make_async_copy(slot, slot, sem).wait()
                add(slot)
        return own

    def onward(self, kind, cut, spot, stage, sign):
        flow = cut[0]
        _, device = self.toward(flow, stage, sign)
        gx, gy = flow.device(spot)
        to = flow.here[stage] + sign
        index_same = self.entry(kind, stage, spot, stage, None) if flow.most[stage] > 2 else None
        done = to == spot[stage]
        p_same = flow.here[0] == spot[0]
        q_same = flow.here[1] == spot[1]
        if stage == 2:
            deeper = jnp.where(q_same, jnp.where(p_same,
                               self.entry(kind, -1, spot, 2, -sign),
                               self.entry(kind, 0, spot, 2, -sign)),
                               self.entry(kind, 1, spot, 2, -sign))
        elif stage == 1:
            deeper = jnp.where(p_same, self.entry(kind, -1, spot, 1, -sign),
                               self.entry(kind, 0, spot, 1, -sign))
        else:
            deeper = self.entry(kind, -1, spot, 0, -sign)
        index = deeper if index_same is None else jnp.where(done, deeper, index_same)
        slot, sem = self.slot(kind, index)
        ny2 = self.plan.ny // 2
        return pltpu.make_async_remote_copy(
            src_ref=self.block(self.part, cut, gx, gy), dst_ref=slot,
            send_sem=self.send_sem.at[kind, gx * ny2 + gy // 2], recv_sem=sem,
            device_id=device, device_id_type=MESH,
        )

    def toward(self, flow, axis, sign):
        return flow.step(axis, sign)

    def order(self, kind):
        most = self.cuts[kind][0].most
        return [(stage, k) for stage in (2, 1, 0) for k in range(most[stage] - 1, 0, -1)]

    def steps(self):
        return max(len(self.order(kind)) for kind in range(len(self.cuts)))

    def walk(self, visit, kind, stage, k):
        cut = self.cuts[kind]
        p, q, r = cut[0].here
        np_, nq, nr = cut[0].limit
        mp, mq, mr = cut[0].most

        def one(n, _):
            dp, dq = lax.rem(n, mp), n // mp
            for sign in (-1, 1):
                if stage == 2:
                    d = r + sign * k
                    spot, good = (dp, dq, d), (d >= 0) & (d < nr) & (dq < nq) & (dp < np_)
                elif stage == 1:
                    d = q + sign * k
                    spot, good = (dp, d, r), (d >= 0) & (d < nq) & (dp < np_)
                else:
                    d = p + sign * k
                    spot, good = (d, q, r), (d >= 0) & (d < np_)
                pl.when(good)(functools.partial(visit, kind, cut, spot, stage, sign))
            return 0
        lax.fori_loop(0, {2: mq * mp, 1: mp, 0: 1}[stage], one, 0)

    def pass_on(self, step):
        def visit(kind, cut, spot, stage, sign):
            self.add_in(kind, cut, spot, stage, sign)
            self.onward(kind, cut, spot, stage, sign).start()
        for kind in range(len(self.cuts)):
            order = self.order(kind)
            if step < len(order):
                self.walk(visit, kind, *order[step])

    def own_sum(self, out_ref, factor):
        for kind, cut in enumerate(self.cuts):
            flow = cut[0]
            own = self.add_in(kind, cut, flow.here, -1, None)
            out_ref[pl.ds(cut[1], cut[2]), :] = own[...].astype(jnp.float32) * factor

    def finish_sends(self):
        self.each_twin(lambda copy: copy.wait_send())
        def visit(kind, cut, spot, stage, sign):
            self.onward(kind, cut, spot, stage, sign).wait_send()
        for kind in range(len(self.cuts)):
            for stage, k in self.order(kind):
                self.walk(visit, kind, stage, k)

    def twin_column(self, gy):
        y, flow = gy // 2, self.cuts[0][0]

        @pl.when(gy % 2 != flow.core)
        def _():
            for kind, cut in enumerate(self.cuts):
                def one(gx, _, kind=kind, cut=cut):
                    self.twin_copy(kind, cut, gx, y).start()
                    return 0
                lax.fori_loop(0, self.plan.nx, one, 0)


def reduce_scratch(plan, width):
    counts = [sum(c) for c in Reduce.slot_counts(plan)]
    return [
        pltpu.VMEM((plan.hh, plan.ny * width), jnp.bfloat16),
        pltpu.VMEM((plan.hh, plan.ny // 2 * width), jnp.bfloat16),
        *[pltpu.VMEM((c, cut[1], width), jnp.bfloat16) for c, cut in zip(counts, plan.cuts)],
        pltpu.SemaphoreType.DMA((len(plan.cuts), plan.blocks // 2)),
        pltpu.SemaphoreType.DMA((2, len(plan.cuts), plan.blocks // 2)),
        *[pltpu.SemaphoreType.DMA((c,)) for c in counts],
    ]


def reduce_from(plan, width, refs):
    n = len(plan.cuts)
    part, twin, slots, sems, recv = refs[0], refs[1], refs[2:2 + n], refs[2 + n:4 + n], refs[4 + n:]
    return Reduce(plan, width, part, twin, slots, *sems, recv)


def reduce_kernel(plan, width, factor, x_ref, o_ref, *rest):
    reduce = reduce_from(plan, width, rest[:-1])
    load = pltpu.make_async_copy(x_ref, reduce.part, rest[-1])
    load.start()
    greet(plan)
    load.wait()
    reduce.start_twin()
    for step in range(reduce.steps()):
        reduce.pass_on(step)
    reduce.own_sum(o_ref, factor)
    reduce.finish_sends()


def reduce_all(plan, value, factor, collective_id):
    width = value.shape[1] // plan.ny
    return pl.pallas_call(
        functools.partial(reduce_kernel, plan, width, factor),
        out_shape=jax.ShapeDtypeStruct((plan.hp, width), jnp.float32),
        in_specs=[pl.BlockSpec(memory_space=pl.ANY)],
        out_specs=pl.BlockSpec(memory_space=pltpu.VMEM),
        scratch_shapes=[*reduce_scratch(plan, width), pltpu.SemaphoreType.DMA],
        compiler_params=pltpu.CompilerParams(
            collective_id=collective_id, has_side_effects=True, vmem_limit_bytes=60 * 1024 * 1024),
    )(value)


def backward_kernel(plan, total_cells, *refs):
    (part_hbm, up_hbm, small_hbm, layers_hbm, scaled_hbm, keep_hbm, sample_ref, rows_ref, loss_ref,
     center_ref, log_var_ref, draws_ref,
     readout_out, sums_out, small_part, grad_ref,
     small_ref, up_ref, layer_ref, scaled_ref, keep_ref, lane_ref, column_ref, latent_ref,
     moment_ref, wide, tall, meet_send, meet_recv, load_sem, *rest) = refs
    reduce = reduce_from(plan, plan.frame, rest)

    def load(k):
        slot = k % 2
        return (
            pltpu.make_async_copy(scaled_hbm.at[k], scaled_ref.at[slot], load_sem.at[3 * slot]),
            pltpu.make_async_copy(keep_hbm.at[k], keep_ref.at[slot], load_sem.at[3 * slot + 1]),
        )

    def load_layer(k):
        return pltpu.make_async_copy(
            layers_hbm.at[k], layer_ref.at[k % 2, pl.ds(0, plan.hh), :], load_sem.at[3 * (k % 2) + 2])

    first = pltpu.make_async_copy(part_hbm, reduce.part, load_sem.at[6])
    second = pltpu.make_async_copy(up_hbm, up_ref, load_sem.at[7])
    third = pltpu.make_async_copy(small_hbm, small_ref, load_sem.at[8])
    first.start()
    second.start()
    for copy in load(3):
        copy.start()
    third.start()
    load_layer(2).start()
    for copy in load(2):
        copy.start()
    load_layer(1).start()
    peers = Meet.peers(plan)
    barrier = pltpu.get_barrier_semaphore()
    for device in peers:
        pl.semaphore_signal(barrier, inc=1, device_id=device, device_id_type=MESH)
    pl.semaphore_wait(barrier, len(peers))
    first.wait()
    reduce.start_twin()
    tail = layer_ref.shape[1] - plan.hh
    if tail:
        for k in range(2):
            layer_ref[k, plan.hh:, :] = jnp.zeros((tail, plan.cells), jnp.bfloat16)
    latent_ref[...] = jnp.zeros_like(latent_ref)

    todo = [functools.partial(reduce.pass_on, step) for step in range(reduce.steps())]
    todo.append(lambda: reduce.own_sum(readout_out, 1.0 / total_cells))

    def between(second):
        if todo:
            todo.pop(0)()

    def layer(k):
        slot = k % 2
        for copy in load(k):
            copy.wait()

        def columns(i):
            column_ref[0] = unit_column(plan, small_ref, i, plan.latent + k)
            column_ref[1] = unit_column(plan, small_ref, i, plan.latent + 4 + k)
            column_ref[2] = as_column(
                lax.rsqrt(rows_ref[k, 1:2, aligned(i * LANES)] / total_cells + norm_eps))

        def block(i, _):
            columns(i)

            def chunk(j, _):
                rows = aligned(i * LANES + j * 16, 16)
                here = aligned(j * 16, 16)
                gain, bias = tiled(column_ref[0, here, :], plan), tiled(column_ref[1, here, :], plan)
                scaled = scaled_ref[slot, rows, :]
                normed = gain * scaled + bias
                sigma = jax.nn.sigmoid(normed)
                slope = up_ref[rows, :] * keep_ref[slot, rows, :].astype(jnp.float32) * sigma * (
                    1.0 + normed * (1.0 - sigma))
                up_ref[rows, :] = slope
                lane_ref[0, here, :] = lane_sums(slope)
                lane_ref[1, here, :] = lane_sums(slope * scaled)
                return 0
            lax.fori_loop(0, LANES // 16, chunk, 0)
            sums_out[k, 0:1, aligned(i * LANES)] = as_row(lane_ref[0])
            sums_out[k, 1:2, aligned(i * LANES)] = as_row(lane_ref[1])
            return 0
        lax.fori_loop(0, plan.hh // LANES, block, 0)
        sums_out[k, 2:3, :] = loss_ref[...]
        meet = Meet(plan, wide.at[k], tall.at[k], meet_send.at[k], meet_recv.at[k])
        sums_out[k] = meet.run(sums_out[k], merge_sums, 1.0, between)

        def last(i, _):
            columns(i)
            column_ref[3] = as_column(sums_out[k, 0:1, aligned(i * LANES)] / total_cells)
            column_ref[4] = as_column(sums_out[k, 1:2, aligned(i * LANES)] / total_cells)

            def chunk(j, _):
                rows = aligned(i * LANES + j * 16, 16)
                here = aligned(j * 16, 16)
                factor = tiled(column_ref[0, here, :] * column_ref[2, here, :], plan)
                shift, gain = tiled(column_ref[3, here, :], plan), tiled(column_ref[4, here, :], plan)
                grad = factor * (up_ref[rows, :] - (shift + scaled_ref[slot, rows, :] * gain))
                grad_ref[rows, :] = grad.astype(jnp.bfloat16)
                return 0
            lax.fori_loop(0, LANES // 16, chunk, 0)
            return 0
        lax.fori_loop(0, plan.hh // LANES, last, 0)
        if k >= 2:
            for copy in load(k - 2):
                copy.start()

    def put(j, lane, value):
        at = j * plan.small + lane
        small_part[:, at:at + value.shape[1]] = value.astype(jnp.bfloat16)

    def middle(source, lane):
        for j in range(plan.ny):
            at, row = j * plan.small + lane, j * plan.midp
            put(j, lane, over_cells(grad_ref[...], source[row:row + plan.midl, :]))
            up_ref[row:row + plan.midp, :] = over_rows(
                small_ref[:, at:at + plan.midl], grad_ref[...])[:plan.midp]

    second.wait()
    third.wait()
    layer(3)
    load_layer(2).wait()
    middle(layer_ref.at[0], plan.o4)
    load_layer(0).start()
    layer(2)
    lifting = over_cells(grad_ref[...], sample_ref[...])
    for j in range(plan.ny):
        put(j, plan.ol, lifting)
    reach = over_rows(small_ref[:, plan.ol:plan.ol + plan.ll], grad_ref[...])[:plan.latent]
    center, log_var = center_ref[...], log_var_ref[...]
    latent_ref[0, 0:plan.latent, :] = reach + kl_weight * center
    latent_ref[1, 0:plan.latent, :] = (
        reach * 0.5 * jnp.exp(0.5 * log_var) * draws_ref[...]
        + kl_weight * 0.5 * (jnp.exp(log_var) - 1.0))
    half, tall_rows = plan.ny // 2, round_up(plan.moments, 16)
    moment_ref[...] = jnp.zeros_like(moment_ref)
    for j in range(plan.ny):
        spot = (j % half) * plan.moments
        piece = latent_ref[j // half, spot:spot + tall_rows, :]
        row = lax.broadcasted_iota(jnp.int32, piece.shape, 0)
        piece = jnp.where(row < plan.moments, piece, 0.0)
        moment_ref[j * plan.ml:j * plan.ml + tall_rows, :] = piece.astype(jnp.bfloat16)
    load_layer(1).wait()
    for j in range(plan.ny):
        at, row = j * plan.small + plan.op, j * plan.ml
        moments = moment_ref[row:row + plan.ml, :]
        put(j, plan.op, over_cells(layer_ref[1, 0:plan.hh, :], moments))
        part = rows_dot(small_ref[:, at:at + plan.ml], moments)
        up_ref[...] = part if j == 0 else up_ref[...] + part
    layer(1)
    load_layer(0).wait()
    middle(layer_ref.at[0], plan.o2)
    layer(0)
    while todo:
        between(False)
    reduce.finish_sends()


def backward_all(plan, total_cells, *arrays):
    any_spec, vmem = pl.BlockSpec(memory_space=pl.ANY), pl.BlockSpec(memory_space=pltpu.VMEM)
    f32, bf16 = jnp.float32, jnp.bfloat16
    n = plan.nx + plan.ny - 2
    shape = jax.ShapeDtypeStruct
    return pl.pallas_call(
        functools.partial(backward_kernel, plan, total_cells),
        out_shape=[
            shape((plan.hp, plan.frame), f32), shape((4, 3, plan.hh), f32),
            shape((plan.hh, plan.ny * plan.small), bf16), shape((plan.hh, plan.cells), bf16)],
        in_specs=[any_spec] * 6 + [vmem] * 6,
        out_specs=[vmem] * 4,
        scratch_shapes=[
            pltpu.VMEM((plan.hh, plan.ny * plan.small), bf16),
            pltpu.VMEM((plan.hh, plan.cells), f32),
            pltpu.VMEM((2, plan.hh + plan.midl - plan.midp, plan.cells), bf16),
            pltpu.VMEM((2, plan.hh, plan.cells), f32),
            pltpu.VMEM((2, plan.hh, plan.cells), bf16),
            pltpu.VMEM((2, LANES, LANES), f32),
            pltpu.VMEM((5, LANES, LANES), f32),
            pltpu.VMEM((2, plan.ll, plan.cells), f32),
            pltpu.VMEM((plan.ny * plan.ml, plan.cells), bf16),
            pltpu.VMEM((4, plan.nx, 3, plan.hh), f32),
            pltpu.VMEM((4, plan.ny, 3, plan.hh), f32),
            pltpu.SemaphoreType.DMA((4, n)),
            pltpu.SemaphoreType.DMA((4, n)),
            pltpu.SemaphoreType.DMA((9,)),
            *reduce_scratch(plan, plan.frame),
        ],
        compiler_params=pltpu.CompilerParams(
            collective_id=6, has_side_effects=True, vmem_limit_bytes=60 * 1024 * 1024),
    )(*arrays)


def embed_kernel(plan, total_cells, *refs):
    (small_hbm, x_hbm, grad_ref, readout_ref, embed_out, small_out, row_out, block_out,
     x_ref, wide, tall, meet_send, meet_recv, load_sem, *rest) = refs
    half = len(rest) // 2
    small, embed = reduce_from(plan, plan.small, rest[:half]), reduce_from(plan, plan.frame, rest[half:])
    first = pltpu.make_async_copy(small_hbm, small.part, load_sem.at[0])
    second = pltpu.make_async_copy(x_hbm, x_ref, load_sem.at[1])
    first.start()
    second.start()
    peers = Meet.peers(plan)
    barrier = pltpu.get_barrier_semaphore()
    for device in peers:
        pl.semaphore_signal(barrier, inc=1, device_id=device, device_id_type=MESH)
    pl.semaphore_wait(barrier, len(peers))
    first.wait()
    small.start_twin()
    second.wait()
    factor = 1.0 / total_cells
    piece = plan.frame // 3 // LANES * LANES
    for j in range(plan.ny):
        start, stop = plan.frame_start[j], min(plan.frame_start[j] + plan.frame, plan.genes)
        for at in range(start, stop, piece):
            end = min(at + piece, stop)
            to = j * plan.frame + at - start
            embed.part[:, to:to + end - at] = over_cells(
                grad_ref[...], x_ref[at:end, :]).astype(jnp.bfloat16)
        done = stop - start
        if done < plan.frame:
            inside = done // LANES * LANES
            lanes = lax.broadcasted_iota(jnp.int32, (plan.hh, LANES), 1)
            at = j * plan.frame + inside
            if inside < done:
                value = embed.part[:, at:at + LANES]
                embed.part[:, at:at + LANES] = jnp.where(
                    lanes < done - inside, value.astype(jnp.float32), 0.0).astype(jnp.bfloat16)
                inside += LANES
            for at in range(j * plan.frame + inside, (j + 1) * plan.frame, LANES):
                embed.part[:, at:at + LANES] = jnp.zeros((plan.hh, LANES), jnp.bfloat16)
        embed.twin_column(j)
        if j < small.steps():
            small.pass_on(j)
    for step in range(plan.ny, small.steps()):
        small.pass_on(step)
    embed.pass_on(0)
    small.own_sum(small_out, factor)
    meet = Meet(plan, wide, tall, meet_send, meet_recv)
    wide[meet.gx, :, 0:plan.frame] = readout_ref[...]
    wide[meet.gx, :, plan.frame:] = small_out[plan.h:plan.h + 1, plan.op:plan.op + plan.ml]
    tall[meet.gy] = small_out[:, plan.ol:plan.ol + plan.ll]
    copies = meet.copies(False) + meet.copies(True)
    for copy in copies:
        copy.start()
    for step in range(1, embed.steps()):
        embed.pass_on(step)
    for copy in copies:
        copy.wait_recv()
    row_out[...] = wide[0]
    block_out[...] = tall[0]
    embed.own_sum(embed_out, factor)
    for copy in copies:
        copy.wait_send()
    small.finish_sends()
    embed.finish_sends()


def embed_all_sums(plan, total_cells, *arrays):
    any_spec, vmem = pl.BlockSpec(memory_space=pl.ANY), pl.BlockSpec(memory_space=pltpu.VMEM)
    f32, bf16 = jnp.float32, jnp.bfloat16
    n = plan.nx + plan.ny - 2
    shape = jax.ShapeDtypeStruct
    row, block = (1, plan.frame + plan.ml), (plan.hp, plan.ll)
    return pl.pallas_call(
        functools.partial(embed_kernel, plan, total_cells),
        out_shape=[shape((plan.hp, plan.frame), f32), shape((plan.hp, plan.small), f32),
                   shape(row, f32), shape(block, f32)],
        in_specs=[any_spec] * 2 + [vmem] * 2,
        out_specs=[vmem] * 4,
        scratch_shapes=[
            pltpu.VMEM((plan.genes, plan.cells), bf16),
            pltpu.VMEM((plan.nx, *row), f32),
            pltpu.VMEM((plan.ny, *block), f32),
            pltpu.SemaphoreType.DMA((n,)),
            pltpu.SemaphoreType.DMA((n,)),
            pltpu.SemaphoreType.DMA((2,)),
            *reduce_scratch(plan, plan.small),
            *reduce_scratch(plan, plan.frame),
        ],
        compiler_params=pltpu.CompilerParams(
            collective_id=7, has_side_effects=True, vmem_limit_bytes=60 * 1024 * 1024),
    )(*arrays)


def rows_dot(left, right):
    return lax.dot_general(left, right, (((1,), (0,)), ((), ())), preferred_element_type=jnp.float32)


def over_cells(left, right):
    return lax.dot_general(left, right, (((1,), (1,)), ((), ())), preferred_element_type=jnp.float32)


def over_rows(left, right):
    return lax.dot_general(left, right, (((0,), (0,)), ((), ())), preferred_element_type=jnp.float32)


def pad_to(value, rows, lanes):
    return jnp.pad(value, ((0, rows - value.shape[0]), (0, lanes - value.shape[1])))


def middle_piece(plan, matrix):
    turned = matrix.T.reshape(plan.h, plan.groups, plan.h)
    wide = jnp.pad(turned, ((0, plan.hp - plan.h), (0, 0), (0, plan.hp - plan.h)))
    return pad_to(wide.reshape(plan.hp, plan.midp), plan.hp, plan.midl)


def middle_back(plan, piece):
    cut = piece[:plan.h, :plan.midp].reshape(plan.h, plan.groups, plan.hp)[:, :, :plan.h]
    return cut.reshape(plan.h, plan.mid).T


def with_row(plan, block, row, first):
    spare = jnp.where(first, row, jnp.zeros_like(row))[None]
    return pad_to(jnp.concatenate([block, spare], axis=0), plan.hp, block.shape[1])


def on_device(
    nx, ny,
    transcript_profiles,
    experiment_labels,
    measured_flags,
    retained_unit_flags,
    standard_normal_draws,
    compressor_first_matrix,
    compressor_second_matrix,
    posterior_matrix,
    posterior_intercepts,
    expander_first_matrix,
    expander_second_matrix,
    output_matrix,
    output_intercept,
    normalizer_factors,
    normalizer_translations,
):
    cells = transcript_profiles.shape[0]
    plan = Plan(nx, ny, cells, output_matrix.shape[1], output_matrix.shape[0], expander_first_matrix.shape[0])
    total_cells = float(cells * nx * ny)
    gx, gy = lax.axis_index("gx"), lax.axis_index("gy")
    first = gx == 0

    wide = jnp.concatenate([
        pad_to(compressor_first_matrix.T, plan.hp, plan.g),
        with_row(plan, output_matrix, output_intercept, first)], axis=0)
    strip = lax.ppermute(wide[:, :plan.strip], "gy", [(j + 1, j) for j in range(ny - 1)])
    wide = jnp.concatenate([wide, strip], axis=1)
    wide = pad_to(wide, 2 * plan.hp, plan.gp + plan.strip + plan.shift * ny)
    wide = lax.dynamic_slice_in_dim(wide, gy * plan.shift, plan.gp, 1)
    last = jnp.concatenate([
        expander_first_matrix.T, normalizer_factors.T, normalizer_translations.T], axis=1)
    small = jnp.concatenate([
        middle_piece(plan, compressor_second_matrix),
        middle_piece(plan, expander_second_matrix),
        pad_to(with_row(plan, posterior_matrix, posterior_intercepts, first), plan.hp, plan.ml),
        pad_to(last, plan.hp, plan.ll)], axis=1)
    profiles = transcript_profiles.T
    draws = standard_normal_draws.T
    (embed_all, small_all, readout_all, center, log_var, sample, layers, scaled_values, keep_values,
     norm_rows) = forward_all(
        plan, total_cells, wide[:plan.hp], small, wide[plan.hp:], profiles,
        jnp.swapaxes(retained_unit_flags, 1, 2), draws)
    output = over_rows(readout_all[:, :plan.genes], layers[3])
    residual = output - profiles.astype(jnp.float32)
    picker = (jnp.arange(measured_flags.shape[0], dtype=jnp.int32)[:, None]
              == experiment_labels[None, :]).astype(jnp.bfloat16)
    slab = over_rows(measured_flags.astype(jnp.bfloat16), picker)
    weighted = slab * residual
    rebuild = 0.5 * jnp.sum(weighted * residual)
    diverge = 0.5 * jnp.sum(jnp.exp(log_var) + center * center - 1.0 - log_var)
    own_loss = rebuild + kl_weight * diverge
    output_grad = weighted.astype(jnp.bfloat16)

    def frames(product):
        padded = pad_to(product, plan.hh, max(plan.frame_start) + plan.frame)
        return jnp.concatenate(
            [padded[:, s:s + plan.frame] for s in plan.frame_start], axis=1).astype(jnp.bfloat16)

    readout_part = frames(over_cells(layers[3], output_grad))
    upstream = rows_dot(readout_all[:, :plan.genes], output_grad)
    if plan.fits:
        readout_sum, sums, small_part, grad_one = backward_all(
            plan, total_cells, readout_part, upstream, small_all, layers, scaled_values, keep_values,
            sample, norm_rows, jnp.full((1, plan.hh), own_loss), center, log_var, draws)
        loss_sum = sums[0, 2, 0]
        gains_sum, shifts_sum = [sums[k, 1] for k in range(4)], [sums[k, 0] for k in range(4)]
        embed_sum, small_sum, row, lifting_own = embed_all_sums(
            plan, total_cells, small_part, profiles, grad_one, readout_sum[plan.h:plan.h + 1])
    else:
        parts = small_all.reshape(plan.hh, ny, plan.small)
        encoder_all = parts[:, :, plan.o2:plan.o2 + plan.midp].reshape(plan.hh, plan.hh)
        decoder_all = parts[:, :, plan.o4:plan.o4 + plan.midp].reshape(plan.hh, plan.hh)
        projector_all = parts[:, :, plan.op:plan.op + plan.moments].reshape(plan.hh, 2 * plan.latent)
        lifting_all = parts[:, 0, plan.ol:plan.ol + plan.latent]
        rows = parts[:, 0, plan.ol + plan.latent:plan.ol + plan.latent + 8].astype(jnp.float32)
        gains = [rows[:, k:k + 1] for k in range(4)]
        biases = [rows[:, 4 + k:5 + k] for k in range(4)]

        spread = jnp.exp(0.5 * log_var)

        def kept_layer(k):
            inverse = lax.rsqrt(norm_rows[k, 1] / total_cells + norm_eps)[:, None]
            return layers[k], gains[k] * scaled_values[k] + biases[k], scaled_values[k], inverse

        one, two, three, four = (kept_layer(k) for k in range(4))

        def backward_layer(upstream, kept, k, loss, ident):
            _, normed, scaled, inverse = kept
            sigma = jax.nn.sigmoid(normed)
            slope = upstream * keep_values[k].astype(jnp.float32) * sigma * (
                1.0 + normed * (1.0 - sigma))
            pair = jnp.stack([jnp.sum(slope, axis=1), jnp.sum(slope * scaled, axis=1),
                              jnp.full((plan.hh,), loss)])
            merged = meet_all(plan, pair, merge_sums, 2)
            shift, gain = merged[0], merged[1]
            grad = gains[k] * inverse * (
                slope - (shift[:, None] + scaled * gain[:, None]) / total_cells)
            return grad.astype(jnp.bfloat16), gain, shift, merged[2, 0]

        grad_four, gain_four, shift_four, loss_sum = backward_layer(upstream, four, 3, own_loss, 5)
        upstream = over_rows(decoder_all, grad_four)
        grad_three, gain_three, shift_three, _ = backward_layer(upstream, three, 2, own_loss, 6)
        sample_grad = over_rows(lifting_all, grad_three)[:plan.latent]
        center_grad = sample_grad + kl_weight * center
        logvar_grad = sample_grad * 0.5 * spread * draws + kl_weight * 0.5 * (jnp.exp(log_var) - 1.0)
        moment_grad = jnp.concatenate([center_grad, logvar_grad], axis=0).astype(jnp.bfloat16)
        upstream = rows_dot(projector_all, moment_grad)
        grad_two, gain_two, shift_two, _ = backward_layer(upstream, two, 1, own_loss, 7)
        upstream = over_rows(encoder_all, grad_two)
        grad_one, gain_one, shift_one, _ = backward_layer(upstream, one, 0, own_loss, 8)
        gains_sum = [gain_one, gain_two, gain_three, gain_four]
        shifts_sum = [shift_one, shift_two, shift_three, shift_four]
        encoder_part = over_cells(grad_two, one[0]).reshape(plan.hh, ny, plan.midp)
        decoder_part = over_cells(grad_four, three[0]).reshape(plan.hh, ny, plan.midp)
        projector_part = over_cells(two[0], moment_grad).reshape(plan.hh, ny, plan.moments)
        lifting_part = over_cells(grad_three, sample)[:, :plan.latent]

        def lanes(value, width):
            return jnp.pad(value, ((0, 0), (0, 0), (0, width - value.shape[2])))

        small_part = jnp.concatenate([
            lanes(encoder_part, plan.midl), lanes(decoder_part, plan.midl),
            lanes(projector_part, plan.ml),
            jnp.broadcast_to(pad_to(lifting_part, plan.hh, plan.ll)[:, None, :], (plan.hh, ny, plan.ll)),
        ], axis=2).reshape(plan.hh, ny * plan.small).astype(jnp.bfloat16)
        embed_part = frames(over_cells(grad_one, profiles))

        readout_sum = reduce_all(plan, readout_part, 1.0 / total_cells, 3)
        small_sum = reduce_all(plan, small_part, 1.0 / total_cells, 4)
        embed_sum = reduce_all(plan, embed_part, 1.0 / total_cells, 3)

        row, lifting_own = share_all(plan, jnp.concatenate([
            readout_sum[plan.h:plan.h + 1],
            small_sum[plan.h:plan.h + 1, plan.op:plan.op + plan.ml]], axis=1),
            small_sum[:, plan.ol:plan.ol + plan.ll], 5)
    input_grad = (over_rows(embed_all[:, :plan.genes], grad_one) - weighted).astype(jnp.bfloat16)

    starts = jnp.array([plan.g * j - plan.frame_start[j] for j in range(ny)], jnp.int32)
    readout_own = lax.dynamic_slice_in_dim(readout_sum, starts[gy], plan.g, 1)
    embed_own = lax.dynamic_slice_in_dim(embed_sum, starts[gy], plan.g, 1)
    baseline_own = lax.dynamic_slice_in_dim(row[0, :plan.frame], starts[gy], plan.g, 0)

    def own_units(values):
        stack = jnp.stack(values, axis=0) / total_cells
        return lax.dynamic_slice_in_dim(stack, gx * plan.hp, plan.h, 1)

    small_h = small_sum[:plan.h]
    return (
        output.astype(jnp.bfloat16).T,
        center.T,
        loss_sum / total_cells,
        input_grad.T,
        embed_own[:plan.h].T,
        middle_back(plan, small_sum[:, plan.o2:plan.o2 + plan.midl]),
        small_h[:, plan.op:plan.op + plan.moments],
        row[0, plan.frame:plan.frame + plan.moments],
        lifting_own[:plan.h, :plan.latent].T,
        middle_back(plan, small_sum[:, plan.o4:plan.o4 + plan.midl]),
        readout_own[:plan.h],
        baseline_own,
        own_units(gains_sum),
        own_units(shifts_sum),
    )


def solution(mesh):
    return jax.shard_map(
        functools.partial(on_device, mesh.shape["gx"], mesh.shape["gy"]),
        mesh=mesh,
        in_specs=(
            P(("gx", "gy"), None),
            P(("gx", "gy")),
            P(),
            P(None, ("gx", "gy"), None),
            P(("gx", "gy"), None),
            P("gy", "gx"),
            P("gy", "gx"),
            P("gx", "gy"),
            P("gy"),
            P(None, "gx"),
            P("gy", "gx"),
            P("gx", "gy"),
            P("gy"),
            P(None, "gx"),
            P(None, "gx"),
        ),
        out_specs=(
            P(("gx", "gy"), None),
            P(("gx", "gy"), None),
            P(),
            P(("gx", "gy"), None),
            P("gy", "gx"),
            P("gy", "gx"),
            P("gx", "gy"),
            P("gy"),
            P(None, "gx"),
            P("gy", "gx"),
            P("gx", "gy"),
            P("gy"),
            P(None, "gx"),
            P(None, "gx"),
        ),
        check_vma=False,
    )
```

```python
import functools

import jax
import jax.numpy as jnp
from jax import lax
from jax.experimental import pallas as pl
from jax.experimental.pallas import tpu as pltpu
from jax.sharding import PartitionSpec as P

norm_eps = 1e-05
keep_scale = 1.25
kl_weight = 5e-05
MESH = pl.DeviceIdType.MESH
LANES = 128


def round_up(value, multiple):
    return -(-value // multiple) * multiple


class Plan:
    def __init__(self, nx, ny, cells, genes_piece, hidden_piece, latent):
        self.nx, self.ny, self.cells = nx, ny, cells
        self.g, self.h, self.latent = genes_piece, hidden_piece, latent
        self.genes, self.hidden = genes_piece * ny, hidden_piece * nx
        self.hp = round_up(hidden_piece + 1, 16)
        self.hh = self.hp * nx
        tiles = round_up(self.genes, LANES) // LANES
        self.gp = round_up(tiles, ny) // ny * LANES
        self.gg = self.gp * ny
        self.shift = self.gp - self.g
        self.strip = round_up(self.shift * ny, LANES)
        starts = [self.g * j // LANES for j in range(ny)]
        ends = [round_up(self.g * (j + 1), LANES) // LANES for j in range(ny)]
        self.frame_start = [s * LANES for s in starts]
        self.frame = max(e - s for s, e in zip(starts, ends)) * LANES
        self.groups = nx // ny
        self.mid = self.hidden // ny
        self.midp = self.hp * self.groups
        self.midl = round_up(self.midp, LANES)
        self.moments = 2 * latent // ny
        self.ml = round_up(self.moments, LANES)
        self.ll = round_up(latent + 8, LANES)
        self.small = 2 * self.midl + self.ml + self.ll
        self.o2, self.o4 = 0, self.midl
        self.op, self.ol = 2 * self.midl, 2 * self.midl + self.ml
        self.blocks = nx * ny
        rows = round_up(self.hp * 2 // 3, 16)
        self.cuts = ((0, rows), (rows, self.hp - rows)) if rows < self.hp else ((0, rows),)
        self.whole_cuts = ((0, self.hp),)
        self.fits = self.blocks <= 32 and self.hh * ny * self.frame <= 7 * 1024 * 1024


class Flow:
    def __init__(self, plan, kind):
        gx, gy = lax.axis_index("gx"), lax.axis_index("gy")
        self.plan, self.gx, self.gy = plan, gx, gy
        self.sizes = (plan.ny // 2, plan.nx // 2, 2)
        self.core = lax.rem(gy, 2)
        self.at = (gy // 2, gx // 2, lax.rem(gx, 2))
        self.orders = (((0, 1, 2), (2, 1, 0)), ((1, 2, 0), (1, 0, 2)))[kind]
        first, second = self.orders
        self.most = tuple(max(self.sizes[i], self.sizes[j]) for i, j in zip(first, second))
        self.least = tuple(min(self.sizes[i], self.sizes[j]) for i, j in zip(first, second))
        self.limit = tuple(self.pick(self.sizes[i], self.sizes[j]) for i, j in zip(first, second))
        self.here = tuple(self.pick(self.at[i], self.at[j]) for i, j in zip(first, second))

    def pick(self, zero, one):
        if isinstance(zero, int) and isinstance(one, int) and zero == one:
            return zero
        return jnp.where(self.core == 0, zero, one)

    def device(self, spot):
        place = [None] * 3
        for axis in range(3):
            place[axis] = self.pick(
                spot[self.orders[0].index(axis)], spot[self.orders[1].index(axis)]
            )
        return (place[1] * 2 + place[2], place[0] * 2 + self.core)

    def twin(self):
        return (self.gx, self.gy + 1 - 2 * self.core)

    def step(self, axis, sign):
        to = self.here[axis] + sign
        spot = tuple(to if i == axis else self.here[i] for i in range(3))
        return jnp.logical_and(to >= 0, to < self.limit[axis]), self.device(spot)


def neighbours(plan):
    flow = Flow(plan, 0)
    out = [(None, flow.twin())]
    for axis in range(3):
        for sign in (-1, 1):
            out.append(flow.step(axis, sign))
    return out


def when(condition):
    return (lambda f: f()) if condition is None else pl.when(condition)


def greet(plan, extra=()):
    barrier = pltpu.get_barrier_semaphore()
    count = jnp.int32(len(extra))
    for there, device in neighbours(plan):
        @when(there)
        def _(device=device):
            pl.semaphore_signal(barrier, inc=1, device_id=device, device_id_type=MESH)
        count = count + (1 if there is None else there.astype(jnp.int32))
    for device in extra:
        pl.semaphore_signal(barrier, inc=1, device_id=device, device_id_type=MESH)
    pl.semaphore_wait(barrier, count)


class Gather:
    def __init__(self, plan, source, target, width, send_sem, recv_sem):
        self.plan, self.source, self.target, self.width = plan, source, target, width
        self.send_sem, self.recv_sem = send_sem, recv_sem
        self.cuts = [(Flow(plan, kind), *cut) for kind, cut in enumerate(plan.cuts)]
        self.phases = 1 + max(sum(m - 1 for m in cut[0].most) for cut in self.cuts)

    def slot(self, cut, gx, gy):
        _, start, rows = cut
        return self.target.at[
            pl.ds(pl.multiple_of(gx * self.plan.hp + start, 16), rows),
            pl.ds(pl.multiple_of(gy * self.width, LANES), self.width),
        ]

    def own_copy(self, sem):
        plan = self.plan
        gx, gy = lax.axis_index("gx"), lax.axis_index("gy")
        place = self.target.at[
            pl.ds(pl.multiple_of(gx * plan.hp, 16), plan.hp),
            pl.ds(pl.multiple_of(gy * self.width, LANES), self.width),
        ]
        return pltpu.make_async_copy(self.source, place, sem)

    def copies(self, kind, cut, spot, own):
        flow = cut[0]
        gx, gy = flow.device(spot)
        dst = self.slot(cut, gx, gy)
        src = self.source.at[pl.ds(cut[1], cut[2]), :] if own else dst
        index = gx * (self.plan.ny // 2) + gy // 2
        goals = [(None, flow.twin(), 6)]
        level = None
        for axis in (2, 1, 0):
            for sign in (-1, 1):
                if flow.most[axis] < 2:
                    continue
                there, device = flow.step(axis, sign)
                if not own:
                    there = there & ((flow.here[axis] - spot[axis]) * sign >= 0)
                    if level is not None:
                        there = there & level
                goals.append((there, device, 2 * axis + (sign + 1) // 2))
            same = spot[axis] == flow.here[axis]
            level = same if level is None else level & same
        out = []
        for there, device, k in goals:
            out.append((there, pltpu.make_async_remote_copy(
                src_ref=src, dst_ref=dst,
                send_sem=self.send_sem.at[kind, index, k],
                recv_sem=self.recv_sem.at[kind, gx * self.plan.ny + gy],
                device_id=device, device_id_type=MESH,
            )))
        return out

    def arrived(self, kind, cut, gx, gy):
        ref = self.slot(cut, gx, gy)
        pltpu.make_async_copy(ref, ref, self.recv_sem.at[kind, gx * self.plan.ny + gy]).wait()

    def start_own(self):
        for kind, cut in enumerate(self.cuts):
            for there, copy in self.copies(kind, cut, cut[0].here, True):
                when(there)(copy.start)

    def walk(self, visit, phase=None, only=None, part=(0, 1)):
        for kind, cut in enumerate(self.cuts):
            if only is not None and kind != only:
                continue
            flow = cut[0]
            mp, mq, mr = flow.most
            total = mp * mq * mr

            def one(n, _, kind=kind, cut=cut, flow=flow):
                spot = (lax.rem(n, mp), lax.rem(n // mp, mq), n // (mp * mq))
                hops, good = 0, None
                for here, limit, at in zip(flow.here, flow.limit, spot):
                    hops = hops + jnp.abs(at - here)
                    good = at < limit if good is None else good & (at < limit)
                good = good & ((hops > 0) if phase is None else (hops == phase))
                pl.when(good)(functools.partial(visit, kind, cut, spot))
                return 0
            lax.fori_loop(total * part[0] // part[1], total * (part[0] + 1) // part[1], one, 0)

    def visit(self, kind, cut, spot):
        self.arrived(kind, cut, *cut[0].device(spot))
        for there, copy in self.copies(kind, cut, spot, False):
            when(there)(copy.start)

    def forward(self, phase):
        if phase < self.phases:
            self.walk(self.visit, phase)

    def items(self, parts):
        return [functools.partial(self.walk, self.visit, phase, kind, (i, parts))
                for phase in range(1, self.phases) for i in range(parts)
                for kind in range(len(self.cuts))]

    def finish_twin(self):
        plan = self.plan
        for kind, cut in enumerate(self.cuts):
            flow = cut[0]
            def one(n, _, kind=kind, cut=cut, flow=flow):
                gx, y = n // (plan.ny // 2), lax.rem(n, plan.ny // 2)
                self.arrived(kind, cut, gx, 2 * y + 1 - flow.core)
                return 0
            lax.fori_loop(0, plan.blocks // 2, one, 0)

    def finish_sends(self):
        for kind, cut in enumerate(self.cuts):
            for there, copy in self.copies(kind, cut, cut[0].here, True):
                when(there)(copy.wait_send)
        def visit(kind, cut, spot):
            for there, copy in self.copies(kind, cut, spot, False):
                when(there)(copy.wait_send)
        self.walk(visit)


class Meet:
    def __init__(self, plan, wide, tall, send_sem, recv_sem):
        self.plan, self.wide, self.tall = plan, wide, tall
        self.send_sem, self.recv_sem = send_sem, recv_sem
        self.gx, self.gy = lax.axis_index("gx"), lax.axis_index("gy")

    @staticmethod
    def peers(plan):
        gx, gy = lax.axis_index("gx"), lax.axis_index("gy")
        return ([(lax.rem(gx + k, plan.nx), gy) for k in range(1, plan.nx)]
                + [(gx, lax.rem(gy + k, plan.ny)) for k in range(1, plan.ny)])

    def copies(self, second):
        plan = self.plan
        n = plan.ny if second else plan.nx
        ref = self.tall if second else self.wide
        own = self.gy if second else self.gx
        out = []
        for k in range(1, n):
            to = lax.rem(own + k, n)
            at = (plan.nx - 1 if second else 0) + k - 1
            out.append(pltpu.make_async_remote_copy(
                src_ref=ref.at[own], dst_ref=ref.at[own],
                send_sem=self.send_sem.at[at], recv_sem=self.recv_sem.at[at],
                device_id=(self.gx, to) if second else (to, self.gy), device_id_type=MESH,
            ))
        return out

    def run(self, value, merge, members, between=None):
        plan = self.plan
        for second in (False, True):
            ref = self.tall if second else self.wide
            ref[self.gy if second else self.gx] = value
            copies = self.copies(second)
            for copy in copies:
                copy.start()
            if between is not None:
                between(second)
            for copy in copies:
                copy.wait_recv()
            value = merge([ref[i] for i in range(ref.shape[0])], members)
            members = members * plan.nx
            for copy in copies:
                copy.wait_send()
        return value


def merge_sums(parts, members):
    total = parts[0]
    for part in parts[1:]:
        total = total + part
    return total


def merge_moments(parts, members):
    n = len(parts)
    mean = merge_sums([part[0:1] for part in parts], 0) / n
    squares = merge_sums([part[1:2] for part in parts], 0)
    between = merge_sums([(part[0:1] - mean) * (part[0:1] - mean) for part in parts], 0)
    return jnp.concatenate([mean, squares + members * between], axis=0)


def tiled(column, plan):
    return jnp.concatenate([column] * (plan.cells // LANES), axis=1)


def lane_sums(value):
    total = value[:, :LANES]
    for at in range(LANES, value.shape[1], LANES):
        total = total + value[:, at:at + LANES]
    return total


def as_row(value):
    return jnp.sum(value.T, axis=0, keepdims=True)


def as_column(row):
    return jnp.broadcast_to(row, (LANES, LANES)).T


def aligned(start, rows=LANES):
    return pl.ds(pl.multiple_of(start, rows), rows)


def moment_rows(plan, h_ref, row_ref):
    def block(i, _):
        value = h_ref[aligned(i * LANES), :]
        sums = lane_sums(value)
        mean = jnp.sum(sums, axis=1, keepdims=True) / plan.cells
        offset = value - mean
        row_ref[0:1, aligned(i * LANES)] = as_row(sums) / plan.cells
        row_ref[1:2, aligned(i * LANES)] = as_row(lane_sums(offset * offset))
        return 0
    lax.fori_loop(0, plan.hh // LANES, block, 0)


def unit_column(slab_ref, i, at):
    slab = slab_ref[aligned(i * LANES), :]
    return jnp.broadcast_to(slab.astype(jnp.float32)[:, at:at + 1], (LANES, LANES))


def activate(plan, k, h_ref, row_ref, slab_ref, keep_ref, out_ref, column_ref, total_cells, spare,
             tick=lambda: None):
    def block(i, _):
        column_ref[0] = as_column(row_ref[0:1, aligned(i * LANES)])
        column_ref[1] = as_column(lax.rsqrt(row_ref[1:2, aligned(i * LANES)] / total_cells + norm_eps))
        column_ref[2] = unit_column(slab_ref, i, k)
        column_ref[3] = unit_column(slab_ref, i, 4 + k)

        def chunk(j, _):
            rows = aligned(i * LANES + j * 16, 16)
            mean, inverse, gain, bias = (
                tiled(column_ref[n, aligned(j * 16, 16), :], plan) for n in range(4))
            scaled = (h_ref[rows, :] - mean) * inverse
            h_ref[rows, :] = scaled
            normed = gain * scaled + bias
            active = normed * jax.nn.sigmoid(normed) * keep_ref[k, rows, :].astype(jnp.float32)
            if spare:
                row = lax.broadcasted_iota(jnp.int32, active.shape, 0) + (i * LANES + j * 16)
                active = jnp.where(lax.rem(row, plan.hp) == plan.h, 1.0, active)
            out_ref[rows, :] = active.astype(jnp.bfloat16)
            return 0
        lax.fori_loop(0, LANES // 16, chunk, 0)
        return 0
    cut = plan.hh // LANES // 2
    lax.fori_loop(0, cut, block, 0)
    tick()
    lax.fori_loop(cut, plan.hh // LANES, block, 0)


def keep_rows(plan, flags_ref, keep_ref, k):
    def lane(t, _):
        lanes = aligned(t * LANES)
        for group in range(plan.nx):
            for start in range(0, plan.hp, 16):
                at = group * plan.h + start
                value = flags_ref[at:at + 16, lanes].astype(jnp.float32) * keep_scale
                if start + 16 > plan.h:
                    row = lax.broadcasted_iota(jnp.int32, value.shape, 0)
                    value = jnp.where(row < plan.h - start, value, 0.0)
                at = group * plan.hp + start
                keep_ref[k, at:at + 16, lanes] = value.astype(jnp.bfloat16)
        return 0
    lax.fori_loop(0, plan.cells // LANES, lane, 0)


def forward_kernel(plan, total_cells, *refs):
    (w1, wsmall, wout, x_hbm, flags_hbm, draws_ref,
     embed_all, small_out, readout_all, center_out, log_var_out, sample_out, layers_out, scaled_out,
     keep_out, rows_out,
     w1_ref, small_ref, x_ref, keep_ref, flags_ref, h_ref, layer_ref, column_ref, latent_ref,
     wide, tall, send_sem, recv_sem, meet_send, meet_recv, own_sem, load_sem, flag_sem, out_sem) = refs
    mid = plan.midp
    load = pltpu.make_async_copy(x_hbm, x_ref, load_sem)
    deep = flags_ref.shape[0]

    def flags(k):
        return pltpu.make_async_copy(
            flags_hbm.at[k], flags_ref.at[k % deep, pl.ds(0, plan.hidden), :], flag_sem.at[k % deep])

    for k in range(deep):
        flags(k).start()
    load.start()
    sets = send_sem.shape[0]
    embed, small, readout = (
        Gather(plan, source, target, width, send_sem.at[u % sets], recv_sem.at[u])
        for u, (source, target, width) in enumerate((
            (w1, w1_ref, plan.gp), (wsmall, small_ref, plan.small), (wout, readout_all, plan.gp))))
    own = [g.own_copy(own_sem.at[u]) for u, g in enumerate((embed, small, readout))]
    for copy in own:
        copy.start()
    peers = Meet.peers(plan)
    barrier = pltpu.get_barrier_semaphore()
    for device in peers:
        pl.semaphore_signal(barrier, inc=1, device_id=device, device_id_type=MESH)
    pl.semaphore_wait(barrier, len(peers))

    def keepers(k):
        flags(k).wait()
        keep_rows(plan, flags_ref.at[k % deep], keep_ref, k)
        if k + deep < 4:
            flags(k + deep).start()

    embed.start_own()
    late = embed.phases - 2
    for phase in range(1, embed.phases):
        if phase <= 4:
            keepers(phase - 1)
        if phase == late:
            if sets == 1:
                pass
            else:
                small.start_own()
        embed.forward(phase)
    for k in range(embed.phases - 1, 4):
        keepers(k)
    if sets == 1:
        embed.finish_sends()
        small.start_own()
    load.wait()
    tail = layer_ref.shape[1] - plan.hh
    slots = layer_ref.shape[0]
    for k in range(slots):
        if tail:
            layer_ref[k, plan.hh:, :] = jnp.zeros((tail, plan.cells), jnp.bfloat16)
    latent_ref[...] = jnp.zeros_like(latent_ref)
    latent_ref[2, 0:plan.latent, :] = draws_ref[...]
    own[0].wait()
    embed.finish_twin()
    outs = [pltpu.make_async_copy(w1_ref, embed_all, out_sem.at[0])]
    outs[0].start()

    queue = [] if sets == 1 else small.items(2)
    marks = {}
    if sets > 1:
        queue.insert(5, readout.start_own)
        marks["small"] = len(queue)
        queue += readout.items(2)
    total = len(queue)

    def tick(count=1):
        for _ in range(count):
            if queue:
                queue.pop(0)()

    half_rows = plan.hh // 2
    for j in range(plan.ny):
        start, stop = j * plan.gp, min((j + 1) * plan.gp, plan.genes)
        for top in (0, half_rows):
            part = rows_dot(w1_ref[top:top + half_rows, start:stop], x_ref[start:stop, :])
            spot = pl.ds(top, half_rows)
            h_ref[0, spot, :] = part if j == 0 else h_ref[0, spot, :] + part
            tick()

    layer_writes = []

    def norm(k, spare):
        h = h_ref.at[k % 2]
        tick()
        moment_rows(plan, h, rows_out.at[k])
        meet = Meet(plan, wide.at[k], tall.at[k], meet_send.at[k], meet_recv.at[k])
        rows_out[k] = meet.run(rows_out[k], merge_moments, float(plan.cells), lambda second: tick(2))
        slab = w1_ref.at[:, pl.ds(plan.gg - LANES, LANES)]
        if k >= slots:
            finish(layer_writes[k - slots])
        activate(plan, k, h, rows_out.at[k], slab, keep_ref, layer_ref.at[k % slots], column_ref,
                 total_cells, spare, tick)
        for n, (source, target) in enumerate((
                (h, scaled_out.at[k]),
                (layer_ref.at[k % slots, pl.ds(0, plan.hh), :], layers_out.at[k]),
                (keep_ref.at[k], keep_out.at[k]))):
            outs.append(pltpu.make_async_copy(source, target, out_sem.at[3 + 3 * k + n]))
            outs[-1].start()
        layer_writes.append(outs[-2])
        return outs[-3]

    def finish(copy):
        copy.wait()
        outs[:] = [other for other in outs if other is not copy]

    def whole_small():
        if sets > 1:
            while total - len(queue) < marks["small"]:
                tick()
        else:
            for item in small.items(1):
                item()
        own[1].wait()
        small.finish_twin()
        if sets == 1:
            small.finish_sends()
            readout.start_own()
            queue.extend(readout.items(1))
        outs.append(pltpu.make_async_copy(small_ref, small_out, out_sem.at[1]))
        outs[-1].start()
        own[2].wait()

    def hidden(source, lane, target):
        for j in range(plan.ny):
            at = j * plan.small + lane
            part = rows_dot(small_ref[:, at:at + plan.midl], source[mid * j:mid * j + plan.midl, :])
            target[...] = part if j == 0 else target[...] + part
            if j % 2:
                tick()

    wrote_one = norm(0, False)
    whole_small()
    hidden(layer_ref.at[0], plan.o2, h_ref.at[1])
    wrote_two = norm(1, True)
    half = plan.ny // 2
    for j in range(plan.ny):
        at = j * plan.small + plan.op
        part = over_rows(small_ref[:, at:at + plan.ml], layer_ref[1, 0:plan.hh, :])
        spot = (j % half) * plan.moments
        latent_ref[j // half, spot:spot + plan.moments, :] = part[:plan.moments]
    center, log_var = latent_ref[0], latent_ref[1]
    sample = center + jnp.exp(0.5 * log_var) * latent_ref[2]
    row = lax.broadcasted_iota(jnp.int32, sample.shape, 0)
    sample_out[...] = jnp.where(row < plan.latent, sample, 0.0).astype(jnp.bfloat16)
    center_out[...] = latent_ref[0, 0:plan.latent, :]
    log_var_out[...] = latent_ref[1, 0:plan.latent, :]
    finish(wrote_one)
    h_ref[0] = rows_dot(small_ref[:, plan.ol:plan.ol + plan.ll], sample_out[...])
    norm(2, False)
    finish(wrote_two)
    hidden(layer_ref.at[2 % slots], plan.o4, h_ref.at[1])
    norm(3, True)
    while queue:
        tick()
    readout.finish_twin()
    if sets > 1:
        embed.finish_sends()
        small.finish_sends()
    readout.finish_sends()
    for copy in outs:
        copy.wait()


def forward_all(plan, total_cells, w1, wsmall, wout, profiles, flags, draws):
    any_spec, vmem = pl.BlockSpec(memory_space=pl.ANY), pl.BlockSpec(memory_space=pltpu.VMEM)
    f32, bf16 = jnp.float32, jnp.bfloat16
    n = plan.nx + plan.ny - 2
    cuts = len(plan.cuts)
    sets = 3 if plan.blocks <= 32 else 1
    shape = jax.ShapeDtypeStruct
    return pl.pallas_call(
        functools.partial(forward_kernel, plan, total_cells),
        out_shape=[
            shape((plan.hh, plan.gg), bf16), shape((plan.hh, plan.ny * plan.small), bf16),
            shape((plan.hh, plan.gg), bf16), shape((plan.latent, plan.cells), f32),
            shape((plan.latent, plan.cells), f32), shape((plan.ll, plan.cells), bf16),
            shape((4, plan.hh, plan.cells), bf16), shape((4, plan.hh, plan.cells), f32),
            shape((4, plan.hh, plan.cells), bf16), shape((4, 2, plan.hh), f32)],
        in_specs=[any_spec] * 5 + [vmem],
        out_specs=[any_spec] * 3 + [vmem] * 3 + [any_spec] * 3 + [vmem],
        scratch_shapes=[
            pltpu.VMEM((plan.hh, plan.gg), bf16),
            pltpu.VMEM((plan.hh, plan.ny * plan.small), bf16),
            pltpu.VMEM((plan.genes, plan.cells), bf16),
            pltpu.VMEM((4, plan.hh, plan.cells), bf16),
            pltpu.VMEM((2 if sets > 1 else 1, plan.hidden + 16, plan.cells), jnp.int32),
            pltpu.VMEM((2, plan.hh, plan.cells), f32),
            pltpu.VMEM((4 if sets > 1 else 2, plan.hh + plan.midl - plan.midp, plan.cells), bf16),
            pltpu.VMEM((4, LANES, LANES), f32),
            pltpu.VMEM((3, plan.ll, plan.cells), f32),
            pltpu.VMEM((4, plan.nx, 2, plan.hh), f32),
            pltpu.VMEM((4, plan.ny, 2, plan.hh), f32),
            pltpu.SemaphoreType.DMA((sets, cuts, plan.blocks // 2, 7)),
            pltpu.SemaphoreType.DMA((3, cuts, plan.blocks)),
            pltpu.SemaphoreType.DMA((4, n)),
            pltpu.SemaphoreType.DMA((4, n)),
            pltpu.SemaphoreType.DMA((3,)),
            pltpu.SemaphoreType.DMA,
            pltpu.SemaphoreType.DMA((2,)),
            pltpu.SemaphoreType.DMA((15,)),
        ],
        compiler_params=pltpu.CompilerParams(
            collective_id=0, has_side_effects=True, vmem_limit_bytes=60 * 1024 * 1024),
    )(w1, wsmall, wout, profiles, flags, draws)


def meet_kernel(plan, merge, x_ref, o_ref, wide, tall, send_sem, recv_sem):
    peers = Meet.peers(plan)
    barrier = pltpu.get_barrier_semaphore()
    for device in peers:
        pl.semaphore_signal(barrier, inc=1, device_id=device, device_id_type=MESH)
    pl.semaphore_wait(barrier, len(peers))
    meet = Meet(plan, wide, tall, send_sem, recv_sem)
    o_ref[...] = meet.run(x_ref[...], merge, float(plan.cells))


def meet_all(plan, value, merge, collective_id):
    rows, width = value.shape
    n = plan.nx + plan.ny - 2
    return pl.pallas_call(
        functools.partial(meet_kernel, plan, merge),
        out_shape=jax.ShapeDtypeStruct(value.shape, jnp.float32),
        in_specs=[pl.BlockSpec(memory_space=pltpu.VMEM)],
        out_specs=pl.BlockSpec(memory_space=pltpu.VMEM),
        scratch_shapes=[
            pltpu.VMEM((plan.nx, rows, width), jnp.float32),
            pltpu.VMEM((plan.ny, rows, width), jnp.float32),
            pltpu.SemaphoreType.DMA((n,)),
            pltpu.SemaphoreType.DMA((n,)),
        ],
        compiler_params=pltpu.CompilerParams(collective_id=collective_id, has_side_effects=True),
    )(value)


def share_kernel(plan, row_ref, block_ref, row_out, block_out, wide, tall, send_sem, recv_sem):
    peers = Meet.peers(plan)
    barrier = pltpu.get_barrier_semaphore()
    for device in peers:
        pl.semaphore_signal(barrier, inc=1, device_id=device, device_id_type=MESH)
    pl.semaphore_wait(barrier, len(peers))
    meet = Meet(plan, wide, tall, send_sem, recv_sem)
    wide[meet.gx] = row_ref[...]
    tall[meet.gy] = block_ref[...]
    copies = meet.copies(False) + meet.copies(True)
    for copy in copies:
        copy.start()
    for copy in copies:
        copy.wait_recv()
    row_out[...] = wide[0]
    block_out[...] = tall[0]
    for copy in copies:
        copy.wait_send()


def share_all(plan, row, block, collective_id):
    n = plan.nx + plan.ny - 2
    return pl.pallas_call(
        functools.partial(share_kernel, plan),
        out_shape=[jax.ShapeDtypeStruct(row.shape, jnp.float32),
                   jax.ShapeDtypeStruct(block.shape, jnp.float32)],
        in_specs=[pl.BlockSpec(memory_space=pltpu.VMEM)] * 2,
        out_specs=[pl.BlockSpec(memory_space=pltpu.VMEM)] * 2,
        scratch_shapes=[
            pltpu.VMEM((plan.nx, *row.shape), jnp.float32),
            pltpu.VMEM((plan.ny, *block.shape), jnp.float32),
            pltpu.SemaphoreType.DMA((n,)),
            pltpu.SemaphoreType.DMA((n,)),
        ],
        compiler_params=pltpu.CompilerParams(collective_id=collective_id, has_side_effects=True),
    )(row, block)


class Reduce:
    def __init__(self, plan, width, part, twin, slots, send_sem, twin_sem, recv_sem):
        self.plan, self.width, self.part, self.twin, self.slots = plan, width, part, twin, slots
        self.send_sem, self.twin_sem, self.recv_sem = send_sem, twin_sem, recv_sem
        self.cuts = [(Flow(plan, kind), *cut) for kind, cut in enumerate(plan.whole_cuts)]

    @staticmethod
    def slot_counts(plan):
        counts = []
        for kind in range(len(plan.whole_cuts)):
            sizes = (plan.ny // 2, plan.nx // 2, 2)
            first, second = (((0, 1, 2), (2, 1, 0)), ((1, 2, 0), (1, 0, 2)))[kind]
            mp, mq, mr = (max(sizes[i], sizes[j]) for i, j in zip(first, second))
            a, b, c = (Reduce.sides(m) for m in (mp, mq, mr))
            far_r = (mr > 2) * (mr * mq * mp)
            counts.append((far_r, mq * mp * (c + (mq > 2)), mp * (c + b + (mp > 2)), c + b + a))
        return counts

    @staticmethod
    def sides(most):
        return 1 if most == 2 else (2 if most > 2 else 0)

    def block(self, ref, cut, gx, gy):
        return ref.at[
            pl.ds(pl.multiple_of(gx * self.plan.hp + cut[1], 16), cut[2]),
            pl.ds(pl.multiple_of(gy * self.width, LANES), self.width),
        ]

    def twin_block(self, cut, gx, y):
        return self.twin.at[
            pl.ds(pl.multiple_of(gx * self.plan.hp + cut[1], 16), cut[2]),
            pl.ds(pl.multiple_of(y * self.width, LANES), self.width),
        ]

    def twin_copy(self, kind, cut, gx, y):
        flow = cut[0]
        return pltpu.make_async_remote_copy(
            src_ref=self.block(self.part, cut, gx, 2 * y + 1 - flow.core),
            dst_ref=self.twin_block(cut, gx, y),
            send_sem=self.twin_sem.at[0, kind, gx * (self.plan.ny // 2) + y],
            recv_sem=self.twin_sem.at[1, kind, gx * (self.plan.ny // 2) + y],
            device_id=flow.twin(), device_id_type=MESH,
        )

    def each_twin(self, visit, ys=None):
        ny2 = self.plan.ny // 2
        a, na = self.cuts[0][0].at[1], self.plan.nx // 2

        def along(n, _):
            to = a + (na - 1 - n // 2) * (1 - 2 * lax.rem(n, 2))

            @pl.when((to >= 0) & (to < na))
            def _():
                for kind, cut in enumerate(self.cuts):
                    def one(i, _, kind=kind, cut=cut):
                        visit(self.twin_copy(kind, cut, to * 2 + i // ny2, lax.rem(i, ny2)))
                        return 0
                    lax.fori_loop(0, 2 * ny2, one, 0)
            return 0
        lax.fori_loop(0, 2 * na - 1, along, 0)

    def start_twin(self):
        self.each_twin(lambda copy: copy.start())

    def entry(self, kind, stage, spot, axis, came_from):
        flow = self.cuts[kind][0]
        mp, mq, mr = flow.most
        far_r, far_q, far_p, _ = Reduce.slot_counts(self.plan)[kind]
        sides = [Reduce.sides(m) for m in flow.most]
        dp, dq, dr = spot
        if stage == 2:
            return (dr * mq + dq) * mp + dp
        if stage == 1:
            base, which = far_r, (dq * mp + dp) * (sides[2] + (mq > 2))
        elif stage == 0:
            base, which = far_r + far_q, dp * (sides[2] + sides[1] + (mp > 2))
        else:
            base, which = far_r + far_q + far_p, 0
        offset = 0
        for later in (2, 1, 0):
            if later == stage:
                return base + which + offset
            if later == axis:
                side = 0 if sides[axis] == 1 else (came_from + 1) // 2
                return base + which + offset + side
            offset += sides[later]

    def slot(self, kind, index):
        cut = self.cuts[kind]
        total = sum(Reduce.slot_counts(self.plan)[kind])
        return self.slots[kind].at[index], self.recv_sem[kind].at[index]

    def gather_terms(self, kind, cut, spot, stage, sign):
        flow = cut[0]
        ny2 = self.plan.ny // 2
        gx, gy = flow.device(spot)
        y = gy // 2
        copy = self.twin_copy(kind, cut, gx, y)
        copy.wait_recv()
        own = self.block(self.part, cut, gx, gy)
        twin = self.twin_block(cut, gx, y)
        arrivals = []
        for axis in (2, 1, 0):
            if axis > stage:
                for side in (-1, 1):
                    there, _ = flow.step(axis, side)
                    if flow.most[axis] < 2:
                        continue
                    arrivals.append((there, self.entry(kind, stage, spot, axis, side)))
            elif axis == stage and flow.most[axis] > 2:
                away = self.here_away(flow, axis, sign)
                arrivals.append((away, self.entry(kind, stage, spot, axis, None)))
        return own, twin, arrivals

    def here_away(self, flow, axis, sign):
        to = flow.here[axis] - sign
        return (to >= 0) & (to < flow.limit[axis])

    def add_in(self, kind, cut, spot, stage, sign):
        own, twin, arrivals = self.gather_terms(kind, cut, spot, stage, sign)

        def add(other):
            def chunk(i, _):
                rows = aligned(i * 16, 16)
                own[rows, :] = own[rows, :] + other[rows, :]
                return 0
            lax.fori_loop(0, cut[2] // 16, chunk, 0)

        add(twin)
        for there, index in arrivals:
            slot, sem = self.slot(kind, index)
            @when(there)
            def _(slot=slot, sem=sem):
                pltpu.make_async_copy(slot, slot, sem).wait()
                add(slot)
        return own

    def onward(self, kind, cut, spot, stage, sign):
        flow = cut[0]
        _, device = self.toward(flow, stage, sign)
        gx, gy = flow.device(spot)
        to = flow.here[stage] + sign
        index_same = self.entry(kind, stage, spot, stage, None) if flow.most[stage] > 2 else None
        done = to == spot[stage]
        p_same = flow.here[0] == spot[0]
        q_same = flow.here[1] == spot[1]
        if stage == 2:
            deeper = jnp.where(q_same, jnp.where(p_same,
                               self.entry(kind, -1, spot, 2, -sign),
                               self.entry(kind, 0, spot, 2, -sign)),
                               self.entry(kind, 1, spot, 2, -sign))
        elif stage == 1:
            deeper = jnp.where(p_same, self.entry(kind, -1, spot, 1, -sign),
                               self.entry(kind, 0, spot, 1, -sign))
        else:
            deeper = self.entry(kind, -1, spot, 0, -sign)
        index = deeper if index_same is None else jnp.where(done, deeper, index_same)
        slot, sem = self.slot(kind, index)
        ny2 = self.plan.ny // 2
        return pltpu.make_async_remote_copy(
            src_ref=self.block(self.part, cut, gx, gy), dst_ref=slot,
            send_sem=self.send_sem.at[kind, gx * ny2 + gy // 2], recv_sem=sem,
            device_id=device, device_id_type=MESH,
        )

    def toward(self, flow, axis, sign):
        return flow.step(axis, sign)

    def order(self, kind):
        mp, mq, mr = self.cuts[kind][0].most
        out = [(2, k, far) for k in range(mr - 1, 0, -1) for far in range(mq - 1, -1, -1)]
        return out + [(stage, k, 0) for stage in (1, 0)
                      for k in range(self.cuts[kind][0].most[stage] - 1, 0, -1)]

    def walk(self, visit, kind, stage, k, far):
        cut = self.cuts[kind]
        p, q, r = cut[0].here
        np_, nq, nr = cut[0].limit
        mp, mq, mr = cut[0].most

        def one(n, _):
            dp = p + (mp - 1 - n // 2) * (1 - 2 * lax.rem(n, 2))
            for sign in (-1, 1):
                if stage == 2:
                    d = r + sign * k
                    for side in ((-1, 1) if far else (1,)):
                        dq = q + side * far
                        good = ((d >= 0) & (d < nr) & (dq >= 0) & (dq < nq)
                                & (dp >= 0) & (dp < np_))
                        pl.when(good)(functools.partial(visit, kind, cut, (dp, dq, d), stage, sign))
                    continue
                if stage == 1:
                    d = q + sign * k
                    spot, good = (dp, d, r), (d >= 0) & (d < nq) & (dp >= 0) & (dp < np_)
                else:
                    d = p + sign * k
                    spot, good = (d, q, r), (d >= 0) & (d < np_)
                pl.when(good)(functools.partial(visit, kind, cut, spot, stage, sign))
            return 0
        lax.fori_loop(0, 1 if stage == 0 else 2 * mp - 1, one, 0)

    def visit(self, kind, cut, spot, stage, sign):
        self.add_in(kind, cut, spot, stage, sign)
        self.onward(kind, cut, spot, stage, sign).start()

    def items(self):
        lines = [[functools.partial(self.walk, self.visit, kind, *step) for step in self.order(kind)]
                 for kind in range(len(self.cuts))]
        out = []
        for i in range(max(len(line) for line in lines)):
            out += [line[i] for line in lines if i < len(line)]
        return out

    def own_sum(self, out_ref, factor):
        for kind, cut in enumerate(self.cuts):
            flow = cut[0]
            own = self.add_in(kind, cut, flow.here, -1, None)
            out_ref[pl.ds(cut[1], cut[2]), :] = own[...].astype(jnp.float32) * factor

    def finish_sends(self):
        self.each_twin(lambda copy: copy.wait_send())
        def visit(kind, cut, spot, stage, sign):
            self.onward(kind, cut, spot, stage, sign).wait_send()
        for kind in range(len(self.cuts)):
            for step in self.order(kind):
                self.walk(visit, kind, *step)

    def twin_column(self, gy):
        y, flow = gy // 2, self.cuts[0][0]

        @pl.when(gy % 2 != flow.core)
        def _():
            for kind, cut in enumerate(self.cuts):
                def one(gx, _, kind=kind, cut=cut):
                    self.twin_copy(kind, cut, gx, y).start()
                    return 0
                lax.fori_loop(0, self.plan.nx, one, 0)


def reduce_scratch(plan, width):
    counts = [sum(c) for c in Reduce.slot_counts(plan)]
    return [
        pltpu.VMEM((plan.hh, plan.ny * width), jnp.bfloat16),
        pltpu.VMEM((plan.hh, plan.ny // 2 * width), jnp.bfloat16),
        *[pltpu.VMEM((c, cut[1], width), jnp.bfloat16) for c, cut in zip(counts, plan.whole_cuts)],
        pltpu.SemaphoreType.DMA((len(plan.whole_cuts), plan.blocks // 2)),
        pltpu.SemaphoreType.DMA((2, len(plan.whole_cuts), plan.blocks // 2)),
        *[pltpu.SemaphoreType.DMA((c,)) for c in counts],
    ]


def reduce_from(plan, width, refs):
    n = len(plan.whole_cuts)
    part, twin, slots, sems, recv = refs[0], refs[1], refs[2:2 + n], refs[2 + n:4 + n], refs[4 + n:]
    return Reduce(plan, width, part, twin, slots, *sems, recv)


def reduce_kernel(plan, width, factor, x_ref, o_ref, *rest):
    reduce = reduce_from(plan, width, rest[:-1])
    load = pltpu.make_async_copy(x_ref, reduce.part, rest[-1])
    load.start()
    greet(plan)
    load.wait()
    reduce.start_twin()
    for item in reduce.items():
        item()
    reduce.own_sum(o_ref, factor)
    reduce.finish_sends()


def reduce_all(plan, value, factor, collective_id):
    width = value.shape[1] // plan.ny
    return pl.pallas_call(
        functools.partial(reduce_kernel, plan, width, factor),
        out_shape=jax.ShapeDtypeStruct((plan.hp, width), jnp.float32),
        in_specs=[pl.BlockSpec(memory_space=pl.ANY)],
        out_specs=pl.BlockSpec(memory_space=pltpu.VMEM),
        scratch_shapes=[*reduce_scratch(plan, width), pltpu.SemaphoreType.DMA],
        compiler_params=pltpu.CompilerParams(
            collective_id=collective_id, has_side_effects=True, vmem_limit_bytes=60 * 1024 * 1024),
    )(value)


def backward_kernel(plan, total_cells, *refs):
    (part_hbm, up_hbm, small_hbm, layers_hbm, scaled_hbm, keep_hbm, sample_ref, rows_ref, loss_ref,
     center_ref, log_var_ref, draws_ref,
     readout_out, sums_out, small_part, grad_ref,
     small_ref, up_ref, layer_ref, scaled_ref, keep_ref, lane_ref, column_ref, latent_ref,
     moment_ref, wide, tall, meet_send, meet_recv, load_sem, *rest) = refs
    reduce = reduce_from(plan, plan.frame, rest)

    def load(k):
        slot = k % 2
        return (
            pltpu.make_async_copy(scaled_hbm.at[k], scaled_ref.at[slot], load_sem.at[3 * slot]),
            pltpu.make_async_copy(keep_hbm.at[k], keep_ref.at[slot], load_sem.at[3 * slot + 1]),
        )

    def load_layer(k):
        return pltpu.make_async_copy(
            layers_hbm.at[k], layer_ref.at[k % 2, pl.ds(0, plan.hh), :], load_sem.at[3 * (k % 2) + 2])

    frames = [pltpu.make_async_copy(
        part_hbm.at[:, pl.ds(start, plan.frame)],
        reduce.part.at[:, pl.ds(j * plan.frame, plan.frame)], load_sem.at[6 + j])
        for j, start in enumerate(plan.frame_start)]
    second = pltpu.make_async_copy(up_hbm, up_ref, load_sem.at[6 + plan.ny])
    third = pltpu.make_async_copy(small_hbm, small_ref, load_sem.at[7 + plan.ny])
    for copy in frames:
        copy.start()
    second.start()
    for copy in load(3):
        copy.start()
    third.start()
    load_layer(2).start()
    for copy in load(2):
        copy.start()
    load_layer(1).start()
    peers = Meet.peers(plan)
    barrier = pltpu.get_barrier_semaphore()
    for device in peers:
        pl.semaphore_signal(barrier, inc=1, device_id=device, device_id_type=MESH)
    pl.semaphore_wait(barrier, len(peers))
    for copy in frames:
        copy.wait()
    reduce.start_twin()
    tail = layer_ref.shape[1] - plan.hh
    if tail:
        for k in range(2):
            layer_ref[k, plan.hh:, :] = jnp.zeros((tail, plan.cells), jnp.bfloat16)
    latent_ref[...] = jnp.zeros_like(latent_ref)

    todo = reduce.items()
    todo.append(lambda: reduce.own_sum(readout_out, 1.0 / total_cells))

    def between(second):
        if todo:
            todo.pop(0)()

    def layer(k):
        slot = k % 2
        for copy in load(k):
            copy.wait()

        def columns(i):
            slab = small_ref.at[:, pl.ds(plan.ol + plan.ll - LANES, LANES)]
            base = plan.latent - (plan.ll - LANES)
            column_ref[0] = unit_column(slab, i, base + k)
            column_ref[1] = unit_column(slab, i, base + 4 + k)
            column_ref[2] = as_column(
                lax.rsqrt(rows_ref[k, 1:2, aligned(i * LANES)] / total_cells + norm_eps))

        def block(i, _):
            columns(i)

            def chunk(j, _):
                rows = aligned(i * LANES + j * 16, 16)
                here = aligned(j * 16, 16)
                gain, bias = tiled(column_ref[0, here, :], plan), tiled(column_ref[1, here, :], plan)
                scaled = scaled_ref[slot, rows, :]
                normed = gain * scaled + bias
                sigma = jax.nn.sigmoid(normed)
                slope = up_ref[rows, :] * keep_ref[slot, rows, :].astype(jnp.float32) * sigma * (
                    1.0 + normed * (1.0 - sigma))
                up_ref[rows, :] = slope
                lane_ref[0, here, :] = lane_sums(slope)
                lane_ref[1, here, :] = lane_sums(slope * scaled)
                return 0
            lax.fori_loop(0, LANES // 16, chunk, 0)
            sums_out[k, 0:1, aligned(i * LANES)] = as_row(lane_ref[0])
            sums_out[k, 1:2, aligned(i * LANES)] = as_row(lane_ref[1])
            return 0
        lax.fori_loop(0, plan.hh // LANES, block, 0)
        between(None)
        sums_out[k, 2:3, :] = loss_ref[...]
        meet = Meet(plan, wide.at[k], tall.at[k], meet_send.at[k], meet_recv.at[k])
        sums_out[k] = meet.run(sums_out[k], merge_sums, 1.0, between)

        def last(i, _):
            columns(i)
            column_ref[3] = as_column(sums_out[k, 0:1, aligned(i * LANES)] / total_cells)
            column_ref[4] = as_column(sums_out[k, 1:2, aligned(i * LANES)] / total_cells)

            def chunk(j, _):
                rows = aligned(i * LANES + j * 16, 16)
                here = aligned(j * 16, 16)
                factor = tiled(column_ref[0, here, :] * column_ref[2, here, :], plan)
                shift, gain = tiled(column_ref[3, here, :], plan), tiled(column_ref[4, here, :], plan)
                grad = factor * (up_ref[rows, :] - (shift + scaled_ref[slot, rows, :] * gain))
                grad_ref[rows, :] = grad.astype(jnp.bfloat16)
                return 0
            lax.fori_loop(0, LANES // 16, chunk, 0)
            return 0
        lax.fori_loop(0, plan.hh // LANES, last, 0)
        if k >= 2:
            for copy in load(k - 2):
                copy.start()

    def put(j, lane, value):
        at = j * plan.small + lane
        small_part[:, at:at + value.shape[1]] = value.astype(jnp.bfloat16)

    def middle(source, lane):
        for j in range(plan.ny):
            at, row = j * plan.small + lane, j * plan.midp
            put(j, lane, over_cells(grad_ref[...], source[row:row + plan.midl, :]))
            if j % 2:
                between(None)
            up_ref[row:row + plan.midp, :] = over_rows(
                small_ref[:, at:at + plan.midl], grad_ref[...])[:plan.midp]

    second.wait()
    third.wait()
    layer(3)
    load_layer(2).wait()
    middle(layer_ref.at[0], plan.o4)
    load_layer(0).start()
    layer(2)
    lifting = over_cells(grad_ref[...], sample_ref[...])
    for j in range(plan.ny):
        put(j, plan.ol, lifting)
    reach = over_rows(small_ref[:, plan.ol:plan.ol + plan.ll], grad_ref[...])[:plan.latent]
    center, log_var = center_ref[...], log_var_ref[...]
    latent_ref[0, 0:plan.latent, :] = reach + kl_weight * center
    latent_ref[1, 0:plan.latent, :] = (
        reach * 0.5 * jnp.exp(0.5 * log_var) * draws_ref[...]
        + kl_weight * 0.5 * (jnp.exp(log_var) - 1.0))
    half, tall_rows = plan.ny // 2, round_up(plan.moments, 16)
    moment_ref[...] = jnp.zeros_like(moment_ref)
    for j in range(plan.ny):
        spot = (j % half) * plan.moments
        piece = latent_ref[j // half, spot:spot + tall_rows, :]
        row = lax.broadcasted_iota(jnp.int32, piece.shape, 0)
        piece = jnp.where(row < plan.moments, piece, 0.0)
        moment_ref[j * plan.ml:j * plan.ml + tall_rows, :] = piece.astype(jnp.bfloat16)
    load_layer(1).wait()
    for j in range(plan.ny):
        at, row = j * plan.small + plan.op, j * plan.ml
        moments = moment_ref[row:row + plan.ml, :]
        put(j, plan.op, over_cells(layer_ref[1, 0:plan.hh, :], moments))
        part = rows_dot(small_ref[:, at:at + plan.ml], moments)
        up_ref[...] = part if j == 0 else up_ref[...] + part
    layer(1)
    load_layer(0).wait()
    middle(layer_ref.at[0], plan.o2)
    layer(0)
    while todo:
        between(False)
    reduce.finish_sends()


def backward_all(plan, total_cells, *arrays):
    any_spec, vmem = pl.BlockSpec(memory_space=pl.ANY), pl.BlockSpec(memory_space=pltpu.VMEM)
    f32, bf16 = jnp.float32, jnp.bfloat16
    n = plan.nx + plan.ny - 2
    shape = jax.ShapeDtypeStruct
    return pl.pallas_call(
        functools.partial(backward_kernel, plan, total_cells),
        out_shape=[
            shape((plan.hp, plan.frame), f32), shape((4, 3, plan.hh), f32),
            shape((plan.hh, plan.ny * plan.small), bf16), shape((plan.hh, plan.cells), bf16)],
        in_specs=[any_spec] * 6 + [vmem] * 6,
        out_specs=[vmem] * 4,
        scratch_shapes=[
            pltpu.VMEM((plan.hh, plan.ny * plan.small), bf16),
            pltpu.VMEM((plan.hh, plan.cells), f32),
            pltpu.VMEM((2, plan.hh + plan.midl - plan.midp, plan.cells), bf16),
            pltpu.VMEM((2, plan.hh, plan.cells), f32),
            pltpu.VMEM((2, plan.hh, plan.cells), bf16),
            pltpu.VMEM((2, LANES, LANES), f32),
            pltpu.VMEM((5, LANES, LANES), f32),
            pltpu.VMEM((2, plan.ll, plan.cells), f32),
            pltpu.VMEM((plan.ny * plan.ml, plan.cells), bf16),
            pltpu.VMEM((4, plan.nx, 3, plan.hh), f32),
            pltpu.VMEM((4, plan.ny, 3, plan.hh), f32),
            pltpu.SemaphoreType.DMA((4, n)),
            pltpu.SemaphoreType.DMA((4, n)),
            pltpu.SemaphoreType.DMA((8 + plan.ny,)),
            *reduce_scratch(plan, plan.frame),
        ],
        compiler_params=pltpu.CompilerParams(
            collective_id=6, has_side_effects=True, vmem_limit_bytes=60 * 1024 * 1024),
    )(*arrays)


def embed_kernel(plan, total_cells, *refs):
    (small_hbm, x_hbm, grad_ref, readout_ref, embed_out, small_out, row_out, block_out,
     x_ref, wide, tall, meet_send, meet_recv, load_sem, *rest) = refs
    half = len(rest) // 2
    small, embed = reduce_from(plan, plan.small, rest[:half]), reduce_from(plan, plan.frame, rest[half:])
    first = pltpu.make_async_copy(small_hbm, small.part, load_sem.at[0])
    second = pltpu.make_async_copy(x_hbm, x_ref, load_sem.at[1])
    first.start()
    second.start()
    peers = Meet.peers(plan)
    barrier = pltpu.get_barrier_semaphore()
    for device in peers:
        pl.semaphore_signal(barrier, inc=1, device_id=device, device_id_type=MESH)
    pl.semaphore_wait(barrier, len(peers))
    first.wait()
    small.start_twin()
    second.wait()
    factor = 1.0 / total_cells
    queue = small.items()

    def tick():
        if queue:
            queue.pop(0)()

    piece = plan.frame // 3 // LANES * LANES
    for j in range(plan.ny):
        start, stop = plan.frame_start[j], min(plan.frame_start[j] + plan.frame, plan.genes)
        for at in range(start, stop, piece):
            end = min(at + piece, stop)
            to = j * plan.frame + at - start
            embed.part[:, to:to + end - at] = over_cells(
                grad_ref[...], x_ref[at:end, :]).astype(jnp.bfloat16)
            tick()
        done = stop - start
        if done < plan.frame:
            inside = done // LANES * LANES
            lanes = lax.broadcasted_iota(jnp.int32, (plan.hh, LANES), 1)
            at = j * plan.frame + inside
            if inside < done:
                value = embed.part[:, at:at + LANES]
                embed.part[:, at:at + LANES] = jnp.where(
                    lanes < done - inside, value.astype(jnp.float32), 0.0).astype(jnp.bfloat16)
                inside += LANES
            for at in range(j * plan.frame + inside, (j + 1) * plan.frame, LANES):
                embed.part[:, at:at + LANES] = jnp.zeros((plan.hh, LANES), jnp.bfloat16)
        embed.twin_column(j)
        tick()
    todo = embed.items()
    first_items = max(len(todo) // 3, 1)
    for item in todo[:first_items]:
        item()
        tick()
    while queue:
        tick()
    small.own_sum(small_out, factor)
    meet = Meet(plan, wide, tall, meet_send, meet_recv)
    wide[meet.gx, :, 0:plan.frame] = readout_ref[...]
    wide[meet.gx, :, plan.frame:] = small_out[plan.h:plan.h + 1, plan.op:plan.op + plan.ml]
    tall[meet.gy] = small_out[:, plan.ol:plan.ol + plan.ll]
    copies = meet.copies(False) + meet.copies(True)
    for copy in copies:
        copy.start()
    for item in todo[first_items:]:
        item()
    for copy in copies:
        copy.wait_recv()
    row_out[...] = wide[0]
    block_out[...] = tall[0]
    embed.own_sum(embed_out, factor)
    for copy in copies:
        copy.wait_send()
    small.finish_sends()
    embed.finish_sends()


def embed_all_sums(plan, total_cells, *arrays):
    any_spec, vmem = pl.BlockSpec(memory_space=pl.ANY), pl.BlockSpec(memory_space=pltpu.VMEM)
    f32, bf16 = jnp.float32, jnp.bfloat16
    n = plan.nx + plan.ny - 2
    shape = jax.ShapeDtypeStruct
    row, block = (1, plan.frame + plan.ml), (plan.hp, plan.ll)
    return pl.pallas_call(
        functools.partial(embed_kernel, plan, total_cells),
        out_shape=[shape((plan.hp, plan.frame), f32), shape((plan.hp, plan.small), f32),
                   shape(row, f32), shape(block, f32)],
        in_specs=[any_spec] * 2 + [vmem] * 2,
        out_specs=[vmem] * 4,
        scratch_shapes=[
            pltpu.VMEM((plan.genes, plan.cells), bf16),
            pltpu.VMEM((plan.nx, *row), f32),
            pltpu.VMEM((plan.ny, *block), f32),
            pltpu.SemaphoreType.DMA((n,)),
            pltpu.SemaphoreType.DMA((n,)),
            pltpu.SemaphoreType.DMA((2,)),
            *reduce_scratch(plan, plan.small),
            *reduce_scratch(plan, plan.frame),
        ],
        compiler_params=pltpu.CompilerParams(
            collective_id=7, has_side_effects=True, vmem_limit_bytes=60 * 1024 * 1024),
    )(*arrays)


def output_kernel(plan, chunk, w_ref, layer_ref, x_ref, flag_ref, pick_ref,
                  out_ref, og_ref, part_ref, up_ref, loss_ref, raw_ref, slab_ref):
    i = pl.program_id(0)

    @pl.when(i == 0)
    def _():
        up_ref[...] = jnp.zeros_like(up_ref)
        loss_ref[...] = jnp.zeros_like(loss_ref)
    weight, layer = w_ref[...], layer_ref[0]
    raw_ref[...] = over_rows(weight, layer)
    slab_ref[...] = over_rows(flag_ref[...].astype(jnp.float32).astype(jnp.bfloat16), pick_ref[...])

    def rows_of(j, total):
        rows = aligned(j * 16, 16)
        raw = raw_ref[rows, :]
        out_ref[rows, :] = raw.astype(jnp.bfloat16)
        residual = raw - x_ref[rows, :].astype(jnp.float32)
        row = lax.broadcasted_iota(jnp.int32, raw.shape, 0) + (i * chunk + j * 16)
        weighted = jnp.where(row < plan.genes, slab_ref[rows, :] * residual, 0.0)
        og_ref[rows, :] = weighted.astype(jnp.bfloat16)
        terms = lane_sums(jnp.where(row < plan.genes, weighted * residual, 0.0))
        return total + terms[:8] + terms[8:]
    loss_ref[...] += lax.fori_loop(0, chunk // 16, rows_of, jnp.zeros((8, LANES), jnp.float32))
    grad = og_ref[...]
    part_ref[...] = over_cells(layer, grad).astype(jnp.bfloat16)
    up_ref[...] += rows_dot(weight, grad)


def output_all(plan, readout_all, layers, profiles, flags, picker):
    chunk = 4 * LANES
    steps = plan.gg // chunk
    f32, bf16 = jnp.float32, jnp.bfloat16
    shape = jax.ShapeDtypeStruct
    studies = flags.shape[0]
    return pl.pallas_call(
        functools.partial(output_kernel, plan, chunk),
        grid=(steps,),
        out_shape=[shape((plan.genes, plan.cells), bf16), shape((plan.gg, plan.cells), bf16),
                   shape((plan.hh, plan.gg), bf16), shape((plan.hh, plan.cells), f32),
                   shape((8, LANES), f32)],
        in_specs=[
            pl.BlockSpec((plan.hh, chunk), lambda i: (0, i)),
            pl.BlockSpec((1, plan.hh, plan.cells), lambda i: (3, 0, 0)),
            pl.BlockSpec((chunk, plan.cells), lambda i: (i, 0)),
            pl.BlockSpec((studies, chunk), lambda i: (0, i)),
            pl.BlockSpec((studies, plan.cells), lambda i: (0, 0))],
        out_specs=[
            pl.BlockSpec((chunk, plan.cells), lambda i: (i, 0)),
            pl.BlockSpec((chunk, plan.cells), lambda i: (i, 0)),
            pl.BlockSpec((plan.hh, chunk), lambda i: (0, i)),
            pl.BlockSpec((plan.hh, plan.cells), lambda i: (0, 0)),
            pl.BlockSpec((8, LANES), lambda i: (0, 0))],
        scratch_shapes=[pltpu.VMEM((chunk, plan.cells), f32), pltpu.VMEM((chunk, plan.cells), f32)],
        compiler_params=pltpu.CompilerParams(vmem_limit_bytes=48 * 1024 * 1024),
    )(readout_all, layers, profiles, flags, picker)


def input_kernel(w_ref, grad_ref, og_ref, out_ref):
    back = over_rows(w_ref[...], grad_ref[...])
    out_ref[...] = (back - og_ref[...].astype(jnp.float32)).astype(jnp.bfloat16)


def input_all(plan, embed_all, grad, output_grad):
    chunk = 4 * LANES
    return pl.pallas_call(
        input_kernel,
        grid=(plan.gg // chunk,),
        out_shape=jax.ShapeDtypeStruct((plan.genes, plan.cells), jnp.bfloat16),
        in_specs=[
            pl.BlockSpec((plan.hh, chunk), lambda i: (0, i)),
            pl.BlockSpec((plan.hh, plan.cells), lambda i: (0, 0)),
            pl.BlockSpec((chunk, plan.cells), lambda i: (i, 0))],
        out_specs=pl.BlockSpec((chunk, plan.cells), lambda i: (i, 0)),
        compiler_params=pltpu.CompilerParams(vmem_limit_bytes=48 * 1024 * 1024),
    )(embed_all, grad, output_grad)


def rows_dot(left, right):
    return lax.dot_general(left, right, (((1,), (0,)), ((), ())), preferred_element_type=jnp.float32)


def over_cells(left, right):
    return lax.dot_general(left, right, (((1,), (1,)), ((), ())), preferred_element_type=jnp.float32)


def over_rows(left, right):
    return lax.dot_general(left, right, (((0,), (0,)), ((), ())), preferred_element_type=jnp.float32)


def pad_to(value, rows, lanes):
    return jnp.pad(value, ((0, rows - value.shape[0]), (0, lanes - value.shape[1])))


def middle_piece(plan, matrix):
    turned = matrix.T.reshape(plan.h, plan.groups, plan.h)
    wide = jnp.pad(turned, ((0, plan.hp - plan.h), (0, 0), (0, plan.hp - plan.h)))
    return pad_to(wide.reshape(plan.hp, plan.midp), plan.hp, plan.midl)


def middle_back(plan, piece):
    cut = piece[:plan.h, :plan.midp].reshape(plan.h, plan.groups, plan.hp)[:, :, :plan.h]
    return cut.reshape(plan.h, plan.mid).T


def with_row(plan, block, row, first):
    spare = jnp.where(first, row, jnp.zeros_like(row))[None]
    return pad_to(jnp.concatenate([block, spare], axis=0), plan.hp, block.shape[1])


def on_device(
    nx, ny,
    transcript_profiles,
    experiment_labels,
    measured_flags,
    retained_unit_flags,
    standard_normal_draws,
    compressor_first_matrix,
    compressor_second_matrix,
    posterior_matrix,
    posterior_intercepts,
    expander_first_matrix,
    expander_second_matrix,
    output_matrix,
    output_intercept,
    normalizer_factors,
    normalizer_translations,
):
    cells = transcript_profiles.shape[0]
    plan = Plan(nx, ny, cells, output_matrix.shape[1], output_matrix.shape[0], expander_first_matrix.shape[0])
    total_cells = float(cells * nx * ny)
    gx, gy = lax.axis_index("gx"), lax.axis_index("gy")
    first = gx == 0

    wide = jnp.concatenate([
        pad_to(compressor_first_matrix.T, plan.hp, plan.g),
        with_row(plan, output_matrix, output_intercept, first)], axis=0)
    strip = lax.ppermute(wide[:, :plan.strip], "gy", [(j + 1, j) for j in range(ny - 1)])
    wide = jnp.concatenate([wide, strip], axis=1)
    wide = pad_to(wide, 2 * plan.hp, plan.gp + plan.strip + plan.shift * ny)
    wide = lax.dynamic_slice_in_dim(wide, gy * plan.shift, plan.gp, 1)
    norms = jnp.concatenate([normalizer_factors.T, normalizer_translations.T], axis=1)
    last = jnp.concatenate([expander_first_matrix.T, norms], axis=1)
    tile = jnp.where(gy == ny - 1, pad_to(norms, plan.hp, LANES), wide[:plan.hp, plan.gp - LANES:])
    first_piece = jnp.concatenate([wide[:plan.hp, :plan.gp - LANES], tile], axis=1)
    small = jnp.concatenate([
        middle_piece(plan, compressor_second_matrix),
        middle_piece(plan, expander_second_matrix),
        pad_to(with_row(plan, posterior_matrix, posterior_intercepts, first), plan.hp, plan.ml),
        pad_to(last, plan.hp, plan.ll)], axis=1)
    profiles = transcript_profiles.T
    draws = standard_normal_draws.T
    (embed_all, small_all, readout_all, center, log_var, sample, layers, scaled_values, keep_values,
     norm_rows) = forward_all(
        plan, total_cells, first_piece, small, wide[plan.hp:], profiles,
        jnp.swapaxes(retained_unit_flags, 1, 2), draws)
    picker = (jnp.arange(measured_flags.shape[0], dtype=jnp.int32)[:, None]
              == experiment_labels[None, :]).astype(jnp.bfloat16)
    output, output_grad, readout_part, upstream, losses = output_all(
        plan, readout_all, layers, profiles, measured_flags, picker)
    diverge = 0.5 * jnp.sum(jnp.exp(log_var) + center * center - 1.0 - log_var)
    own_loss = 0.5 * jnp.sum(losses) + kl_weight * diverge

    def frames(product):
        padded = pad_to(product, plan.hh, max(product.shape[1], max(plan.frame_start) + plan.frame))
        return jnp.concatenate(
            [padded[:, s:s + plan.frame] for s in plan.frame_start], axis=1).astype(jnp.bfloat16)

    if plan.fits:
        readout_sum, sums, small_part, grad_one = backward_all(
            plan, total_cells, readout_part, upstream, small_all, layers, scaled_values, keep_values,
            sample, norm_rows, jnp.full((1, plan.hh), own_loss), center, log_var, draws)
        loss_sum = sums[0, 2, 0]
        gains_sum, shifts_sum = [sums[k, 1] for k in range(4)], [sums[k, 0] for k in range(4)]
        embed_sum, small_sum, row, lifting_own = embed_all_sums(
            plan, total_cells, small_part, profiles, grad_one, readout_sum[plan.h:plan.h + 1])
    else:
        parts = small_all.reshape(plan.hh, ny, plan.small)
        encoder_all = parts[:, :, plan.o2:plan.o2 + plan.midp].reshape(plan.hh, plan.hh)
        decoder_all = parts[:, :, plan.o4:plan.o4 + plan.midp].reshape(plan.hh, plan.hh)
        projector_all = parts[:, :, plan.op:plan.op + plan.moments].reshape(plan.hh, 2 * plan.latent)
        lifting_all = parts[:, 0, plan.ol:plan.ol + plan.latent]
        rows = parts[:, 0, plan.ol + plan.latent:plan.ol + plan.latent + 8].astype(jnp.float32)
        gains = [rows[:, k:k + 1] for k in range(4)]
        biases = [rows[:, 4 + k:5 + k] for k in range(4)]

        spread = jnp.exp(0.5 * log_var)

        def kept_layer(k):
            inverse = lax.rsqrt(norm_rows[k, 1] / total_cells + norm_eps)[:, None]
            return layers[k], gains[k] * scaled_values[k] + biases[k], scaled_values[k], inverse

        one, two, three, four = (kept_layer(k) for k in range(4))

        def backward_layer(upstream, kept, k, loss, ident):
            _, normed, scaled, inverse = kept
            sigma = jax.nn.sigmoid(normed)
            slope = upstream * keep_values[k].astype(jnp.float32) * sigma * (
                1.0 + normed * (1.0 - sigma))
            pair = jnp.stack([jnp.sum(slope, axis=1), jnp.sum(slope * scaled, axis=1),
                              jnp.full((plan.hh,), loss)])
            merged = meet_all(plan, pair, merge_sums, 2)
            shift, gain = merged[0], merged[1]
            grad = gains[k] * inverse * (
                slope - (shift[:, None] + scaled * gain[:, None]) / total_cells)
            return grad.astype(jnp.bfloat16), gain, shift, merged[2, 0]

        grad_four, gain_four, shift_four, loss_sum = backward_layer(upstream, four, 3, own_loss, 5)
        upstream = over_rows(decoder_all, grad_four)
        grad_three, gain_three, shift_three, _ = backward_layer(upstream, three, 2, own_loss, 6)
        sample_grad = over_rows(lifting_all, grad_three)[:plan.latent]
        center_grad = sample_grad + kl_weight * center
        logvar_grad = sample_grad * 0.5 * spread * draws + kl_weight * 0.5 * (jnp.exp(log_var) - 1.0)
        moment_grad = jnp.concatenate([center_grad, logvar_grad], axis=0).astype(jnp.bfloat16)
        upstream = rows_dot(projector_all, moment_grad)
        grad_two, gain_two, shift_two, _ = backward_layer(upstream, two, 1, own_loss, 7)
        upstream = over_rows(encoder_all, grad_two)
        grad_one, gain_one, shift_one, _ = backward_layer(upstream, one, 0, own_loss, 8)
        gains_sum = [gain_one, gain_two, gain_three, gain_four]
        shifts_sum = [shift_one, shift_two, shift_three, shift_four]
        encoder_part = over_cells(grad_two, one[0]).reshape(plan.hh, ny, plan.midp)
        decoder_part = over_cells(grad_four, three[0]).reshape(plan.hh, ny, plan.midp)
        projector_part = over_cells(two[0], moment_grad).reshape(plan.hh, ny, plan.moments)
        lifting_part = over_cells(grad_three, sample)[:, :plan.latent]

        def lanes(value, width):
            return jnp.pad(value, ((0, 0), (0, 0), (0, width - value.shape[2])))

        small_part = jnp.concatenate([
            lanes(encoder_part, plan.midl), lanes(decoder_part, plan.midl),
            lanes(projector_part, plan.ml),
            jnp.broadcast_to(pad_to(lifting_part, plan.hh, plan.ll)[:, None, :], (plan.hh, ny, plan.ll)),
        ], axis=2).reshape(plan.hh, ny * plan.small).astype(jnp.bfloat16)
        embed_part = frames(over_cells(grad_one, profiles))

        readout_sum = reduce_all(plan, frames(readout_part), 1.0 / total_cells, 3)
        small_sum = reduce_all(plan, small_part, 1.0 / total_cells, 4)
        embed_sum = reduce_all(plan, embed_part, 1.0 / total_cells, 3)

        row, lifting_own = share_all(plan, jnp.concatenate([
            readout_sum[plan.h:plan.h + 1],
            small_sum[plan.h:plan.h + 1, plan.op:plan.op + plan.ml]], axis=1),
            small_sum[:, plan.ol:plan.ol + plan.ll], 5)
    input_grad = input_all(plan, embed_all, grad_one, output_grad)

    starts = jnp.array([plan.g * j - plan.frame_start[j] for j in range(ny)], jnp.int32)
    readout_own = lax.dynamic_slice_in_dim(readout_sum, starts[gy], plan.g, 1)
    embed_own = lax.dynamic_slice_in_dim(embed_sum, starts[gy], plan.g, 1)
    baseline_own = lax.dynamic_slice_in_dim(row[0, :plan.frame], starts[gy], plan.g, 0)

    def own_units(values):
        stack = jnp.stack(values, axis=0) / total_cells
        return lax.dynamic_slice_in_dim(stack, gx * plan.hp, plan.h, 1)

    small_h = small_sum[:plan.h]
    return (
        output.T,
        center.T,
        loss_sum / total_cells,
        input_grad.T,
        embed_own[:plan.h].T,
        middle_back(plan, small_sum[:, plan.o2:plan.o2 + plan.midl]),
        small_h[:, plan.op:plan.op + plan.moments],
        row[0, plan.frame:plan.frame + plan.moments],
        lifting_own[:plan.h, :plan.latent].T,
        middle_back(plan, small_sum[:, plan.o4:plan.o4 + plan.midl]),
        readout_own[:plan.h],
        baseline_own,
        own_units(gains_sum),
        own_units(shifts_sum),
    )


def solution(mesh):
    return jax.shard_map(
        functools.partial(on_device, mesh.shape["gx"], mesh.shape["gy"]),
        mesh=mesh,
        in_specs=(
            P(("gx", "gy"), None),
            P(("gx", "gy")),
            P(),
            P(None, ("gx", "gy"), None),
            P(("gx", "gy"), None),
            P("gy", "gx"),
            P("gy", "gx"),
            P("gx", "gy"),
            P("gy"),
            P(None, "gx"),
            P("gy", "gx"),
            P("gx", "gy"),
            P("gy"),
            P(None, "gx"),
            P(None, "gx"),
        ),
        out_specs=(
            P(("gx", "gy"), None),
            P(("gx", "gy"), None),
            P(),
            P(("gx", "gy"), None),
            P("gy", "gx"),
            P("gy", "gx"),
            P("gx", "gy"),
            P("gy"),
            P(None, "gx"),
            P("gy", "gx"),
            P("gx", "gy"),
            P("gy"),
            P(None, "gx"),
            P(None, "gx"),
        ),
        check_vma=False,
    )
```

```python
import functools

import jax
import jax.numpy as jnp
from jax import lax
from jax.experimental import pallas as pl
from jax.experimental.pallas import tpu as pltpu
from jax.sharding import PartitionSpec as P

norm_eps = 1e-05
keep_scale = 1.25
kl_weight = 5e-05
MESH = pl.DeviceIdType.MESH
LANES = 128


def round_up(value, multiple):
    return -(-value // multiple) * multiple


class Plan:
    def __init__(self, nx, ny, cells, genes_piece, hidden_piece, latent):
        self.nx, self.ny, self.cells = nx, ny, cells
        self.g, self.h, self.latent = genes_piece, hidden_piece, latent
        self.genes, self.hidden = genes_piece * ny, hidden_piece * nx
        self.hp = round_up(hidden_piece + 1, 16)
        self.hh = self.hp * nx
        tiles = round_up(self.genes, LANES) // LANES
        self.gp = round_up(tiles, ny) // ny * LANES
        self.gg = self.gp * ny
        self.shift = self.gp - self.g
        self.strip = round_up(self.shift * ny, LANES)
        starts = [self.g * j // LANES for j in range(ny)]
        ends = [round_up(self.g * (j + 1), LANES) // LANES for j in range(ny)]
        self.frame_start = [s * LANES for s in starts]
        self.frame = max(e - s for s, e in zip(starts, ends)) * LANES
        self.groups = nx // ny
        self.mid = self.hidden // ny
        self.midp = self.hp * self.groups
        self.midl = round_up(self.midp, LANES)
        self.moments = 2 * latent // ny
        self.ml = round_up(self.moments, LANES)
        self.ll = round_up(latent + 8, LANES)
        self.small = 2 * self.midl + self.ml + self.ll
        self.o2, self.o4 = 0, self.midl
        self.op, self.ol = 2 * self.midl, 2 * self.midl + self.ml
        self.blocks = nx * ny
        rows = round_up(self.hp * 2 // 3, 16)
        self.cuts = ((0, rows), (rows, self.hp - rows)) if rows < self.hp else ((0, rows),)
        self.whole_cuts = ((0, self.hp),)
        self.fits = self.blocks <= 32 and self.hh * ny * self.frame <= 7 * 1024 * 1024


class Flow:
    def __init__(self, plan, kind):
        gx, gy = lax.axis_index("gx"), lax.axis_index("gy")
        self.plan, self.gx, self.gy = plan, gx, gy
        self.sizes = (plan.ny // 2, plan.nx // 2, 2)
        self.core = lax.rem(gy, 2)
        self.at = (gy // 2, gx // 2, lax.rem(gx, 2))
        self.orders = (((0, 1, 2), (2, 1, 0)), ((1, 2, 0), (1, 0, 2)))[kind]
        first, second = self.orders
        self.most = tuple(max(self.sizes[i], self.sizes[j]) for i, j in zip(first, second))
        self.least = tuple(min(self.sizes[i], self.sizes[j]) for i, j in zip(first, second))
        self.limit = tuple(self.pick(self.sizes[i], self.sizes[j]) for i, j in zip(first, second))
        self.here = tuple(self.pick(self.at[i], self.at[j]) for i, j in zip(first, second))

    def pick(self, zero, one):
        if isinstance(zero, int) and isinstance(one, int) and zero == one:
            return zero
        return jnp.where(self.core == 0, zero, one)

    def device(self, spot):
        place = [None] * 3
        for axis in range(3):
            place[axis] = self.pick(
                spot[self.orders[0].index(axis)], spot[self.orders[1].index(axis)]
            )
        return (place[1] * 2 + place[2], place[0] * 2 + self.core)

    def twin(self):
        return (self.gx, self.gy + 1 - 2 * self.core)

    def step(self, axis, sign):
        to = self.here[axis] + sign
        spot = tuple(to if i == axis else self.here[i] for i in range(3))
        return jnp.logical_and(to >= 0, to < self.limit[axis]), self.device(spot)


def neighbours(plan):
    flow = Flow(plan, 0)
    out = [(None, flow.twin())]
    for axis in range(3):
        for sign in (-1, 1):
            out.append(flow.step(axis, sign))
    return out


def when(condition):
    return (lambda f: f()) if condition is None else pl.when(condition)


def greet(plan, extra=()):
    barrier = pltpu.get_barrier_semaphore()
    count = jnp.int32(len(extra))
    for there, device in neighbours(plan):
        @when(there)
        def _(device=device):
            pl.semaphore_signal(barrier, inc=1, device_id=device, device_id_type=MESH)
        count = count + (1 if there is None else there.astype(jnp.int32))
    for device in extra:
        pl.semaphore_signal(barrier, inc=1, device_id=device, device_id_type=MESH)
    pl.semaphore_wait(barrier, count)


class Gather:
    def __init__(self, plan, source, target, width, send_sem, recv_sem):
        self.plan, self.source, self.target, self.width = plan, source, target, width
        self.send_sem, self.recv_sem = send_sem, recv_sem
        self.cuts = [(Flow(plan, kind), *cut) for kind, cut in enumerate(plan.cuts)]
        self.phases = 1 + max(sum(m - 1 for m in cut[0].most) for cut in self.cuts)

    def slot(self, cut, gx, gy):
        _, start, rows = cut
        return self.target.at[
            pl.ds(pl.multiple_of(gx * self.plan.hp + start, 16), rows),
            pl.ds(pl.multiple_of(gy * self.width, LANES), self.width),
        ]

    def own_copy(self, sem):
        plan = self.plan
        gx, gy = lax.axis_index("gx"), lax.axis_index("gy")
        place = self.target.at[
            pl.ds(pl.multiple_of(gx * plan.hp, 16), plan.hp),
            pl.ds(pl.multiple_of(gy * self.width, LANES), self.width),
        ]
        return pltpu.make_async_copy(self.source, place, sem)

    def copies(self, kind, cut, spot, own):
        flow = cut[0]
        gx, gy = flow.device(spot)
        dst = self.slot(cut, gx, gy)
        src = self.source.at[pl.ds(cut[1], cut[2]), :] if own else dst
        index = gx * (self.plan.ny // 2) + gy // 2
        goals = [(None, flow.twin(), 6)]
        level = None
        for axis in (2, 1, 0):
            for sign in (-1, 1):
                if flow.most[axis] < 2:
                    continue
                there, device = flow.step(axis, sign)
                if not own:
                    there = there & ((flow.here[axis] - spot[axis]) * sign >= 0)
                    if level is not None:
                        there = there & level
                goals.append((there, device, 2 * axis + (sign + 1) // 2))
            same = spot[axis] == flow.here[axis]
            level = same if level is None else level & same
        out = []
        for there, device, k in goals:
            out.append((there, pltpu.make_async_remote_copy(
                src_ref=src, dst_ref=dst,
                send_sem=self.send_sem.at[kind, index, k],
                recv_sem=self.recv_sem.at[kind, gx * self.plan.ny + gy],
                device_id=device, device_id_type=MESH,
            )))
        return out

    def arrived(self, kind, cut, gx, gy):
        ref = self.slot(cut, gx, gy)
        pltpu.make_async_copy(ref, ref, self.recv_sem.at[kind, gx * self.plan.ny + gy]).wait()

    def start_own(self):
        for kind, cut in enumerate(self.cuts):
            for there, copy in self.copies(kind, cut, cut[0].here, True):
                when(there)(copy.start)

    def walk(self, visit, phase=None, only=None, part=(0, 1)):
        for kind, cut in enumerate(self.cuts):
            if only is not None and kind != only:
                continue
            flow = cut[0]
            mp, mq, mr = flow.most
            total = mp * mq * mr

            def one(n, _, kind=kind, cut=cut, flow=flow):
                spot = (lax.rem(n, mp), lax.rem(n // mp, mq), n // (mp * mq))
                hops, good = 0, None
                for here, limit, at in zip(flow.here, flow.limit, spot):
                    hops = hops + jnp.abs(at - here)
                    good = at < limit if good is None else good & (at < limit)
                good = good & ((hops > 0) if phase is None else (hops == phase))
                pl.when(good)(functools.partial(visit, kind, cut, spot))
                return 0
            lax.fori_loop(total * part[0] // part[1], total * (part[0] + 1) // part[1], one, 0)

    def visit(self, kind, cut, spot):
        self.arrived(kind, cut, *cut[0].device(spot))
        for there, copy in self.copies(kind, cut, spot, False):
            when(there)(copy.start)

    def forward(self, phase):
        if phase < self.phases:
            self.walk(self.visit, phase)

    def items(self, parts):
        return [functools.partial(self.walk, self.visit, phase, kind, (i, parts))
                for phase in range(1, self.phases) for i in range(parts)
                for kind in range(len(self.cuts))]

    def finish_twin(self):
        plan = self.plan
        for kind, cut in enumerate(self.cuts):
            flow = cut[0]
            def one(n, _, kind=kind, cut=cut, flow=flow):
                gx, y = n // (plan.ny // 2), lax.rem(n, plan.ny // 2)
                self.arrived(kind, cut, gx, 2 * y + 1 - flow.core)
                return 0
            lax.fori_loop(0, plan.blocks // 2, one, 0)

    def finish_sends(self):
        for kind, cut in enumerate(self.cuts):
            for there, copy in self.copies(kind, cut, cut[0].here, True):
                when(there)(copy.wait_send)
        def visit(kind, cut, spot):
            for there, copy in self.copies(kind, cut, spot, False):
                when(there)(copy.wait_send)
        self.walk(visit)


class Meet:
    def __init__(self, plan, wide, tall, send_sem, recv_sem):
        self.plan, self.wide, self.tall = plan, wide, tall
        self.send_sem, self.recv_sem = send_sem, recv_sem
        self.gx, self.gy = lax.axis_index("gx"), lax.axis_index("gy")

    @staticmethod
    def peers(plan):
        gx, gy = lax.axis_index("gx"), lax.axis_index("gy")
        return ([(lax.rem(gx + k, plan.nx), gy) for k in range(1, plan.nx)]
                + [(gx, lax.rem(gy + k, plan.ny)) for k in range(1, plan.ny)])

    def copies(self, second):
        plan = self.plan
        n = plan.ny if second else plan.nx
        ref = self.tall if second else self.wide
        own = self.gy if second else self.gx
        out = []
        for k in range(1, n):
            to = lax.rem(own + k, n)
            at = (plan.nx - 1 if second else 0) + k - 1
            out.append(pltpu.make_async_remote_copy(
                src_ref=ref.at[own], dst_ref=ref.at[own],
                send_sem=self.send_sem.at[at], recv_sem=self.recv_sem.at[at],
                device_id=(self.gx, to) if second else (to, self.gy), device_id_type=MESH,
            ))
        return out

    def run(self, value, merge, members, between=None):
        plan = self.plan
        for second in (False, True):
            ref = self.tall if second else self.wide
            ref[self.gy if second else self.gx] = value
            copies = self.copies(second)
            for copy in copies:
                copy.start()
            if between is not None:
                between(second)
            for copy in copies:
                copy.wait_recv()
            value = merge([ref[i] for i in range(ref.shape[0])], members)
            members = members * plan.nx
            for copy in copies:
                copy.wait_send()
        return value


def merge_sums(parts, members):
    total = parts[0]
    for part in parts[1:]:
        total = total + part
    return total


def merge_moments(parts, members):
    n = len(parts)
    mean = merge_sums([part[0:1] for part in parts], 0) / n
    squares = merge_sums([part[1:2] for part in parts], 0)
    between = merge_sums([(part[0:1] - mean) * (part[0:1] - mean) for part in parts], 0)
    return jnp.concatenate([mean, squares + members * between], axis=0)


def tiled(column, plan):
    return jnp.concatenate([column] * (plan.cells // LANES), axis=1)


def lane_sums(value):
    total = value[:, :LANES]
    for at in range(LANES, value.shape[1], LANES):
        total = total + value[:, at:at + LANES]
    return total


def as_row(value):
    return jnp.sum(value.T, axis=0, keepdims=True)


def as_column(row):
    return jnp.broadcast_to(row, (LANES, LANES)).T


def aligned(start, rows=LANES):
    return pl.ds(pl.multiple_of(start, rows), rows)


def moment_rows(plan, h_ref, row_ref):
    def block(i, _):
        value = h_ref[aligned(i * LANES), :]
        sums = lane_sums(value)
        mean = jnp.sum(sums, axis=1, keepdims=True) / plan.cells
        offset = value - mean
        row_ref[0:1, aligned(i * LANES)] = as_row(sums) / plan.cells
        row_ref[1:2, aligned(i * LANES)] = as_row(lane_sums(offset * offset))
        return 0
    lax.fori_loop(0, plan.hh // LANES, block, 0)


def unit_column(slab_ref, i, at):
    slab = slab_ref[aligned(i * LANES), :]
    return jnp.broadcast_to(slab.astype(jnp.float32)[:, at:at + 1], (LANES, LANES))


def activate(plan, k, h_ref, row_ref, slab_ref, keep_ref, out_ref, column_ref, total_cells, spare,
             tick=lambda: None):
    def block(i, _):
        column_ref[0] = as_column(row_ref[0:1, aligned(i * LANES)])
        column_ref[1] = as_column(lax.rsqrt(row_ref[1:2, aligned(i * LANES)] / total_cells + norm_eps))
        column_ref[2] = unit_column(slab_ref, i, k)
        column_ref[3] = unit_column(slab_ref, i, 4 + k)

        def chunk(j, _):
            rows = aligned(i * LANES + j * 16, 16)
            mean, inverse, gain, bias = (
                tiled(column_ref[n, aligned(j * 16, 16), :], plan) for n in range(4))
            scaled = (h_ref[rows, :] - mean) * inverse
            h_ref[rows, :] = scaled
            normed = gain * scaled + bias
            active = normed * jax.nn.sigmoid(normed) * keep_ref[k, rows, :].astype(jnp.float32)
            if spare:
                row = lax.broadcasted_iota(jnp.int32, active.shape, 0) + (i * LANES + j * 16)
                active = jnp.where(lax.rem(row, plan.hp) == plan.h, 1.0, active)
            out_ref[rows, :] = active.astype(jnp.bfloat16)
            return 0
        lax.fori_loop(0, LANES // 16, chunk, 0)
        return 0
    cut = plan.hh // LANES // 2
    lax.fori_loop(0, cut, block, 0)
    tick()
    lax.fori_loop(cut, plan.hh // LANES, block, 0)


def keep_rows(plan, flags_ref, keep_ref, k):
    def lane(t, _):
        lanes = aligned(t * LANES)
        for group in range(plan.nx):
            for start in range(0, plan.hp, 16):
                at = group * plan.h + start
                value = flags_ref[at:at + 16, lanes].astype(jnp.float32) * keep_scale
                if start + 16 > plan.h:
                    row = lax.broadcasted_iota(jnp.int32, value.shape, 0)
                    value = jnp.where(row < plan.h - start, value, 0.0)
                at = group * plan.hp + start
                keep_ref[k, at:at + 16, lanes] = value.astype(jnp.bfloat16)
        return 0
    lax.fori_loop(0, plan.cells // LANES, lane, 0)


def forward_kernel(plan, total_cells, *refs):
    (w1, wsmall, wout, x_hbm, flags_hbm, draws_ref,
     embed_all, small_out, readout_all, center_out, log_var_out, sample_out, layers_out, scaled_out,
     keep_out, rows_out,
     w1_ref, small_ref, x_ref, keep_ref, flags_ref, h_ref, layer_ref, column_ref, latent_ref,
     wide, tall, send_sem, recv_sem, meet_send, meet_recv, own_sem, load_sem, flag_sem, out_sem) = refs
    mid = plan.midp
    load = pltpu.make_async_copy(x_hbm, x_ref, load_sem)
    deep = flags_ref.shape[0]

    def flags(k):
        return pltpu.make_async_copy(
            flags_hbm.at[k], flags_ref.at[k % deep, pl.ds(0, plan.hidden), :], flag_sem.at[k % deep])

    for k in range(deep):
        flags(k).start()
    load.start()
    sets = send_sem.shape[0]
    embed, small, readout = (
        Gather(plan, source, target, width, send_sem.at[u % sets], recv_sem.at[u])
        for u, (source, target, width) in enumerate((
            (w1, w1_ref, plan.gp), (wsmall, small_ref, plan.small), (wout, readout_all, plan.gp))))
    own = [g.own_copy(own_sem.at[u]) for u, g in enumerate((embed, small, readout))]
    for copy in own:
        copy.start()
    peers = Meet.peers(plan)
    barrier = pltpu.get_barrier_semaphore()
    for device in peers:
        pl.semaphore_signal(barrier, inc=1, device_id=device, device_id_type=MESH)
    pl.semaphore_wait(barrier, len(peers))

    def keepers(k):
        flags(k).wait()
        keep_rows(plan, flags_ref.at[k % deep], keep_ref, k)
        if k + deep < 4:
            flags(k + deep).start()

    embed.start_own()
    late = embed.phases - 2
    for phase in range(1, embed.phases):
        if phase <= 4:
            keepers(phase - 1)
        if phase == late:
            if sets == 1:
                pass
            else:
                small.start_own()
        embed.forward(phase)
    for k in range(embed.phases - 1, 4):
        keepers(k)
    if sets == 1:
        embed.finish_sends()
        small.start_own()
    load.wait()
    tail = layer_ref.shape[1] - plan.hh
    slots = layer_ref.shape[0]
    for k in range(slots):
        if tail:
            layer_ref[k, plan.hh:, :] = jnp.zeros((tail, plan.cells), jnp.bfloat16)
    latent_ref[...] = jnp.zeros_like(latent_ref)
    latent_ref[2, 0:plan.latent, :] = draws_ref[...]
    own[0].wait()
    embed.finish_twin()
    outs = [pltpu.make_async_copy(w1_ref, embed_all, out_sem.at[0])]
    outs[0].start()

    queue = [] if sets == 1 else small.items(2)
    marks = {}
    if sets > 1:
        queue.insert(5, readout.start_own)
        marks["small"] = len(queue)
        queue += readout.items(2)
    total = len(queue)

    def tick(count=1):
        for _ in range(count):
            if queue:
                queue.pop(0)()

    half_rows = plan.hh // 2
    for j in range(plan.ny):
        start, stop = j * plan.gp, min((j + 1) * plan.gp, plan.genes)
        for top in (0, half_rows):
            part = rows_dot(w1_ref[top:top + half_rows, start:stop], x_ref[start:stop, :])
            spot = pl.ds(top, half_rows)
            h_ref[0, spot, :] = part if j == 0 else h_ref[0, spot, :] + part
            tick()

    layer_writes = []

    def norm(k, spare):
        h = h_ref.at[k % 2]
        tick()
        moment_rows(plan, h, rows_out.at[k])
        meet = Meet(plan, wide.at[k], tall.at[k], meet_send.at[k], meet_recv.at[k])
        rows_out[k] = meet.run(rows_out[k], merge_moments, float(plan.cells), lambda second: tick(2))
        slab = w1_ref.at[:, pl.ds(plan.gg - LANES, LANES)]
        if k >= slots:
            finish(layer_writes[k - slots])
        activate(plan, k, h, rows_out.at[k], slab, keep_ref, layer_ref.at[k % slots], column_ref,
                 total_cells, spare, tick)
        for n, (source, target) in enumerate((
                (h, scaled_out.at[k]),
                (layer_ref.at[k % slots, pl.ds(0, plan.hh), :], layers_out.at[k]),
                (keep_ref.at[k], keep_out.at[k]))):
            outs.append(pltpu.make_async_copy(source, target, out_sem.at[3 + 3 * k + n]))
            outs[-1].start()
        layer_writes.append(outs[-2])
        return outs[-3]

    def finish(copy):
        copy.wait()
        outs[:] = [other for other in outs if other is not copy]

    def whole_small():
        if sets > 1:
            while total - len(queue) < marks["small"]:
                tick()
        else:
            for item in small.items(1):
                item()
        own[1].wait()
        small.finish_twin()
        if sets == 1:
            small.finish_sends()
            readout.start_own()
            queue.extend(readout.items(1))
        outs.append(pltpu.make_async_copy(small_ref, small_out, out_sem.at[1]))
        outs[-1].start()
        own[2].wait()

    def hidden(source, lane, target):
        for j in range(plan.ny):
            at = j * plan.small + lane
            part = rows_dot(small_ref[:, at:at + plan.midl], source[mid * j:mid * j + plan.midl, :])
            target[...] = part if j == 0 else target[...] + part
            if j % 2:
                tick()

    wrote_one = norm(0, False)
    whole_small()
    hidden(layer_ref.at[0], plan.o2, h_ref.at[1])
    wrote_two = norm(1, True)
    half = plan.ny // 2
    for j in range(plan.ny):
        at = j * plan.small + plan.op
        part = over_rows(small_ref[:, at:at + plan.ml], layer_ref[1, 0:plan.hh, :])
        spot = (j % half) * plan.moments
        latent_ref[j // half, spot:spot + plan.moments, :] = part[:plan.moments]
    center, log_var = latent_ref[0], latent_ref[1]
    sample = center + jnp.exp(0.5 * log_var) * latent_ref[2]
    row = lax.broadcasted_iota(jnp.int32, sample.shape, 0)
    sample_out[...] = jnp.where(row < plan.latent, sample, 0.0).astype(jnp.bfloat16)
    center_out[...] = latent_ref[0, 0:plan.latent, :]
    log_var_out[...] = latent_ref[1, 0:plan.latent, :]
    finish(wrote_one)
    h_ref[0] = rows_dot(small_ref[:, plan.ol:plan.ol + plan.ll], sample_out[...])
    norm(2, False)
    finish(wrote_two)
    hidden(layer_ref.at[2 % slots], plan.o4, h_ref.at[1])
    norm(3, True)
    while queue:
        tick()
    readout.finish_twin()
    if sets > 1:
        embed.finish_sends()
        small.finish_sends()
    readout.finish_sends()
    for copy in outs:
        copy.wait()


def forward_all(plan, total_cells, w1, wsmall, wout, profiles, flags, draws):
    any_spec, vmem = pl.BlockSpec(memory_space=pl.ANY), pl.BlockSpec(memory_space=pltpu.VMEM)
    f32, bf16 = jnp.float32, jnp.bfloat16
    n = plan.nx + plan.ny - 2
    cuts = len(plan.cuts)
    sets = 3 if plan.blocks <= 32 else 1
    shape = jax.ShapeDtypeStruct
    return pl.pallas_call(
        functools.partial(forward_kernel, plan, total_cells),
        out_shape=[
            shape((plan.hh, plan.gg), bf16), shape((plan.hh, plan.ny * plan.small), bf16),
            shape((plan.hh, plan.gg), bf16), shape((plan.latent, plan.cells), f32),
            shape((plan.latent, plan.cells), f32), shape((plan.ll, plan.cells), bf16),
            shape((4, plan.hh, plan.cells), bf16), shape((4, plan.hh, plan.cells), f32),
            shape((4, plan.hh, plan.cells), bf16), shape((4, 2, plan.hh), f32)],
        in_specs=[any_spec] * 5 + [vmem],
        out_specs=[any_spec] * 3 + [vmem] * 3 + [any_spec] * 3 + [vmem],
        scratch_shapes=[
            pltpu.VMEM((plan.hh, plan.gg), bf16),
            pltpu.VMEM((plan.hh, plan.ny * plan.small), bf16),
            pltpu.VMEM((plan.genes, plan.cells), bf16),
            pltpu.VMEM((4, plan.hh, plan.cells), bf16),
            pltpu.VMEM((2 if sets > 1 else 1, plan.hidden + 16, plan.cells), jnp.int32),
            pltpu.VMEM((2, plan.hh, plan.cells), f32),
            pltpu.VMEM((4 if sets > 1 else 2, plan.hh + plan.midl - plan.midp, plan.cells), bf16),
            pltpu.VMEM((4, LANES, LANES), f32),
            pltpu.VMEM((3, plan.ll, plan.cells), f32),
            pltpu.VMEM((4, plan.nx, 2, plan.hh), f32),
            pltpu.VMEM((4, plan.ny, 2, plan.hh), f32),
            pltpu.SemaphoreType.DMA((sets, cuts, plan.blocks // 2, 7)),
            pltpu.SemaphoreType.DMA((3, cuts, plan.blocks)),
            pltpu.SemaphoreType.DMA((4, n)),
            pltpu.SemaphoreType.DMA((4, n)),
            pltpu.SemaphoreType.DMA((3,)),
            pltpu.SemaphoreType.DMA,
            pltpu.SemaphoreType.DMA((2,)),
            pltpu.SemaphoreType.DMA((15,)),
        ],
        compiler_params=pltpu.CompilerParams(
            collective_id=0, has_side_effects=True, vmem_limit_bytes=60 * 1024 * 1024),
    )(w1, wsmall, wout, profiles, flags, draws)


def meet_kernel(plan, merge, x_ref, o_ref, wide, tall, send_sem, recv_sem):
    peers = Meet.peers(plan)
    barrier = pltpu.get_barrier_semaphore()
    for device in peers:
        pl.semaphore_signal(barrier, inc=1, device_id=device, device_id_type=MESH)
    pl.semaphore_wait(barrier, len(peers))
    meet = Meet(plan, wide, tall, send_sem, recv_sem)
    o_ref[...] = meet.run(x_ref[...], merge, float(plan.cells))


def meet_all(plan, value, merge, collective_id):
    rows, width = value.shape
    n = plan.nx + plan.ny - 2
    return pl.pallas_call(
        functools.partial(meet_kernel, plan, merge),
        out_shape=jax.ShapeDtypeStruct(value.shape, jnp.float32),
        in_specs=[pl.BlockSpec(memory_space=pltpu.VMEM)],
        out_specs=pl.BlockSpec(memory_space=pltpu.VMEM),
        scratch_shapes=[
            pltpu.VMEM((plan.nx, rows, width), jnp.float32),
            pltpu.VMEM((plan.ny, rows, width), jnp.float32),
            pltpu.SemaphoreType.DMA((n,)),
            pltpu.SemaphoreType.DMA((n,)),
        ],
        compiler_params=pltpu.CompilerParams(collective_id=collective_id, has_side_effects=True),
    )(value)


def share_kernel(plan, row_ref, block_ref, row_out, block_out, wide, tall, send_sem, recv_sem):
    peers = Meet.peers(plan)
    barrier = pltpu.get_barrier_semaphore()
    for device in peers:
        pl.semaphore_signal(barrier, inc=1, device_id=device, device_id_type=MESH)
    pl.semaphore_wait(barrier, len(peers))
    meet = Meet(plan, wide, tall, send_sem, recv_sem)
    wide[meet.gx] = row_ref[...]
    tall[meet.gy] = block_ref[...]
    copies = meet.copies(False) + meet.copies(True)
    for copy in copies:
        copy.start()
    for copy in copies:
        copy.wait_recv()
    row_out[...] = wide[0]
    block_out[...] = tall[0]
    for copy in copies:
        copy.wait_send()


def share_all(plan, row, block, collective_id):
    n = plan.nx + plan.ny - 2
    return pl.pallas_call(
        functools.partial(share_kernel, plan),
        out_shape=[jax.ShapeDtypeStruct(row.shape, jnp.float32),
                   jax.ShapeDtypeStruct(block.shape, jnp.float32)],
        in_specs=[pl.BlockSpec(memory_space=pltpu.VMEM)] * 2,
        out_specs=[pl.BlockSpec(memory_space=pltpu.VMEM)] * 2,
        scratch_shapes=[
            pltpu.VMEM((plan.nx, *row.shape), jnp.float32),
            pltpu.VMEM((plan.ny, *block.shape), jnp.float32),
            pltpu.SemaphoreType.DMA((n,)),
            pltpu.SemaphoreType.DMA((n,)),
        ],
        compiler_params=pltpu.CompilerParams(collective_id=collective_id, has_side_effects=True),
    )(row, block)


class Reduce:
    def __init__(self, plan, width, part, twin, slots, send_sem, twin_sem, recv_sem, flow=0):
        self.first = flow
        self.plan, self.width, self.part, self.twin, self.slots = plan, width, part, twin, slots
        self.send_sem, self.twin_sem, self.recv_sem = send_sem, twin_sem, recv_sem
        self.cuts = [(Flow(plan, flow), *cut) for cut in plan.whole_cuts]

    @staticmethod
    def slot_counts(plan, flow):
        counts = []
        for kind in (flow,):
            sizes = (plan.ny // 2, plan.nx // 2, 2)
            first, second = (((0, 1, 2), (2, 1, 0)), ((1, 2, 0), (1, 0, 2)))[kind]
            mp, mq, mr = (max(sizes[i], sizes[j]) for i, j in zip(first, second))
            a, b, c = (Reduce.sides(m) for m in (mp, mq, mr))
            far_r = (mr > 2) * (mr * mq * mp)
            counts.append((far_r, mq * mp * (c + (mq > 2)), mp * (c + b + (mp > 2)), c + b + a))
        return counts

    @staticmethod
    def sides(most):
        return 1 if most == 2 else (2 if most > 2 else 0)

    def block(self, ref, cut, gx, gy):
        return ref.at[
            pl.ds(pl.multiple_of(gx * self.plan.hp + cut[1], 16), cut[2]),
            pl.ds(pl.multiple_of(gy * self.width, LANES), self.width),
        ]

    def twin_block(self, cut, gx, y):
        return self.twin.at[
            pl.ds(pl.multiple_of(gx * self.plan.hp + cut[1], 16), cut[2]),
            pl.ds(pl.multiple_of(y * self.width, LANES), self.width),
        ]

    def twin_copy(self, kind, cut, gx, y):
        flow = cut[0]
        return pltpu.make_async_remote_copy(
            src_ref=self.block(self.part, cut, gx, 2 * y + 1 - flow.core),
            dst_ref=self.twin_block(cut, gx, y),
            send_sem=self.twin_sem.at[0, kind, gx * (self.plan.ny // 2) + y],
            recv_sem=self.twin_sem.at[1, kind, gx * (self.plan.ny // 2) + y],
            device_id=flow.twin(), device_id_type=MESH,
        )

    def each_twin(self, visit, ys=None):
        ny2 = self.plan.ny // 2
        a, na = self.cuts[0][0].at[1], self.plan.nx // 2

        def along(n, _):
            to = a + (na - 1 - n // 2) * (1 - 2 * lax.rem(n, 2))

            @pl.when((to >= 0) & (to < na))
            def _():
                for kind, cut in enumerate(self.cuts):
                    def one(i, _, kind=kind, cut=cut):
                        visit(self.twin_copy(kind, cut, to * 2 + i // ny2, lax.rem(i, ny2)))
                        return 0
                    lax.fori_loop(0, 2 * ny2, one, 0)
            return 0
        lax.fori_loop(0, 2 * na - 1, along, 0)

    def start_twin(self):
        self.each_twin(lambda copy: copy.start())

    def entry(self, kind, stage, spot, axis, came_from):
        flow = self.cuts[kind][0]
        mp, mq, mr = flow.most
        far_r, far_q, far_p, _ = Reduce.slot_counts(self.plan, self.first)[kind]
        sides = [Reduce.sides(m) for m in flow.most]
        dp, dq, dr = spot
        if stage == 2:
            return (dr * mq + dq) * mp + dp
        if stage == 1:
            base, which = far_r, (dq * mp + dp) * (sides[2] + (mq > 2))
        elif stage == 0:
            base, which = far_r + far_q, dp * (sides[2] + sides[1] + (mp > 2))
        else:
            base, which = far_r + far_q + far_p, 0
        offset = 0
        for later in (2, 1, 0):
            if later == stage:
                return base + which + offset
            if later == axis:
                side = 0 if sides[axis] == 1 else (came_from + 1) // 2
                return base + which + offset + side
            offset += sides[later]

    def slot(self, kind, index):
        cut = self.cuts[kind]
        total = sum(Reduce.slot_counts(self.plan, self.first)[kind])
        return self.slots[kind].at[index], self.recv_sem[kind].at[index]

    def gather_terms(self, kind, cut, spot, stage, sign):
        flow = cut[0]
        ny2 = self.plan.ny // 2
        gx, gy = flow.device(spot)
        y = gy // 2
        copy = self.twin_copy(kind, cut, gx, y)
        copy.wait_recv()
        own = self.block(self.part, cut, gx, gy)
        twin = self.twin_block(cut, gx, y)
        arrivals = []
        for axis in (2, 1, 0):
            if axis > stage:
                for side in (-1, 1):
                    there, _ = flow.step(axis, side)
                    if flow.most[axis] < 2:
                        continue
                    arrivals.append((there, self.entry(kind, stage, spot, axis, side)))
            elif axis == stage and flow.most[axis] > 2:
                away = self.here_away(flow, axis, sign)
                arrivals.append((away, self.entry(kind, stage, spot, axis, None)))
        return own, twin, arrivals

    def here_away(self, flow, axis, sign):
        to = flow.here[axis] - sign
        return (to >= 0) & (to < flow.limit[axis])

    def add_in(self, kind, cut, spot, stage, sign):
        own, twin, arrivals = self.gather_terms(kind, cut, spot, stage, sign)

        def add(other):
            def chunk(i, _):
                rows = aligned(i * 16, 16)
                own[rows, :] = own[rows, :] + other[rows, :]
                return 0
            lax.fori_loop(0, cut[2] // 16, chunk, 0)

        add(twin)
        for there, index in arrivals:
            slot, sem = self.slot(kind, index)
            @when(there)
            def _(slot=slot, sem=sem):
                pltpu.make_async_copy(slot, slot, sem).wait()
                add(slot)
        return own

    def onward(self, kind, cut, spot, stage, sign):
        flow = cut[0]
        _, device = self.toward(flow, stage, sign)
        gx, gy = flow.device(spot)
        to = flow.here[stage] + sign
        index_same = self.entry(kind, stage, spot, stage, None) if flow.most[stage] > 2 else None
        done = to == spot[stage]
        p_same = flow.here[0] == spot[0]
        q_same = flow.here[1] == spot[1]
        if stage == 2:
            deeper = jnp.where(q_same, jnp.where(p_same,
                               self.entry(kind, -1, spot, 2, -sign),
                               self.entry(kind, 0, spot, 2, -sign)),
                               self.entry(kind, 1, spot, 2, -sign))
        elif stage == 1:
            deeper = jnp.where(p_same, self.entry(kind, -1, spot, 1, -sign),
                               self.entry(kind, 0, spot, 1, -sign))
        else:
            deeper = self.entry(kind, -1, spot, 0, -sign)
        index = deeper if index_same is None else jnp.where(done, deeper, index_same)
        slot, sem = self.slot(kind, index)
        ny2 = self.plan.ny // 2
        return pltpu.make_async_remote_copy(
            src_ref=self.block(self.part, cut, gx, gy), dst_ref=slot,
            send_sem=self.send_sem.at[kind, gx * ny2 + gy // 2], recv_sem=sem,
            device_id=device, device_id_type=MESH,
        )

    def toward(self, flow, axis, sign):
        return flow.step(axis, sign)

    def order(self, kind):
        mp, mq, mr = self.cuts[kind][0].most
        out = [(2, k, far) for k in range(mr - 1, 0, -1) for far in range(mq - 1, -1, -1)]
        return out + [(stage, k, 0) for stage in (1, 0)
                      for k in range(self.cuts[kind][0].most[stage] - 1, 0, -1)]

    def walk(self, visit, kind, stage, k, far):
        cut = self.cuts[kind]
        p, q, r = cut[0].here
        np_, nq, nr = cut[0].limit
        mp, mq, mr = cut[0].most

        def one(n, _):
            dp = p + (mp - 1 - n // 2) * (1 - 2 * lax.rem(n, 2))
            for sign in (-1, 1):
                if stage == 2:
                    d = r + sign * k
                    for side in ((-1, 1) if far else (1,)):
                        dq = q + side * far
                        good = ((d >= 0) & (d < nr) & (dq >= 0) & (dq < nq)
                                & (dp >= 0) & (dp < np_))
                        pl.when(good)(functools.partial(visit, kind, cut, (dp, dq, d), stage, sign))
                    continue
                if stage == 1:
                    d = q + sign * k
                    spot, good = (dp, d, r), (d >= 0) & (d < nq) & (dp >= 0) & (dp < np_)
                else:
                    d = p + sign * k
                    spot, good = (d, q, r), (d >= 0) & (d < np_)
                pl.when(good)(functools.partial(visit, kind, cut, spot, stage, sign))
            return 0
        lax.fori_loop(0, 1 if stage == 0 else 2 * mp - 1, one, 0)

    def visit(self, kind, cut, spot, stage, sign):
        self.add_in(kind, cut, spot, stage, sign)
        self.onward(kind, cut, spot, stage, sign).start()

    def items(self):
        lines = [[functools.partial(self.walk, self.visit, kind, *step) for step in self.order(kind)]
                 for kind in range(len(self.cuts))]
        out = []
        for i in range(max(len(line) for line in lines)):
            out += [line[i] for line in lines if i < len(line)]
        return out

    def own_sum(self, out_ref, factor):
        for kind, cut in enumerate(self.cuts):
            flow = cut[0]
            own = self.add_in(kind, cut, flow.here, -1, None)
            out_ref[pl.ds(cut[1], cut[2]), :] = own[...].astype(jnp.float32) * factor

    def finish_sends(self):
        self.each_twin(lambda copy: copy.wait_send())
        def visit(kind, cut, spot, stage, sign):
            self.onward(kind, cut, spot, stage, sign).wait_send()
        for kind in range(len(self.cuts)):
            for step in self.order(kind):
                self.walk(visit, kind, *step)

    def twin_column(self, gy):
        y, flow = gy // 2, self.cuts[0][0]

        @pl.when(gy % 2 != flow.core)
        def _():
            for kind, cut in enumerate(self.cuts):
                def one(gx, _, kind=kind, cut=cut):
                    self.twin_copy(kind, cut, gx, y).start()
                    return 0
                lax.fori_loop(0, self.plan.nx, one, 0)


def reduce_scratch(plan, width, flow=0):
    counts = [sum(c) for c in Reduce.slot_counts(plan, flow)]
    return [
        pltpu.VMEM((plan.hh, plan.ny * width), jnp.bfloat16),
        pltpu.VMEM((plan.hh, plan.ny // 2 * width), jnp.bfloat16),
        *[pltpu.VMEM((c, cut[1], width), jnp.bfloat16) for c, cut in zip(counts, plan.whole_cuts)],
        pltpu.SemaphoreType.DMA((len(plan.whole_cuts), plan.blocks // 2)),
        pltpu.SemaphoreType.DMA((2, len(plan.whole_cuts), plan.blocks // 2)),
        *[pltpu.SemaphoreType.DMA((c,)) for c in counts],
    ]


def reduce_from(plan, width, refs, flow=0):
    n = len(plan.whole_cuts)
    part, twin, slots, sems, recv = refs[0], refs[1], refs[2:2 + n], refs[2 + n:4 + n], refs[4 + n:]
    return Reduce(plan, width, part, twin, slots, *sems, recv, flow)


def reduce_kernel(plan, width, factor, x_ref, o_ref, *rest):
    reduce = reduce_from(plan, width, rest[:-1])
    load = pltpu.make_async_copy(x_ref, reduce.part, rest[-1])
    load.start()
    greet(plan)
    load.wait()
    reduce.start_twin()
    for item in reduce.items():
        item()
    reduce.own_sum(o_ref, factor)
    reduce.finish_sends()


def reduce_all(plan, value, factor, collective_id):
    width = value.shape[1] // plan.ny
    return pl.pallas_call(
        functools.partial(reduce_kernel, plan, width, factor),
        out_shape=jax.ShapeDtypeStruct((plan.hp, width), jnp.float32),
        in_specs=[pl.BlockSpec(memory_space=pl.ANY)],
        out_specs=pl.BlockSpec(memory_space=pltpu.VMEM),
        scratch_shapes=[*reduce_scratch(plan, width), pltpu.SemaphoreType.DMA],
        compiler_params=pltpu.CompilerParams(
            collective_id=collective_id, has_side_effects=True, vmem_limit_bytes=60 * 1024 * 1024),
    )(value)


def backward_kernel(plan, total_cells, *refs):
    (part_hbm, up_hbm, small_hbm, layers_hbm, scaled_hbm, keep_hbm, sample_ref, rows_ref, loss_ref,
     center_ref, log_var_ref, draws_ref,
     readout_out, sums_out, small_part, grad_ref,
     small_ref, up_ref, layer_ref, scaled_ref, keep_ref, lane_ref, column_ref, latent_ref,
     moment_ref, wide, tall, meet_send, meet_recv, load_sem, *rest) = refs
    reduce = reduce_from(plan, plan.frame, rest)

    def load(k):
        slot = k % 2
        return (
            pltpu.make_async_copy(scaled_hbm.at[k], scaled_ref.at[slot], load_sem.at[3 * slot]),
            pltpu.make_async_copy(keep_hbm.at[k], keep_ref.at[slot], load_sem.at[3 * slot + 1]),
        )

    def load_layer(k):
        return pltpu.make_async_copy(
            layers_hbm.at[k], layer_ref.at[k % 2, pl.ds(0, plan.hh), :], load_sem.at[3 * (k % 2) + 2])

    frames = [pltpu.make_async_copy(
        part_hbm.at[:, pl.ds(start, plan.frame)],
        reduce.part.at[:, pl.ds(j * plan.frame, plan.frame)], load_sem.at[6 + j])
        for j, start in enumerate(plan.frame_start)]
    second = pltpu.make_async_copy(up_hbm, up_ref, load_sem.at[6 + plan.ny])
    third = pltpu.make_async_copy(small_hbm, small_ref, load_sem.at[7 + plan.ny])
    for copy in frames:
        copy.start()
    second.start()
    for copy in load(3):
        copy.start()
    third.start()
    load_layer(2).start()
    for copy in load(2):
        copy.start()
    load_layer(1).start()
    peers = Meet.peers(plan)
    barrier = pltpu.get_barrier_semaphore()
    for device in peers:
        pl.semaphore_signal(barrier, inc=1, device_id=device, device_id_type=MESH)
    pl.semaphore_wait(barrier, len(peers))
    for copy in frames:
        copy.wait()
    reduce.start_twin()
    tail = layer_ref.shape[1] - plan.hh
    if tail:
        for k in range(2):
            layer_ref[k, plan.hh:, :] = jnp.zeros((tail, plan.cells), jnp.bfloat16)
    latent_ref[...] = jnp.zeros_like(latent_ref)

    todo = reduce.items()
    todo.append(lambda: reduce.own_sum(readout_out, 1.0 / total_cells))

    def between(second):
        if todo:
            todo.pop(0)()

    def layer(k):
        slot = k % 2
        for copy in load(k):
            copy.wait()

        def columns(i):
            slab = small_ref.at[:, pl.ds(plan.ol + plan.ll - LANES, LANES)]
            base = plan.latent - (plan.ll - LANES)
            column_ref[0] = unit_column(slab, i, base + k)
            column_ref[1] = unit_column(slab, i, base + 4 + k)
            column_ref[2] = as_column(
                lax.rsqrt(rows_ref[k, 1:2, aligned(i * LANES)] / total_cells + norm_eps))

        def block(i, _):
            columns(i)

            def chunk(j, _):
                rows = aligned(i * LANES + j * 16, 16)
                here = aligned(j * 16, 16)
                gain, bias = tiled(column_ref[0, here, :], plan), tiled(column_ref[1, here, :], plan)
                scaled = scaled_ref[slot, rows, :]
                normed = gain * scaled + bias
                sigma = jax.nn.sigmoid(normed)
                slope = up_ref[rows, :] * keep_ref[slot, rows, :].astype(jnp.float32) * sigma * (
                    1.0 + normed * (1.0 - sigma))
                up_ref[rows, :] = slope
                lane_ref[0, here, :] = lane_sums(slope)
                lane_ref[1, here, :] = lane_sums(slope * scaled)
                return 0
            lax.fori_loop(0, LANES // 16, chunk, 0)
            sums_out[k, 0:1, aligned(i * LANES)] = as_row(lane_ref[0])
            sums_out[k, 1:2, aligned(i * LANES)] = as_row(lane_ref[1])
            return 0
        lax.fori_loop(0, plan.hh // LANES, block, 0)
        between(None)
        sums_out[k, 2:3, :] = loss_ref[...]
        meet = Meet(plan, wide.at[k], tall.at[k], meet_send.at[k], meet_recv.at[k])
        sums_out[k] = meet.run(sums_out[k], merge_sums, 1.0, between)

        def last(i, _):
            columns(i)
            column_ref[3] = as_column(sums_out[k, 0:1, aligned(i * LANES)] / total_cells)
            column_ref[4] = as_column(sums_out[k, 1:2, aligned(i * LANES)] / total_cells)

            def chunk(j, _):
                rows = aligned(i * LANES + j * 16, 16)
                here = aligned(j * 16, 16)
                factor = tiled(column_ref[0, here, :] * column_ref[2, here, :], plan)
                shift, gain = tiled(column_ref[3, here, :], plan), tiled(column_ref[4, here, :], plan)
                grad = factor * (up_ref[rows, :] - (shift + scaled_ref[slot, rows, :] * gain))
                grad_ref[rows, :] = grad.astype(jnp.bfloat16)
                return 0
            lax.fori_loop(0, LANES // 16, chunk, 0)
            return 0
        lax.fori_loop(0, plan.hh // LANES, last, 0)
        if k >= 2:
            for copy in load(k - 2):
                copy.start()

    def put(j, lane, value):
        at = j * plan.small + lane
        small_part[:, at:at + value.shape[1]] = value.astype(jnp.bfloat16)

    def middle(source, lane):
        for j in range(plan.ny):
            at, row = j * plan.small + lane, j * plan.midp
            put(j, lane, over_cells(grad_ref[...], source[row:row + plan.midl, :]))
            if j % 2:
                between(None)
            up_ref[row:row + plan.midp, :] = over_rows(
                small_ref[:, at:at + plan.midl], grad_ref[...])[:plan.midp]

    second.wait()
    third.wait()
    layer(3)
    load_layer(2).wait()
    middle(layer_ref.at[0], plan.o4)
    load_layer(0).start()
    layer(2)
    lifting = over_cells(grad_ref[...], sample_ref[...])
    for j in range(plan.ny):
        put(j, plan.ol, lifting)
    reach = over_rows(small_ref[:, plan.ol:plan.ol + plan.ll], grad_ref[...])[:plan.latent]
    center, log_var = center_ref[...], log_var_ref[...]
    latent_ref[0, 0:plan.latent, :] = reach + kl_weight * center
    latent_ref[1, 0:plan.latent, :] = (
        reach * 0.5 * jnp.exp(0.5 * log_var) * draws_ref[...]
        + kl_weight * 0.5 * (jnp.exp(log_var) - 1.0))
    half, tall_rows = plan.ny // 2, round_up(plan.moments, 16)
    moment_ref[...] = jnp.zeros_like(moment_ref)
    for j in range(plan.ny):
        spot = (j % half) * plan.moments
        piece = latent_ref[j // half, spot:spot + tall_rows, :]
        row = lax.broadcasted_iota(jnp.int32, piece.shape, 0)
        piece = jnp.where(row < plan.moments, piece, 0.0)
        moment_ref[j * plan.ml:j * plan.ml + tall_rows, :] = piece.astype(jnp.bfloat16)
    load_layer(1).wait()
    for j in range(plan.ny):
        at, row = j * plan.small + plan.op, j * plan.ml
        moments = moment_ref[row:row + plan.ml, :]
        put(j, plan.op, over_cells(layer_ref[1, 0:plan.hh, :], moments))
        part = rows_dot(small_ref[:, at:at + plan.ml], moments)
        up_ref[...] = part if j == 0 else up_ref[...] + part
    layer(1)
    load_layer(0).wait()
    middle(layer_ref.at[0], plan.o2)
    layer(0)
    while todo:
        between(False)
    reduce.finish_sends()


def backward_all(plan, total_cells, *arrays):
    any_spec, vmem = pl.BlockSpec(memory_space=pl.ANY), pl.BlockSpec(memory_space=pltpu.VMEM)
    f32, bf16 = jnp.float32, jnp.bfloat16
    n = plan.nx + plan.ny - 2
    shape = jax.ShapeDtypeStruct
    return pl.pallas_call(
        functools.partial(backward_kernel, plan, total_cells),
        out_shape=[
            shape((plan.hp, plan.frame), f32), shape((4, 3, plan.hh), f32),
            shape((plan.hh, plan.ny * plan.small), bf16), shape((plan.hh, plan.cells), bf16)],
        in_specs=[any_spec] * 6 + [vmem] * 6,
        out_specs=[vmem] * 4,
        scratch_shapes=[
            pltpu.VMEM((plan.hh, plan.ny * plan.small), bf16),
            pltpu.VMEM((plan.hh, plan.cells), f32),
            pltpu.VMEM((2, plan.hh + plan.midl - plan.midp, plan.cells), bf16),
            pltpu.VMEM((2, plan.hh, plan.cells), f32),
            pltpu.VMEM((2, plan.hh, plan.cells), bf16),
            pltpu.VMEM((2, LANES, LANES), f32),
            pltpu.VMEM((5, LANES, LANES), f32),
            pltpu.VMEM((2, plan.ll, plan.cells), f32),
            pltpu.VMEM((plan.ny * plan.ml, plan.cells), bf16),
            pltpu.VMEM((4, plan.nx, 3, plan.hh), f32),
            pltpu.VMEM((4, plan.ny, 3, plan.hh), f32),
            pltpu.SemaphoreType.DMA((4, n)),
            pltpu.SemaphoreType.DMA((4, n)),
            pltpu.SemaphoreType.DMA((8 + plan.ny,)),
            *reduce_scratch(plan, plan.frame),
        ],
        compiler_params=pltpu.CompilerParams(
            collective_id=6, has_side_effects=True, vmem_limit_bytes=60 * 1024 * 1024),
    )(*arrays)


def embed_kernel(plan, total_cells, *refs):
    (small_hbm, x_hbm, grad_ref, readout_ref, embed_out, small_out, row_out, block_out,
     x_ref, wide, tall, meet_send, meet_recv, load_sem, *rest) = refs
    half = len(rest) // 2
    small = reduce_from(plan, plan.small, rest[:half])
    embed = reduce_from(plan, plan.frame, rest[half:])
    first = pltpu.make_async_copy(small_hbm, small.part, load_sem.at[0])
    second = pltpu.make_async_copy(x_hbm, x_ref, load_sem.at[1])
    first.start()
    second.start()
    peers = Meet.peers(plan)
    barrier = pltpu.get_barrier_semaphore()
    for device in peers:
        pl.semaphore_signal(barrier, inc=1, device_id=device, device_id_type=MESH)
    pl.semaphore_wait(barrier, len(peers))
    first.wait()
    small.start_twin()
    second.wait()
    factor = 1.0 / total_cells
    queue = small.items()

    def tick():
        if queue:
            queue.pop(0)()

    piece = plan.frame // 3 // LANES * LANES
    for j in range(plan.ny):
        start, stop = plan.frame_start[j], min(plan.frame_start[j] + plan.frame, plan.genes)
        for at in range(start, stop, piece):
            end = min(at + piece, stop)
            to = j * plan.frame + at - start
            embed.part[:, to:to + end - at] = over_cells(
                grad_ref[...], x_ref[at:end, :]).astype(jnp.bfloat16)
            tick()
        done = stop - start
        if done < plan.frame:
            inside = done // LANES * LANES
            lanes = lax.broadcasted_iota(jnp.int32, (plan.hh, LANES), 1)
            at = j * plan.frame + inside
            if inside < done:
                value = embed.part[:, at:at + LANES]
                embed.part[:, at:at + LANES] = jnp.where(
                    lanes < done - inside, value.astype(jnp.float32), 0.0).astype(jnp.bfloat16)
                inside += LANES
            for at in range(j * plan.frame + inside, (j + 1) * plan.frame, LANES):
                embed.part[:, at:at + LANES] = jnp.zeros((plan.hh, LANES), jnp.bfloat16)
        embed.twin_column(j)
        tick()
    todo = embed.items()
    first_items = 4
    for item in todo[:first_items]:
        item()
    while queue:
        tick()
    small.own_sum(small_out, factor)
    meet = Meet(plan, wide, tall, meet_send, meet_recv)
    wide[meet.gx, :, 0:plan.frame] = readout_ref[...]
    wide[meet.gx, :, plan.frame:] = small_out[plan.h:plan.h + 1, plan.op:plan.op + plan.ml]
    tall[meet.gy] = small_out[:, plan.ol:plan.ol + plan.ll]
    copies = meet.copies(False) + meet.copies(True)
    for copy in copies:
        copy.start()
    for item in todo[first_items:]:
        item()
    for copy in copies:
        copy.wait_recv()
    row_out[...] = wide[0]
    block_out[...] = tall[0]
    embed.own_sum(embed_out, factor)
    for copy in copies:
        copy.wait_send()
    small.finish_sends()
    embed.finish_sends()


def embed_all_sums(plan, total_cells, *arrays):
    any_spec, vmem = pl.BlockSpec(memory_space=pl.ANY), pl.BlockSpec(memory_space=pltpu.VMEM)
    f32, bf16 = jnp.float32, jnp.bfloat16
    n = plan.nx + plan.ny - 2
    shape = jax.ShapeDtypeStruct
    row, block = (1, plan.frame + plan.ml), (plan.hp, plan.ll)
    return pl.pallas_call(
        functools.partial(embed_kernel, plan, total_cells),
        out_shape=[shape((plan.hp, plan.frame), f32), shape((plan.hp, plan.small), f32),
                   shape(row, f32), shape(block, f32)],
        in_specs=[any_spec] * 2 + [vmem] * 2,
        out_specs=[vmem] * 4,
        scratch_shapes=[
            pltpu.VMEM((plan.genes, plan.cells), bf16),
            pltpu.VMEM((plan.nx, *row), f32),
            pltpu.VMEM((plan.ny, *block), f32),
            pltpu.SemaphoreType.DMA((n,)),
            pltpu.SemaphoreType.DMA((n,)),
            pltpu.SemaphoreType.DMA((2,)),
            *reduce_scratch(plan, plan.small),
            *reduce_scratch(plan, plan.frame),
        ],
        compiler_params=pltpu.CompilerParams(
            collective_id=7, has_side_effects=True, vmem_limit_bytes=60 * 1024 * 1024),
    )(*arrays)


def output_kernel(plan, chunk, w_ref, layer_ref, x_ref, flag_ref, pick_ref,
                  out_ref, og_ref, part_ref, up_ref, loss_ref):
    i = pl.program_id(0)

    @pl.when(i == 0)
    def _():
        up_ref[...] = jnp.zeros_like(up_ref)
        loss_ref[...] = jnp.zeros_like(loss_ref)
    weight, layer = w_ref[...], layer_ref[0]
    raw = over_rows(weight, layer)
    slab = over_rows(flag_ref[...].astype(jnp.float32).astype(jnp.bfloat16), pick_ref[...])
    out_ref[...] = raw.astype(jnp.bfloat16)
    residual = raw - x_ref[...].astype(jnp.float32)
    inside = lax.broadcasted_iota(jnp.int32, raw.shape, 0) + i * chunk < plan.genes
    weighted = jnp.where(inside, slab * residual, 0.0)
    grad = weighted.astype(jnp.bfloat16)
    og_ref[...] = grad
    terms = lane_sums(jnp.where(inside, weighted * residual, 0.0))
    loss_ref[...] += jnp.sum(terms.reshape(chunk // 8, 8, LANES), axis=0)
    part_ref[...] = over_cells(layer, grad).astype(jnp.bfloat16)
    up_ref[...] += rows_dot(weight, grad)


def output_all(plan, readout_all, layers, profiles, flags, picker):
    chunk = 4 * LANES
    steps = plan.gg // chunk
    f32, bf16 = jnp.float32, jnp.bfloat16
    shape = jax.ShapeDtypeStruct
    studies = flags.shape[0]
    return pl.pallas_call(
        functools.partial(output_kernel, plan, chunk),
        grid=(steps,),
        out_shape=[shape((plan.genes, plan.cells), bf16), shape((plan.gg, plan.cells), bf16),
                   shape((plan.hh, plan.gg), bf16), shape((plan.hh, plan.cells), f32),
                   shape((8, LANES), f32)],
        in_specs=[
            pl.BlockSpec((plan.hh, chunk), lambda i: (0, i)),
            pl.BlockSpec((1, plan.hh, plan.cells), lambda i: (3, 0, 0)),
            pl.BlockSpec((chunk, plan.cells), lambda i: (i, 0)),
            pl.BlockSpec((studies, chunk), lambda i: (0, i)),
            pl.BlockSpec((studies, plan.cells), lambda i: (0, 0))],
        out_specs=[
            pl.BlockSpec((chunk, plan.cells), lambda i: (i, 0)),
            pl.BlockSpec((chunk, plan.cells), lambda i: (i, 0)),
            pl.BlockSpec((plan.hh, chunk), lambda i: (0, i)),
            pl.BlockSpec((plan.hh, plan.cells), lambda i: (0, 0)),
            pl.BlockSpec((8, LANES), lambda i: (0, 0))],
        compiler_params=pltpu.CompilerParams(vmem_limit_bytes=48 * 1024 * 1024),
    )(readout_all, layers, profiles, flags, picker)


def input_kernel(w_ref, grad_ref, og_ref, out_ref):
    back = over_rows(w_ref[...], grad_ref[...])
    out_ref[...] = (back - og_ref[...].astype(jnp.float32)).astype(jnp.bfloat16)


def input_all(plan, embed_all, grad, output_grad):
    chunk = 14 * LANES
    return pl.pallas_call(
        input_kernel,
        grid=(plan.gg // chunk,),
        out_shape=jax.ShapeDtypeStruct((plan.genes, plan.cells), jnp.bfloat16),
        in_specs=[
            pl.BlockSpec((plan.hh, chunk), lambda i: (0, i)),
            pl.BlockSpec((plan.hh, plan.cells), lambda i: (0, 0)),
            pl.BlockSpec((chunk, plan.cells), lambda i: (i, 0))],
        out_specs=pl.BlockSpec((chunk, plan.cells), lambda i: (i, 0)),
        compiler_params=pltpu.CompilerParams(vmem_limit_bytes=48 * 1024 * 1024),
    )(embed_all, grad, output_grad)


def rows_dot(left, right):
    return lax.dot_general(left, right, (((1,), (0,)), ((), ())), preferred_element_type=jnp.float32)


def over_cells(left, right):
    return lax.dot_general(left, right, (((1,), (1,)), ((), ())), preferred_element_type=jnp.float32)


def over_rows(left, right):
    return lax.dot_general(left, right, (((0,), (0,)), ((), ())), preferred_element_type=jnp.float32)


def pad_to(value, rows, lanes):
    return jnp.pad(value, ((0, rows - value.shape[0]), (0, lanes - value.shape[1])))


def middle_piece(plan, matrix):
    turned = matrix.T.reshape(plan.h, plan.groups, plan.h)
    wide = jnp.pad(turned, ((0, plan.hp - plan.h), (0, 0), (0, plan.hp - plan.h)))
    return pad_to(wide.reshape(plan.hp, plan.midp), plan.hp, plan.midl)


def middle_back(plan, piece):
    cut = piece[:plan.h, :plan.midp].reshape(plan.h, plan.groups, plan.hp)[:, :, :plan.h]
    return cut.reshape(plan.h, plan.mid).T


def with_row(plan, block, row, first):
    spare = jnp.where(first, row, jnp.zeros_like(row))[None]
    return pad_to(jnp.concatenate([block, spare], axis=0), plan.hp, block.shape[1])


def on_device(
    nx, ny,
    transcript_profiles,
    experiment_labels,
    measured_flags,
    retained_unit_flags,
    standard_normal_draws,
    compressor_first_matrix,
    compressor_second_matrix,
    posterior_matrix,
    posterior_intercepts,
    expander_first_matrix,
    expander_second_matrix,
    output_matrix,
    output_intercept,
    normalizer_factors,
    normalizer_translations,
):
    cells = transcript_profiles.shape[0]
    plan = Plan(nx, ny, cells, output_matrix.shape[1], output_matrix.shape[0], expander_first_matrix.shape[0])
    total_cells = float(cells * nx * ny)
    gx, gy = lax.axis_index("gx"), lax.axis_index("gy")
    first = gx == 0

    wide = jnp.concatenate([
        pad_to(compressor_first_matrix.T, plan.hp, plan.g),
        with_row(plan, output_matrix, output_intercept, first)], axis=0)
    strip = lax.ppermute(wide[:, :plan.strip], "gy", [(j + 1, j) for j in range(ny - 1)])
    wide = jnp.concatenate([wide, strip], axis=1)
    wide = pad_to(wide, 2 * plan.hp, plan.gp + plan.strip + plan.shift * ny)
    wide = lax.dynamic_slice_in_dim(wide, gy * plan.shift, plan.gp, 1)
    norms = jnp.concatenate([normalizer_factors.T, normalizer_translations.T], axis=1)
    last = jnp.concatenate([expander_first_matrix.T, norms], axis=1)
    tile = jnp.where(gy == ny - 1, pad_to(norms, plan.hp, LANES), wide[:plan.hp, plan.gp - LANES:])
    first_piece = jnp.concatenate([wide[:plan.hp, :plan.gp - LANES], tile], axis=1)
    small = jnp.concatenate([
        middle_piece(plan, compressor_second_matrix),
        middle_piece(plan, expander_second_matrix),
        pad_to(with_row(plan, posterior_matrix, posterior_intercepts, first), plan.hp, plan.ml),
        pad_to(last, plan.hp, plan.ll)], axis=1)
    profiles = transcript_profiles.T
    draws = standard_normal_draws.T
    (embed_all, small_all, readout_all, center, log_var, sample, layers, scaled_values, keep_values,
     norm_rows) = forward_all(
        plan, total_cells, first_piece, small, wide[plan.hp:], profiles,
        jnp.swapaxes(retained_unit_flags, 1, 2), draws)
    picker = (jnp.arange(measured_flags.shape[0], dtype=jnp.int32)[:, None]
              == experiment_labels[None, :]).astype(jnp.bfloat16)
    output, output_grad, readout_part, upstream, losses = output_all(
        plan, readout_all, layers, profiles, measured_flags, picker)
    diverge = 0.5 * jnp.sum(jnp.exp(log_var) + center * center - 1.0 - log_var)
    own_loss = 0.5 * jnp.sum(losses) + kl_weight * diverge

    def frames(product):
        padded = pad_to(product, plan.hh, max(product.shape[1], max(plan.frame_start) + plan.frame))
        return jnp.concatenate(
            [padded[:, s:s + plan.frame] for s in plan.frame_start], axis=1).astype(jnp.bfloat16)

    if plan.fits:
        readout_sum, sums, small_part, grad_one = backward_all(
            plan, total_cells, readout_part, upstream, small_all, layers, scaled_values, keep_values,
            sample, norm_rows, jnp.full((1, plan.hh), own_loss), center, log_var, draws)
        loss_sum = sums[0, 2, 0]
        gains_sum, shifts_sum = [sums[k, 1] for k in range(4)], [sums[k, 0] for k in range(4)]
        embed_sum, small_sum, row, lifting_own = embed_all_sums(
            plan, total_cells, small_part, profiles, grad_one, readout_sum[plan.h:plan.h + 1])
    else:
        parts = small_all.reshape(plan.hh, ny, plan.small)
        encoder_all = parts[:, :, plan.o2:plan.o2 + plan.midp].reshape(plan.hh, plan.hh)
        decoder_all = parts[:, :, plan.o4:plan.o4 + plan.midp].reshape(plan.hh, plan.hh)
        projector_all = parts[:, :, plan.op:plan.op + plan.moments].reshape(plan.hh, 2 * plan.latent)
        lifting_all = parts[:, 0, plan.ol:plan.ol + plan.latent]
        rows = parts[:, 0, plan.ol + plan.latent:plan.ol + plan.latent + 8].astype(jnp.float32)
        gains = [rows[:, k:k + 1] for k in range(4)]
        biases = [rows[:, 4 + k:5 + k] for k in range(4)]

        spread = jnp.exp(0.5 * log_var)

        def kept_layer(k):
            inverse = lax.rsqrt(norm_rows[k, 1] / total_cells + norm_eps)[:, None]
            return layers[k], gains[k] * scaled_values[k] + biases[k], scaled_values[k], inverse

        one, two, three, four = (kept_layer(k) for k in range(4))

        def backward_layer(upstream, kept, k, loss, ident):
            _, normed, scaled, inverse = kept
            sigma = jax.nn.sigmoid(normed)
            slope = upstream * keep_values[k].astype(jnp.float32) * sigma * (
                1.0 + normed * (1.0 - sigma))
            pair = jnp.stack([jnp.sum(slope, axis=1), jnp.sum(slope * scaled, axis=1),
                              jnp.full((plan.hh,), loss)])
            merged = meet_all(plan, pair, merge_sums, 2)
            shift, gain = merged[0], merged[1]
            grad = gains[k] * inverse * (
                slope - (shift[:, None] + scaled * gain[:, None]) / total_cells)
            return grad.astype(jnp.bfloat16), gain, shift, merged[2, 0]

        grad_four, gain_four, shift_four, loss_sum = backward_layer(upstream, four, 3, own_loss, 5)
        upstream = over_rows(decoder_all, grad_four)
        grad_three, gain_three, shift_three, _ = backward_layer(upstream, three, 2, own_loss, 6)
        sample_grad = over_rows(lifting_all, grad_three)[:plan.latent]
        center_grad = sample_grad + kl_weight * center
        logvar_grad = sample_grad * 0.5 * spread * draws + kl_weight * 0.5 * (jnp.exp(log_var) - 1.0)
        moment_grad = jnp.concatenate([center_grad, logvar_grad], axis=0).astype(jnp.bfloat16)
        upstream = rows_dot(projector_all, moment_grad)
        grad_two, gain_two, shift_two, _ = backward_layer(upstream, two, 1, own_loss, 7)
        upstream = over_rows(encoder_all, grad_two)
        grad_one, gain_one, shift_one, _ = backward_layer(upstream, one, 0, own_loss, 8)
        gains_sum = [gain_one, gain_two, gain_three, gain_four]
        shifts_sum = [shift_one, shift_two, shift_three, shift_four]
        encoder_part = over_cells(grad_two, one[0]).reshape(plan.hh, ny, plan.midp)
        decoder_part = over_cells(grad_four, three[0]).reshape(plan.hh, ny, plan.midp)
        projector_part = over_cells(two[0], moment_grad).reshape(plan.hh, ny, plan.moments)
        lifting_part = over_cells(grad_three, sample)[:, :plan.latent]

        def lanes(value, width):
            return jnp.pad(value, ((0, 0), (0, 0), (0, width - value.shape[2])))

        small_part = jnp.concatenate([
            lanes(encoder_part, plan.midl), lanes(decoder_part, plan.midl),
            lanes(projector_part, plan.ml),
            jnp.broadcast_to(pad_to(lifting_part, plan.hh, plan.ll)[:, None, :], (plan.hh, ny, plan.ll)),
        ], axis=2).reshape(plan.hh, ny * plan.small).astype(jnp.bfloat16)
        embed_part = frames(over_cells(grad_one, profiles))

        readout_sum = reduce_all(plan, frames(readout_part), 1.0 / total_cells, 3)
        small_sum = reduce_all(plan, small_part, 1.0 / total_cells, 4)
        embed_sum = reduce_all(plan, embed_part, 1.0 / total_cells, 3)

        row, lifting_own = share_all(plan, jnp.concatenate([
            readout_sum[plan.h:plan.h + 1],
            small_sum[plan.h:plan.h + 1, plan.op:plan.op + plan.ml]], axis=1),
            small_sum[:, plan.ol:plan.ol + plan.ll], 5)
    input_grad = input_all(plan, embed_all, grad_one, output_grad)

    starts = jnp.array([plan.g * j - plan.frame_start[j] for j in range(ny)], jnp.int32)
    readout_own = lax.dynamic_slice_in_dim(readout_sum, starts[gy], plan.g, 1)
    embed_own = lax.dynamic_slice_in_dim(embed_sum, starts[gy], plan.g, 1)
    baseline_own = lax.dynamic_slice_in_dim(row[0, :plan.frame], starts[gy], plan.g, 0)

    def own_units(values):
        stack = jnp.stack(values, axis=0) / total_cells
        return lax.dynamic_slice_in_dim(stack, gx * plan.hp, plan.h, 1)

    small_h = small_sum[:plan.h]
    return (
        output.T,
        center.T,
        loss_sum / total_cells,
        input_grad.T,
        embed_own[:plan.h].T,
        middle_back(plan, small_sum[:, plan.o2:plan.o2 + plan.midl]),
        small_h[:, plan.op:plan.op + plan.moments],
        row[0, plan.frame:plan.frame + plan.moments],
        lifting_own[:plan.h, :plan.latent].T,
        middle_back(plan, small_sum[:, plan.o4:plan.o4 + plan.midl]),
        readout_own[:plan.h],
        baseline_own,
        own_units(gains_sum),
        own_units(shifts_sum),
    )


def solution(mesh):
    return jax.shard_map(
        functools.partial(on_device, mesh.shape["gx"], mesh.shape["gy"]),
        mesh=mesh,
        in_specs=(
            P(("gx", "gy"), None),
            P(("gx", "gy")),
            P(),
            P(None, ("gx", "gy"), None),
            P(("gx", "gy"), None),
            P("gy", "gx"),
            P("gy", "gx"),
            P("gx", "gy"),
            P("gy"),
            P(None, "gx"),
            P("gy", "gx"),
            P("gx", "gy"),
            P("gy"),
            P(None, "gx"),
            P(None, "gx"),
        ),
        out_specs=(
            P(("gx", "gy"), None),
            P(("gx", "gy"), None),
            P(),
            P(("gx", "gy"), None),
            P("gy", "gx"),
            P("gy", "gx"),
            P("gx", "gy"),
            P("gy"),
            P(None, "gx"),
            P("gy", "gx"),
            P("gx", "gy"),
            P("gy"),
            P(None, "gx"),
            P(None, "gx"),
        ),
        check_vma=False,
    )
```

```python
import functools

import jax
import jax.numpy as jnp
from jax import lax
from jax.experimental import pallas as pl
from jax.experimental.pallas import tpu as pltpu
from jax.sharding import PartitionSpec as P

norm_eps = 1e-05
keep_scale = 1.25
kl_weight = 5e-05
MESH = pl.DeviceIdType.MESH
LANES = 128


def round_up(value, multiple):
    return -(-value // multiple) * multiple


class Plan:
    def __init__(self, nx, ny, cells, genes_piece, hidden_piece, latent):
        self.nx, self.ny, self.cells = nx, ny, cells
        self.g, self.h, self.latent = genes_piece, hidden_piece, latent
        self.genes, self.hidden = genes_piece * ny, hidden_piece * nx
        self.hp = round_up(hidden_piece + 1, 16)
        self.hh = self.hp * nx
        tiles = round_up(self.genes, LANES) // LANES
        self.gp = round_up(tiles, ny) // ny * LANES
        self.gg = self.gp * ny
        self.shift = self.gp - self.g
        self.strip = round_up(self.shift * ny, LANES)
        starts = [self.g * j // LANES for j in range(ny)]
        ends = [round_up(self.g * (j + 1), LANES) // LANES for j in range(ny)]
        self.frame_start = [s * LANES for s in starts]
        self.frame = max(e - s for s, e in zip(starts, ends)) * LANES
        self.groups = nx // ny
        self.mid = self.hidden // ny
        self.midp = self.hp * self.groups
        self.midl = round_up(self.midp, LANES)
        self.moments = 2 * latent // ny
        self.ml = round_up(self.moments, LANES)
        self.ll = round_up(latent + 8, LANES)
        self.small = 2 * self.midl + self.ml + self.ll
        self.o2, self.o4 = 0, self.midl
        self.op, self.ol = 2 * self.midl, 2 * self.midl + self.ml
        self.blocks = nx * ny
        rows = round_up(self.hp * 2 // 3, 16)
        self.cuts = ((0, rows), (rows, self.hp - rows)) if rows < self.hp else ((0, rows),)
        self.whole_cuts = ((0, self.hp),)
        self.fits = self.blocks <= 32 and self.hh * ny * self.frame <= 7 * 1024 * 1024


class Flow:
    def __init__(self, plan, kind):
        gx, gy = lax.axis_index("gx"), lax.axis_index("gy")
        self.plan, self.gx, self.gy = plan, gx, gy
        self.sizes = (plan.ny // 2, plan.nx // 2, 2)
        self.core = lax.rem(gy, 2)
        self.at = (gy // 2, gx // 2, lax.rem(gx, 2))
        self.orders = (((0, 1, 2), (2, 1, 0)), ((1, 2, 0), (1, 0, 2)))[kind]
        first, second = self.orders
        self.most = tuple(max(self.sizes[i], self.sizes[j]) for i, j in zip(first, second))
        self.least = tuple(min(self.sizes[i], self.sizes[j]) for i, j in zip(first, second))
        self.limit = tuple(self.pick(self.sizes[i], self.sizes[j]) for i, j in zip(first, second))
        self.here = tuple(self.pick(self.at[i], self.at[j]) for i, j in zip(first, second))

    def pick(self, zero, one):
        if isinstance(zero, int) and isinstance(one, int) and zero == one:
            return zero
        return jnp.where(self.core == 0, zero, one)

    def device(self, spot):
        place = [None] * 3
        for axis in range(3):
            place[axis] = self.pick(
                spot[self.orders[0].index(axis)], spot[self.orders[1].index(axis)]
            )
        return (place[1] * 2 + place[2], place[0] * 2 + self.core)

    def twin(self):
        return (self.gx, self.gy + 1 - 2 * self.core)

    def step(self, axis, sign):
        to = self.here[axis] + sign
        spot = tuple(to if i == axis else self.here[i] for i in range(3))
        return jnp.logical_and(to >= 0, to < self.limit[axis]), self.device(spot)


def neighbours(plan):
    flow = Flow(plan, 0)
    out = [(None, flow.twin())]
    for axis in range(3):
        for sign in (-1, 1):
            out.append(flow.step(axis, sign))
    return out


def when(condition):
    return (lambda f: f()) if condition is None else pl.when(condition)


def greet(plan, extra=()):
    barrier = pltpu.get_barrier_semaphore()
    count = jnp.int32(len(extra))
    for there, device in neighbours(plan):
        @when(there)
        def _(device=device):
            pl.semaphore_signal(barrier, inc=1, device_id=device, device_id_type=MESH)
        count = count + (1 if there is None else there.astype(jnp.int32))
    for device in extra:
        pl.semaphore_signal(barrier, inc=1, device_id=device, device_id_type=MESH)
    pl.semaphore_wait(barrier, count)


class Gather:
    def __init__(self, plan, source, target, width, send_sem, recv_sem):
        self.plan, self.source, self.target, self.width = plan, source, target, width
        self.send_sem, self.recv_sem = send_sem, recv_sem
        self.cuts = [(Flow(plan, kind), *cut) for kind, cut in enumerate(plan.cuts)]
        self.phases = 1 + max(sum(m - 1 for m in cut[0].most) for cut in self.cuts)

    def slot(self, cut, gx, gy):
        _, start, rows = cut
        return self.target.at[
            pl.ds(pl.multiple_of(gx * self.plan.hp + start, 16), rows),
            pl.ds(pl.multiple_of(gy * self.width, LANES), self.width),
        ]

    def own_copy(self, sem):
        plan = self.plan
        gx, gy = lax.axis_index("gx"), lax.axis_index("gy")
        place = self.target.at[
            pl.ds(pl.multiple_of(gx * plan.hp, 16), plan.hp),
            pl.ds(pl.multiple_of(gy * self.width, LANES), self.width),
        ]
        return pltpu.make_async_copy(self.source, place, sem)

    def copies(self, kind, cut, spot, own):
        flow = cut[0]
        gx, gy = flow.device(spot)
        dst = self.slot(cut, gx, gy)
        src = self.source.at[pl.ds(cut[1], cut[2]), :] if own else dst
        index = gx * (self.plan.ny // 2) + gy // 2
        goals = [(None, flow.twin(), 6)]
        level = None
        for axis in (2, 1, 0):
            for sign in (-1, 1):
                if flow.most[axis] < 2:
                    continue
                there, device = flow.step(axis, sign)
                if not own:
                    there = there & ((flow.here[axis] - spot[axis]) * sign >= 0)
                    if level is not None:
                        there = there & level
                goals.append((there, device, 2 * axis + (sign + 1) // 2))
            same = spot[axis] == flow.here[axis]
            level = same if level is None else level & same
        out = []
        for there, device, k in goals:
            out.append((there, pltpu.make_async_remote_copy(
                src_ref=src, dst_ref=dst,
                send_sem=self.send_sem.at[kind, index, k],
                recv_sem=self.recv_sem.at[kind, gx * self.plan.ny + gy],
                device_id=device, device_id_type=MESH,
            )))
        return out

    def arrived(self, kind, cut, gx, gy):
        ref = self.slot(cut, gx, gy)
        pltpu.make_async_copy(ref, ref, self.recv_sem.at[kind, gx * self.plan.ny + gy]).wait()

    def start_own(self):
        for kind, cut in enumerate(self.cuts):
            for there, copy in self.copies(kind, cut, cut[0].here, True):
                when(there)(copy.start)

    def walk(self, visit, phase=None, only=None, part=(0, 1)):
        for kind, cut in enumerate(self.cuts):
            if only is not None and kind != only:
                continue
            flow = cut[0]
            mp, mq, mr = flow.most
            total = mp * mq * mr

            def one(n, _, kind=kind, cut=cut, flow=flow):
                spot = (lax.rem(n, mp), lax.rem(n // mp, mq), n // (mp * mq))
                hops, good = 0, None
                for here, limit, at in zip(flow.here, flow.limit, spot):
                    hops = hops + jnp.abs(at - here)
                    good = at < limit if good is None else good & (at < limit)
                good = good & ((hops > 0) if phase is None else (hops == phase))
                pl.when(good)(functools.partial(visit, kind, cut, spot))
                return 0
            lax.fori_loop(total * part[0] // part[1], total * (part[0] + 1) // part[1], one, 0)

    def visit(self, kind, cut, spot):
        self.arrived(kind, cut, *cut[0].device(spot))
        for there, copy in self.copies(kind, cut, spot, False):
            when(there)(copy.start)

    def forward(self, phase):
        if phase < self.phases:
            self.walk(self.visit, phase)

    def items(self, parts):
        return [functools.partial(self.walk, self.visit, phase, kind, (i, parts))
                for phase in range(1, self.phases) for i in range(parts)
                for kind in range(len(self.cuts))]

    def finish_twin(self):
        plan = self.plan
        for kind, cut in enumerate(self.cuts):
            flow = cut[0]
            def one(n, _, kind=kind, cut=cut, flow=flow):
                gx, y = n // (plan.ny // 2), lax.rem(n, plan.ny // 2)
                self.arrived(kind, cut, gx, 2 * y + 1 - flow.core)
                return 0
            lax.fori_loop(0, plan.blocks // 2, one, 0)

    def finish_sends(self):
        for kind, cut in enumerate(self.cuts):
            for there, copy in self.copies(kind, cut, cut[0].here, True):
                when(there)(copy.wait_send)
        def visit(kind, cut, spot):
            for there, copy in self.copies(kind, cut, spot, False):
                when(there)(copy.wait_send)
        self.walk(visit)


class Meet:
    def __init__(self, plan, wide, tall, send_sem, recv_sem):
        self.plan, self.wide, self.tall = plan, wide, tall
        self.send_sem, self.recv_sem = send_sem, recv_sem
        self.gx, self.gy = lax.axis_index("gx"), lax.axis_index("gy")

    @staticmethod
    def peers(plan):
        gx, gy = lax.axis_index("gx"), lax.axis_index("gy")
        return ([(lax.rem(gx + k, plan.nx), gy) for k in range(1, plan.nx)]
                + [(gx, lax.rem(gy + k, plan.ny)) for k in range(1, plan.ny)])

    def copies(self, second):
        plan = self.plan
        n = plan.ny if second else plan.nx
        ref = self.tall if second else self.wide
        own = self.gy if second else self.gx
        out = []
        for k in range(1, n):
            to = lax.rem(own + k, n)
            at = (plan.nx - 1 if second else 0) + k - 1
            out.append(pltpu.make_async_remote_copy(
                src_ref=ref.at[own], dst_ref=ref.at[own],
                send_sem=self.send_sem.at[at], recv_sem=self.recv_sem.at[at],
                device_id=(self.gx, to) if second else (to, self.gy), device_id_type=MESH,
            ))
        return out

    def run(self, value, merge, members, between=None):
        plan = self.plan
        for second in (False, True):
            ref = self.tall if second else self.wide
            ref[self.gy if second else self.gx] = value
            copies = self.copies(second)
            for copy in copies:
                copy.start()
            if between is not None:
                between(second)
            for copy in copies:
                copy.wait_recv()
            value = merge([ref[i] for i in range(ref.shape[0])], members)
            members = members * plan.nx
            for copy in copies:
                copy.wait_send()
        return value


def merge_sums(parts, members):
    total = parts[0]
    for part in parts[1:]:
        total = total + part
    return total


def merge_moments(parts, members):
    n = len(parts)
    mean = merge_sums([part[0:1] for part in parts], 0) / n
    squares = merge_sums([part[1:2] for part in parts], 0)
    between = merge_sums([(part[0:1] - mean) * (part[0:1] - mean) for part in parts], 0)
    return jnp.concatenate([mean, squares + members * between], axis=0)


def tiled(column, plan):
    return jnp.concatenate([column] * (plan.cells // LANES), axis=1)


def lane_sums(value):
    total = value[:, :LANES]
    for at in range(LANES, value.shape[1], LANES):
        total = total + value[:, at:at + LANES]
    return total


def as_row(value):
    return jnp.sum(value.T, axis=0, keepdims=True)


def as_column(row):
    return jnp.broadcast_to(row, (LANES, LANES)).T


def aligned(start, rows=LANES):
    return pl.ds(pl.multiple_of(start, rows), rows)


def moment_rows(plan, h_ref, row_ref):
    def block(i, _):
        value = h_ref[aligned(i * LANES), :]
        sums = lane_sums(value)
        mean = jnp.sum(sums, axis=1, keepdims=True) / plan.cells
        offset = value - mean
        row_ref[0:1, aligned(i * LANES)] = as_row(sums) / plan.cells
        row_ref[1:2, aligned(i * LANES)] = as_row(lane_sums(offset * offset))
        return 0
    lax.fori_loop(0, plan.hh // LANES, block, 0)


def unit_column(slab_ref, i, at):
    slab = slab_ref[aligned(i * LANES), :]
    return jnp.broadcast_to(slab.astype(jnp.float32)[:, at:at + 1], (LANES, LANES))


def activate(plan, k, h_ref, row_ref, slab_ref, keep_ref, out_ref, column_ref, total_cells, spare,
             tick=lambda: None):
    def block(i, _):
        column_ref[0] = as_column(row_ref[0:1, aligned(i * LANES)])
        column_ref[1] = as_column(lax.rsqrt(row_ref[1:2, aligned(i * LANES)] / total_cells + norm_eps))
        column_ref[2] = unit_column(slab_ref, i, k)
        column_ref[3] = unit_column(slab_ref, i, 4 + k)

        def chunk(j, _):
            rows = aligned(i * LANES + j * 16, 16)
            mean, inverse, gain, bias = (
                tiled(column_ref[n, aligned(j * 16, 16), :], plan) for n in range(4))
            scaled = (h_ref[rows, :] - mean) * inverse
            h_ref[rows, :] = scaled
            normed = gain * scaled + bias
            active = normed * jax.nn.sigmoid(normed) * keep_ref[k, rows, :].astype(jnp.float32)
            if spare:
                row = lax.broadcasted_iota(jnp.int32, active.shape, 0) + (i * LANES + j * 16)
                active = jnp.where(lax.rem(row, plan.hp) == plan.h, 1.0, active)
            out_ref[rows, :] = active.astype(jnp.bfloat16)
            return 0
        lax.fori_loop(0, LANES // 16, chunk, 0)
        return 0
    cut = plan.hh // LANES // 2
    lax.fori_loop(0, cut, block, 0)
    tick()
    lax.fori_loop(cut, plan.hh // LANES, block, 0)


def keep_rows(plan, flags_ref, keep_ref, k):
    def lane(t, _):
        lanes = aligned(t * LANES)
        for group in range(plan.nx):
            for start in range(0, plan.hp, 16):
                at = group * plan.h + start
                value = flags_ref[at:at + 16, lanes].astype(jnp.float32) * keep_scale
                if start + 16 > plan.h:
                    row = lax.broadcasted_iota(jnp.int32, value.shape, 0)
                    value = jnp.where(row < plan.h - start, value, 0.0)
                at = group * plan.hp + start
                keep_ref[k, at:at + 16, lanes] = value.astype(jnp.bfloat16)
        return 0
    lax.fori_loop(0, plan.cells // LANES, lane, 0)


def forward_kernel(plan, total_cells, *refs):
    (w1, wsmall, wout, x_hbm, flags_hbm, draws_ref,
     embed_all, small_out, readout_all, center_out, log_var_out, sample_out, layers_out, scaled_out,
     keep_out, rows_out,
     w1_ref, small_ref, x_ref, keep_ref, flags_ref, h_ref, layer_ref, column_ref, latent_ref,
     wide, tall, send_sem, recv_sem, meet_send, meet_recv, own_sem, load_sem, flag_sem, out_sem) = refs
    mid = plan.midp
    load = pltpu.make_async_copy(x_hbm, x_ref, load_sem)
    deep = flags_ref.shape[0]

    def flags(k):
        return pltpu.make_async_copy(
            flags_hbm.at[k], flags_ref.at[k % deep, pl.ds(0, plan.hidden), :], flag_sem.at[k % deep])

    for k in range(deep):
        flags(k).start()
    load.start()
    sets = send_sem.shape[0]
    embed, small, readout = (
        Gather(plan, source, target, width, send_sem.at[u % sets], recv_sem.at[u])
        for u, (source, target, width) in enumerate((
            (w1, w1_ref, plan.gp), (wsmall, small_ref, plan.small), (wout, readout_all, plan.gp))))
    own = [g.own_copy(own_sem.at[u]) for u, g in enumerate((embed, small, readout))]
    for copy in own:
        copy.start()
    peers = Meet.peers(plan)
    barrier = pltpu.get_barrier_semaphore()
    for device in peers:
        pl.semaphore_signal(barrier, inc=1, device_id=device, device_id_type=MESH)
    pl.semaphore_wait(barrier, len(peers))

    def keepers(k):
        flags(k).wait()
        keep_rows(plan, flags_ref.at[k % deep], keep_ref, k)
        if k + deep < 4:
            flags(k + deep).start()

    embed.start_own()
    late = embed.phases - 2
    for phase in range(1, embed.phases):
        if phase <= 4:
            keepers(phase - 1)
        if phase == late:
            if sets == 1:
                pass
            else:
                small.start_own()
        embed.forward(phase)
    for k in range(embed.phases - 1, 4):
        keepers(k)
    if sets == 1:
        embed.finish_sends()
        small.start_own()
    load.wait()
    tail = layer_ref.shape[1] - plan.hh
    slots = layer_ref.shape[0]
    for k in range(slots):
        if tail:
            layer_ref[k, plan.hh:, :] = jnp.zeros((tail, plan.cells), jnp.bfloat16)
    latent_ref[...] = jnp.zeros_like(latent_ref)
    latent_ref[2, 0:plan.latent, :] = draws_ref[...]
    own[0].wait()
    embed.finish_twin()
    outs = [pltpu.make_async_copy(w1_ref, embed_all, out_sem.at[0])]
    outs[0].start()

    queue = [] if sets == 1 else small.items(2)
    marks = {}
    if sets > 1:
        queue.insert(5, readout.start_own)
        marks["small"] = len(queue)
        queue += readout.items(2)
    total = len(queue)

    def tick(count=1):
        for _ in range(count):
            if queue:
                queue.pop(0)()

    half_rows = plan.hh // 2
    for j in range(plan.ny):
        start, stop = j * plan.gp, min((j + 1) * plan.gp, plan.genes)
        for top in (0, half_rows):
            part = rows_dot(w1_ref[top:top + half_rows, start:stop], x_ref[start:stop, :])
            spot = pl.ds(top, half_rows)
            h_ref[0, spot, :] = part if j == 0 else h_ref[0, spot, :] + part
            tick()

    layer_writes = []

    def norm(k, spare):
        h = h_ref.at[k % 2]
        moment_rows(plan, h, rows_out.at[k])
        meet = Meet(plan, wide.at[k], tall.at[k], meet_send.at[k], meet_recv.at[k])
        rows_out[k] = meet.run(rows_out[k], merge_moments, float(plan.cells), lambda second: tick(2))
        slab = w1_ref.at[:, pl.ds(plan.gg - LANES, LANES)]
        if k >= slots:
            finish(layer_writes[k - slots])
        activate(plan, k, h, rows_out.at[k], slab, keep_ref, layer_ref.at[k % slots], column_ref,
                 total_cells, spare, tick)
        for n, (source, target) in enumerate((
                (h, scaled_out.at[k]),
                (layer_ref.at[k % slots, pl.ds(0, plan.hh), :], layers_out.at[k]),
                (keep_ref.at[k], keep_out.at[k]))):
            outs.append(pltpu.make_async_copy(source, target, out_sem.at[3 + 3 * k + n]))
            outs[-1].start()
        layer_writes.append(outs[-2])
        return outs[-3]

    def finish(copy):
        copy.wait()
        outs[:] = [other for other in outs if other is not copy]

    def whole_small():
        if sets > 1:
            while total - len(queue) < marks["small"]:
                tick()
        else:
            for item in small.items(1):
                item()
        own[1].wait()
        small.finish_twin()
        if sets == 1:
            small.finish_sends()
            readout.start_own()
            queue.extend(readout.items(1))
        outs.append(pltpu.make_async_copy(small_ref, small_out, out_sem.at[1]))
        outs[-1].start()
        own[2].wait()

    def hidden(source, lane, target):
        for j in range(plan.ny):
            at = j * plan.small + lane
            part = rows_dot(small_ref[:, at:at + plan.midl], source[mid * j:mid * j + plan.midl, :])
            target[...] = part if j == 0 else target[...] + part
            if j % 2:
                tick()

    wrote_one = norm(0, False)
    whole_small()
    hidden(layer_ref.at[0], plan.o2, h_ref.at[1])
    wrote_two = norm(1, True)
    half = plan.ny // 2
    for j in range(plan.ny):
        at = j * plan.small + plan.op
        part = over_rows(small_ref[:, at:at + plan.ml], layer_ref[1, 0:plan.hh, :])
        spot = (j % half) * plan.moments
        latent_ref[j // half, spot:spot + plan.moments, :] = part[:plan.moments]
    center, log_var = latent_ref[0], latent_ref[1]
    sample = center + jnp.exp(0.5 * log_var) * latent_ref[2]
    row = lax.broadcasted_iota(jnp.int32, sample.shape, 0)
    sample_out[...] = jnp.where(row < plan.latent, sample, 0.0).astype(jnp.bfloat16)
    center_out[...] = latent_ref[0, 0:plan.latent, :]
    log_var_out[...] = latent_ref[1, 0:plan.latent, :]
    finish(wrote_one)
    h_ref[0] = rows_dot(small_ref[:, plan.ol:plan.ol + plan.ll], sample_out[...])
    norm(2, False)
    finish(wrote_two)
    hidden(layer_ref.at[2 % slots], plan.o4, h_ref.at[1])
    norm(3, True)
    while queue:
        tick()
    readout.finish_twin()
    if sets > 1:
        embed.finish_sends()
        small.finish_sends()
    readout.finish_sends()
    for copy in outs:
        copy.wait()


def forward_all(plan, total_cells, w1, wsmall, wout, profiles, flags, draws):
    any_spec, vmem = pl.BlockSpec(memory_space=pl.ANY), pl.BlockSpec(memory_space=pltpu.VMEM)
    f32, bf16 = jnp.float32, jnp.bfloat16
    n = plan.nx + plan.ny - 2
    cuts = len(plan.cuts)
    sets = 3 if plan.blocks <= 32 else 1
    shape = jax.ShapeDtypeStruct
    return pl.pallas_call(
        functools.partial(forward_kernel, plan, total_cells),
        out_shape=[
            shape((plan.hh, plan.gg), bf16), shape((plan.hh, plan.ny * plan.small), bf16),
            shape((plan.hh, plan.gg), bf16), shape((plan.latent, plan.cells), f32),
            shape((plan.latent, plan.cells), f32), shape((plan.ll, plan.cells), bf16),
            shape((4, plan.hh, plan.cells), bf16), shape((4, plan.hh, plan.cells), f32),
            shape((4, plan.hh, plan.cells), bf16), shape((4, 2, plan.hh), f32)],
        in_specs=[any_spec] * 5 + [vmem],
        out_specs=[any_spec] * 3 + [vmem] * 3 + [any_spec] * 3 + [vmem],
        scratch_shapes=[
            pltpu.VMEM((plan.hh, plan.gg), bf16),
            pltpu.VMEM((plan.hh, plan.ny * plan.small), bf16),
            pltpu.VMEM((plan.genes, plan.cells), bf16),
            pltpu.VMEM((4, plan.hh, plan.cells), bf16),
            pltpu.VMEM((2 if sets > 1 else 1, plan.hidden + 16, plan.cells), jnp.int32),
            pltpu.VMEM((2, plan.hh, plan.cells), f32),
            pltpu.VMEM((4 if sets > 1 else 2, plan.hh + plan.midl - plan.midp, plan.cells), bf16),
            pltpu.VMEM((4, LANES, LANES), f32),
            pltpu.VMEM((3, plan.ll, plan.cells), f32),
            pltpu.VMEM((4, plan.nx, 2, plan.hh), f32),
            pltpu.VMEM((4, plan.ny, 2, plan.hh), f32),
            pltpu.SemaphoreType.DMA((sets, cuts, plan.blocks // 2, 7)),
            pltpu.SemaphoreType.DMA((3, cuts, plan.blocks)),
            pltpu.SemaphoreType.DMA((4, n)),
            pltpu.SemaphoreType.DMA((4, n)),
            pltpu.SemaphoreType.DMA((3,)),
            pltpu.SemaphoreType.DMA,
            pltpu.SemaphoreType.DMA((2,)),
            pltpu.SemaphoreType.DMA((15,)),
        ],
        compiler_params=pltpu.CompilerParams(
            collective_id=0, has_side_effects=True, vmem_limit_bytes=60 * 1024 * 1024),
    )(w1, wsmall, wout, profiles, flags, draws)


def meet_kernel(plan, merge, x_ref, o_ref, wide, tall, send_sem, recv_sem):
    peers = Meet.peers(plan)
    barrier = pltpu.get_barrier_semaphore()
    for device in peers:
        pl.semaphore_signal(barrier, inc=1, device_id=device, device_id_type=MESH)
    pl.semaphore_wait(barrier, len(peers))
    meet = Meet(plan, wide, tall, send_sem, recv_sem)
    o_ref[...] = meet.run(x_ref[...], merge, float(plan.cells))


def meet_all(plan, value, merge, collective_id):
    rows, width = value.shape
    n = plan.nx + plan.ny - 2
    return pl.pallas_call(
        functools.partial(meet_kernel, plan, merge),
        out_shape=jax.ShapeDtypeStruct(value.shape, jnp.float32),
        in_specs=[pl.BlockSpec(memory_space=pltpu.VMEM)],
        out_specs=pl.BlockSpec(memory_space=pltpu.VMEM),
        scratch_shapes=[
            pltpu.VMEM((plan.nx, rows, width), jnp.float32),
            pltpu.VMEM((plan.ny, rows, width), jnp.float32),
            pltpu.SemaphoreType.DMA((n,)),
            pltpu.SemaphoreType.DMA((n,)),
        ],
        compiler_params=pltpu.CompilerParams(collective_id=collective_id, has_side_effects=True),
    )(value)


def share_kernel(plan, row_ref, block_ref, row_out, block_out, wide, tall, send_sem, recv_sem):
    peers = Meet.peers(plan)
    barrier = pltpu.get_barrier_semaphore()
    for device in peers:
        pl.semaphore_signal(barrier, inc=1, device_id=device, device_id_type=MESH)
    pl.semaphore_wait(barrier, len(peers))
    meet = Meet(plan, wide, tall, send_sem, recv_sem)
    wide[meet.gx] = row_ref[...]
    tall[meet.gy] = block_ref[...]
    copies = meet.copies(False) + meet.copies(True)
    for copy in copies:
        copy.start()
    for copy in copies:
        copy.wait_recv()
    row_out[...] = wide[0]
    block_out[...] = tall[0]
    for copy in copies:
        copy.wait_send()


def share_all(plan, row, block, collective_id):
    n = plan.nx + plan.ny - 2
    return pl.pallas_call(
        functools.partial(share_kernel, plan),
        out_shape=[jax.ShapeDtypeStruct(row.shape, jnp.float32),
                   jax.ShapeDtypeStruct(block.shape, jnp.float32)],
        in_specs=[pl.BlockSpec(memory_space=pltpu.VMEM)] * 2,
        out_specs=[pl.BlockSpec(memory_space=pltpu.VMEM)] * 2,
        scratch_shapes=[
            pltpu.VMEM((plan.nx, *row.shape), jnp.float32),
            pltpu.VMEM((plan.ny, *block.shape), jnp.float32),
            pltpu.SemaphoreType.DMA((n,)),
            pltpu.SemaphoreType.DMA((n,)),
        ],
        compiler_params=pltpu.CompilerParams(collective_id=collective_id, has_side_effects=True),
    )(row, block)


class Reduce:
    def __init__(self, plan, width, part, twin, slots, send_sem, twin_sem, recv_sem, flow=0):
        self.first = flow
        self.plan, self.width, self.part, self.twin, self.slots = plan, width, part, twin, slots
        self.send_sem, self.twin_sem, self.recv_sem = send_sem, twin_sem, recv_sem
        self.cuts = [(Flow(plan, flow), *cut) for cut in plan.whole_cuts]

    @staticmethod
    def slot_counts(plan, flow):
        counts = []
        for kind in (flow,):
            sizes = (plan.ny // 2, plan.nx // 2, 2)
            first, second = (((0, 1, 2), (2, 1, 0)), ((1, 2, 0), (1, 0, 2)))[kind]
            mp, mq, mr = (max(sizes[i], sizes[j]) for i, j in zip(first, second))
            a, b, c = (Reduce.sides(m) for m in (mp, mq, mr))
            far_r = (mr > 2) * (mr * mq * mp)
            counts.append((far_r, mq * mp * (c + (mq > 2)), mp * (c + b + (mp > 2)), c + b + a))
        return counts

    @staticmethod
    def sides(most):
        return 1 if most == 2 else (2 if most > 2 else 0)

    def block(self, ref, cut, gx, gy):
        return ref.at[
            pl.ds(pl.multiple_of(gx * self.plan.hp + cut[1], 16), cut[2]),
            pl.ds(pl.multiple_of(gy * self.width, LANES), self.width),
        ]

    def twin_block(self, cut, gx, y):
        return self.twin.at[
            pl.ds(pl.multiple_of(gx * self.plan.hp + cut[1], 16), cut[2]),
            pl.ds(pl.multiple_of(y * self.width, LANES), self.width),
        ]

    def twin_copy(self, kind, cut, gx, y):
        flow = cut[0]
        return pltpu.make_async_remote_copy(
            src_ref=self.block(self.part, cut, gx, 2 * y + 1 - flow.core),
            dst_ref=self.twin_block(cut, gx, y),
            send_sem=self.twin_sem.at[0, kind, gx * (self.plan.ny // 2) + y],
            recv_sem=self.twin_sem.at[1, kind, gx * (self.plan.ny // 2) + y],
            device_id=flow.twin(), device_id_type=MESH,
        )

    def each_twin(self, visit, ys=None):
        ny2 = self.plan.ny // 2
        a, na = self.cuts[0][0].at[1], self.plan.nx // 2

        def along(n, _):
            to = a + (na - 1 - n // 2) * (1 - 2 * lax.rem(n, 2))

            @pl.when((to >= 0) & (to < na))
            def _():
                for kind, cut in enumerate(self.cuts):
                    def one(i, _, kind=kind, cut=cut):
                        visit(self.twin_copy(kind, cut, to * 2 + i // ny2, lax.rem(i, ny2)))
                        return 0
                    lax.fori_loop(0, 2 * ny2, one, 0)
            return 0
        lax.fori_loop(0, 2 * na - 1, along, 0)

    def start_twin(self):
        self.each_twin(lambda copy: copy.start())

    def entry(self, kind, stage, spot, axis, came_from):
        flow = self.cuts[kind][0]
        mp, mq, mr = flow.most
        far_r, far_q, far_p, _ = Reduce.slot_counts(self.plan, self.first)[kind]
        sides = [Reduce.sides(m) for m in flow.most]
        dp, dq, dr = spot
        if stage == 2:
            return (dr * mq + dq) * mp + dp
        if stage == 1:
            base, which = far_r, (dq * mp + dp) * (sides[2] + (mq > 2))
        elif stage == 0:
            base, which = far_r + far_q, dp * (sides[2] + sides[1] + (mp > 2))
        else:
            base, which = far_r + far_q + far_p, 0
        offset = 0
        for later in (2, 1, 0):
            if later == stage:
                return base + which + offset
            if later == axis:
                side = 0 if sides[axis] == 1 else (came_from + 1) // 2
                return base + which + offset + side
            offset += sides[later]

    def slot(self, kind, index):
        cut = self.cuts[kind]
        total = sum(Reduce.slot_counts(self.plan, self.first)[kind])
        return self.slots[kind].at[index], self.recv_sem[kind].at[index]

    def gather_terms(self, kind, cut, spot, stage, sign):
        flow = cut[0]
        ny2 = self.plan.ny // 2
        gx, gy = flow.device(spot)
        y = gy // 2
        copy = self.twin_copy(kind, cut, gx, y)
        copy.wait_recv()
        own = self.block(self.part, cut, gx, gy)
        twin = self.twin_block(cut, gx, y)
        arrivals = []
        for axis in (2, 1, 0):
            if axis > stage:
                for side in (-1, 1):
                    there, _ = flow.step(axis, side)
                    if flow.most[axis] < 2:
                        continue
                    arrivals.append((there, self.entry(kind, stage, spot, axis, side)))
            elif axis == stage and flow.most[axis] > 2:
                away = self.here_away(flow, axis, sign)
                arrivals.append((away, self.entry(kind, stage, spot, axis, None)))
        return own, twin, arrivals

    def here_away(self, flow, axis, sign):
        to = flow.here[axis] - sign
        return (to >= 0) & (to < flow.limit[axis])

    def add_in(self, kind, cut, spot, stage, sign):
        own, twin, arrivals = self.gather_terms(kind, cut, spot, stage, sign)

        def add(other):
            def chunk(i, _):
                rows = aligned(i * 16, 16)
                own[rows, :] = own[rows, :] + other[rows, :]
                return 0
            lax.fori_loop(0, cut[2] // 16, chunk, 0)

        add(twin)
        for there, index in arrivals:
            slot, sem = self.slot(kind, index)
            @when(there)
            def _(slot=slot, sem=sem):
                pltpu.make_async_copy(slot, slot, sem).wait()
                add(slot)
        return own

    def onward(self, kind, cut, spot, stage, sign):
        flow = cut[0]
        _, device = self.toward(flow, stage, sign)
        gx, gy = flow.device(spot)
        to = flow.here[stage] + sign
        index_same = self.entry(kind, stage, spot, stage, None) if flow.most[stage] > 2 else None
        done = to == spot[stage]
        p_same = flow.here[0] == spot[0]
        q_same = flow.here[1] == spot[1]
        if stage == 2:
            deeper = jnp.where(q_same, jnp.where(p_same,
                               self.entry(kind, -1, spot, 2, -sign),
                               self.entry(kind, 0, spot, 2, -sign)),
                               self.entry(kind, 1, spot, 2, -sign))
        elif stage == 1:
            deeper = jnp.where(p_same, self.entry(kind, -1, spot, 1, -sign),
                               self.entry(kind, 0, spot, 1, -sign))
        else:
            deeper = self.entry(kind, -1, spot, 0, -sign)
        index = deeper if index_same is None else jnp.where(done, deeper, index_same)
        slot, sem = self.slot(kind, index)
        ny2 = self.plan.ny // 2
        return pltpu.make_async_remote_copy(
            src_ref=self.block(self.part, cut, gx, gy), dst_ref=slot,
            send_sem=self.send_sem.at[kind, gx * ny2 + gy // 2], recv_sem=sem,
            device_id=device, device_id_type=MESH,
        )

    def toward(self, flow, axis, sign):
        return flow.step(axis, sign)

    def order(self, kind):
        mp, mq, mr = self.cuts[kind][0].most
        out = [(2, k, far) for k in range(mr - 1, 0, -1) for far in range(mq - 1, -1, -1)]
        return out + [(stage, k, 0) for stage in (1, 0)
                      for k in range(self.cuts[kind][0].most[stage] - 1, 0, -1)]

    def walk(self, visit, kind, stage, k, far):
        cut = self.cuts[kind]
        p, q, r = cut[0].here
        np_, nq, nr = cut[0].limit
        mp, mq, mr = cut[0].most

        def one(n, _):
            dp = p + (mp - 1 - n // 2) * (1 - 2 * lax.rem(n, 2))
            for sign in (-1, 1):
                if stage == 2:
                    d = r + sign * k
                    for side in ((-1, 1) if far else (1,)):
                        dq = q + side * far
                        good = ((d >= 0) & (d < nr) & (dq >= 0) & (dq < nq)
                                & (dp >= 0) & (dp < np_))
                        pl.when(good)(functools.partial(visit, kind, cut, (dp, dq, d), stage, sign))
                    continue
                if stage == 1:
                    d = q + sign * k
                    spot, good = (dp, d, r), (d >= 0) & (d < nq) & (dp >= 0) & (dp < np_)
                else:
                    d = p + sign * k
                    spot, good = (d, q, r), (d >= 0) & (d < np_)
                pl.when(good)(functools.partial(visit, kind, cut, spot, stage, sign))
            return 0
        lax.fori_loop(0, 1 if stage == 0 else 2 * mp - 1, one, 0)

    def visit(self, kind, cut, spot, stage, sign):
        self.add_in(kind, cut, spot, stage, sign)
        self.onward(kind, cut, spot, stage, sign).start()

    def items(self):
        lines = [[functools.partial(self.walk, self.visit, kind, *step) for step in self.order(kind)]
                 for kind in range(len(self.cuts))]
        out = []
        for i in range(max(len(line) for line in lines)):
            out += [line[i] for line in lines if i < len(line)]
        return out

    def own_sum(self, out_ref, factor):
        for kind, cut in enumerate(self.cuts):
            flow = cut[0]
            own = self.add_in(kind, cut, flow.here, -1, None)
            out_ref[pl.ds(cut[1], cut[2]), :] = own[...].astype(jnp.float32) * factor

    def finish_sends(self):
        self.each_twin(lambda copy: copy.wait_send())
        def visit(kind, cut, spot, stage, sign):
            self.onward(kind, cut, spot, stage, sign).wait_send()
        for kind in range(len(self.cuts)):
            for step in self.order(kind):
                self.walk(visit, kind, *step)

    def twin_column(self, gy):
        y, flow = gy // 2, self.cuts[0][0]

        @pl.when(gy % 2 != flow.core)
        def _():
            for kind, cut in enumerate(self.cuts):
                def one(gx, _, kind=kind, cut=cut):
                    self.twin_copy(kind, cut, gx, y).start()
                    return 0
                lax.fori_loop(0, self.plan.nx, one, 0)


def reduce_scratch(plan, width, flow=0):
    counts = [sum(c) for c in Reduce.slot_counts(plan, flow)]
    return [
        pltpu.VMEM((plan.hh, plan.ny * width), jnp.bfloat16),
        pltpu.VMEM((plan.hh, plan.ny // 2 * width), jnp.bfloat16),
        *[pltpu.VMEM((c, cut[1], width), jnp.bfloat16) for c, cut in zip(counts, plan.whole_cuts)],
        pltpu.SemaphoreType.DMA((len(plan.whole_cuts), plan.blocks // 2)),
        pltpu.SemaphoreType.DMA((2, len(plan.whole_cuts), plan.blocks // 2)),
        *[pltpu.SemaphoreType.DMA((c,)) for c in counts],
    ]


def reduce_from(plan, width, refs, flow=0):
    n = len(plan.whole_cuts)
    part, twin, slots, sems, recv = refs[0], refs[1], refs[2:2 + n], refs[2 + n:4 + n], refs[4 + n:]
    return Reduce(plan, width, part, twin, slots, *sems, recv, flow)


def reduce_kernel(plan, width, factor, x_ref, o_ref, *rest):
    reduce = reduce_from(plan, width, rest[:-1])
    load = pltpu.make_async_copy(x_ref, reduce.part, rest[-1])
    load.start()
    greet(plan)
    load.wait()
    reduce.start_twin()
    for item in reduce.items():
        item()
    reduce.own_sum(o_ref, factor)
    reduce.finish_sends()


def reduce_all(plan, value, factor, collective_id):
    width = value.shape[1] // plan.ny
    return pl.pallas_call(
        functools.partial(reduce_kernel, plan, width, factor),
        out_shape=jax.ShapeDtypeStruct((plan.hp, width), jnp.float32),
        in_specs=[pl.BlockSpec(memory_space=pl.ANY)],
        out_specs=pl.BlockSpec(memory_space=pltpu.VMEM),
        scratch_shapes=[*reduce_scratch(plan, width), pltpu.SemaphoreType.DMA],
        compiler_params=pltpu.CompilerParams(
            collective_id=collective_id, has_side_effects=True, vmem_limit_bytes=60 * 1024 * 1024),
    )(value)


def backward_kernel(plan, total_cells, *refs):
    (part_hbm, up_hbm, small_hbm, layers_hbm, scaled_hbm, keep_hbm, sample_ref, rows_ref, loss_ref,
     center_ref, log_var_ref, draws_ref,
     readout_out, sums_out, small_part, grad_ref,
     small_ref, up_ref, layer_ref, scaled_ref, keep_ref, lane_ref, column_ref, latent_ref,
     moment_ref, wide, tall, meet_send, meet_recv, load_sem, *rest) = refs
    reduce = reduce_from(plan, plan.frame, rest)

    def load(k):
        slot = k % 2
        return (
            pltpu.make_async_copy(scaled_hbm.at[k], scaled_ref.at[slot], load_sem.at[3 * slot]),
            pltpu.make_async_copy(keep_hbm.at[k], keep_ref.at[slot], load_sem.at[3 * slot + 1]),
        )

    def load_layer(k):
        return pltpu.make_async_copy(
            layers_hbm.at[k], layer_ref.at[k % 2, pl.ds(0, plan.hh), :], load_sem.at[3 * (k % 2) + 2])

    frames = [pltpu.make_async_copy(
        part_hbm.at[:, pl.ds(start, plan.frame)],
        reduce.part.at[:, pl.ds(j * plan.frame, plan.frame)], load_sem.at[6 + j])
        for j, start in enumerate(plan.frame_start)]
    second = pltpu.make_async_copy(up_hbm, up_ref, load_sem.at[6 + plan.ny])
    third = pltpu.make_async_copy(small_hbm, small_ref, load_sem.at[7 + plan.ny])
    for copy in frames:
        copy.start()
    second.start()
    for copy in load(3):
        copy.start()
    third.start()
    load_layer(2).start()
    for copy in load(2):
        copy.start()
    load_layer(1).start()
    peers = Meet.peers(plan)
    barrier = pltpu.get_barrier_semaphore()
    for device in peers:
        pl.semaphore_signal(barrier, inc=1, device_id=device, device_id_type=MESH)
    pl.semaphore_wait(barrier, len(peers))
    for copy in frames:
        copy.wait()
    reduce.start_twin()
    tail = layer_ref.shape[1] - plan.hh
    if tail:
        for k in range(2):
            layer_ref[k, plan.hh:, :] = jnp.zeros((tail, plan.cells), jnp.bfloat16)
    latent_ref[...] = jnp.zeros_like(latent_ref)

    todo = reduce.items()
    todo.append(lambda: reduce.own_sum(readout_out, 1.0 / total_cells))

    def between(second):
        if todo:
            todo.pop(0)()

    def layer(k):
        slot = k % 2
        for copy in load(k):
            copy.wait()

        def columns(i):
            slab = small_ref.at[:, pl.ds(plan.ol + plan.ll - LANES, LANES)]
            base = plan.latent - (plan.ll - LANES)
            column_ref[0] = unit_column(slab, i, base + k)
            column_ref[1] = unit_column(slab, i, base + 4 + k)
            column_ref[2] = as_column(
                lax.rsqrt(rows_ref[k, 1:2, aligned(i * LANES)] / total_cells + norm_eps))

        def block(i, _):
            columns(i)

            def chunk(j, _):
                rows = aligned(i * LANES + j * 16, 16)
                here = aligned(j * 16, 16)
                gain, bias = tiled(column_ref[0, here, :], plan), tiled(column_ref[1, here, :], plan)
                scaled = scaled_ref[slot, rows, :]
                normed = gain * scaled + bias
                sigma = jax.nn.sigmoid(normed)
                slope = up_ref[rows, :] * keep_ref[slot, rows, :].astype(jnp.float32) * sigma * (
                    1.0 + normed * (1.0 - sigma))
                up_ref[rows, :] = slope
                lane_ref[0, here, :] = lane_sums(slope)
                lane_ref[1, here, :] = lane_sums(slope * scaled)
                return 0
            lax.fori_loop(0, LANES // 16, chunk, 0)
            sums_out[k, 0:1, aligned(i * LANES)] = as_row(lane_ref[0])
            sums_out[k, 1:2, aligned(i * LANES)] = as_row(lane_ref[1])
            return 0
        lax.fori_loop(0, plan.hh // LANES, block, 0)
        sums_out[k, 2:3, :] = jnp.broadcast_to(own_loss, (1, plan.hh))
        meet = Meet(plan, wide.at[k], tall.at[k], meet_send.at[k], meet_recv.at[k])
        sums_out[k] = meet.run(sums_out[k], merge_sums, 1.0, between)

        def last(i, _):
            columns(i)
            column_ref[3] = as_column(sums_out[k, 0:1, aligned(i * LANES)] / total_cells)
            column_ref[4] = as_column(sums_out[k, 1:2, aligned(i * LANES)] / total_cells)

            def chunk(j, _):
                rows = aligned(i * LANES + j * 16, 16)
                here = aligned(j * 16, 16)
                factor = tiled(column_ref[0, here, :] * column_ref[2, here, :], plan)
                shift, gain = tiled(column_ref[3, here, :], plan), tiled(column_ref[4, here, :], plan)
                grad = factor * (up_ref[rows, :] - (shift + scaled_ref[slot, rows, :] * gain))
                grad_ref[rows, :] = grad.astype(jnp.bfloat16)
                return 0
            lax.fori_loop(0, LANES // 16, chunk, 0)
            return 0
        lax.fori_loop(0, plan.hh // LANES, last, 0)
        if k >= 2:
            for copy in load(k - 2):
                copy.start()

    def put(j, lane, value):
        at = j * plan.small + lane
        small_part[:, at:at + value.shape[1]] = value.astype(jnp.bfloat16)

    def middle(source, lane):
        for j in range(plan.ny):
            at, row = j * plan.small + lane, j * plan.midp
            put(j, lane, over_cells(grad_ref[...], source[row:row + plan.midl, :]))
            if j % 2:
                between(None)
            up_ref[row:row + plan.midp, :] = over_rows(
                small_ref[:, at:at + plan.midl], grad_ref[...])[:plan.midp]

    kl_terms = (jnp.exp(log_var_ref[...]) + center_ref[...] * center_ref[...] - 1.0 - log_var_ref[...])
    own_loss = (0.5 * jnp.sum(jnp.sum(loss_ref[...], axis=0, keepdims=True), axis=1, keepdims=True)
                + kl_weight * 0.5 * jnp.sum(
                    jnp.sum(kl_terms, axis=0, keepdims=True), axis=1, keepdims=True))
    second.wait()
    third.wait()
    layer(3)
    load_layer(2).wait()
    middle(layer_ref.at[0], plan.o4)
    load_layer(0).start()
    layer(2)
    lifting = over_cells(grad_ref[...], sample_ref[...])
    for j in range(plan.ny):
        put(j, plan.ol, lifting)
    reach = over_rows(small_ref[:, plan.ol:plan.ol + plan.ll], grad_ref[...])[:plan.latent]
    center, log_var = center_ref[...], log_var_ref[...]
    latent_ref[0, 0:plan.latent, :] = reach + kl_weight * center
    latent_ref[1, 0:plan.latent, :] = (
        reach * 0.5 * jnp.exp(0.5 * log_var) * draws_ref[...]
        + kl_weight * 0.5 * (jnp.exp(log_var) - 1.0))
    half, tall_rows = plan.ny // 2, round_up(plan.moments, 16)
    moment_ref[...] = jnp.zeros_like(moment_ref)
    for j in range(plan.ny):
        spot = (j % half) * plan.moments
        piece = latent_ref[j // half, spot:spot + tall_rows, :]
        row = lax.broadcasted_iota(jnp.int32, piece.shape, 0)
        piece = jnp.where(row < plan.moments, piece, 0.0)
        moment_ref[j * plan.ml:j * plan.ml + tall_rows, :] = piece.astype(jnp.bfloat16)
    load_layer(1).wait()
    for j in range(plan.ny):
        at, row = j * plan.small + plan.op, j * plan.ml
        moments = moment_ref[row:row + plan.ml, :]
        put(j, plan.op, over_cells(layer_ref[1, 0:plan.hh, :], moments))
        part = rows_dot(small_ref[:, at:at + plan.ml], moments)
        up_ref[...] = part if j == 0 else up_ref[...] + part
    layer(1)
    load_layer(0).wait()
    middle(layer_ref.at[0], plan.o2)
    layer(0)
    while todo:
        between(False)
    reduce.finish_sends()


def backward_all(plan, total_cells, *arrays):
    any_spec, vmem = pl.BlockSpec(memory_space=pl.ANY), pl.BlockSpec(memory_space=pltpu.VMEM)
    f32, bf16 = jnp.float32, jnp.bfloat16
    n = plan.nx + plan.ny - 2
    shape = jax.ShapeDtypeStruct
    return pl.pallas_call(
        functools.partial(backward_kernel, plan, total_cells),
        out_shape=[
            shape((plan.hp, plan.frame), f32), shape((4, 3, plan.hh), f32),
            shape((plan.hh, plan.ny * plan.small), bf16), shape((plan.hh, plan.cells), bf16)],
        in_specs=[any_spec] * 6 + [vmem] * 6,
        out_specs=[vmem] * 4,
        scratch_shapes=[
            pltpu.VMEM((plan.hh, plan.ny * plan.small), bf16),
            pltpu.VMEM((plan.hh, plan.cells), f32),
            pltpu.VMEM((2, plan.hh + plan.midl - plan.midp, plan.cells), bf16),
            pltpu.VMEM((2, plan.hh, plan.cells), f32),
            pltpu.VMEM((2, plan.hh, plan.cells), bf16),
            pltpu.VMEM((2, LANES, LANES), f32),
            pltpu.VMEM((5, LANES, LANES), f32),
            pltpu.VMEM((2, plan.ll, plan.cells), f32),
            pltpu.VMEM((plan.ny * plan.ml, plan.cells), bf16),
            pltpu.VMEM((4, plan.nx, 3, plan.hh), f32),
            pltpu.VMEM((4, plan.ny, 3, plan.hh), f32),
            pltpu.SemaphoreType.DMA((4, n)),
            pltpu.SemaphoreType.DMA((4, n)),
            pltpu.SemaphoreType.DMA((8 + plan.ny,)),
            *reduce_scratch(plan, plan.frame),
        ],
        compiler_params=pltpu.CompilerParams(
            collective_id=6, has_side_effects=True, vmem_limit_bytes=60 * 1024 * 1024),
    )(*arrays)


def embed_kernel(plan, total_cells, *refs):
    (small_hbm, x_hbm, grad_ref, readout_ref, embed_out, small_out, row_out, block_out,
     x_ref, wide, tall, meet_send, meet_recv, load_sem, *rest) = refs
    half = len(rest) // 2
    small = reduce_from(plan, plan.small, rest[:half])
    embed = reduce_from(plan, plan.frame, rest[half:])
    first = pltpu.make_async_copy(small_hbm, small.part, load_sem.at[0])
    second = pltpu.make_async_copy(x_hbm, x_ref, load_sem.at[1])
    first.start()
    second.start()
    peers = Meet.peers(plan)
    barrier = pltpu.get_barrier_semaphore()
    for device in peers:
        pl.semaphore_signal(barrier, inc=1, device_id=device, device_id_type=MESH)
    pl.semaphore_wait(barrier, len(peers))
    first.wait()
    small.start_twin()
    second.wait()
    factor = 1.0 / total_cells
    queue = small.items()

    def tick():
        if queue:
            queue.pop(0)()

    piece = plan.frame // 3 // LANES * LANES
    for j in range(plan.ny):
        start, stop = plan.frame_start[j], min(plan.frame_start[j] + plan.frame, plan.genes)
        for at in range(start, stop, piece):
            end = min(at + piece, stop)
            to = j * plan.frame + at - start
            embed.part[:, to:to + end - at] = over_cells(
                grad_ref[...], x_ref[at:end, :]).astype(jnp.bfloat16)
            tick()
        done = stop - start
        if done < plan.frame:
            inside = done // LANES * LANES
            lanes = lax.broadcasted_iota(jnp.int32, (plan.hh, LANES), 1)
            at = j * plan.frame + inside
            if inside < done:
                value = embed.part[:, at:at + LANES]
                embed.part[:, at:at + LANES] = jnp.where(
                    lanes < done - inside, value.astype(jnp.float32), 0.0).astype(jnp.bfloat16)
                inside += LANES
            for at in range(j * plan.frame + inside, (j + 1) * plan.frame, LANES):
                embed.part[:, at:at + LANES] = jnp.zeros((plan.hh, LANES), jnp.bfloat16)
        embed.twin_column(j)
        tick()
    todo = embed.items()
    first_items = 4
    for item in todo[:first_items]:
        item()
    while queue:
        tick()
    small.own_sum(small_out, factor)
    meet = Meet(plan, wide, tall, meet_send, meet_recv)
    wide[meet.gx, :, 0:plan.frame] = readout_ref[plan.h:plan.h + 1, :]
    wide[meet.gx, :, plan.frame:] = small_out[plan.h:plan.h + 1, plan.op:plan.op + plan.ml]
    tall[meet.gy] = small_out[:, plan.ol:plan.ol + plan.ll]
    copies = meet.copies(False) + meet.copies(True)
    for copy in copies:
        copy.start()
    for item in todo[first_items:]:
        item()
    for copy in copies:
        copy.wait_recv()
    row_out[...] = wide[0]
    block_out[...] = tall[0]
    embed.own_sum(embed_out, factor)
    for copy in copies:
        copy.wait_send()
    small.finish_sends()
    embed.finish_sends()


def embed_all_sums(plan, total_cells, *arrays):
    any_spec, vmem = pl.BlockSpec(memory_space=pl.ANY), pl.BlockSpec(memory_space=pltpu.VMEM)
    f32, bf16 = jnp.float32, jnp.bfloat16
    n = plan.nx + plan.ny - 2
    shape = jax.ShapeDtypeStruct
    row, block = (1, plan.frame + plan.ml), (plan.hp, plan.ll)
    return pl.pallas_call(
        functools.partial(embed_kernel, plan, total_cells),
        out_shape=[shape((plan.hp, plan.frame), f32), shape((plan.hp, plan.small), f32),
                   shape(row, f32), shape(block, f32)],
        in_specs=[any_spec] * 2 + [vmem] * 2,
        out_specs=[vmem] * 4,
        scratch_shapes=[
            pltpu.VMEM((plan.genes, plan.cells), bf16),
            pltpu.VMEM((plan.nx, *row), f32),
            pltpu.VMEM((plan.ny, *block), f32),
            pltpu.SemaphoreType.DMA((n,)),
            pltpu.SemaphoreType.DMA((n,)),
            pltpu.SemaphoreType.DMA((2,)),
            *reduce_scratch(plan, plan.small),
            *reduce_scratch(plan, plan.frame),
        ],
        compiler_params=pltpu.CompilerParams(
            collective_id=7, has_side_effects=True, vmem_limit_bytes=60 * 1024 * 1024),
    )(*arrays)


def output_kernel(plan, chunk, w_ref, layer_ref, x_ref, flag_ref, pick_ref,
                  out_ref, og_ref, part_ref, up_ref, loss_ref):
    i = pl.program_id(0)

    @pl.when(i == 0)
    def _():
        up_ref[...] = jnp.zeros_like(up_ref)
        loss_ref[...] = jnp.zeros_like(loss_ref)
    weight, layer = w_ref[...], layer_ref[0]
    raw = over_rows(weight, layer)
    slab = over_rows(flag_ref[...].astype(jnp.float32).astype(jnp.bfloat16), pick_ref[...])
    out_ref[...] = raw.astype(jnp.bfloat16)
    residual = raw - x_ref[...].astype(jnp.float32)
    inside = lax.broadcasted_iota(jnp.int32, raw.shape, 0) + i * chunk < plan.genes
    weighted = jnp.where(inside, slab * residual, 0.0)
    grad = weighted.astype(jnp.bfloat16)
    og_ref[...] = grad
    terms = lane_sums(jnp.where(inside, weighted * residual, 0.0))
    loss_ref[...] += jnp.sum(terms.reshape(chunk // 8, 8, LANES), axis=0)
    part_ref[...] = over_cells(layer, grad).astype(jnp.bfloat16)
    up_ref[...] += rows_dot(weight, grad)


def output_all(plan, readout_all, layers, profiles, flags, picker):
    chunk = 4 * LANES
    steps = plan.gg // chunk
    f32, bf16 = jnp.float32, jnp.bfloat16
    shape = jax.ShapeDtypeStruct
    studies = flags.shape[0]
    return pl.pallas_call(
        functools.partial(output_kernel, plan, chunk),
        grid=(steps,),
        out_shape=[shape((plan.genes, plan.cells), bf16), shape((plan.gg, plan.cells), bf16),
                   shape((plan.hh, plan.gg), bf16), shape((plan.hh, plan.cells), f32),
                   shape((8, LANES), f32)],
        in_specs=[
            pl.BlockSpec((plan.hh, chunk), lambda i: (0, i)),
            pl.BlockSpec((1, plan.hh, plan.cells), lambda i: (3, 0, 0)),
            pl.BlockSpec((chunk, plan.cells), lambda i: (i, 0)),
            pl.BlockSpec((studies, chunk), lambda i: (0, i)),
            pl.BlockSpec((studies, plan.cells), lambda i: (0, 0))],
        out_specs=[
            pl.BlockSpec((chunk, plan.cells), lambda i: (i, 0)),
            pl.BlockSpec((chunk, plan.cells), lambda i: (i, 0)),
            pl.BlockSpec((plan.hh, chunk), lambda i: (0, i)),
            pl.BlockSpec((plan.hh, plan.cells), lambda i: (0, 0)),
            pl.BlockSpec((8, LANES), lambda i: (0, 0))],
        compiler_params=pltpu.CompilerParams(vmem_limit_bytes=48 * 1024 * 1024),
    )(readout_all, layers, profiles, flags, picker)


def input_kernel(w_ref, grad_ref, og_ref, out_ref):
    back = over_rows(w_ref[...], grad_ref[...])
    out_ref[...] = (back - og_ref[...].astype(jnp.float32)).astype(jnp.bfloat16)


def input_all(plan, embed_all, grad, output_grad):
    chunk = 14 * LANES
    return pl.pallas_call(
        input_kernel,
        grid=(plan.gg // chunk,),
        out_shape=jax.ShapeDtypeStruct((plan.genes, plan.cells), jnp.bfloat16),
        in_specs=[
            pl.BlockSpec((plan.hh, chunk), lambda i: (0, i)),
            pl.BlockSpec((plan.hh, plan.cells), lambda i: (0, 0)),
            pl.BlockSpec((chunk, plan.cells), lambda i: (i, 0))],
        out_specs=pl.BlockSpec((chunk, plan.cells), lambda i: (i, 0)),
        compiler_params=pltpu.CompilerParams(vmem_limit_bytes=48 * 1024 * 1024),
    )(embed_all, grad, output_grad)


def rows_dot(left, right):
    return lax.dot_general(left, right, (((1,), (0,)), ((), ())), preferred_element_type=jnp.float32)


def over_cells(left, right):
    return lax.dot_general(left, right, (((1,), (1,)), ((), ())), preferred_element_type=jnp.float32)


def over_rows(left, right):
    return lax.dot_general(left, right, (((0,), (0,)), ((), ())), preferred_element_type=jnp.float32)


def pad_to(value, rows, lanes):
    return jnp.pad(value, ((0, rows - value.shape[0]), (0, lanes - value.shape[1])))


def middle_piece(plan, matrix):
    turned = matrix.T.reshape(plan.h, plan.groups, plan.h)
    wide = jnp.pad(turned, ((0, plan.hp - plan.h), (0, 0), (0, plan.hp - plan.h)))
    return pad_to(wide.reshape(plan.hp, plan.midp), plan.hp, plan.midl)


def middle_back(plan, piece):
    cut = piece[:plan.h, :plan.midp].reshape(plan.h, plan.groups, plan.hp)[:, :, :plan.h]
    return cut.reshape(plan.h, plan.mid).T


def with_row(plan, block, row, first):
    spare = jnp.where(first, row, jnp.zeros_like(row))[None]
    return pad_to(jnp.concatenate([block, spare], axis=0), plan.hp, block.shape[1])


def on_device(
    nx, ny,
    transcript_profiles,
    experiment_labels,
    measured_flags,
    retained_unit_flags,
    standard_normal_draws,
    compressor_first_matrix,
    compressor_second_matrix,
    posterior_matrix,
    posterior_intercepts,
    expander_first_matrix,
    expander_second_matrix,
    output_matrix,
    output_intercept,
    normalizer_factors,
    normalizer_translations,
):
    cells = transcript_profiles.shape[0]
    plan = Plan(nx, ny, cells, output_matrix.shape[1], output_matrix.shape[0], expander_first_matrix.shape[0])
    total_cells = float(cells * nx * ny)
    gx, gy = lax.axis_index("gx"), lax.axis_index("gy")
    first = gx == 0

    wide = jnp.concatenate([
        pad_to(compressor_first_matrix.T, plan.hp, plan.g),
        with_row(plan, output_matrix, output_intercept, first)], axis=0)
    strip = lax.ppermute(wide[:, :plan.strip], "gy", [(j + 1, j) for j in range(ny - 1)])
    wide = jnp.concatenate([wide, strip], axis=1)
    wide = pad_to(wide, 2 * plan.hp, plan.gp + plan.strip + plan.shift * ny)
    wide = lax.dynamic_slice_in_dim(wide, gy * plan.shift, plan.gp, 1)
    norms = jnp.concatenate([normalizer_factors.T, normalizer_translations.T], axis=1)
    last = jnp.concatenate([expander_first_matrix.T, norms], axis=1)
    tile = jnp.where(gy == ny - 1, pad_to(norms, plan.hp, LANES), wide[:plan.hp, plan.gp - LANES:])
    first_piece = jnp.concatenate([wide[:plan.hp, :plan.gp - LANES], tile], axis=1)
    small = jnp.concatenate([
        middle_piece(plan, compressor_second_matrix),
        middle_piece(plan, expander_second_matrix),
        pad_to(with_row(plan, posterior_matrix, posterior_intercepts, first), plan.hp, plan.ml),
        pad_to(last, plan.hp, plan.ll)], axis=1)
    profiles = transcript_profiles.T
    draws = standard_normal_draws.T
    (embed_all, small_all, readout_all, center, log_var, sample, layers, scaled_values, keep_values,
     norm_rows) = forward_all(
        plan, total_cells, first_piece, small, wide[plan.hp:], profiles,
        jnp.swapaxes(retained_unit_flags, 1, 2), draws)
    picker = (jnp.arange(measured_flags.shape[0], dtype=jnp.int32)[:, None]
              == experiment_labels[None, :]).astype(jnp.bfloat16)
    output, output_grad, readout_part, upstream, losses = output_all(
        plan, readout_all, layers, profiles, measured_flags, picker)
    def frames(product):
        padded = pad_to(product, plan.hh, max(product.shape[1], max(plan.frame_start) + plan.frame))
        return jnp.concatenate(
            [padded[:, s:s + plan.frame] for s in plan.frame_start], axis=1).astype(jnp.bfloat16)

    if plan.fits:
        readout_sum, sums, small_part, grad_one = backward_all(
            plan, total_cells, readout_part, upstream, small_all, layers, scaled_values, keep_values,
            sample, norm_rows, losses, center, log_var, draws)
        loss_sum = sums[0, 2, 0]
        gains_sum, shifts_sum = [sums[k, 1] for k in range(4)], [sums[k, 0] for k in range(4)]
        embed_sum, small_sum, row, lifting_own = embed_all_sums(
            plan, total_cells, small_part, profiles, grad_one, readout_sum)
    else:
        diverge = 0.5 * jnp.sum(jnp.exp(log_var) + center * center - 1.0 - log_var)
        own_loss = 0.5 * jnp.sum(losses) + kl_weight * diverge
        parts = small_all.reshape(plan.hh, ny, plan.small)
        encoder_all = parts[:, :, plan.o2:plan.o2 + plan.midp].reshape(plan.hh, plan.hh)
        decoder_all = parts[:, :, plan.o4:plan.o4 + plan.midp].reshape(plan.hh, plan.hh)
        projector_all = parts[:, :, plan.op:plan.op + plan.moments].reshape(plan.hh, 2 * plan.latent)
        lifting_all = parts[:, 0, plan.ol:plan.ol + plan.latent]
        rows = parts[:, 0, plan.ol + plan.latent:plan.ol + plan.latent + 8].astype(jnp.float32)
        gains = [rows[:, k:k + 1] for k in range(4)]
        biases = [rows[:, 4 + k:5 + k] for k in range(4)]

        spread = jnp.exp(0.5 * log_var)

        def kept_layer(k):
            inverse = lax.rsqrt(norm_rows[k, 1] / total_cells + norm_eps)[:, None]
            return layers[k], gains[k] * scaled_values[k] + biases[k], scaled_values[k], inverse

        one, two, three, four = (kept_layer(k) for k in range(4))

        def backward_layer(upstream, kept, k, loss, ident):
            _, normed, scaled, inverse = kept
            sigma = jax.nn.sigmoid(normed)
            slope = upstream * keep_values[k].astype(jnp.float32) * sigma * (
                1.0 + normed * (1.0 - sigma))
            pair = jnp.stack([jnp.sum(slope, axis=1), jnp.sum(slope * scaled, axis=1),
                              jnp.full((plan.hh,), loss)])
            merged = meet_all(plan, pair, merge_sums, 2)
            shift, gain = merged[0], merged[1]
            grad = gains[k] * inverse * (
                slope - (shift[:, None] + scaled * gain[:, None]) / total_cells)
            return grad.astype(jnp.bfloat16), gain, shift, merged[2, 0]

        grad_four, gain_four, shift_four, loss_sum = backward_layer(upstream, four, 3, own_loss, 5)
        upstream = over_rows(decoder_all, grad_four)
        grad_three, gain_three, shift_three, _ = backward_layer(upstream, three, 2, own_loss, 6)
        sample_grad = over_rows(lifting_all, grad_three)[:plan.latent]
        center_grad = sample_grad + kl_weight * center
        logvar_grad = sample_grad * 0.5 * spread * draws + kl_weight * 0.5 * (jnp.exp(log_var) - 1.0)
        moment_grad = jnp.concatenate([center_grad, logvar_grad], axis=0).astype(jnp.bfloat16)
        upstream = rows_dot(projector_all, moment_grad)
        grad_two, gain_two, shift_two, _ = backward_layer(upstream, two, 1, own_loss, 7)
        upstream = over_rows(encoder_all, grad_two)
        grad_one, gain_one, shift_one, _ = backward_layer(upstream, one, 0, own_loss, 8)
        gains_sum = [gain_one, gain_two, gain_three, gain_four]
        shifts_sum = [shift_one, shift_two, shift_three, shift_four]
        encoder_part = over_cells(grad_two, one[0]).reshape(plan.hh, ny, plan.midp)
        decoder_part = over_cells(grad_four, three[0]).reshape(plan.hh, ny, plan.midp)
        projector_part = over_cells(two[0], moment_grad).reshape(plan.hh, ny, plan.moments)
        lifting_part = over_cells(grad_three, sample)[:, :plan.latent]

        def lanes(value, width):
            return jnp.pad(value, ((0, 0), (0, 0), (0, width - value.shape[2])))

        small_part = jnp.concatenate([
            lanes(encoder_part, plan.midl), lanes(decoder_part, plan.midl),
            lanes(projector_part, plan.ml),
            jnp.broadcast_to(pad_to(lifting_part, plan.hh, plan.ll)[:, None, :], (plan.hh, ny, plan.ll)),
        ], axis=2).reshape(plan.hh, ny * plan.small).astype(jnp.bfloat16)
        embed_part = frames(over_cells(grad_one, profiles))

        readout_sum = reduce_all(plan, frames(readout_part), 1.0 / total_cells, 3)
        small_sum = reduce_all(plan, small_part, 1.0 / total_cells, 4)
        embed_sum = reduce_all(plan, embed_part, 1.0 / total_cells, 3)

        row, lifting_own = share_all(plan, jnp.concatenate([
            readout_sum[plan.h:plan.h + 1],
            small_sum[plan.h:plan.h + 1, plan.op:plan.op + plan.ml]], axis=1),
            small_sum[:, plan.ol:plan.ol + plan.ll], 5)
    input_grad = input_all(plan, embed_all, grad_one, output_grad)

    starts = jnp.array([plan.g * j - plan.frame_start[j] for j in range(ny)], jnp.int32)
    readout_own = lax.dynamic_slice_in_dim(readout_sum, starts[gy], plan.g, 1)
    embed_own = lax.dynamic_slice_in_dim(embed_sum, starts[gy], plan.g, 1)
    baseline_own = lax.dynamic_slice_in_dim(row[0, :plan.frame], starts[gy], plan.g, 0)

    def own_units(values):
        stack = jnp.stack(values, axis=0) / total_cells
        return lax.dynamic_slice_in_dim(stack, gx * plan.hp, plan.h, 1)

    small_h = small_sum[:plan.h]
    return (
        output.T,
        center.T,
        loss_sum / total_cells,
        input_grad.T,
        embed_own[:plan.h].T,
        middle_back(plan, small_sum[:, plan.o2:plan.o2 + plan.midl]),
        small_h[:, plan.op:plan.op + plan.moments],
        row[0, plan.frame:plan.frame + plan.moments],
        lifting_own[:plan.h, :plan.latent].T,
        middle_back(plan, small_sum[:, plan.o4:plan.o4 + plan.midl]),
        readout_own[:plan.h],
        baseline_own,
        own_units(gains_sum),
        own_units(shifts_sum),
    )


def solution(mesh):
    return jax.shard_map(
        functools.partial(on_device, mesh.shape["gx"], mesh.shape["gy"]),
        mesh=mesh,
        in_specs=(
            P(("gx", "gy"), None),
            P(("gx", "gy")),
            P(),
            P(None, ("gx", "gy"), None),
            P(("gx", "gy"), None),
            P("gy", "gx"),
            P("gy", "gx"),
            P("gx", "gy"),
            P("gy"),
            P(None, "gx"),
            P("gy", "gx"),
            P("gx", "gy"),
            P("gy"),
            P(None, "gx"),
            P(None, "gx"),
        ),
        out_specs=(
            P(("gx", "gy"), None),
            P(("gx", "gy"), None),
            P(),
            P(("gx", "gy"), None),
            P("gy", "gx"),
            P("gy", "gx"),
            P("gx", "gy"),
            P("gy"),
            P(None, "gx"),
            P("gy", "gx"),
            P("gx", "gy"),
            P("gy"),
            P(None, "gx"),
            P(None, "gx"),
        ),
        check_vma=False,
    )
```

```python
import functools

import jax
import jax.numpy as jnp
from jax import lax
from jax.experimental import pallas as pl
from jax.experimental.pallas import tpu as pltpu
from jax.sharding import PartitionSpec as P

norm_eps = 1e-05
keep_scale = 1.25
kl_weight = 5e-05
MESH = pl.DeviceIdType.MESH
LANES = 128


def round_up(value, multiple):
    return -(-value // multiple) * multiple


class Plan:
    def __init__(self, nx, ny, cells, genes_piece, hidden_piece, latent):
        self.nx, self.ny, self.cells = nx, ny, cells
        self.g, self.h, self.latent = genes_piece, hidden_piece, latent
        self.genes, self.hidden = genes_piece * ny, hidden_piece * nx
        self.hp = round_up(hidden_piece + 1, 16)
        self.hh = self.hp * nx
        tiles = round_up(self.genes, LANES) // LANES
        self.gp = round_up(tiles, ny) // ny * LANES
        self.gg = self.gp * ny
        self.shift = self.gp - self.g
        self.strip = round_up(self.shift * (ny - 1), LANES)
        starts = [self.g * j // LANES for j in range(ny)]
        ends = [round_up(self.g * (j + 1), LANES) // LANES for j in range(ny)]
        self.frame_start = [s * LANES for s in starts]
        self.frame = max(e - s for s, e in zip(starts, ends)) * LANES
        self.groups = nx // ny
        self.mid = self.hidden // ny
        self.midp = self.hp * self.groups
        self.midl = round_up(self.midp, LANES)
        self.moments = 2 * latent // ny
        self.ml = round_up(self.moments, LANES)
        self.ll = round_up(latent + 8, LANES)
        self.small = 2 * self.midl + self.ml + self.ll
        self.o2, self.o4 = 0, self.midl
        self.op, self.ol = 2 * self.midl, 2 * self.midl + self.ml
        self.blocks = nx * ny
        rows = round_up(self.hp * 2 // 3, 16)
        self.cuts = ((0, rows), (rows, self.hp - rows)) if rows < self.hp else ((0, rows),)
        self.whole_cuts = ((0, self.hp),)
        self.fits = self.blocks <= 32 and self.hh * ny * self.frame <= 7 * 1024 * 1024


class Flow:
    def __init__(self, plan, kind):
        gx, gy = lax.axis_index("gx"), lax.axis_index("gy")
        self.plan, self.gx, self.gy = plan, gx, gy
        self.sizes = (plan.ny // 2, plan.nx // 2, 2)
        self.core = lax.rem(gy, 2)
        self.at = (gy // 2, gx // 2, lax.rem(gx, 2))
        self.orders = (((0, 1, 2), (2, 1, 0)), ((1, 2, 0), (1, 0, 2)))[kind]
        first, second = self.orders
        self.most = tuple(max(self.sizes[i], self.sizes[j]) for i, j in zip(first, second))
        self.least = tuple(min(self.sizes[i], self.sizes[j]) for i, j in zip(first, second))
        self.limit = tuple(self.pick(self.sizes[i], self.sizes[j]) for i, j in zip(first, second))
        self.here = tuple(self.pick(self.at[i], self.at[j]) for i, j in zip(first, second))

    def pick(self, zero, one):
        if isinstance(zero, int) and isinstance(one, int) and zero == one:
            return zero
        return jnp.where(self.core == 0, zero, one)

    def device(self, spot):
        place = [None] * 3
        for axis in range(3):
            place[axis] = self.pick(
                spot[self.orders[0].index(axis)], spot[self.orders[1].index(axis)]
            )
        return (place[1] * 2 + place[2], place[0] * 2 + self.core)

    def twin(self):
        return (self.gx, self.gy + 1 - 2 * self.core)

    def step(self, axis, sign):
        to = self.here[axis] + sign
        spot = tuple(to if i == axis else self.here[i] for i in range(3))
        return jnp.logical_and(to >= 0, to < self.limit[axis]), self.device(spot)


def neighbours(plan):
    flow = Flow(plan, 0)
    out = [(None, flow.twin())]
    for axis in range(3):
        for sign in (-1, 1):
            out.append(flow.step(axis, sign))
    return out


def when(condition):
    return (lambda f: f()) if condition is None else pl.when(condition)


def greet(plan, extra=()):
    barrier = pltpu.get_barrier_semaphore()
    count = jnp.int32(len(extra))
    for there, device in neighbours(plan):
        @when(there)
        def _(device=device):
            pl.semaphore_signal(barrier, inc=1, device_id=device, device_id_type=MESH)
        count = count + (1 if there is None else there.astype(jnp.int32))
    for device in extra:
        pl.semaphore_signal(barrier, inc=1, device_id=device, device_id_type=MESH)
    pl.semaphore_wait(barrier, count)


class Gather:
    def __init__(self, plan, source, target, width, send_sem, recv_sem):
        self.plan, self.source, self.target, self.width = plan, source, target, width
        self.send_sem, self.recv_sem = send_sem, recv_sem
        self.cuts = [(Flow(plan, kind), *cut) for kind, cut in enumerate(plan.cuts)]
        self.phases = 1 + max(sum(m - 1 for m in cut[0].most) for cut in self.cuts)

    def slot(self, cut, gx, gy):
        _, start, rows = cut
        return self.target.at[
            pl.ds(pl.multiple_of(gx * self.plan.hp + start, 16), rows),
            pl.ds(pl.multiple_of(gy * self.width, LANES), self.width),
        ]

    def own_copy(self, sem):
        plan = self.plan
        gx, gy = lax.axis_index("gx"), lax.axis_index("gy")
        place = self.target.at[
            pl.ds(pl.multiple_of(gx * plan.hp, 16), plan.hp),
            pl.ds(pl.multiple_of(gy * self.width, LANES), self.width),
        ]
        return pltpu.make_async_copy(self.source, place, sem)

    def copies(self, kind, cut, spot, own):
        flow = cut[0]
        gx, gy = flow.device(spot)
        dst = self.slot(cut, gx, gy)
        src = self.source.at[pl.ds(cut[1], cut[2]), :] if own else dst
        index = gx * (self.plan.ny // 2) + gy // 2
        goals = [(None, flow.twin(), 6)]
        level = None
        for axis in (2, 1, 0):
            for sign in (-1, 1):
                if flow.most[axis] < 2:
                    continue
                there, device = flow.step(axis, sign)
                if not own:
                    there = there & ((flow.here[axis] - spot[axis]) * sign >= 0)
                    if level is not None:
                        there = there & level
                goals.append((there, device, 2 * axis + (sign + 1) // 2))
            same = spot[axis] == flow.here[axis]
            level = same if level is None else level & same
        out = []
        for there, device, k in goals:
            out.append((there, pltpu.make_async_remote_copy(
                src_ref=src, dst_ref=dst,
                send_sem=self.send_sem.at[kind, index, k],
                recv_sem=self.recv_sem.at[kind, gx * self.plan.ny + gy],
                device_id=device, device_id_type=MESH,
            )))
        return out

    def arrived(self, kind, cut, gx, gy):
        ref = self.slot(cut, gx, gy)
        pltpu.make_async_copy(ref, ref, self.recv_sem.at[kind, gx * self.plan.ny + gy]).wait()

    def start_own(self):
        for kind, cut in enumerate(self.cuts):
            for there, copy in self.copies(kind, cut, cut[0].here, True):
                when(there)(copy.start)

    def walk(self, visit, phase=None, only=None, part=(0, 1)):
        for kind, cut in enumerate(self.cuts):
            if only is not None and kind != only:
                continue
            flow = cut[0]
            mp, mq, mr = flow.most
            total = mp * mq * mr

            def one(n, _, kind=kind, cut=cut, flow=flow):
                spot = (lax.rem(n, mp), lax.rem(n // mp, mq), n // (mp * mq))
                hops, good = 0, None
                for here, limit, at in zip(flow.here, flow.limit, spot):
                    hops = hops + jnp.abs(at - here)
                    good = at < limit if good is None else good & (at < limit)
                good = good & ((hops > 0) if phase is None else (hops == phase))
                pl.when(good)(functools.partial(visit, kind, cut, spot))
                return 0
            lax.fori_loop(total * part[0] // part[1], total * (part[0] + 1) // part[1], one, 0)

    def visit(self, kind, cut, spot):
        self.arrived(kind, cut, *cut[0].device(spot))
        for there, copy in self.copies(kind, cut, spot, False):
            when(there)(copy.start)

    def forward(self, phase):
        if phase < self.phases:
            self.walk(self.visit, phase)

    def items(self, parts):
        return [functools.partial(self.walk, self.visit, phase, kind, (i, parts))
                for phase in range(1, self.phases) for i in range(parts)
                for kind in range(len(self.cuts))]

    def finish_twin(self):
        plan = self.plan
        for kind, cut in enumerate(self.cuts):
            flow = cut[0]
            def one(n, _, kind=kind, cut=cut, flow=flow):
                gx, y = n // (plan.ny // 2), lax.rem(n, plan.ny // 2)
                self.arrived(kind, cut, gx, 2 * y + 1 - flow.core)
                return 0
            lax.fori_loop(0, plan.blocks // 2, one, 0)

    def finish_sends(self):
        for kind, cut in enumerate(self.cuts):
            for there, copy in self.copies(kind, cut, cut[0].here, True):
                when(there)(copy.wait_send)
        def visit(kind, cut, spot):
            for there, copy in self.copies(kind, cut, spot, False):
                when(there)(copy.wait_send)
        self.walk(visit)


class Meet:
    def __init__(self, plan, wide, tall, send_sem, recv_sem):
        self.plan, self.wide, self.tall = plan, wide, tall
        self.send_sem, self.recv_sem = send_sem, recv_sem
        self.gx, self.gy = lax.axis_index("gx"), lax.axis_index("gy")

    @staticmethod
    def peers(plan):
        gx, gy = lax.axis_index("gx"), lax.axis_index("gy")
        return ([(lax.rem(gx + k, plan.nx), gy) for k in range(1, plan.nx)]
                + [(gx, lax.rem(gy + k, plan.ny)) for k in range(1, plan.ny)])

    def copies(self, second):
        plan = self.plan
        n = plan.ny if second else plan.nx
        ref = self.tall if second else self.wide
        own = self.gy if second else self.gx
        out = []
        for k in range(1, n):
            to = lax.rem(own + k, n)
            at = (plan.nx - 1 if second else 0) + k - 1
            out.append(pltpu.make_async_remote_copy(
                src_ref=ref.at[own], dst_ref=ref.at[own],
                send_sem=self.send_sem.at[at], recv_sem=self.recv_sem.at[at],
                device_id=(self.gx, to) if second else (to, self.gy), device_id_type=MESH,
            ))
        return out

    def run(self, value, merge, members, between=None):
        plan = self.plan
        for second in (False, True):
            ref = self.tall if second else self.wide
            ref[self.gy if second else self.gx] = value
            copies = self.copies(second)
            for copy in copies:
                copy.start()
            if between is not None:
                between(second)
            for copy in copies:
                copy.wait_recv()
            value = merge([ref[i] for i in range(ref.shape[0])], members)
            members = members * plan.nx
            for copy in copies:
                copy.wait_send()
        return value


def merge_sums(parts, members):
    total = parts[0]
    for part in parts[1:]:
        total = total + part
    return total


def merge_moments(parts, members):
    n = len(parts)
    mean = merge_sums([part[0:1] for part in parts], 0) / n
    squares = merge_sums([part[1:2] for part in parts], 0)
    between = merge_sums([(part[0:1] - mean) * (part[0:1] - mean) for part in parts], 0)
    return jnp.concatenate([mean, squares + members * between], axis=0)


def tiled(column, plan):
    return jnp.concatenate([column] * (plan.cells // LANES), axis=1)


def lane_sums(value):
    total = value[:, :LANES]
    for at in range(LANES, value.shape[1], LANES):
        total = total + value[:, at:at + LANES]
    return total


def as_row(value):
    return jnp.sum(value.T, axis=0, keepdims=True)


def as_column(row):
    return jnp.broadcast_to(row, (LANES, LANES)).T


def aligned(start, rows=LANES):
    return pl.ds(pl.multiple_of(start, rows), rows)


def moment_rows(plan, h_ref, row_ref):
    def block(i, _):
        value = h_ref[aligned(i * LANES), :]
        sums = lane_sums(value)
        mean = jnp.sum(sums, axis=1, keepdims=True) / plan.cells
        offset = value - mean
        row_ref[0:1, aligned(i * LANES)] = as_row(sums) / plan.cells
        row_ref[1:2, aligned(i * LANES)] = as_row(lane_sums(offset * offset))
        return 0
    lax.fori_loop(0, plan.hh // LANES, block, 0)


def unit_column(slab_ref, i, at):
    slab = slab_ref[aligned(i * LANES), :]
    return jnp.broadcast_to(slab.astype(jnp.float32)[:, at:at + 1], (LANES, LANES))


def activate(plan, k, h_ref, row_ref, slab_ref, keep_ref, out_ref, column_ref, total_cells, spare,
             tick=lambda: None):
    def block(i, _):
        column_ref[0] = as_column(row_ref[0:1, aligned(i * LANES)])
        column_ref[1] = as_column(lax.rsqrt(row_ref[1:2, aligned(i * LANES)] / total_cells + norm_eps))
        column_ref[2] = unit_column(slab_ref, i, k)
        column_ref[3] = unit_column(slab_ref, i, 4 + k)

        def chunk(j, _):
            rows = aligned(i * LANES + j * 16, 16)
            mean, inverse, gain, bias = (
                tiled(column_ref[n, aligned(j * 16, 16), :], plan) for n in range(4))
            scaled = (h_ref[rows, :] - mean) * inverse
            h_ref[rows, :] = scaled
            normed = gain * scaled + bias
            active = normed * jax.nn.sigmoid(normed) * keep_ref[k, rows, :].astype(jnp.float32)
            if spare:
                row = lax.broadcasted_iota(jnp.int32, active.shape, 0) + (i * LANES + j * 16)
                active = jnp.where(lax.rem(row, plan.hp) == plan.h, 1.0, active)
            out_ref[rows, :] = active.astype(jnp.bfloat16)
            return 0
        lax.fori_loop(0, LANES // 16, chunk, 0)
        return 0
    cut = plan.hh // LANES // 2
    lax.fori_loop(0, cut, block, 0)
    tick()
    lax.fori_loop(cut, plan.hh // LANES, block, 0)


def keep_rows(plan, flags_ref, keep_ref, k):
    def lane(t, _):
        lanes = aligned(t * LANES)
        for group in range(plan.nx):
            for start in range(0, plan.hp, 16):
                at = group * plan.h + start
                value = flags_ref[at:at + 16, lanes].astype(jnp.float32) * keep_scale
                if start + 16 > plan.h:
                    row = lax.broadcasted_iota(jnp.int32, value.shape, 0)
                    value = jnp.where(row < plan.h - start, value, 0.0)
                at = group * plan.hp + start
                keep_ref[k, at:at + 16, lanes] = value.astype(jnp.bfloat16)
        return 0
    lax.fori_loop(0, plan.cells // LANES, lane, 0)


def forward_kernel(plan, total_cells, *refs):
    (w1, wsmall, wout, x_hbm, flags_hbm, draws_ref,
     embed_all, small_out, readout_all, center_out, log_var_out, sample_out, layers_out, scaled_out,
     keep_out, rows_out,
     w1_ref, small_ref, x_ref, keep_ref, flags_ref, h_ref, layer_ref, column_ref, latent_ref,
     wide, tall, send_sem, recv_sem, meet_send, meet_recv, own_sem, load_sem, flag_sem, out_sem) = refs
    mid = plan.midp
    load = pltpu.make_async_copy(x_hbm, x_ref, load_sem)
    deep = flags_ref.shape[0]

    def flags(k):
        return pltpu.make_async_copy(
            flags_hbm.at[k], flags_ref.at[k % deep, pl.ds(0, plan.hidden), :], flag_sem.at[k % deep])

    for k in range(deep):
        flags(k).start()
    load.start()
    sets = send_sem.shape[0]
    embed, small, readout = (
        Gather(plan, source, target, width, send_sem.at[u % sets], recv_sem.at[u])
        for u, (source, target, width) in enumerate((
            (w1, w1_ref, plan.gp), (wsmall, small_ref, plan.small), (wout, readout_all, plan.gp))))
    own = [g.own_copy(own_sem.at[u]) for u, g in enumerate((embed, small, readout))]
    for copy in own:
        copy.start()
    peers = Meet.peers(plan)
    barrier = pltpu.get_barrier_semaphore()
    for device in peers:
        pl.semaphore_signal(barrier, inc=1, device_id=device, device_id_type=MESH)
    pl.semaphore_wait(barrier, len(peers))

    def keepers(k):
        flags(k).wait()
        keep_rows(plan, flags_ref.at[k % deep], keep_ref, k)
        if k + deep < 4:
            flags(k + deep).start()

    embed.start_own()
    late = embed.phases - 2
    for phase in range(1, embed.phases):
        if phase <= 4:
            keepers(phase - 1)
        if phase == late:
            if sets == 1:
                pass
            else:
                small.start_own()
        embed.forward(phase)
    for k in range(embed.phases - 1, 4):
        keepers(k)
    if sets == 1:
        embed.finish_sends()
        small.start_own()
    load.wait()
    tail = layer_ref.shape[1] - plan.hh
    slots = layer_ref.shape[0]
    for k in range(slots):
        if tail:
            layer_ref[k, plan.hh:, :] = jnp.zeros((tail, plan.cells), jnp.bfloat16)
    latent_ref[...] = jnp.zeros_like(latent_ref)
    latent_ref[2, 0:plan.latent, :] = draws_ref[...]
    own[0].wait()
    embed.finish_twin()
    outs = [pltpu.make_async_copy(w1_ref, embed_all, out_sem.at[0])]
    outs[0].start()

    queue = [] if sets == 1 else small.items(2)
    marks = {}
    if sets > 1:
        queue.insert(5, readout.start_own)
        marks["small"] = len(queue)
        queue += readout.items(2)
    total = len(queue)

    def tick(count=1):
        for _ in range(count):
            if queue:
                queue.pop(0)()

    half_rows = plan.hh // 2
    for j in range(plan.ny):
        start, stop = j * plan.gp, min((j + 1) * plan.gp, plan.genes)
        for top in (0, half_rows):
            part = rows_dot(w1_ref[top:top + half_rows, start:stop], x_ref[start:stop, :])
            spot = pl.ds(top, half_rows)
            h_ref[0, spot, :] = part if j == 0 else h_ref[0, spot, :] + part
            tick()

    layer_writes = []

    def norm(k, spare):
        h = h_ref.at[k % 2]
        moment_rows(plan, h, rows_out.at[k])
        meet = Meet(plan, wide.at[k], tall.at[k], meet_send.at[k], meet_recv.at[k])
        rows_out[k] = meet.run(rows_out[k], merge_moments, float(plan.cells), lambda second: tick(2))
        slab = w1_ref.at[:, pl.ds(plan.gg - LANES, LANES)]
        if k >= slots:
            finish(layer_writes[k - slots])
        activate(plan, k, h, rows_out.at[k], slab, keep_ref, layer_ref.at[k % slots], column_ref,
                 total_cells, spare, tick)
        for n, (source, target) in enumerate((
                (h, scaled_out.at[k]),
                (layer_ref.at[k % slots, pl.ds(0, plan.hh), :], layers_out.at[k]),
                (keep_ref.at[k], keep_out.at[k]))):
            outs.append(pltpu.make_async_copy(source, target, out_sem.at[3 + 3 * k + n]))
            outs[-1].start()
        layer_writes.append(outs[-2])
        return outs[-3]

    def finish(copy):
        copy.wait()
        outs[:] = [other for other in outs if other is not copy]

    def whole_small():
        if sets > 1:
            while total - len(queue) < marks["small"]:
                tick()
        else:
            for item in small.items(1):
                item()
        own[1].wait()
        small.finish_twin()
        if sets == 1:
            small.finish_sends()
            readout.start_own()
            queue.extend(readout.items(1))
        outs.append(pltpu.make_async_copy(small_ref, small_out, out_sem.at[1]))
        outs[-1].start()
        own[2].wait()

    def hidden(source, lane, target):
        for j in range(plan.ny):
            at = j * plan.small + lane
            part = rows_dot(small_ref[:, at:at + plan.midl], source[mid * j:mid * j + plan.midl, :])
            target[...] = part if j == 0 else target[...] + part

    wrote_one = norm(0, False)
    whole_small()
    hidden(layer_ref.at[0], plan.o2, h_ref.at[1])
    wrote_two = norm(1, True)
    half = plan.ny // 2
    for j in range(plan.ny):
        at = j * plan.small + plan.op
        part = over_rows(small_ref[:, at:at + plan.ml], layer_ref[1, 0:plan.hh, :])
        spot = (j % half) * plan.moments
        latent_ref[j // half, spot:spot + plan.moments, :] = part[:plan.moments]
    center, log_var = latent_ref[0], latent_ref[1]
    sample = center + jnp.exp(0.5 * log_var) * latent_ref[2]
    row = lax.broadcasted_iota(jnp.int32, sample.shape, 0)
    sample_out[...] = jnp.where(row < plan.latent, sample, 0.0).astype(jnp.bfloat16)
    center_out[...] = latent_ref[0, 0:plan.latent, :]
    log_var_out[...] = latent_ref[1, 0:plan.latent, :]
    finish(wrote_one)
    h_ref[0] = rows_dot(small_ref[:, plan.ol:plan.ol + plan.ll], sample_out[...])
    norm(2, False)
    finish(wrote_two)
    hidden(layer_ref.at[2 % slots], plan.o4, h_ref.at[1])
    norm(3, True)
    while queue:
        tick()
    readout.finish_twin()
    if sets > 1:
        embed.finish_sends()
        small.finish_sends()
    readout.finish_sends()
    for copy in outs:
        copy.wait()


def forward_all(plan, total_cells, w1, wsmall, wout, profiles, flags, draws):
    any_spec, vmem = pl.BlockSpec(memory_space=pl.ANY), pl.BlockSpec(memory_space=pltpu.VMEM)
    f32, bf16 = jnp.float32, jnp.bfloat16
    n = plan.nx + plan.ny - 2
    cuts = len(plan.cuts)
    sets = 3 if plan.blocks <= 32 else 1
    shape = jax.ShapeDtypeStruct
    return pl.pallas_call(
        functools.partial(forward_kernel, plan, total_cells),
        out_shape=[
            shape((plan.hh, plan.gg), bf16), shape((plan.hh, plan.ny * plan.small), bf16),
            shape((plan.hh, plan.gg), bf16), shape((plan.latent, plan.cells), f32),
            shape((plan.latent, plan.cells), f32), shape((plan.ll, plan.cells), bf16),
            shape((4, plan.hh, plan.cells), bf16), shape((4, plan.hh, plan.cells), f32),
            shape((4, plan.hh, plan.cells), bf16), shape((4, 2, plan.hh), f32)],
        in_specs=[any_spec] * 5 + [vmem],
        out_specs=[any_spec] * 3 + [vmem] * 3 + [any_spec] * 3 + [vmem],
        scratch_shapes=[
            pltpu.VMEM((plan.hh, plan.gg), bf16),
            pltpu.VMEM((plan.hh, plan.ny * plan.small), bf16),
            pltpu.VMEM((plan.genes, plan.cells), bf16),
            pltpu.VMEM((4, plan.hh, plan.cells), bf16),
            pltpu.VMEM((2 if sets > 1 else 1, plan.hidden + 16, plan.cells), jnp.int32),
            pltpu.VMEM((2, plan.hh, plan.cells), f32),
            pltpu.VMEM((4 if sets > 1 else 2, plan.hh + plan.midl - plan.midp, plan.cells), bf16),
            pltpu.VMEM((4, LANES, LANES), f32),
            pltpu.VMEM((3, plan.ll, plan.cells), f32),
            pltpu.VMEM((4, plan.nx, 2, plan.hh), f32),
            pltpu.VMEM((4, plan.ny, 2, plan.hh), f32),
            pltpu.SemaphoreType.DMA((sets, cuts, plan.blocks // 2, 7)),
            pltpu.SemaphoreType.DMA((3, cuts, plan.blocks)),
            pltpu.SemaphoreType.DMA((4, n)),
            pltpu.SemaphoreType.DMA((4, n)),
            pltpu.SemaphoreType.DMA((3,)),
            pltpu.SemaphoreType.DMA,
            pltpu.SemaphoreType.DMA((2,)),
            pltpu.SemaphoreType.DMA((15,)),
        ],
        compiler_params=pltpu.CompilerParams(
            collective_id=0, has_side_effects=True, vmem_limit_bytes=60 * 1024 * 1024),
    )(w1, wsmall, wout, profiles, flags, draws)


def meet_kernel(plan, merge, x_ref, o_ref, wide, tall, send_sem, recv_sem):
    peers = Meet.peers(plan)
    barrier = pltpu.get_barrier_semaphore()
    for device in peers:
        pl.semaphore_signal(barrier, inc=1, device_id=device, device_id_type=MESH)
    pl.semaphore_wait(barrier, len(peers))
    meet = Meet(plan, wide, tall, send_sem, recv_sem)
    o_ref[...] = meet.run(x_ref[...], merge, float(plan.cells))


def meet_all(plan, value, merge, collective_id):
    rows, width = value.shape
    n = plan.nx + plan.ny - 2
    return pl.pallas_call(
        functools.partial(meet_kernel, plan, merge),
        out_shape=jax.ShapeDtypeStruct(value.shape, jnp.float32),
        in_specs=[pl.BlockSpec(memory_space=pltpu.VMEM)],
        out_specs=pl.BlockSpec(memory_space=pltpu.VMEM),
        scratch_shapes=[
            pltpu.VMEM((plan.nx, rows, width), jnp.float32),
            pltpu.VMEM((plan.ny, rows, width), jnp.float32),
            pltpu.SemaphoreType.DMA((n,)),
            pltpu.SemaphoreType.DMA((n,)),
        ],
        compiler_params=pltpu.CompilerParams(collective_id=collective_id, has_side_effects=True),
    )(value)


def share_kernel(plan, row_ref, block_ref, row_out, block_out, wide, tall, send_sem, recv_sem):
    peers = Meet.peers(plan)
    barrier = pltpu.get_barrier_semaphore()
    for device in peers:
        pl.semaphore_signal(barrier, inc=1, device_id=device, device_id_type=MESH)
    pl.semaphore_wait(barrier, len(peers))
    meet = Meet(plan, wide, tall, send_sem, recv_sem)
    wide[meet.gx] = row_ref[...]
    tall[meet.gy] = block_ref[...]
    copies = meet.copies(False) + meet.copies(True)
    for copy in copies:
        copy.start()
    for copy in copies:
        copy.wait_recv()
    row_out[...] = wide[0]
    block_out[...] = tall[0]
    for copy in copies:
        copy.wait_send()


def share_all(plan, row, block, collective_id):
    n = plan.nx + plan.ny - 2
    return pl.pallas_call(
        functools.partial(share_kernel, plan),
        out_shape=[jax.ShapeDtypeStruct(row.shape, jnp.float32),
                   jax.ShapeDtypeStruct(block.shape, jnp.float32)],
        in_specs=[pl.BlockSpec(memory_space=pltpu.VMEM)] * 2,
        out_specs=[pl.BlockSpec(memory_space=pltpu.VMEM)] * 2,
        scratch_shapes=[
            pltpu.VMEM((plan.nx, *row.shape), jnp.float32),
            pltpu.VMEM((plan.ny, *block.shape), jnp.float32),
            pltpu.SemaphoreType.DMA((n,)),
            pltpu.SemaphoreType.DMA((n,)),
        ],
        compiler_params=pltpu.CompilerParams(collective_id=collective_id, has_side_effects=True),
    )(row, block)


class Reduce:
    def __init__(self, plan, width, part, twin, slots, send_sem, twin_sem, recv_sem, flow=0):
        self.first = flow
        self.plan, self.width, self.part, self.twin, self.slots = plan, width, part, twin, slots
        self.send_sem, self.twin_sem, self.recv_sem = send_sem, twin_sem, recv_sem
        self.cuts = [(Flow(plan, flow), *cut) for cut in plan.whole_cuts]

    @staticmethod
    def slot_counts(plan, flow):
        counts = []
        for kind in (flow,):
            sizes = (plan.ny // 2, plan.nx // 2, 2)
            first, second = (((0, 1, 2), (2, 1, 0)), ((1, 2, 0), (1, 0, 2)))[kind]
            mp, mq, mr = (max(sizes[i], sizes[j]) for i, j in zip(first, second))
            a, b, c = (Reduce.sides(m) for m in (mp, mq, mr))
            far_r = (mr > 2) * (mr * mq * mp)
            counts.append((far_r, mq * mp * (c + (mq > 2)), mp * (c + b + (mp > 2)), c + b + a))
        return counts

    @staticmethod
    def sides(most):
        return 1 if most == 2 else (2 if most > 2 else 0)

    def block(self, ref, cut, gx, gy):
        return ref.at[
            pl.ds(pl.multiple_of(gx * self.plan.hp + cut[1], 16), cut[2]),
            pl.ds(pl.multiple_of(gy * self.width, LANES), self.width),
        ]

    def twin_block(self, cut, gx, y):
        return self.twin.at[
            pl.ds(pl.multiple_of(gx * self.plan.hp + cut[1], 16), cut[2]),
            pl.ds(pl.multiple_of(y * self.width, LANES), self.width),
        ]

    def twin_copy(self, kind, cut, gx, y):
        flow = cut[0]
        return pltpu.make_async_remote_copy(
            src_ref=self.block(self.part, cut, gx, 2 * y + 1 - flow.core),
            dst_ref=self.twin_block(cut, gx, y),
            send_sem=self.twin_sem.at[0, kind, gx * (self.plan.ny // 2) + y],
            recv_sem=self.twin_sem.at[1, kind, gx * (self.plan.ny // 2) + y],
            device_id=flow.twin(), device_id_type=MESH,
        )

    def each_twin(self, visit, ys=None):
        ny2 = self.plan.ny // 2
        a, na = self.cuts[0][0].at[1], self.plan.nx // 2

        def along(n, _):
            to = a + (na - 1 - n // 2) * (1 - 2 * lax.rem(n, 2))

            @pl.when((to >= 0) & (to < na))
            def _():
                for kind, cut in enumerate(self.cuts):
                    def one(i, _, kind=kind, cut=cut):
                        visit(self.twin_copy(kind, cut, to * 2 + i // ny2, lax.rem(i, ny2)))
                        return 0
                    lax.fori_loop(0, 2 * ny2, one, 0)
            return 0
        lax.fori_loop(0, 2 * na - 1, along, 0)

    def start_twin(self):
        self.each_twin(lambda copy: copy.start())

    def entry(self, kind, stage, spot, axis, came_from):
        flow = self.cuts[kind][0]
        mp, mq, mr = flow.most
        far_r, far_q, far_p, _ = Reduce.slot_counts(self.plan, self.first)[kind]
        sides = [Reduce.sides(m) for m in flow.most]
        dp, dq, dr = spot
        if stage == 2:
            return (dr * mq + dq) * mp + dp
        if stage == 1:
            base, which = far_r, (dq * mp + dp) * (sides[2] + (mq > 2))
        elif stage == 0:
            base, which = far_r + far_q, dp * (sides[2] + sides[1] + (mp > 2))
        else:
            base, which = far_r + far_q + far_p, 0
        offset = 0
        for later in (2, 1, 0):
            if later == stage:
                return base + which + offset
            if later == axis:
                side = 0 if sides[axis] == 1 else (came_from + 1) // 2
                return base + which + offset + side
            offset += sides[later]

    def slot(self, kind, index):
        cut = self.cuts[kind]
        total = sum(Reduce.slot_counts(self.plan, self.first)[kind])
        return self.slots[kind].at[index], self.recv_sem[kind].at[index]

    def gather_terms(self, kind, cut, spot, stage, sign):
        flow = cut[0]
        ny2 = self.plan.ny // 2
        gx, gy = flow.device(spot)
        y = gy // 2
        copy = self.twin_copy(kind, cut, gx, y)
        copy.wait_recv()
        own = self.block(self.part, cut, gx, gy)
        twin = self.twin_block(cut, gx, y)
        arrivals = []
        for axis in (2, 1, 0):
            if axis > stage:
                for side in (-1, 1):
                    there, _ = flow.step(axis, side)
                    if flow.most[axis] < 2:
                        continue
                    arrivals.append((there, self.entry(kind, stage, spot, axis, side)))
            elif axis == stage and flow.most[axis] > 2:
                away = self.here_away(flow, axis, sign)
                arrivals.append((away, self.entry(kind, stage, spot, axis, None)))
        return own, twin, arrivals

    def here_away(self, flow, axis, sign):
        to = flow.here[axis] - sign
        return (to >= 0) & (to < flow.limit[axis])

    def add_in(self, kind, cut, spot, stage, sign):
        own, twin, arrivals = self.gather_terms(kind, cut, spot, stage, sign)

        def add(other):
            def chunk(i, _):
                rows = aligned(i * 16, 16)
                own[rows, :] = own[rows, :] + other[rows, :]
                return 0
            lax.fori_loop(0, cut[2] // 16, chunk, 0)

        add(twin)
        for there, index in arrivals:
            slot, sem = self.slot(kind, index)
            @when(there)
            def _(slot=slot, sem=sem):
                pltpu.make_async_copy(slot, slot, sem).wait()
                add(slot)
        return own

    def onward(self, kind, cut, spot, stage, sign):
        flow = cut[0]
        _, device = self.toward(flow, stage, sign)
        gx, gy = flow.device(spot)
        to = flow.here[stage] + sign
        index_same = self.entry(kind, stage, spot, stage, None) if flow.most[stage] > 2 else None
        done = to == spot[stage]
        p_same = flow.here[0] == spot[0]
        q_same = flow.here[1] == spot[1]
        if stage == 2:
            deeper = jnp.where(q_same, jnp.where(p_same,
                               self.entry(kind, -1, spot, 2, -sign),
                               self.entry(kind, 0, spot, 2, -sign)),
                               self.entry(kind, 1, spot, 2, -sign))
        elif stage == 1:
            deeper = jnp.where(p_same, self.entry(kind, -1, spot, 1, -sign),
                               self.entry(kind, 0, spot, 1, -sign))
        else:
            deeper = self.entry(kind, -1, spot, 0, -sign)
        index = deeper if index_same is None else jnp.where(done, deeper, index_same)
        slot, sem = self.slot(kind, index)
        ny2 = self.plan.ny // 2
        return pltpu.make_async_remote_copy(
            src_ref=self.block(self.part, cut, gx, gy), dst_ref=slot,
            send_sem=self.send_sem.at[kind, gx * ny2 + gy // 2], recv_sem=sem,
            device_id=device, device_id_type=MESH,
        )

    def toward(self, flow, axis, sign):
        return flow.step(axis, sign)

    def order(self, kind):
        mp, mq, mr = self.cuts[kind][0].most
        out = [(2, k, far) for k in range(mr - 1, 0, -1) for far in range(mq - 1, -1, -1)]
        return out + [(stage, k, 0) for stage in (1, 0)
                      for k in range(self.cuts[kind][0].most[stage] - 1, 0, -1)]

    def walk(self, visit, kind, stage, k, far):
        cut = self.cuts[kind]
        p, q, r = cut[0].here
        np_, nq, nr = cut[0].limit
        mp, mq, mr = cut[0].most

        def one(n, _):
            dp = p + (mp - 1 - n // 2) * (1 - 2 * lax.rem(n, 2))
            for sign in (-1, 1):
                if stage == 2:
                    d = r + sign * k
                    for side in ((-1, 1) if far else (1,)):
                        dq = q + side * far
                        good = ((d >= 0) & (d < nr) & (dq >= 0) & (dq < nq)
                                & (dp >= 0) & (dp < np_))
                        pl.when(good)(functools.partial(visit, kind, cut, (dp, dq, d), stage, sign))
                    continue
                if stage == 1:
                    d = q + sign * k
                    spot, good = (dp, d, r), (d >= 0) & (d < nq) & (dp >= 0) & (dp < np_)
                else:
                    d = p + sign * k
                    spot, good = (d, q, r), (d >= 0) & (d < np_)
                pl.when(good)(functools.partial(visit, kind, cut, spot, stage, sign))
            return 0
        lax.fori_loop(0, 1 if stage == 0 else 2 * mp - 1, one, 0)

    def visit(self, kind, cut, spot, stage, sign):
        self.add_in(kind, cut, spot, stage, sign)
        self.onward(kind, cut, spot, stage, sign).start()

    def items(self):
        lines = [[functools.partial(self.walk, self.visit, kind, *step) for step in self.order(kind)]
                 for kind in range(len(self.cuts))]
        out = []
        for i in range(max(len(line) for line in lines)):
            out += [line[i] for line in lines if i < len(line)]
        return out

    def own_sum(self, out_ref, factor):
        for kind, cut in enumerate(self.cuts):
            flow = cut[0]
            own = self.add_in(kind, cut, flow.here, -1, None)
            out_ref[pl.ds(cut[1], cut[2]), :] = own[...].astype(jnp.float32) * factor

    def finish_sends(self):
        self.each_twin(lambda copy: copy.wait_send())
        def visit(kind, cut, spot, stage, sign):
            self.onward(kind, cut, spot, stage, sign).wait_send()
        for kind in range(len(self.cuts)):
            for step in self.order(kind):
                self.walk(visit, kind, *step)

    def twin_column(self, gy):
        y, flow = gy // 2, self.cuts[0][0]

        @pl.when(gy % 2 != flow.core)
        def _():
            for kind, cut in enumerate(self.cuts):
                def one(gx, _, kind=kind, cut=cut):
                    self.twin_copy(kind, cut, gx, y).start()
                    return 0
                lax.fori_loop(0, self.plan.nx, one, 0)


def reduce_scratch(plan, width, flow=0):
    counts = [sum(c) for c in Reduce.slot_counts(plan, flow)]
    return [
        pltpu.VMEM((plan.hh, plan.ny * width), jnp.bfloat16),
        pltpu.VMEM((plan.hh, plan.ny // 2 * width), jnp.bfloat16),
        *[pltpu.VMEM((c, cut[1], width), jnp.bfloat16) for c, cut in zip(counts, plan.whole_cuts)],
        pltpu.SemaphoreType.DMA((len(plan.whole_cuts), plan.blocks // 2)),
        pltpu.SemaphoreType.DMA((2, len(plan.whole_cuts), plan.blocks // 2)),
        *[pltpu.SemaphoreType.DMA((c,)) for c in counts],
    ]


def reduce_from(plan, width, refs, flow=0):
    n = len(plan.whole_cuts)
    part, twin, slots, sems, recv = refs[0], refs[1], refs[2:2 + n], refs[2 + n:4 + n], refs[4 + n:]
    return Reduce(plan, width, part, twin, slots, *sems, recv, flow)


def reduce_kernel(plan, width, factor, x_ref, o_ref, *rest):
    reduce = reduce_from(plan, width, rest[:-1])
    load = pltpu.make_async_copy(x_ref, reduce.part, rest[-1])
    load.start()
    greet(plan)
    load.wait()
    reduce.start_twin()
    for item in reduce.items():
        item()
    reduce.own_sum(o_ref, factor)
    reduce.finish_sends()


def reduce_all(plan, value, factor, collective_id):
    width = value.shape[1] // plan.ny
    return pl.pallas_call(
        functools.partial(reduce_kernel, plan, width, factor),
        out_shape=jax.ShapeDtypeStruct((plan.hp, width), jnp.float32),
        in_specs=[pl.BlockSpec(memory_space=pl.ANY)],
        out_specs=pl.BlockSpec(memory_space=pltpu.VMEM),
        scratch_shapes=[*reduce_scratch(plan, width), pltpu.SemaphoreType.DMA],
        compiler_params=pltpu.CompilerParams(
            collective_id=collective_id, has_side_effects=True, vmem_limit_bytes=60 * 1024 * 1024),
    )(value)


def backward_kernel(plan, total_cells, *refs):
    (part_hbm, up_hbm, small_hbm, layers_hbm, scaled_hbm, keep_hbm, sample_ref, rows_ref, loss_ref,
     center_ref, log_var_ref, draws_ref,
     readout_out, sums_out, small_part, grad_ref,
     small_ref, up_ref, layer_ref, scaled_ref, keep_ref, lane_ref, column_ref, latent_ref,
     moment_ref, wide, tall, meet_send, meet_recv, load_sem, *rest) = refs
    reduce = reduce_from(plan, plan.frame, rest)

    def load(k):
        slot = k % 2
        return (
            pltpu.make_async_copy(scaled_hbm.at[k], scaled_ref.at[slot], load_sem.at[3 * slot]),
            pltpu.make_async_copy(keep_hbm.at[k], keep_ref.at[slot], load_sem.at[3 * slot + 1]),
        )

    def load_layer(k):
        return pltpu.make_async_copy(
            layers_hbm.at[k], layer_ref.at[k % 2, pl.ds(0, plan.hh), :], load_sem.at[3 * (k % 2) + 2])

    frames = [pltpu.make_async_copy(
        part_hbm.at[:, pl.ds(start, plan.frame)],
        reduce.part.at[:, pl.ds(j * plan.frame, plan.frame)], load_sem.at[6 + j])
        for j, start in enumerate(plan.frame_start)]
    second = pltpu.make_async_copy(up_hbm, up_ref, load_sem.at[6 + plan.ny])
    third = pltpu.make_async_copy(small_hbm, small_ref, load_sem.at[7 + plan.ny])
    for copy in frames:
        copy.start()
    second.start()
    for copy in load(3):
        copy.start()
    third.start()
    load_layer(2).start()
    for copy in load(2):
        copy.start()
    load_layer(1).start()
    peers = Meet.peers(plan)
    barrier = pltpu.get_barrier_semaphore()
    for device in peers:
        pl.semaphore_signal(barrier, inc=1, device_id=device, device_id_type=MESH)
    pl.semaphore_wait(barrier, len(peers))
    for copy in frames:
        copy.wait()
    reduce.start_twin()
    tail = layer_ref.shape[1] - plan.hh
    if tail:
        for k in range(2):
            layer_ref[k, plan.hh:, :] = jnp.zeros((tail, plan.cells), jnp.bfloat16)
    latent_ref[...] = jnp.zeros_like(latent_ref)

    todo = reduce.items()
    todo.append(lambda: reduce.own_sum(readout_out, 1.0 / total_cells))

    def between(second):
        if todo:
            todo.pop(0)()

    def layer(k):
        slot = k % 2
        for copy in load(k):
            copy.wait()

        def columns(i):
            slab = small_ref.at[:, pl.ds(plan.ol + plan.ll - LANES, LANES)]
            base = plan.latent - (plan.ll - LANES)
            column_ref[0] = unit_column(slab, i, base + k)
            column_ref[1] = unit_column(slab, i, base + 4 + k)
            column_ref[2] = as_column(
                lax.rsqrt(rows_ref[k, 1:2, aligned(i * LANES)] / total_cells + norm_eps))

        def block(i, _):
            columns(i)

            def chunk(j, _):
                rows = aligned(i * LANES + j * 16, 16)
                here = aligned(j * 16, 16)
                gain, bias = tiled(column_ref[0, here, :], plan), tiled(column_ref[1, here, :], plan)
                scaled = scaled_ref[slot, rows, :]
                normed = gain * scaled + bias
                sigma = jax.nn.sigmoid(normed)
                slope = up_ref[rows, :] * keep_ref[slot, rows, :].astype(jnp.float32) * sigma * (
                    1.0 + normed * (1.0 - sigma))
                up_ref[rows, :] = slope
                lane_ref[0, here, :] = lane_sums(slope)
                lane_ref[1, here, :] = lane_sums(slope * scaled)
                return 0
            lax.fori_loop(0, LANES // 16, chunk, 0)
            sums_out[k, 0:1, aligned(i * LANES)] = as_row(lane_ref[0])
            sums_out[k, 1:2, aligned(i * LANES)] = as_row(lane_ref[1])
            return 0
        lax.fori_loop(0, plan.hh // LANES, block, 0)
        sums_out[k, 2:3, :] = jnp.broadcast_to(own_loss, (1, plan.hh))
        meet = Meet(plan, wide.at[k], tall.at[k], meet_send.at[k], meet_recv.at[k])
        sums_out[k] = meet.run(sums_out[k], merge_sums, 1.0, between)

        def last(i, _):
            columns(i)
            column_ref[3] = as_column(sums_out[k, 0:1, aligned(i * LANES)] / total_cells)
            column_ref[4] = as_column(sums_out[k, 1:2, aligned(i * LANES)] / total_cells)

            def chunk(j, _):
                rows = aligned(i * LANES + j * 16, 16)
                here = aligned(j * 16, 16)
                factor = tiled(column_ref[0, here, :] * column_ref[2, here, :], plan)
                shift, gain = tiled(column_ref[3, here, :], plan), tiled(column_ref[4, here, :], plan)
                grad = factor * (up_ref[rows, :] - (shift + scaled_ref[slot, rows, :] * gain))
                grad_ref[rows, :] = grad.astype(jnp.bfloat16)
                return 0
            lax.fori_loop(0, LANES // 16, chunk, 0)
            return 0
        lax.fori_loop(0, plan.hh // LANES, last, 0)
        if k >= 2:
            for copy in load(k - 2):
                copy.start()

    def put(j, lane, value):
        at = j * plan.small + lane
        small_part[:, at:at + value.shape[1]] = value.astype(jnp.bfloat16)

    def middle(source, lane):
        for j in range(plan.ny):
            at, row = j * plan.small + lane, j * plan.midp
            put(j, lane, over_cells(grad_ref[...], source[row:row + plan.midl, :]))
            if j % 2:
                between(None)
            up_ref[row:row + plan.midp, :] = over_rows(
                small_ref[:, at:at + plan.midl], grad_ref[...])[:plan.midp]

    kl_terms = (jnp.exp(log_var_ref[...]) + center_ref[...] * center_ref[...] - 1.0 - log_var_ref[...])
    own_loss = (0.5 * jnp.sum(jnp.sum(loss_ref[...], axis=0, keepdims=True), axis=1, keepdims=True)
                + kl_weight * 0.5 * jnp.sum(
                    jnp.sum(kl_terms, axis=0, keepdims=True), axis=1, keepdims=True))
    second.wait()
    third.wait()
    layer(3)
    load_layer(2).wait()
    middle(layer_ref.at[0], plan.o4)
    load_layer(0).start()
    layer(2)
    lifting = over_cells(grad_ref[...], sample_ref[...])
    for j in range(plan.ny):
        put(j, plan.ol, lifting)
    reach = over_rows(small_ref[:, plan.ol:plan.ol + plan.ll], grad_ref[...])[:plan.latent]
    center, log_var = center_ref[...], log_var_ref[...]
    latent_ref[0, 0:plan.latent, :] = reach + kl_weight * center
    latent_ref[1, 0:plan.latent, :] = (
        reach * 0.5 * jnp.exp(0.5 * log_var) * draws_ref[...]
        + kl_weight * 0.5 * (jnp.exp(log_var) - 1.0))
    half, tall_rows = plan.ny // 2, round_up(plan.moments, 16)
    moment_ref[...] = jnp.zeros_like(moment_ref)
    for j in range(plan.ny):
        spot = (j % half) * plan.moments
        piece = latent_ref[j // half, spot:spot + tall_rows, :]
        row = lax.broadcasted_iota(jnp.int32, piece.shape, 0)
        piece = jnp.where(row < plan.moments, piece, 0.0)
        moment_ref[j * plan.ml:j * plan.ml + tall_rows, :] = piece.astype(jnp.bfloat16)
    load_layer(1).wait()
    for j in range(plan.ny):
        at, row = j * plan.small + plan.op, j * plan.ml
        moments = moment_ref[row:row + plan.ml, :]
        put(j, plan.op, over_cells(layer_ref[1, 0:plan.hh, :], moments))
        part = rows_dot(small_ref[:, at:at + plan.ml], moments)
        up_ref[...] = part if j == 0 else up_ref[...] + part
    layer(1)
    load_layer(0).wait()
    middle(layer_ref.at[0], plan.o2)
    layer(0)
    while todo:
        between(False)
    reduce.finish_sends()


def backward_all(plan, total_cells, *arrays):
    any_spec, vmem = pl.BlockSpec(memory_space=pl.ANY), pl.BlockSpec(memory_space=pltpu.VMEM)
    f32, bf16 = jnp.float32, jnp.bfloat16
    n = plan.nx + plan.ny - 2
    shape = jax.ShapeDtypeStruct
    return pl.pallas_call(
        functools.partial(backward_kernel, plan, total_cells),
        out_shape=[
            shape((plan.hp, plan.frame), f32), shape((4, 3, plan.hh), f32),
            shape((plan.hh, plan.ny * plan.small), bf16), shape((plan.hh, plan.cells), bf16)],
        in_specs=[any_spec] * 6 + [vmem] * 6,
        out_specs=[vmem] * 4,
        scratch_shapes=[
            pltpu.VMEM((plan.hh, plan.ny * plan.small), bf16),
            pltpu.VMEM((plan.hh, plan.cells), f32),
            pltpu.VMEM((2, plan.hh + plan.midl - plan.midp, plan.cells), bf16),
            pltpu.VMEM((2, plan.hh, plan.cells), f32),
            pltpu.VMEM((2, plan.hh, plan.cells), bf16),
            pltpu.VMEM((2, LANES, LANES), f32),
            pltpu.VMEM((5, LANES, LANES), f32),
            pltpu.VMEM((2, plan.ll, plan.cells), f32),
            pltpu.VMEM((plan.ny * plan.ml, plan.cells), bf16),
            pltpu.VMEM((4, plan.nx, 3, plan.hh), f32),
            pltpu.VMEM((4, plan.ny, 3, plan.hh), f32),
            pltpu.SemaphoreType.DMA((4, n)),
            pltpu.SemaphoreType.DMA((4, n)),
            pltpu.SemaphoreType.DMA((8 + plan.ny,)),
            *reduce_scratch(plan, plan.frame),
        ],
        compiler_params=pltpu.CompilerParams(
            collective_id=6, has_side_effects=True, vmem_limit_bytes=60 * 1024 * 1024),
    )(*arrays)


def embed_kernel(plan, total_cells, *refs):
    (small_hbm, x_hbm, grad_ref, readout_ref, embed_out, small_out, row_out, block_out,
     x_ref, wide, tall, meet_send, meet_recv, load_sem, *rest) = refs
    half = len(rest) // 2
    small = reduce_from(plan, plan.small, rest[:half])
    embed = reduce_from(plan, plan.frame, rest[half:])
    first = pltpu.make_async_copy(small_hbm, small.part, load_sem.at[0])
    second = pltpu.make_async_copy(x_hbm, x_ref, load_sem.at[1])
    first.start()
    second.start()
    peers = Meet.peers(plan)
    barrier = pltpu.get_barrier_semaphore()
    for device in peers:
        pl.semaphore_signal(barrier, inc=1, device_id=device, device_id_type=MESH)
    pl.semaphore_wait(barrier, len(peers))
    first.wait()
    small.start_twin()
    second.wait()
    factor = 1.0 / total_cells
    queue = small.items()

    def tick():
        if queue:
            queue.pop(0)()

    piece = plan.frame // 3 // LANES * LANES
    for j in range(plan.ny):
        start, stop = plan.frame_start[j], min(plan.frame_start[j] + plan.frame, plan.genes)
        for at in range(start, stop, piece):
            end = min(at + piece, stop)
            to = j * plan.frame + at - start
            embed.part[:, to:to + end - at] = over_cells(
                grad_ref[...], x_ref[at:end, :]).astype(jnp.bfloat16)
            tick()
        done = stop - start
        if done < plan.frame:
            inside = done // LANES * LANES
            lanes = lax.broadcasted_iota(jnp.int32, (plan.hh, LANES), 1)
            at = j * plan.frame + inside
            if inside < done:
                value = embed.part[:, at:at + LANES]
                embed.part[:, at:at + LANES] = jnp.where(
                    lanes < done - inside, value.astype(jnp.float32), 0.0).astype(jnp.bfloat16)
                inside += LANES
            for at in range(j * plan.frame + inside, (j + 1) * plan.frame, LANES):
                embed.part[:, at:at + LANES] = jnp.zeros((plan.hh, LANES), jnp.bfloat16)
        embed.twin_column(j)
        tick()
    todo = embed.items()
    first_items = 4
    for item in todo[:first_items]:
        item()
    while queue:
        tick()
    small.own_sum(small_out, factor)
    meet = Meet(plan, wide, tall, meet_send, meet_recv)
    wide[meet.gx, :, 0:plan.frame] = readout_ref[plan.h:plan.h + 1, :]
    wide[meet.gx, :, plan.frame:] = small_out[plan.h:plan.h + 1, plan.op:plan.op + plan.ml]
    tall[meet.gy] = small_out[:, plan.ol:plan.ol + plan.ll]
    copies = meet.copies(False) + meet.copies(True)
    for copy in copies:
        copy.start()
    for item in todo[first_items:]:
        item()
    for copy in copies:
        copy.wait_recv()
    row_out[...] = wide[0]
    block_out[...] = tall[0]
    embed.own_sum(embed_out, factor)
    for copy in copies:
        copy.wait_send()
    small.finish_sends()
    embed.finish_sends()


def embed_all_sums(plan, total_cells, *arrays):
    any_spec, vmem = pl.BlockSpec(memory_space=pl.ANY), pl.BlockSpec(memory_space=pltpu.VMEM)
    f32, bf16 = jnp.float32, jnp.bfloat16
    n = plan.nx + plan.ny - 2
    shape = jax.ShapeDtypeStruct
    row, block = (1, plan.frame + plan.ml), (plan.hp, plan.ll)
    return pl.pallas_call(
        functools.partial(embed_kernel, plan, total_cells),
        out_shape=[shape((plan.hp, plan.frame), f32), shape((plan.hp, plan.small), f32),
                   shape(row, f32), shape(block, f32)],
        in_specs=[any_spec] * 2 + [vmem] * 2,
        out_specs=[vmem] * 4,
        scratch_shapes=[
            pltpu.VMEM((plan.genes, plan.cells), bf16),
            pltpu.VMEM((plan.nx, *row), f32),
            pltpu.VMEM((plan.ny, *block), f32),
            pltpu.SemaphoreType.DMA((n,)),
            pltpu.SemaphoreType.DMA((n,)),
            pltpu.SemaphoreType.DMA((2,)),
            *reduce_scratch(plan, plan.small),
            *reduce_scratch(plan, plan.frame),
        ],
        compiler_params=pltpu.CompilerParams(
            collective_id=7, has_side_effects=True, vmem_limit_bytes=60 * 1024 * 1024),
    )(*arrays)


def output_kernel(plan, chunk, w_ref, layer_ref, x_ref, flag_ref, pick_ref,
                  out_ref, og_ref, part_ref, up_ref, loss_ref):
    i = pl.program_id(0)

    @pl.when(i == 0)
    def _():
        up_ref[...] = jnp.zeros_like(up_ref)
        loss_ref[...] = jnp.zeros_like(loss_ref)
    weight, layer = w_ref[...], layer_ref[0]
    raw = over_rows(weight, layer)
    slab = over_rows(flag_ref[...].astype(jnp.float32).astype(jnp.bfloat16), pick_ref[...])
    out_ref[...] = raw.astype(jnp.bfloat16)
    residual = raw - x_ref[...].astype(jnp.float32)
    inside = lax.broadcasted_iota(jnp.int32, raw.shape, 0) + i * chunk < plan.genes
    weighted = jnp.where(inside, slab * residual, 0.0)
    grad = weighted.astype(jnp.bfloat16)
    og_ref[...] = grad
    terms = lane_sums(jnp.where(inside, weighted * residual, 0.0))
    loss_ref[...] += jnp.sum(terms.reshape(chunk // 8, 8, LANES), axis=0)
    part_ref[...] = over_cells(layer, grad).astype(jnp.bfloat16)
    up_ref[...] += rows_dot(weight, grad)


def output_all(plan, readout_all, layers, profiles, flags, picker):
    chunk = 4 * LANES
    steps = plan.gg // chunk
    f32, bf16 = jnp.float32, jnp.bfloat16
    shape = jax.ShapeDtypeStruct
    studies = flags.shape[0]
    return pl.pallas_call(
        functools.partial(output_kernel, plan, chunk),
        grid=(steps,),
        out_shape=[shape((plan.genes, plan.cells), bf16), shape((plan.gg, plan.cells), bf16),
                   shape((plan.hh, plan.gg), bf16), shape((plan.hh, plan.cells), f32),
                   shape((8, LANES), f32)],
        in_specs=[
            pl.BlockSpec((plan.hh, chunk), lambda i: (0, i)),
            pl.BlockSpec((1, plan.hh, plan.cells), lambda i: (3, 0, 0)),
            pl.BlockSpec((chunk, plan.cells), lambda i: (i, 0)),
            pl.BlockSpec((studies, chunk), lambda i: (0, i)),
            pl.BlockSpec((studies, plan.cells), lambda i: (0, 0))],
        out_specs=[
            pl.BlockSpec((chunk, plan.cells), lambda i: (i, 0)),
            pl.BlockSpec((chunk, plan.cells), lambda i: (i, 0)),
            pl.BlockSpec((plan.hh, chunk), lambda i: (0, i)),
            pl.BlockSpec((plan.hh, plan.cells), lambda i: (0, 0)),
            pl.BlockSpec((8, LANES), lambda i: (0, 0))],
        compiler_params=pltpu.CompilerParams(vmem_limit_bytes=48 * 1024 * 1024),
    )(readout_all, layers, profiles, flags, picker)


def input_kernel(w_ref, grad_ref, og_ref, out_ref):
    back = over_rows(w_ref[...], grad_ref[...])
    out_ref[...] = (back - og_ref[...].astype(jnp.float32)).astype(jnp.bfloat16)


def input_all(plan, embed_all, grad, output_grad):
    chunk = 14 * LANES
    return pl.pallas_call(
        input_kernel,
        grid=(plan.gg // chunk,),
        out_shape=jax.ShapeDtypeStruct((plan.genes, plan.cells), jnp.bfloat16),
        in_specs=[
            pl.BlockSpec((plan.hh, chunk), lambda i: (0, i)),
            pl.BlockSpec((plan.hh, plan.cells), lambda i: (0, 0)),
            pl.BlockSpec((chunk, plan.cells), lambda i: (i, 0))],
        out_specs=pl.BlockSpec((chunk, plan.cells), lambda i: (i, 0)),
        compiler_params=pltpu.CompilerParams(vmem_limit_bytes=48 * 1024 * 1024),
    )(embed_all, grad, output_grad)


def rows_dot(left, right):
    return lax.dot_general(left, right, (((1,), (0,)), ((), ())), preferred_element_type=jnp.float32)


def over_cells(left, right):
    return lax.dot_general(left, right, (((1,), (1,)), ((), ())), preferred_element_type=jnp.float32)


def over_rows(left, right):
    return lax.dot_general(left, right, (((0,), (0,)), ((), ())), preferred_element_type=jnp.float32)


def pad_to(value, rows, lanes):
    return jnp.pad(value, ((0, rows - value.shape[0]), (0, lanes - value.shape[1])))


def middle_piece(plan, matrix):
    turned = matrix.T.reshape(plan.h, plan.groups, plan.h)
    wide = jnp.pad(turned, ((0, plan.hp - plan.h), (0, 0), (0, plan.hp - plan.h)))
    return pad_to(wide.reshape(plan.hp, plan.midp), plan.hp, plan.midl)


def middle_back(plan, piece):
    cut = piece[:plan.h, :plan.midp].reshape(plan.h, plan.groups, plan.hp)[:, :, :plan.h]
    return cut.reshape(plan.h, plan.mid).T


def with_row(plan, block, row, first):
    spare = jnp.where(first, row, jnp.zeros_like(row))[None]
    return pad_to(jnp.concatenate([block, spare], axis=0), plan.hp, block.shape[1])


def on_device(
    nx, ny,
    transcript_profiles,
    experiment_labels,
    measured_flags,
    retained_unit_flags,
    standard_normal_draws,
    compressor_first_matrix,
    compressor_second_matrix,
    posterior_matrix,
    posterior_intercepts,
    expander_first_matrix,
    expander_second_matrix,
    output_matrix,
    output_intercept,
    normalizer_factors,
    normalizer_translations,
):
    cells = transcript_profiles.shape[0]
    plan = Plan(nx, ny, cells, output_matrix.shape[1], output_matrix.shape[0], expander_first_matrix.shape[0])
    total_cells = float(cells * nx * ny)
    gx, gy = lax.axis_index("gx"), lax.axis_index("gy")
    first = gx == 0

    wide = jnp.concatenate([
        pad_to(compressor_first_matrix.T, plan.hp, plan.g),
        with_row(plan, output_matrix, output_intercept, first)], axis=0)
    strip = lax.ppermute(wide[:, :plan.strip], "gy", [(j + 1, j) for j in range(ny - 1)])
    wide = jnp.concatenate([wide, strip], axis=1)
    wide = pad_to(wide, 2 * plan.hp, plan.gp + plan.strip + plan.shift * ny)
    wide = lax.dynamic_slice_in_dim(wide, gy * plan.shift, plan.gp, 1)
    norms = jnp.concatenate([normalizer_factors.T, normalizer_translations.T], axis=1)
    last = jnp.concatenate([expander_first_matrix.T, norms], axis=1)
    tile = jnp.where(gy == ny - 1, pad_to(norms, plan.hp, LANES), wide[:plan.hp, plan.gp - LANES:])
    first_piece = jnp.concatenate([wide[:plan.hp, :plan.gp - LANES], tile], axis=1)
    small = jnp.concatenate([
        middle_piece(plan, compressor_second_matrix),
        middle_piece(plan, expander_second_matrix),
        pad_to(with_row(plan, posterior_matrix, posterior_intercepts, first), plan.hp, plan.ml),
        pad_to(last, plan.hp, plan.ll)], axis=1)
    profiles = transcript_profiles.T
    draws = standard_normal_draws.T
    (embed_all, small_all, readout_all, center, log_var, sample, layers, scaled_values, keep_values,
     norm_rows) = forward_all(
        plan, total_cells, first_piece, small, wide[plan.hp:], profiles,
        jnp.swapaxes(retained_unit_flags, 1, 2), draws)
    picker = (jnp.arange(measured_flags.shape[0], dtype=jnp.int32)[:, None]
              == experiment_labels[None, :]).astype(jnp.bfloat16)
    output, output_grad, readout_part, upstream, losses = output_all(
        plan, readout_all, layers, profiles, measured_flags, picker)
    def frames(product):
        padded = pad_to(product, plan.hh, max(product.shape[1], max(plan.frame_start) + plan.frame))
        return jnp.concatenate(
            [padded[:, s:s + plan.frame] for s in plan.frame_start], axis=1).astype(jnp.bfloat16)

    if plan.fits:
        readout_sum, sums, small_part, grad_one = backward_all(
            plan, total_cells, readout_part, upstream, small_all, layers, scaled_values, keep_values,
            sample, norm_rows, losses, center, log_var, draws)
        loss_sum = sums[0, 2, 0]
        gains_sum, shifts_sum = [sums[k, 1] for k in range(4)], [sums[k, 0] for k in range(4)]
        embed_sum, small_sum, row, lifting_own = embed_all_sums(
            plan, total_cells, small_part, profiles, grad_one, readout_sum)
    else:
        diverge = 0.5 * jnp.sum(jnp.exp(log_var) + center * center - 1.0 - log_var)
        own_loss = 0.5 * jnp.sum(losses) + kl_weight * diverge
        parts = small_all.reshape(plan.hh, ny, plan.small)
        encoder_all = parts[:, :, plan.o2:plan.o2 + plan.midp].reshape(plan.hh, plan.hh)
        decoder_all = parts[:, :, plan.o4:plan.o4 + plan.midp].reshape(plan.hh, plan.hh)
        projector_all = parts[:, :, plan.op:plan.op + plan.moments].reshape(plan.hh, 2 * plan.latent)
        lifting_all = parts[:, 0, plan.ol:plan.ol + plan.latent]
        rows = parts[:, 0, plan.ol + plan.latent:plan.ol + plan.latent + 8].astype(jnp.float32)
        gains = [rows[:, k:k + 1] for k in range(4)]
        biases = [rows[:, 4 + k:5 + k] for k in range(4)]

        spread = jnp.exp(0.5 * log_var)

        def kept_layer(k):
            inverse = lax.rsqrt(norm_rows[k, 1] / total_cells + norm_eps)[:, None]
            return layers[k], gains[k] * scaled_values[k] + biases[k], scaled_values[k], inverse

        one, two, three, four = (kept_layer(k) for k in range(4))

        def backward_layer(upstream, kept, k, loss, ident):
            _, normed, scaled, inverse = kept
            sigma = jax.nn.sigmoid(normed)
            slope = upstream * keep_values[k].astype(jnp.float32) * sigma * (
                1.0 + normed * (1.0 - sigma))
            pair = jnp.stack([jnp.sum(slope, axis=1), jnp.sum(slope * scaled, axis=1),
                              jnp.full((plan.hh,), loss)])
            merged = meet_all(plan, pair, merge_sums, 2)
            shift, gain = merged[0], merged[1]
            grad = gains[k] * inverse * (
                slope - (shift[:, None] + scaled * gain[:, None]) / total_cells)
            return grad.astype(jnp.bfloat16), gain, shift, merged[2, 0]

        grad_four, gain_four, shift_four, loss_sum = backward_layer(upstream, four, 3, own_loss, 5)
        upstream = over_rows(decoder_all, grad_four)
        grad_three, gain_three, shift_three, _ = backward_layer(upstream, three, 2, own_loss, 6)
        sample_grad = over_rows(lifting_all, grad_three)[:plan.latent]
        center_grad = sample_grad + kl_weight * center
        logvar_grad = sample_grad * 0.5 * spread * draws + kl_weight * 0.5 * (jnp.exp(log_var) - 1.0)
        moment_grad = jnp.concatenate([center_grad, logvar_grad], axis=0).astype(jnp.bfloat16)
        upstream = rows_dot(projector_all, moment_grad)
        grad_two, gain_two, shift_two, _ = backward_layer(upstream, two, 1, own_loss, 7)
        upstream = over_rows(encoder_all, grad_two)
        grad_one, gain_one, shift_one, _ = backward_layer(upstream, one, 0, own_loss, 8)
        gains_sum = [gain_one, gain_two, gain_three, gain_four]
        shifts_sum = [shift_one, shift_two, shift_three, shift_four]
        encoder_part = over_cells(grad_two, one[0]).reshape(plan.hh, ny, plan.midp)
        decoder_part = over_cells(grad_four, three[0]).reshape(plan.hh, ny, plan.midp)
        projector_part = over_cells(two[0], moment_grad).reshape(plan.hh, ny, plan.moments)
        lifting_part = over_cells(grad_three, sample)[:, :plan.latent]

        def lanes(value, width):
            return jnp.pad(value, ((0, 0), (0, 0), (0, width - value.shape[2])))

        small_part = jnp.concatenate([
            lanes(encoder_part, plan.midl), lanes(decoder_part, plan.midl),
            lanes(projector_part, plan.ml),
            jnp.broadcast_to(pad_to(lifting_part, plan.hh, plan.ll)[:, None, :], (plan.hh, ny, plan.ll)),
        ], axis=2).reshape(plan.hh, ny * plan.small).astype(jnp.bfloat16)
        embed_part = frames(over_cells(grad_one, profiles))

        readout_sum = reduce_all(plan, frames(readout_part), 1.0 / total_cells, 3)
        small_sum = reduce_all(plan, small_part, 1.0 / total_cells, 4)
        embed_sum = reduce_all(plan, embed_part, 1.0 / total_cells, 3)

        row, lifting_own = share_all(plan, jnp.concatenate([
            readout_sum[plan.h:plan.h + 1],
            small_sum[plan.h:plan.h + 1, plan.op:plan.op + plan.ml]], axis=1),
            small_sum[:, plan.ol:plan.ol + plan.ll], 5)
    input_grad = input_all(plan, embed_all, grad_one, output_grad)

    starts = jnp.array([plan.g * j - plan.frame_start[j] for j in range(ny)], jnp.int32)
    readout_own = lax.dynamic_slice_in_dim(readout_sum, starts[gy], plan.g, 1)
    embed_own = lax.dynamic_slice_in_dim(embed_sum, starts[gy], plan.g, 1)
    baseline_own = lax.dynamic_slice_in_dim(row[0, :plan.frame], starts[gy], plan.g, 0)

    def own_units(values):
        stack = jnp.stack(values, axis=0) / total_cells
        return lax.dynamic_slice_in_dim(stack, gx * plan.hp, plan.h, 1)

    small_h = small_sum[:plan.h]
    return (
        output.T,
        center.T,
        loss_sum / total_cells,
        input_grad.T,
        embed_own[:plan.h].T,
        middle_back(plan, small_sum[:, plan.o2:plan.o2 + plan.midl]),
        small_h[:, plan.op:plan.op + plan.moments],
        row[0, plan.frame:plan.frame + plan.moments],
        lifting_own[:plan.h, :plan.latent].T,
        middle_back(plan, small_sum[:, plan.o4:plan.o4 + plan.midl]),
        readout_own[:plan.h],
        baseline_own,
        own_units(gains_sum),
        own_units(shifts_sum),
    )


def solution(mesh):
    return jax.shard_map(
        functools.partial(on_device, mesh.shape["gx"], mesh.shape["gy"]),
        mesh=mesh,
        in_specs=(
            P(("gx", "gy"), None),
            P(("gx", "gy")),
            P(),
            P(None, ("gx", "gy"), None),
            P(("gx", "gy"), None),
            P("gy", "gx"),
            P("gy", "gx"),
            P("gx", "gy"),
            P("gy"),
            P(None, "gx"),
            P("gy", "gx"),
            P("gx", "gy"),
            P("gy"),
            P(None, "gx"),
            P(None, "gx"),
        ),
        out_specs=(
            P(("gx", "gy"), None),
            P(("gx", "gy"), None),
            P(),
            P(("gx", "gy"), None),
            P("gy", "gx"),
            P("gy", "gx"),
            P("gx", "gy"),
            P("gy"),
            P(None, "gx"),
            P("gy", "gx"),
            P("gx", "gy"),
            P("gy"),
            P(None, "gx"),
            P(None, "gx"),
        ),
        check_vma=False,
    )
```
